32 devices in a mesh: dp: 4 (over x, core), expert: 8 (over z, y).
Axes of the slice: x: 2, y: 2, z: 4, core: 2. Of those that a mesh axis runs over, the one named last changes fastest.
Arguments:
- tokens: bfloat16 [8, 1536, 768], P('expert', 'dp'), may hold values from -6 to 6
- doc_lengths: int32 [8, 4, 4], P('expert', 'dp'), may hold values from 1 to 64, 128 in all within a row
- assign: int32 [8, 1536, 1], P('expert', 'dp'), may hold values from 0 to 7, as said below
- ln_gain: float32 [768, 4], replicated, may hold values from 0.5 to 1.5
- ln_bias: float32 [768, 4], replicated, may hold values from -1 to 1
- attn_in: bfloat16 [768, 2, 2304], replicated, may hold values from -0.21875 to 0.21875
- attn_out: bfloat16 [768, 2, 768], replicated, may hold values from -0.875 to 0.875
- ffn_in: bfloat16 [768, 3072], replicated, may hold values from -0.21875 to 0.21875
- ffn_out: bfloat16 [3072, 768], replicated, may hold values from -0.109375 to 0.109375
- router: bfloat16 [768, 8], replicated, may hold values from -0.14941406 to 0.14941406
- expert_in: bfloat16 [8, 768, 3072], P('expert'), may hold values from -0.21875 to 0.21875
- expert_out: bfloat16 [8, 3072, 768], P('expert'), may hold values from -0.21875 to 0.21875
- cotangent: bfloat16 [8, 1536, 768], P('expert', 'dp'), may hold values from -6 to 6
Outputs:
- output: bfloat16 [8, 1536, 768], P('expert', 'dp')
- balance: float32 [], replicated
- grad_tokens: bfloat16 [8, 1536, 768], P('expert', 'dp')
- grad_ln_gain: float32 [768, 4], P('dp')
- grad_ln_bias: float32 [768, 4], P('dp')
- grad_attn_in: float32 [768, 2, 2304], P('dp')
- grad_attn_out: float32 [768, 2, 768], P('dp')
- grad_ffn_in: float32 [768, 3072], P('dp')
- grad_ffn_out: float32 [3072, 768], P('dp')
- grad_router: float32 [768, 8], P('dp')
- grad_expert_in: float32 [8, 768, 3072], P('expert', 'dp')
- grad_expert_out: float32 [8, 3072, 768], P('expert', 'dp')
The draws below stay inside these ranges and needn't reach their ends.
Inputs may be any that keep to these rules, and one draw needn't show every extreme that they name: `doc_lengths`: the 4 lengths of one device sum to 128. `assign`: every expert is named by some token.
All inputs are finite; a program needn't handle non-finite values.
Results may differ from the reference program's by a relative error of at most 0.022.
Values may be sent and summed in bfloat16 or wider, within the bound.
A program may use at most 320 MiB of HBM per device.

```python
import math
import jax
import jax.numpy as jnp
import numpy as np
from jax import lax

D = 768
HEADS = 12
HEAD_DIM = 64
FF = 3072
DOCS = 4
LONG_DEV = 256
SHORT_DEV = 128
TOK_DEV = 384
GROUPS = 8
GROUP_TOK = 1536
TOKENS = 12288
EXPERTS = 8
CAP = 60
N_DP = 4


def draw_assign(key, part):
    key = jax.random.fold_in(key, 7)
    first_key, second_key, third_key = jax.random.split(key, 3)
    block_count = GROUP_TOK // TOK_DEV
    stride = EXPERTS // block_count
    group_ids = jnp.arange(GROUPS, dtype=jnp.int32)[:, None]
    row_ids = jnp.arange(GROUP_TOK, dtype=jnp.int32)[None, :]
    block_ids = row_ids // TOK_DEV
    hot_expert = block_ids * stride + group_ids % stride
    hot_limit = 50 + 450 * block_ids // max(block_count - 1, 1)
    ticket = jax.random.randint(first_key, (GROUPS, GROUP_TOK), 0, 1000, dtype=jnp.int32)
    offset = jax.random.randint(second_key, (GROUPS, GROUP_TOK), 1, 4, dtype=jnp.int32)
    spread_pick = jax.random.randint(third_key, (GROUPS, GROUP_TOK), 0, EXPERTS, dtype=jnp.int32)
    picked = jnp.where(ticket < hot_limit, hot_expert, jnp.where(ticket < hot_limit + 150, (hot_expert + offset) % EXPERTS, spread_pick))
    flat_index = group_ids * GROUP_TOK + row_ids
    picked = jnp.where(flat_index < EXPERTS, flat_index, picked)
    return picked[..., None].astype(jnp.int32)


def level_of(stream_key, shape, cuts, low, top_value):
    def one(position, blocks):
        steps = jax.random.uniform(jax.random.fold_in(jax.random.fold_in(stream_key, 6), position), (blocks,), jnp.float32, low / len(cuts), top_value / len(cuts))
        return jnp.repeat(jnp.exp(steps), shape[position] // blocks).reshape((-1,) + (1,) * (len(shape) - position - 1))

    gain = one(*cuts[0])
    for cut in cuts[1:]:
        gain = gain * one(*cut)
    return gain


def profile(count, total, limit, slope):
    portions = [(1 << 20) // math.isqrt(standing ** slope) + 1 for standing in range(2, count + 1)]
    surplus, given = total - limit - (count - 1), [1] * (count - 1)
    while surplus > 0:
        candidates = [i for i in range(count - 1) if given[i] < limit]
        whole, budget = sum([portions[i] for i in candidates]), surplus
        for i in candidates:
            extra = min(limit - given[i], max(1, budget * portions[i] // whole), surplus)
            given[i] = given[i] + extra
            surplus = surplus - extra
    return np.array([limit] + given)


def ragged_sizes(own_key, number_of, total, reach, skew):
    if number_of == 2:
        one = jax.random.randint(own_key, (), max(1, total - reach), min(reach, total - 1) + 1)
        return jnp.stack([one, total - one])
    tallies = jnp.asarray(profile(number_of, total, reach, skew), jnp.int32)
    twos = (number_of - 1) // 2
    donor, taker = tallies[1:1 + 2 * twos:2], tallies[2:2 + 2 * twos:2]
    slack = jnp.minimum(donor - 1, reach - taker)
    shifted = jax.random.randint(jax.random.fold_in(own_key, 1), (twos,), 0, 1 << 20) % (slack + 1)
    tallies = tallies.at[1:1 + 2 * twos:2].set(donor - shifted).at[2:2 + 2 * twos:2].set(taker + shifted)
    return tallies[jax.random.permutation(jax.random.fold_in(own_key, 2), number_of)]


def scatter_about(key, shape, scale, bound, cuts=(), kind=jnp.bfloat16):
    loudness = level_of(key, shape, cuts, -0.22, 0.18) if cuts else 1.0
    entries = jax.random.normal(key, shape, jnp.float32) * scale * loudness
    return jnp.minimum(jnp.maximum(entries, -bound), bound).astype(kind)


def setup_inputs(seed: int = 0) -> dict:
    keys = jax.random.split(jax.random.key(seed), 14)
    return {
        "tokens": scatter_about(keys[0], (GROUPS, GROUP_TOK, D), 1.0, 6.0, ((0, 8), (1, 4))),
        "doc_lengths": jax.vmap(lambda own: ragged_sizes(own, DOCS, SHORT_DEV, SHORT_DEV // 2, 0))(jax.random.split(keys[1], GROUPS * N_DP)).reshape((GROUPS, N_DP, DOCS)).astype(jnp.int32),
        "assign": draw_assign(jax.random.fold_in(keys[13], 71), 0),
        "ln_gain": jnp.clip(1.0 + 0.1 * jax.random.normal(keys[3], (D, 4), jnp.float32), 0.5, 1.5),
        "ln_bias": scatter_about(keys[4], (D, 4), 0.2, 1.0, (), jnp.float32),
        "attn_in": scatter_about(keys[5], (D, 2, 3 * D), D ** -0.5, 0.21875),
        "attn_out": scatter_about(keys[6], (D, 2, D), (D // 16) ** -0.5, 0.875),
        "ffn_in": scatter_about(keys[7], (D, FF), D ** -0.5, 0.21875),
        "ffn_out": scatter_about(keys[8], (FF, D), FF ** -0.5, 0.109375),
        "router": scatter_about(keys[9], (D, EXPERTS), 0.025, 0.14941406),
        "expert_in": scatter_about(keys[10], (EXPERTS, D, FF), D ** -0.5, 0.21875, ((0, 8),)),
        "expert_out": scatter_about(keys[11], (EXPERTS, FF, D), (FF // 4) ** -0.5, 0.21875, ((0, 8),)),
        "cotangent": scatter_about(keys[12], (GROUPS, GROUP_TOK, D), 1.0, 6.0, ((0, 8), (1, 4))),
    }


@jax.custom_vjp
def low(v):
    return lax.optimization_barrier(v.astype(jnp.bfloat16)).astype(jnp.float32)

@jax.custom_vjp
def low_back(v):
    return v

def low_keep(v):
    return (low(v), None)

def low_pass(kept, grad):
    return (grad,)

def back_keep(v):
    return (v, None)

def back_low(kept, grad):
    return (low(grad),)
low.defvjp(low_keep, low_pass)
low_back.defvjp(back_keep, back_low)
epsilon = 1e-05
balance_weight = 0.01
masked_score = -1e+30
highest = lax.Precision.HIGHEST

def layer_norm(stream, norm_gain, norm_shift):
    center = stream - lax.optimization_barrier(jnp.mean(stream, axis=-1, keepdims=True))
    spread = lax.optimization_barrier(jnp.mean(center * center, axis=-1, keepdims=True))
    return center * lax.rsqrt(spread + epsilon) * norm_gain + norm_shift

def masked_attention(mixed_rows, allowed):
    row_count = mixed_rows.shape[0]
    queries = mixed_rows[:, :D].reshape(row_count, HEADS, HEAD_DIM)
    key_rows = mixed_rows[:, D:2 * D].reshape(row_count, HEADS, HEAD_DIM)
    value_rows = mixed_rows[:, 2 * D:].reshape(row_count, HEADS, HEAD_DIM)
    scores = low_back(jnp.einsum('qhd,khd->hqk', queries, key_rows, precision=highest) * HEAD_DIM ** (-0.5))
    scores = jnp.where(allowed, scores, masked_score)
    weights = jax.nn.softmax(scores, axis=-1)
    context = jnp.einsum('hqk,khd->qhd', low(weights), value_rows, precision=highest)
    return context.reshape(row_count, D)

def attend_group(group_pair):
    mixed_rows, doc_ids = group_pair
    blocks = mixed_rows.reshape(N_DP, TOK_DEV, 3 * D)
    long_rows = blocks[:, :LONG_DEV].reshape(N_DP * LONG_DEV, 3 * D)
    long_order = jnp.arange(N_DP * LONG_DEV, dtype=jnp.int32)
    long_context = masked_attention(long_rows, long_order[None, :] <= long_order[:, None])
    places = jnp.arange(SHORT_DEV, dtype=jnp.int32)

    def short_block(block_pair):
        short_rows, short_ids = block_pair
        allowed = (short_ids[:, None] == short_ids[None, :]) & (places[None, :] <= places[:, None])
        return masked_attention(short_rows, allowed)
    short_context = jax.vmap(short_block)((blocks[:, LONG_DEV:], doc_ids))
    joined = jnp.concatenate([long_context.reshape(N_DP, LONG_DEV, D), short_context], axis=1)
    return joined.reshape(N_DP * TOK_DEV, D)

def attention(stream, norm_gain, norm_shift, weight_in, weight_out, doc_ids):
    normed = low(layer_norm(stream, norm_gain, norm_shift))
    mixed = low_back(low(jnp.einsum('gtd,de->gte', normed, weight_in, precision=highest)))
    context = lax.map(jax.checkpoint(attend_group), (mixed, doc_ids))
    context = low_back(low(context))
    return stream + low_back(jnp.einsum('gtd,de->gte', context, weight_out, precision=highest))

def feed_forward(stream, norm_gain, norm_shift, weight_in, weight_out):
    normed = low(layer_norm(stream, norm_gain, norm_shift))
    hidden = low_back(jnp.einsum('gtd,df->gtf', normed, weight_in, precision=highest))
    active = low(jax.nn.gelu(hidden, approximate=False))
    return stream + low_back(jnp.einsum('gtf,fd->gtd', active, weight_out, precision=highest))

def expert_apply(expert_triple):
    slot_rows, weight_in, weight_out = expert_triple
    hidden = low_back(jnp.dot(slot_rows, weight_in, precision=highest, preferred_element_type=jnp.float32))
    active = low(jax.nn.gelu(hidden, approximate=False))
    return low_back(low(jnp.dot(active, weight_out, precision=highest, preferred_element_type=jnp.float32)))

def mixture(stream, norm_gain, norm_shift, router_w, expert_in_w, expert_out_w, dispatch, assign_hot):
    normed = low(layer_norm(stream, norm_gain, norm_shift))
    logits = jnp.einsum('gtd,de->gte', normed, router_w, precision=highest)
    gate_value = jax.nn.sigmoid(lax.optimization_barrier(jnp.sum(logits * assign_hot, axis=-1)))
    token_share = lax.optimization_barrier(jnp.sum(assign_hot, axis=(0, 1))) / TOKENS
    gate_share = lax.optimization_barrier(jnp.sum(gate_value[..., None] * assign_hot, axis=(0, 1))) / TOKENS
    balance = EXPERTS * jnp.sum((token_share - 1.0 / EXPERTS) * gate_share)
    blocks = normed.reshape(GROUPS * N_DP, TOK_DEV, D)
    slots = low_back(jnp.einsum('btc,btd->bcd', dispatch, blocks, precision=highest))
    by_expert = slots.reshape(GROUPS * N_DP, EXPERTS, CAP, D).transpose(1, 0, 2, 3).reshape(EXPERTS, GROUPS * N_DP * CAP, D)
    results = lax.map(jax.checkpoint(expert_apply), (by_expert, expert_in_w, expert_out_w))
    returned_slots = results.reshape(EXPERTS, GROUPS * N_DP, CAP, D).transpose(1, 0, 2, 3).reshape(GROUPS * N_DP, EXPERTS * CAP, D)
    returned = jnp.einsum('btc,bcd->btd', dispatch, returned_slots, precision=highest).reshape(GROUPS, GROUP_TOK, D)
    return (stream + gate_value[..., None] * returned, balance)

def reference(tokens, doc_lengths, assign, ln_gain, ln_bias, attn_in, attn_out, ffn_in, ffn_out, router, expert_in, expert_out, cotangent):
    doc_ends = jnp.cumsum(doc_lengths, axis=-1)
    places = jnp.arange(SHORT_DEV, dtype=jnp.int32)
    doc_ids = lax.optimization_barrier(jnp.sum((places[:, None] >= doc_ends[..., None, :]).astype(jnp.int32), axis=-1))
    chosen = assign[..., 0]
    block_assign = chosen.reshape(GROUPS * N_DP, TOK_DEV)
    block_hot = (block_assign[..., None] == jnp.arange(EXPERTS, dtype=jnp.int32)).astype(jnp.int32)
    before = jnp.cumsum(block_hot, axis=1) - block_hot
    slot_place = lax.optimization_barrier(jnp.sum(before * block_hot, axis=-1))
    slot_index = jnp.where(slot_place < CAP, block_assign * CAP + slot_place, -1)
    dispatch = (slot_index[..., None] == jnp.arange(EXPERTS * CAP, dtype=jnp.int32)).astype(jnp.float32)
    assign_hot = (chosen[..., None] == jnp.arange(EXPERTS, dtype=jnp.int32)).astype(jnp.float32)

    def forward(stream, norm_gain, norm_shift, attn_in_w, attn_out_w, ffn_in_w, ffn_out_w, router_w, expert_in_w, expert_out_w):
        stream = attention(stream, norm_gain[:, 0], norm_shift[:, 0], attn_in_w[:, 0], attn_out_w[:, 0], doc_ids)
        stream = feed_forward(stream, norm_gain[:, 1], norm_shift[:, 1], ffn_in_w, ffn_out_w)
        stream = attention(stream, norm_gain[:, 2], norm_shift[:, 2], attn_in_w[:, 1], attn_out_w[:, 1], doc_ids)
        return mixture(stream, norm_gain[:, 3], norm_shift[:, 3], router_w, expert_in_w, expert_out_w, dispatch, assign_hot)
    (output, balance), pullback = jax.vjp(forward, tokens.astype(jnp.float32), ln_gain.astype(jnp.float32), ln_bias.astype(jnp.float32), attn_in.astype(jnp.float32), attn_out.astype(jnp.float32), ffn_in.astype(jnp.float32), ffn_out.astype(jnp.float32), router.astype(jnp.float32), expert_in.astype(jnp.float32), expert_out.astype(jnp.float32))
    grads = pullback((cotangent.astype(jnp.float32), jnp.asarray(balance_weight, jnp.float32)))
    return (output.astype(jnp.bfloat16), balance, grads[0].astype(jnp.bfloat16), grads[1], grads[2], grads[3], grads[4], grads[5], grads[6], grads[7], grads[8], grads[9])
```

```python
import functools

import jax
import jax.numpy as jnp
from jax import lax
from jax.experimental import pallas as pl
from jax.experimental.pallas import tpu as pltpu
from jax.sharding import PartitionSpec as P

MESH = pl.DeviceIdType.MESH
HEADS = 12
HEAD_DIM = 64
LONG_DEV = 256


epsilon = 1e-05
balance_weight = 0.01
masked_score = -1e30


def bit_of(index, level):
    return (index // (1 << level)) % 2


def flip(index, level):
    return index + (1 << level) * (1 - 2 * bit_of(index, level))


def partner_index(index, mask, levels):
    total = 0
    for level in range(levels):
        own = bit_of(index, level)
        total = total + (1 << level) * (1 - own if (mask >> level) & 1 else own)
    return total


def reduce_plan(n_dp, n_ex, rows):
    dp_levels = n_dp.bit_length() - 1
    ex_levels = n_ex.bit_length() - 1
    halvings, piece = 0, rows
    while halvings < ex_levels and piece % 32 == 0:
        piece //= 2
        halvings += 1
    kinds = [("dp", b) for b in range(dp_levels)]
    kinds += [("half", b) for b in range(halvings)]
    kinds += [("both", b) for b in range(halvings, ex_levels)]
    kinds += [("back", b) for b in reversed(range(halvings))]
    return kinds, halvings, piece


def grad_kernel(n_dp, n_ex, rows, kinds, halvings, firsts, chunks, fin_slots, *refs):
    count, groups = len(kinds), len(firsts)
    x_refs, dy_refs, out_ref = refs[:groups], refs[groups : 2 * groups], refs[2 * groups]
    it = iter(refs[2 * groups + 1 :])
    send_bufs = [next(it) if k[0] != "back" else None for k in kinds]
    recv_bufs = [next(it) if k[0] != "back" else None for k in kinds]
    keep_bufs = [next(it) if k[0] != "back" else None for k in kinds]
    fin = next(it)
    send_sems = [next(it) for _ in kinds]
    recv_sems = [next(it) for _ in kinds]
    t = pl.program_id(0)
    d, e = lax.axis_index("dp"), lax.axis_index("expert")
    dp_levels, ex_levels = n_dp.bit_length() - 1, n_ex.bit_length() - 1

    def peer(kind, level):
        return (flip(d, level), e) if kind == "dp" else (d, flip(e, level))

    @pl.when(t == 0)
    def _():
        barrier = pltpu.get_barrier_semaphore()
        for level in range(dp_levels):
            pl.semaphore_signal(barrier, inc=1, device_id=peer("dp", level), device_id_type=MESH)
        for level in range(ex_levels):
            pl.semaphore_signal(barrier, inc=1, device_id=peer("ex", level), device_id_type=MESH)
        pl.semaphore_wait(barrier, dp_levels + ex_levels)

    def kept_rows(depth):
        start = 0
        for b in range(depth):
            start = start + bit_of(e, b) * (rows >> (b + 1))
        return start

    def copy_of(s, c):
        kind, level = kinds[s]
        slot = lax.rem(c, 2)
        if kind == "back":
            span = rows >> (level + 1)
            at = pl.ds(pl.multiple_of(kept_rows(level + 1), span), span)
            src = fin.at[lax.rem(c, fin_slots), at]
            dst = src
        else:
            src, dst = send_bufs[s].at[slot], recv_bufs[s].at[slot]
        return pltpu.make_async_remote_copy(
            src_ref=src,
            dst_ref=dst,
            send_sem=send_sems[s].at[slot],
            recv_sem=recv_sems[s].at[slot],
            device_id=peer(kind, level),
            device_id_type=MESH,
        )

    def arrive(s, c):
        kind, level = kinds[s]
        copy_of(s, c).wait()
        slot = lax.rem(c, 2)
        if kind == "back":
            return None
        if kind == "dp":
            n = recv_bufs[s].shape[1]
            return [keep_bufs[s][slot, i] + recv_bufs[s][slot, i].astype(jnp.float32) for i in range(n)]
        return [keep_bufs[s][slot] + recv_bufs[s][slot].astype(jnp.float32)]

    def leave(s, c, values):
        kind, level = kinds[s]
        slot = lax.rem(c, 2)
        if kind == "dp":
            for i in range(len(values) // 2):
                send_bufs[s][slot, i] = values[2 * i + 1].astype(jnp.bfloat16)
        elif kind == "half":
            (value,) = values
            half = value.shape[0] // 2
            own = bit_of(e, level)
            top, low = value[:half], value[half:]
            send_bufs[s][slot] = jnp.where(own == 0, low, top).astype(jnp.bfloat16)
        elif kind == "both":
            (value,) = values
            send_bufs[s][slot] = value.astype(jnp.bfloat16)
        elif values is not None:
            (value,) = values
            span = value.shape[0]
            at = pl.ds(pl.multiple_of(kept_rows(halvings), span), span)
            fin[lax.rem(c, fin_slots), at] = value.astype(jnp.bfloat16)
        copy_of(s, c).start()
        if kind == "dp":
            for i in range(len(values) // 2):
                keep_bufs[s][slot, i] = values[2 * i]
        elif kind == "half":
            keep_bufs[s][slot] = jnp.where(own == 0, top, low)
        elif kind == "both":
            keep_bufs[s][slot] = value.astype(jnp.bfloat16).astype(jnp.float32)

    ends = list(firsts[1:]) + [chunks]
    for s in reversed(range(count + 1)):
        c = t - s
        if s == 0:
            for g in range(groups):

                @pl.when((c >= firsts[g]) & (c < ends[g]))
                def _(g=g):
                    dy = dy_refs[g][...]
                    slot = lax.rem(c, 2)

                    def piece(mask):
                        q = partner_index(d, mask, dp_levels)
                        return jnp.dot(x_refs[g][q], dy, preferred_element_type=jnp.float32)

                    for i in range(n_dp // 2):
                        send_bufs[0][slot, i] = piece(2 * i + 1).astype(jnp.bfloat16)
                    copy_of(0, c).start()
                    for i in range(n_dp // 2):
                        keep_bufs[0][slot, i] = piece(2 * i)

        else:

            @pl.when((c >= 0) & (c < chunks))
            def _(s=s, c=c):
                values = arrive(s - 1, c)
                if s < count:
                    leave(s, c, values)
                elif kinds[s - 1][0] == "back":
                    out_ref[...] = fin[lax.rem(c, fin_slots)]
                else:
                    out_ref[...] = values[0].astype(jnp.bfloat16)


def reduce_grads(n_dp, n_ex, pairs, width):
    _, _, rows, tokens = pairs[0][0].shape
    sizes = [x.shape[1] * (dy.shape[1] // width) for x, dy in pairs]
    firsts = [sum(sizes[:i]) for i in range(len(sizes))]
    chunks = sum(sizes)
    kinds, halvings, piece = reduce_plan(n_dp, n_ex, rows)
    count = len(kinds)
    fin_slots = max(1, halvings + 1)
    shapes = []
    for kind, level in kinds:
        if kind == "dp":
            shapes.append((n_dp >> (level + 1), rows, width))
        elif kind == "half":
            shapes.append((rows >> (level + 1), width))
        elif kind == "both":
            shapes.append((piece, width))
    scratch = [pltpu.VMEM((2,) + s, jnp.bfloat16) for s in shapes] * 2
    scratch += [pltpu.VMEM((2,) + s, jnp.float32) for s in shapes]
    scratch += [pltpu.VMEM((fin_slots, rows, width), jnp.bfloat16)]
    scratch += [pltpu.SemaphoreType.DMA((2,)) for _ in kinds] * 2
    in_specs = []
    for (x, dy), first, size in zip(pairs, firsts, sizes):
        many = x.shape[1] > 1

        def x_place(t, first=first, size=size, many=many):
            return (0, jnp.clip(t - first, 0, size - 1) if many else 0, 0, 0)

        in_specs.append(pl.BlockSpec((n_dp, None, rows, tokens), x_place))
    for (x, dy), first, size in zip(pairs, firsts, sizes):
        many = dy.shape[1] > width

        def dy_place(t, first=first, size=size, many=many):
            return (0, jnp.clip(t - first, 0, size - 1) if many else 0)

        in_specs.append(pl.BlockSpec((tokens, width), dy_place))
    return pl.pallas_call(
        functools.partial(grad_kernel, n_dp, n_ex, rows, kinds, halvings, firsts, chunks, fin_slots),
        grid=(chunks + count,),
        out_shape=jax.ShapeDtypeStruct((chunks, rows, width), jnp.bfloat16),
        in_specs=in_specs,
        out_specs=pl.BlockSpec((None, rows, width), lambda t: (jnp.maximum(t - count, 0), 0, 0)),
        scratch_shapes=scratch,
        compiler_params=pltpu.CompilerParams(
            collective_id=1, has_side_effects=True, vmem_limit_bytes=48 * 1024 * 1024
        ),
        name="dense_grads",
    )(*[x for x, _ in pairs], *[dy for _, dy in pairs])


def exact_gelu(values):
    return jax.nn.gelu(values, approximate=False)


def gelu_backward(hidden, upstream):
    _, pullback = jax.vjp(exact_gelu, hidden)
    return pullback(upstream)[0]


def norm_forward(stream, norm_gain, norm_shift):
    center = stream - jnp.mean(stream, axis=-1, keepdims=True)
    inverse = lax.rsqrt(jnp.mean(center * center, axis=-1, keepdims=True) + epsilon)
    unit_rows = center * inverse
    return (unit_rows * norm_gain + norm_shift, unit_rows, inverse)


def norm_backward(unit_rows, inverse, norm_gain, upstream):
    scaled = upstream * norm_gain
    inner = (
        scaled
        - jnp.mean(scaled, axis=-1, keepdims=True)
        - unit_rows * jnp.mean(scaled * unit_rows, axis=-1, keepdims=True)
    )
    return (inverse * inner, jnp.sum(upstream * unit_rows, axis=0), jnp.sum(upstream, axis=0))


def as_heads(flat_rows):
    return flat_rows.reshape(flat_rows.shape[0], HEADS, HEAD_DIM)


def block_scores(queries, key_rows, allowed):
    scores = jnp.einsum(
        "qhd,khd->qhk", queries, as_heads(key_rows), preferred_element_type=jnp.float32
    ) * HEAD_DIM ** (-0.5)
    return jnp.where(allowed[:, None, :], scores, masked_score)


def long_allowed(layout, first_row, row_count):
    is_long, position = layout
    key_place = first_row + jnp.arange(row_count, dtype=jnp.int32)
    return is_long[:, None] & (key_place[None, :] <= position[:, None])


def fold_block(running, queries, key_rows, value_rows, allowed):
    running_top, running_total, weighted = running
    scores = block_scores(queries, key_rows, allowed)
    new_top = jnp.maximum(running_top, jnp.max(scores, axis=-1))
    factor = jnp.exp(running_top - new_top)
    weights = jnp.where(allowed[:, None, :], jnp.exp(scores - new_top[..., None]), 0.0)
    running_total = running_total * factor + jnp.sum(weights, axis=-1)
    weighted = weighted * factor[..., None] + jnp.einsum(
        "qhk,khd->qhd",
        weights.astype(jnp.bfloat16),
        as_heads(value_rows),
        preferred_element_type=jnp.float32,
    )
    return (new_top, running_total, weighted)


def score_grads(queries, grad_heads, log_total, row_delta, block_keys, block_values, allowed):
    scores = block_scores(queries, block_keys, allowed)
    probs_block = jnp.where(allowed[:, None, :], jnp.exp(scores - log_total[..., None]), 0.0)
    grad_probs = jnp.einsum(
        "qhd,khd->qhk", grad_heads, as_heads(block_values), preferred_element_type=jnp.float32
    )
    grad_scores = (probs_block * (grad_probs - row_delta[..., None])).astype(jnp.bfloat16)
    return (probs_block.astype(jnp.bfloat16), grad_scores)


def attend_forward(normed_low, weight_in, layout, short_allowed):
    model_width = normed_low.shape[1]
    row_count = normed_low.shape[0]
    mixed = jnp.dot(normed_low, weight_in, preferred_element_type=jnp.float32).astype(jnp.bfloat16)
    queries = as_heads(mixed[:, :model_width])
    key_rows = mixed[:, model_width : 2 * model_width]
    value_rows = mixed[:, 2 * model_width :]
    running = (
        jnp.full((row_count, HEADS), masked_score, jnp.float32),
        jnp.zeros((row_count, HEADS), jnp.float32),
        jnp.zeros((row_count, HEADS, HEAD_DIM), jnp.float32),
    )
    running = fold_block(
        running, queries, key_rows[LONG_DEV:], value_rows[LONG_DEV:], short_allowed
    )
    both = lax.all_gather(mixed[:LONG_DEV, model_width:], "dp", axis=0, tiled=True)
    key_piece = (both[:, :model_width], both[:, model_width:])
    running = fold_block(
        running,
        queries,
        key_piece[0],
        key_piece[1],
        long_allowed(layout, jnp.int32(0), key_piece[0].shape[0]),
    )
    running_top, running_total, weighted = running
    context = (weighted / running_total[..., None]).reshape(row_count, model_width)
    return (mixed, context, running_top + jnp.log(running_total), key_piece)


def attend_backward(mixed, context, log_total, gathered, grad_context, layout, short_allowed):
    model_width = context.shape[1]
    row_count = context.shape[0]
    queries = as_heads(mixed[:, :model_width])
    key_rows = mixed[:, model_width : 2 * model_width]
    value_rows = mixed[:, 2 * model_width :]
    grad_heads = as_heads(grad_context)
    row_delta = jnp.sum(grad_heads.astype(jnp.float32) * as_heads(context), axis=-1)
    head_scale = HEAD_DIM ** (-0.5)
    short_probs, short_scores = score_grads(
        queries,
        grad_heads,
        log_total,
        row_delta,
        key_rows[LONG_DEV:],
        value_rows[LONG_DEV:],
        short_allowed,
    )
    grad_query = (
        jnp.einsum(
            "qhk,khd->qhd",
            short_scores,
            as_heads(key_rows[LONG_DEV:]),
            preferred_element_type=jnp.float32,
        )
        * head_scale
    )
    short_count = row_count - LONG_DEV
    short_key_grad = (
        jnp.einsum("qhk,qhd->khd", short_scores, queries, preferred_element_type=jnp.float32)
        * head_scale
    ).reshape(short_count, model_width)
    short_value_grad = jnp.einsum(
        "qhk,qhd->khd", short_probs, grad_heads, preferred_element_type=jnp.float32
    ).reshape(short_count, model_width)
    long_count = gathered[0].shape[0]

    def visit(block_step, partial_state):
        query_sum, key_terms, value_terms = partial_state
        first_row = block_step * LONG_DEV
        block_keys = lax.dynamic_slice_in_dim(gathered[0], first_row, LONG_DEV, 0)
        block_values = lax.dynamic_slice_in_dim(gathered[1], first_row, LONG_DEV, 0)
        probs_low, grad_scores = score_grads(
            queries,
            grad_heads,
            log_total,
            row_delta,
            block_keys,
            block_values,
            long_allowed(layout, first_row, LONG_DEV),
        )
        more_query = (
            jnp.einsum(
                "qhk,khd->qhd",
                grad_scores,
                as_heads(block_keys),
                preferred_element_type=jnp.float32,
            )
            * head_scale
        )
        more_key = (
            jnp.einsum("qhk,qhd->khd", grad_scores, queries, preferred_element_type=jnp.float32)
            * head_scale
        ).reshape(LONG_DEV, model_width)
        more_value = jnp.einsum(
            "qhk,qhd->khd", probs_low, grad_heads, preferred_element_type=jnp.float32
        ).reshape(LONG_DEV, model_width)
        return (
            query_sum + more_query,
            lax.dynamic_update_slice_in_dim(key_terms, more_key, first_row, 0),
            lax.dynamic_update_slice_in_dim(value_terms, more_value, first_row, 0),
        )

    start_state = (
        grad_query,
        jnp.zeros((long_count, model_width), jnp.float32),
        jnp.zeros((long_count, model_width), jnp.float32),
    )
    grad_query, key_terms, value_terms = lax.fori_loop(
        0, long_count // LONG_DEV, visit, start_state
    )
    own = lax.psum_scatter(
        jnp.concatenate([key_terms, value_terms], axis=1).astype(jnp.bfloat16), "dp", scatter_dimension=0, tiled=True
    ).astype(jnp.float32)
    own_keys, own_values = own[:, :model_width], own[:, model_width:]
    grad_keys = jnp.concatenate([own_keys, short_key_grad], axis=0)
    grad_values = jnp.concatenate([own_values, short_value_grad], axis=0)
    return jnp.concatenate(
        [grad_query.reshape(row_count, model_width), grad_keys, grad_values], axis=1
    ).astype(jnp.bfloat16)


def attention_forward(stream, norm_gain, norm_shift, weight_in, weight_out, layout, short_allowed):
    normed, unit_rows, inverse = norm_forward(stream, norm_gain, norm_shift)
    normed_low = normed.astype(jnp.bfloat16)
    mixed, context, log_total, gathered = attend_forward(
        normed_low, weight_in, layout, short_allowed
    )
    context_low = context.astype(jnp.bfloat16)
    stream_next = stream + jnp.dot(context_low, weight_out, preferred_element_type=jnp.float32)
    return (
        stream_next,
        (unit_rows, inverse, normed_low, mixed, context, context_low, log_total, gathered),
    )


def attention_backward(
    upstream, kept_state, norm_gain, weight_in, weight_out, layout, short_allowed
):
    unit_rows, inverse, normed_low, mixed, context, context_low, log_total, gathered = kept_state
    upstream_low = upstream.astype(jnp.bfloat16)
    grad_context = jnp.einsum(
        "te,de->td", upstream_low, weight_out, preferred_element_type=jnp.float32
    ).astype(jnp.bfloat16)
    grad_mixed = attend_backward(
        mixed, context, log_total, gathered, grad_context, layout, short_allowed
    )
    grad_normed = jnp.einsum("te,de->td", grad_mixed, weight_in, preferred_element_type=jnp.float32)
    grad_stream, grad_gain, grad_shift = norm_backward(unit_rows, inverse, norm_gain, grad_normed)
    pairs = ((context_low, upstream_low), (normed_low, grad_mixed))
    return (upstream + grad_stream, pairs, grad_gain, grad_shift)


def ffn_forward(stream, norm_gain, norm_shift, weight_in, weight_out):
    normed, unit_rows, inverse = norm_forward(stream, norm_gain, norm_shift)
    normed_low = normed.astype(jnp.bfloat16)
    hidden = jnp.dot(normed_low, weight_in, preferred_element_type=jnp.float32)
    active = exact_gelu(hidden).astype(jnp.bfloat16)
    stream_next = stream + jnp.dot(active, weight_out, preferred_element_type=jnp.float32)
    return (stream_next, (unit_rows, inverse, normed_low, hidden, active))


def ffn_backward(upstream, kept_state, norm_gain, weight_in, weight_out):
    unit_rows, inverse, normed_low, hidden, active = kept_state
    upstream_low = upstream.astype(jnp.bfloat16)
    grad_active = jnp.einsum(
        "td,fd->tf", upstream_low, weight_out, preferred_element_type=jnp.float32
    )
    grad_hidden = gelu_backward(hidden, grad_active).astype(jnp.bfloat16)
    grad_normed = jnp.einsum(
        "tf,df->td", grad_hidden, weight_in, preferred_element_type=jnp.float32
    )
    grad_stream, grad_gain, grad_shift = norm_backward(unit_rows, inverse, norm_gain, grad_normed)
    pairs = ((active, upstream_low), (normed_low, grad_hidden))
    return (upstream + grad_stream, pairs, grad_gain, grad_shift)


def mixture_forward(stream, norm_gain, norm_shift, router, expert_in, expert_out, assign_ids):
    normed, unit_rows, inverse = norm_forward(stream, norm_gain, norm_shift)
    normed_low = normed.astype(jnp.bfloat16)
    model_width = stream.shape[1]
    row_count = stream.shape[0]
    experts_all = router.shape[1]
    capacity = (5 * row_count + 4 * experts_all - 1) // (4 * experts_all)
    logits = jnp.dot(normed_low, router, preferred_element_type=jnp.float32)
    expert_numbers = jnp.arange(experts_all, dtype=jnp.int32)
    chosen_hot = (assign_ids[:, None] == expert_numbers[None, :]).astype(jnp.float32)
    gate_value = jax.nn.sigmoid(jnp.sum(logits * chosen_hot, axis=-1))
    counts = lax.psum(jnp.sum(chosen_hot, axis=0), ("dp", "expert"))
    gate_sums = lax.psum(jnp.sum(gate_value[:, None] * chosen_hot, axis=0), ("dp", "expert"))
    tokens_all = row_count * lax.axis_size("dp") * lax.axis_size("expert")
    token_share = counts / tokens_all
    balance = experts_all * jnp.sum((token_share - 1.0 / experts_all) * (gate_sums / tokens_all))
    hot_count = (assign_ids[:, None] == expert_numbers[None, :]).astype(jnp.int32)
    before = jnp.cumsum(hot_count, axis=0) - hot_count
    slot_place = jnp.sum(before * hot_count, axis=-1)
    slot_index = jnp.where(slot_place < capacity, assign_ids * capacity + slot_place, -1)
    dispatch = (
        slot_index[:, None] == jnp.arange(experts_all * capacity, dtype=jnp.int32)[None, :]
    ).astype(jnp.bfloat16)
    outgoing = jnp.einsum(
        "tc,td->cd", dispatch, normed_low, preferred_element_type=jnp.float32
    ).astype(jnp.bfloat16)
    outgoing = outgoing.reshape(experts_all, capacity, model_width)
    incoming = lax.all_to_all(outgoing, "expert", split_axis=0, concat_axis=0, tiled=True)
    slot_count = incoming.shape[1]
    grouped = incoming.reshape(-1, expert_in.shape[0], slot_count, model_width)
    hidden = jnp.einsum("sjcd,jdf->sjcf", grouped, expert_in, preferred_element_type=jnp.float32)
    active = exact_gelu(hidden).astype(jnp.bfloat16)
    result = jnp.einsum(
        "sjcf,jfd->sjcd", active, expert_out, preferred_element_type=jnp.float32
    ).astype(jnp.bfloat16)
    homeward = lax.all_to_all(
        result.reshape(incoming.shape), "expert", split_axis=0, concat_axis=0, tiled=True
    )
    gathered = jnp.dot(
        dispatch,
        homeward.reshape(experts_all * capacity, model_width),
        preferred_element_type=jnp.float32,
    )
    stream_next = stream + gate_value[:, None] * gathered
    kept_state = (
        unit_rows,
        inverse,
        normed_low,
        gate_value,
        token_share,
        tokens_all,
        chosen_hot,
        dispatch,
        gathered,
        incoming,
    )
    return (stream_next, balance, kept_state)


def mixture_backward(upstream, kept_state, norm_gain, router, expert_in, expert_out):
    (
        unit_rows,
        inverse,
        normed_low,
        gate_value,
        token_share,
        tokens_all,
        chosen_hot,
        dispatch,
        gathered,
        arrived,
    ) = kept_state
    model_width = upstream.shape[1]
    experts_all = router.shape[1]
    grad_gate = jnp.sum(upstream * gathered, axis=-1)
    grad_return = (gate_value[:, None] * upstream).astype(jnp.bfloat16)
    outgoing = jnp.einsum(
        "tc,td->cd", dispatch, grad_return, preferred_element_type=jnp.float32
    ).astype(jnp.bfloat16)
    outgoing = outgoing.reshape(experts_all, -1, model_width)
    incoming = lax.all_to_all(outgoing, "expert", split_axis=0, concat_axis=0, tiled=True)
    slot_count = incoming.shape[1]
    grouped_grad = incoming.reshape(-1, expert_in.shape[0], slot_count, model_width)
    grouped_rows = arrived.reshape(-1, expert_in.shape[0], slot_count, model_width)
    hidden = jnp.einsum(
        "sjcd,jdf->sjcf", grouped_rows, expert_in, preferred_element_type=jnp.float32
    )
    active = exact_gelu(hidden).astype(jnp.bfloat16)
    grad_out_weight = jnp.einsum(
        "sjcf,sjcd->jfd", active, grouped_grad, preferred_element_type=jnp.float32
    )
    grad_active = jnp.einsum(
        "sjcd,jfd->sjcf", grouped_grad, expert_out, preferred_element_type=jnp.float32
    )
    grad_hidden = gelu_backward(hidden, grad_active).astype(jnp.bfloat16)
    grad_in_weight = jnp.einsum(
        "sjcd,sjcf->jdf", grouped_rows, grad_hidden, preferred_element_type=jnp.float32
    )
    grad_rows = jnp.einsum(
        "sjcf,jdf->sjcd", grad_hidden, expert_in, preferred_element_type=jnp.float32
    ).astype(jnp.bfloat16)
    homeward = lax.all_to_all(
        grad_rows.reshape(incoming.shape), "expert", split_axis=0, concat_axis=0, tiled=True
    )
    grad_normed = jnp.dot(
        dispatch, homeward.reshape(-1, model_width), preferred_element_type=jnp.float32
    )
    share_weight = balance_weight * experts_all * (token_share - 1.0 / experts_all) / tokens_all
    grad_gate = grad_gate + jnp.sum(chosen_hot * share_weight[None, :], axis=-1)
    grad_chosen = grad_gate * gate_value * (1.0 - gate_value)
    grad_logits = grad_chosen[:, None] * chosen_hot
    router_float = router.astype(jnp.float32)
    grad_router = jnp.einsum(
        "td,te->de", normed_low.astype(jnp.float32), grad_logits, precision=lax.Precision.HIGHEST
    )
    grad_normed = grad_normed + jnp.einsum(
        "te,de->td", grad_logits, router_float, precision=lax.Precision.HIGHEST
    )
    grad_stream, grad_gain, grad_shift = norm_backward(unit_rows, inverse, norm_gain, grad_normed)
    return (
        upstream + grad_stream,
        grad_in_weight,
        grad_out_weight,
        grad_router,
        grad_gain,
        grad_shift,
    )


def shards(
    tokens,
    doc_lengths,
    assign,
    ln_gain,
    ln_bias,
    attn_in,
    attn_out,
    ffn_in,
    ffn_out,
    router,
    expert_in,
    expert_out,
    cotangent,
):
    stream_first = tokens[0].astype(jnp.float32)
    row_count = stream_first.shape[0]
    row_index = jnp.arange(row_count, dtype=jnp.int32)
    is_long = row_index < LONG_DEV
    layout = (is_long, lax.axis_index("dp") * LONG_DEV + row_index)
    doc_ends = jnp.cumsum(doc_lengths[0, 0])
    short_place = jnp.arange(row_count - LONG_DEV, dtype=jnp.int32)
    short_ids = jnp.sum((short_place[:, None] >= doc_ends[None, :]).astype(jnp.int32), axis=-1)
    row_docs = jnp.concatenate([jnp.full((LONG_DEV,), -1, jnp.int32), short_ids])
    short_allowed = (row_docs[:, None] == short_ids[None, :]) & (
        short_place[None, :] + LONG_DEV <= row_index[:, None]
    )
    stream_one, kept_one = attention_forward(
        stream_first,
        ln_gain[:, 0],
        ln_bias[:, 0],
        attn_in[:, 0],
        attn_out[:, 0],
        layout,
        short_allowed,
    )
    stream_two, kept_two = ffn_forward(stream_one, ln_gain[:, 1], ln_bias[:, 1], ffn_in, ffn_out)
    stream_three, kept_three = attention_forward(
        stream_two,
        ln_gain[:, 2],
        ln_bias[:, 2],
        attn_in[:, 1],
        attn_out[:, 1],
        layout,
        short_allowed,
    )
    stream_four, balance, kept_four = mixture_forward(
        stream_three, ln_gain[:, 3], ln_bias[:, 3], router, expert_in, expert_out, assign[0, :, 0]
    )
    output = stream_four.astype(jnp.bfloat16)[None]
    upstream = cotangent[0].astype(jnp.float32)
    upstream, expert_in_grad, expert_out_grad, router_grad, gain_three, shift_three = (
        mixture_backward(upstream, kept_four, ln_gain[:, 3], router, expert_in, expert_out)
    )
    upstream, second_pairs, gain_two, shift_two = attention_backward(
        upstream, kept_three, ln_gain[:, 2], attn_in[:, 1], attn_out[:, 1], layout, short_allowed
    )
    upstream, dense_pairs, gain_one, shift_one = ffn_backward(upstream, kept_two, ln_gain[:, 1], ffn_in, ffn_out)
    upstream, first_pairs, gain_zero, shift_zero = attention_backward(
        upstream, kept_one, ln_gain[:, 0], attn_in[:, 0], attn_out[:, 0], layout, short_allowed
    )
    grad_tokens = upstream.astype(jnp.bfloat16)[None]
    n_dp, n_ex = lax.axis_size("dp"), lax.axis_size("expert")
    model_width = tokens.shape[2]
    rows = model_width // n_dp

    def blocks_of(acts):
        return acts.T.reshape(n_dp, -1, rows, row_count).astype(jnp.bfloat16)

    pairs = [(blocks_of(x), dy) for x, dy in second_pairs + dense_pairs + first_pairs]
    chunks = reduce_grads(n_dp, n_ex, pairs, model_width).astype(jnp.float32)

    def wide(first, count):
        return chunks[first : first + count].transpose(1, 0, 2).reshape(rows, count * model_width)

    per_in = attn_in.shape[2] // model_width
    per_ffn = ffn_in.shape[1] // model_width
    at = 0
    second_out = chunks[0]
    second_in = wide(1, per_in)
    at = 1 + per_in
    ffn_out_sum = chunks[at : at + per_ffn].reshape(per_ffn * rows, model_width)
    ffn_in_sum = wide(at + per_ffn, per_ffn)
    at = at + 2 * per_ffn
    first_out = chunks[at]
    first_in = wide(at + 1, per_in)
    small = jnp.concatenate(
        [
            jnp.stack([gain_zero, gain_one, gain_two, gain_three, shift_zero, shift_one, shift_two, shift_three], axis=0),
            router_grad.T,
        ],
        axis=0,
    )
    small = lax.psum(small, ("dp", "expert"))
    small = lax.dynamic_slice_in_dim(small, lax.axis_index("dp") * rows, rows, 1).T
    summed = [
        jnp.stack([first_in, second_in], axis=1),
        jnp.stack([first_out, second_out], axis=1),
        ffn_in_sum,
        ffn_out_sum,
        small[:, 8:],
        small[:, :4],
        small[:, 4:8],
    ]
    expert_in_sum, expert_out_sum = (
        lax.psum_scatter(
            expert_in_grad.astype(jnp.bfloat16), "dp", scatter_dimension=1, tiled=True
        ).astype(jnp.float32),
        lax.psum_scatter(
            expert_out_grad.astype(jnp.bfloat16), "dp", scatter_dimension=1, tiled=True
        ).astype(jnp.float32),
    )
    return (
        output,
        balance,
        grad_tokens,
        summed[5],
        summed[6],
        summed[0],
        summed[1],
        summed[2],
        summed[3],
        summed[4],
        expert_in_sum,
        expert_out_sum,
    )


def solution(mesh):
    return jax.shard_map(
        shards,
        mesh=mesh,
        in_specs=(
            P("expert", "dp", None),
            P("expert", "dp", None),
            P("expert", "dp", None),
            P(),
            P(),
            P(),
            P(),
            P(),
            P(),
            P(),
            P("expert", None, None),
            P("expert", None, None),
            P("expert", "dp", None),
        ),
        out_specs=(
            P("expert", "dp", None),
            P(),
            P("expert", "dp", None),
            P("dp", None),
            P("dp", None),
            P("dp", None, None),
            P("dp", None, None),
            P("dp", None),
            P("dp", None),
            P("dp", None),
            P("expert", "dp", None),
            P("expert", "dp", None),
        ),
        check_vma=False,
    )
```

```python
import functools

import jax
import jax.numpy as jnp
from jax import lax
from jax.experimental import pallas as pl
from jax.experimental.pallas import tpu as pltpu
from jax.sharding import PartitionSpec as P

MESH = pl.DeviceIdType.MESH
HEADS = 12
HEAD_DIM = 64
LONG_DEV = 256


epsilon = 1e-05
balance_weight = 0.01
masked_score = -1e30


def bit_of(index, level):
    return (index // (1 << level)) % 2


def flip(index, level):
    return index + (1 << level) * (1 - 2 * bit_of(index, level))


def partner_index(index, mask, levels):
    total = 0
    for level in range(levels):
        own = bit_of(index, level)
        total = total + (1 << level) * (1 - own if (mask >> level) & 1 else own)
    return total


def reduce_plan(n_dp, n_ex, rows):
    dp_levels = n_dp.bit_length() - 1
    ex_levels = n_ex.bit_length() - 1
    halvings, piece = 0, rows
    while halvings < ex_levels and piece % 32 == 0:
        piece //= 2
        halvings += 1
    kinds = [("dp", b) for b in range(dp_levels)]
    kinds += [("half", b) for b in range(halvings)]
    kinds += [("both", b) for b in range(halvings, ex_levels)]
    kinds += [("back", b) for b in reversed(range(halvings))]
    return kinds, halvings, piece


def grad_kernel(n_dp, n_ex, rows, kinds, halvings, firsts, chunks, fin_slots, *refs):
    count, groups = len(kinds), len(firsts)
    x_refs, dy_refs, out_ref = refs[:groups], refs[groups : 2 * groups], refs[2 * groups]
    it = iter(refs[2 * groups + 1 :])
    send_bufs = [next(it) if k[0] != "back" else None for k in kinds]
    recv_bufs = [next(it) if k[0] != "back" else None for k in kinds]
    keep_bufs = [next(it) if k[0] != "back" else None for k in kinds]
    fin = next(it)
    send_sems = [next(it) for _ in kinds]
    recv_sems = [next(it) for _ in kinds]
    t = pl.program_id(0)
    d, e = lax.axis_index("dp"), lax.axis_index("expert")
    dp_levels, ex_levels = n_dp.bit_length() - 1, n_ex.bit_length() - 1

    def peer(kind, level):
        return (flip(d, level), e) if kind == "dp" else (d, flip(e, level))

    @pl.when(t == 0)
    def _():
        barrier = pltpu.get_barrier_semaphore()
        for level in range(dp_levels):
            pl.semaphore_signal(barrier, inc=1, device_id=peer("dp", level), device_id_type=MESH)
        for level in range(ex_levels):
            pl.semaphore_signal(barrier, inc=1, device_id=peer("ex", level), device_id_type=MESH)
        pl.semaphore_wait(barrier, dp_levels + ex_levels)

    def kept_rows(depth):
        start = 0
        for b in range(depth):
            start = start + bit_of(e, b) * (rows >> (b + 1))
        return start

    def copy_of(s, c):
        kind, level = kinds[s]
        slot = lax.rem(c, 2)
        if kind == "back":
            span = rows >> (level + 1)
            at = pl.ds(pl.multiple_of(kept_rows(level + 1), span), span)
            src = fin.at[lax.rem(c, fin_slots), at]
            dst = src
        else:
            src, dst = send_bufs[s].at[slot], recv_bufs[s].at[slot]
        return pltpu.make_async_remote_copy(
            src_ref=src,
            dst_ref=dst,
            send_sem=send_sems[s].at[slot],
            recv_sem=recv_sems[s].at[slot],
            device_id=peer(kind, level),
            device_id_type=MESH,
        )

    def arrive(s, c):
        kind, level = kinds[s]
        copy_of(s, c).wait()
        slot = lax.rem(c, 2)
        if kind == "back":
            return None
        if kind == "dp":
            n = recv_bufs[s].shape[1]
            return [keep_bufs[s][slot, i] + recv_bufs[s][slot, i].astype(jnp.float32) for i in range(n)]
        return [keep_bufs[s][slot] + recv_bufs[s][slot].astype(jnp.float32)]

    def leave(s, c, values):
        kind, level = kinds[s]
        slot = lax.rem(c, 2)
        if kind == "dp":
            for i in range(len(values) // 2):
                send_bufs[s][slot, i] = values[2 * i + 1].astype(jnp.bfloat16)
        elif kind == "half":
            (value,) = values
            half = value.shape[0] // 2
            own = bit_of(e, level)
            top, low = value[:half], value[half:]
            send_bufs[s][slot] = jnp.where(own == 0, low, top).astype(jnp.bfloat16)
        elif kind == "both":
            (value,) = values
            send_bufs[s][slot] = value.astype(jnp.bfloat16)
        elif values is not None:
            (value,) = values
            span = value.shape[0]
            at = pl.ds(pl.multiple_of(kept_rows(halvings), span), span)
            fin[lax.rem(c, fin_slots), at] = value.astype(jnp.bfloat16)
        copy_of(s, c).start()
        if kind == "dp":
            for i in range(len(values) // 2):
                keep_bufs[s][slot, i] = values[2 * i]
        elif kind == "half":
            keep_bufs[s][slot] = jnp.where(own == 0, top, low)
        elif kind == "both":
            keep_bufs[s][slot] = value.astype(jnp.bfloat16).astype(jnp.float32)

    ends = list(firsts[1:]) + [chunks]
    for s in reversed(range(count + 1)):
        c = t - s
        if s == 0:
            for g in range(groups):

                @pl.when((c >= firsts[g]) & (c < ends[g]))
                def _(g=g):
                    dy = dy_refs[g][...]
                    slot = lax.rem(c, 2)

                    def piece(mask):
                        q = partner_index(d, mask, dp_levels)
                        return jnp.dot(x_refs[g][q], dy, preferred_element_type=jnp.float32)

                    for i in range(n_dp // 2):
                        send_bufs[0][slot, i] = piece(2 * i + 1).astype(jnp.bfloat16)
                    copy_of(0, c).start()
                    for i in range(n_dp // 2):
                        keep_bufs[0][slot, i] = piece(2 * i)

        else:

            @pl.when((c >= 0) & (c < chunks))
            def _(s=s, c=c):
                values = arrive(s - 1, c)
                if s < count:
                    leave(s, c, values)
                elif kinds[s - 1][0] == "back":
                    out_ref[...] = fin[lax.rem(c, fin_slots)]
                else:
                    out_ref[...] = values[0].astype(jnp.bfloat16)


def reduce_grads(n_dp, n_ex, pairs, width):
    _, _, rows, tokens = pairs[0][0].shape
    sizes = [x.shape[1] * (dy.shape[1] // width) for x, dy in pairs]
    firsts = [sum(sizes[:i]) for i in range(len(sizes))]
    chunks = sum(sizes)
    kinds, halvings, piece = reduce_plan(n_dp, n_ex, rows)
    count = len(kinds)
    fin_slots = max(1, halvings + 1)
    shapes = []
    for kind, level in kinds:
        if kind == "dp":
            shapes.append((n_dp >> (level + 1), rows, width))
        elif kind == "half":
            shapes.append((rows >> (level + 1), width))
        elif kind == "both":
            shapes.append((piece, width))
    scratch = [pltpu.VMEM((2,) + s, jnp.bfloat16) for s in shapes] * 2
    scratch += [pltpu.VMEM((2,) + s, jnp.float32) for s in shapes]
    scratch += [pltpu.VMEM((fin_slots, rows, width), jnp.bfloat16)]
    scratch += [pltpu.SemaphoreType.DMA((2,)) for _ in kinds] * 2
    in_specs = []
    for (x, dy), first, size in zip(pairs, firsts, sizes):
        many = x.shape[1] > 1

        def x_place(t, first=first, size=size, many=many):
            return (0, jnp.clip(t - first, 0, size - 1) if many else 0, 0, 0)

        in_specs.append(pl.BlockSpec((n_dp, None, rows, tokens), x_place))
    for (x, dy), first, size in zip(pairs, firsts, sizes):
        many = dy.shape[1] > width

        def dy_place(t, first=first, size=size, many=many):
            return (0, jnp.clip(t - first, 0, size - 1) if many else 0)

        in_specs.append(pl.BlockSpec((tokens, width), dy_place))
    return pl.pallas_call(
        functools.partial(grad_kernel, n_dp, n_ex, rows, kinds, halvings, firsts, chunks, fin_slots),
        grid=(chunks + count,),
        out_shape=jax.ShapeDtypeStruct((chunks, rows, width), jnp.bfloat16),
        in_specs=in_specs,
        out_specs=pl.BlockSpec((None, rows, width), lambda t: (jnp.maximum(t - count, 0), 0, 0)),
        scratch_shapes=scratch,
        compiler_params=pltpu.CompilerParams(
            collective_id=1, has_side_effects=True, vmem_limit_bytes=48 * 1024 * 1024
        ),
        name="dense_grads",
    )(*[x for x, _ in pairs], *[dy for _, dy in pairs])


def exact_gelu(values):
    return jax.nn.gelu(values, approximate=False)


def gelu_backward(hidden, upstream):
    _, pullback = jax.vjp(exact_gelu, hidden)
    return pullback(upstream)[0]


def norm_forward(stream, norm_gain, norm_shift):
    center = stream - jnp.mean(stream, axis=-1, keepdims=True)
    inverse = lax.rsqrt(jnp.mean(center * center, axis=-1, keepdims=True) + epsilon)
    unit_rows = center * inverse
    return (unit_rows * norm_gain + norm_shift, unit_rows, inverse)


def norm_backward(unit_rows, inverse, norm_gain, upstream):
    scaled = upstream * norm_gain
    inner = (
        scaled
        - jnp.mean(scaled, axis=-1, keepdims=True)
        - unit_rows * jnp.mean(scaled * unit_rows, axis=-1, keepdims=True)
    )
    return (inverse * inner, jnp.sum(upstream * unit_rows, axis=0), jnp.sum(upstream, axis=0))


def dot(a, b):
    return jnp.dot(a, b, preferred_element_type=jnp.float32)


def dot_rows(a, b):
    return lax.dot_general(a, b, (((1,), (1,)), ((), ())), preferred_element_type=jnp.float32)


def dot_columns(a, b):
    return lax.dot_general(a, b, (((0,), (0,)), ((), ())), preferred_element_type=jnp.float32)


def head_pair(rows):
    first = lax.broadcasted_iota(jnp.int32, rows.shape, 1) < HEAD_DIM
    zero = jnp.zeros_like(rows)
    return jnp.concatenate([jnp.where(first, rows, zero), jnp.where(first, zero, rows)], axis=0)


def pair_rows(both):
    n = both.shape[1] // 2
    return jnp.concatenate([both[:HEAD_DIM, :n], both[HEAD_DIM:, n:]], axis=0)


def causal(keys, queries):
    key = lax.broadcasted_iota(jnp.int32, (keys, 2 * queries), 0)
    query = lax.broadcasted_iota(jnp.int32, (keys, 2 * queries), 1)
    return key <= jnp.where(query >= queries, query - queries, query)


def short_seen(doc_row, doc_col):
    n = doc_row.shape[1]
    same = doc_col == jnp.concatenate([doc_row, doc_row], axis=1)
    return same & causal(n, n)


class Links:
    def __init__(self, n_dp):
        self.me, self.expert = lax.axis_index("dp"), lax.axis_index("expert")
        self.chips = n_dp // 2
        self.chip, self.core = self.me // 2, self.me % 2
        self.twin = self.me + 1 - 2 * self.core

    def greet(self):
        barrier = pltpu.get_barrier_semaphore()
        pl.semaphore_signal(barrier, inc=1, device_id=(self.twin, self.expert), device_id_type=MESH)
        for other in range(self.chips):

            @pl.when(other != self.chip)
            def _():
                there = (2 * other + self.core, self.expert)
                pl.semaphore_signal(barrier, inc=1, device_id=there, device_id_type=MESH)

        pl.semaphore_wait(barrier, self.chips)

    def copy(self, ref, send_sem, recv_sem, index):
        return pltpu.make_async_remote_copy(
            src_ref=ref,
            dst_ref=ref,
            send_sem=send_sem,
            recv_sem=recv_sem,
            device_id=(index, self.expert),
            device_id_type=MESH,
        )

    def before(self, later, other):
        return other > self.chip if later else other < self.chip


class Spread:
    def __init__(self, links, at, parts, later, far_sems, near_sems, recv_sems):
        self.links, self.at, self.later = links, at, later
        self.far_sems, self.near_sems, self.recv_sems = far_sems, near_sems, recv_sems

    def _far(self, other, p):
        k = self.links
        return k.copy(self.at(k.me, p), self.far_sems.at[other, p], self.recv_sems.at[k.me, p], 2 * other + k.core)

    def _near(self, block, p):
        k = self.links
        return k.copy(self.at(block, p), self.near_sems.at[block, p], self.recv_sems.at[block, p], k.twin)

    def _twin_needs(self):
        return self.links.core == (0 if self.later else 1)

    def send(self, p):
        k = self.links
        for other in range(k.chips):

            @pl.when(k.before(self.later, other))
            def _():
                self._far(other, p).start()

        @pl.when(self._twin_needs())
        def _():
            self._near(k.me, p).start()

    def sent(self, p):
        k = self.links
        for other in range(k.chips):

            @pl.when(k.before(self.later, other))
            def _():
                self._far(other, p).wait_send()

            @pl.when(k.before(not self.later, other))
            def _():
                self._near(2 * other + k.core, p).wait_send()

        @pl.when(self._twin_needs())
        def _():
            self._near(k.me, p).wait_send()

    def relay(self, p):
        k = self.links
        for other in range(k.chips):

            @pl.when(k.before(not self.later, other))
            def _():
                block = 2 * other + k.core
                copy = self._near(block, p)
                copy.wait_recv()
                copy.start()

    def each(self, p, use):
        k = self.links

        @pl.when(k.core == (1 if self.later else 0))
        def _():
            self._near(k.twin, p).wait_recv()
            use(k.twin)

        for other in range(k.chips):

            @pl.when(k.before(not self.later, other))
            def _():
                use(2 * other + k.core)
                block = 2 * other + 1 - k.core
                self._near(block, p).wait_recv()
                use(block)


def attend_kernel(
    n_dp,
    x_ref, gain_ref, shift_ref, w_in_ref, w_out_ref, doc_row_ref, doc_col_ref,
    next_ref, normed_t_ref, context_ref, context_t_ref, kv_ref, q_ref, short_kv_ref, short_q_ref, lse_ref,
    acc_ref, top_ref, total_ref,
    kv_far, kv_near, kv_recv, q_far, q_near, q_recv,
):
    links = Links(n_dp)
    me = links.me
    pairs, long = kv_ref.shape[1], kv_ref.shape[3]
    width = x_ref.shape[1]
    x = x_ref[...]
    center = x - jnp.mean(x, axis=-1, keepdims=True)
    inverse = lax.rsqrt(jnp.mean(center * center, axis=-1, keepdims=True) + epsilon)
    normed = (center * inverse * gain_ref[...] + shift_ref[...]).astype(jnp.bfloat16)

    kv = dot(normed, w_in_ref[:, width:]).astype(jnp.bfloat16)
    for h in range(pairs):
        for part in range(2):
            piece = kv[:, part * width + 128 * h : part * width + 128 * h + 128]
            kv_ref[me, h, part] = piece[:long]
            short_kv_ref[h, part] = piece[long:]
    links.greet()
    kv_spread = Spread(links, lambda b, p: kv_ref.at[b, p], pairs, True, kv_far, kv_near, kv_recv)
    q_spread = Spread(links, lambda b, p: q_ref.at[b], 1, False, q_far, q_near, q_recv)
    for h in range(pairs):
        kv_spread.send(h)
    q = (dot(normed, w_in_ref[:, :width]).astype(jnp.bfloat16) * HEAD_DIM ** (-0.5)).astype(jnp.bfloat16)
    for h in range(pairs):
        piece = q[:, 128 * h : 128 * h + 128]
        q_ref[me, h] = piece[:long]
        short_q_ref[h] = piece[long:]
    q_spread.send(0)
    normed_t_ref[...] = normed.T

    def put_context(h, rows_t, first, count):
        at = pl.ds(pl.multiple_of(128 * h, 128), 128)
        context_t_ref[at, first : first + count] = rows_t.astype(jnp.bfloat16)
        context_ref[first : first + count, at] = rows_t.T.astype(jnp.bfloat16)

    def own_part(h, _):
        seen = short_seen(doc_row_ref[...], doc_col_ref[...])
        scores = jnp.where(seen, dot_rows(short_kv_ref[h, 0], head_pair(short_q_ref[h])), masked_score)
        top = jnp.max(scores, axis=0, keepdims=True)
        weights = jnp.exp(scores - top)
        total = jnp.sum(weights, axis=0, keepdims=True)
        rows_t = pair_rows(dot_columns(short_kv_ref[h, 1], weights.astype(jnp.bfloat16)) / total)
        short = rows_t.shape[1]
        put_context(h, rows_t, long, short)
        lse = top + jnp.log(total)
        lse_ref[h, 0:1, long:] = lse[:, :short]
        lse_ref[h, 1:2, long:] = lse[:, short:]
        scores = jnp.where(causal(long, long), dot_rows(kv_ref[me, h, 0], head_pair(q_ref[me, h])), masked_score)
        top = jnp.max(scores, axis=0, keepdims=True)
        weights = jnp.exp(scores - top)
        top_ref[h] = top
        total_ref[h] = jnp.sum(weights, axis=0, keepdims=True)
        acc_ref[h] = dot_columns(kv_ref[me, h, 1], weights.astype(jnp.bfloat16))
        return 0

    lax.fori_loop(0, pairs, own_part, 0)

    def other_part(h, _):
        kv_spread.relay(h)
        queries = head_pair(q_ref[me, h])

        def use(block):
            scores = dot_rows(kv_ref[block, h, 0], queries)
            old = top_ref[h]
            top = jnp.maximum(old, jnp.max(scores, axis=0, keepdims=True))
            factor = jnp.exp(old - top)
            weights = jnp.exp(scores - top)
            top_ref[h] = top
            total_ref[h] = total_ref[h] * factor + jnp.sum(weights, axis=0, keepdims=True)
            acc_ref[h] = acc_ref[h] * factor + dot_columns(kv_ref[block, h, 1], weights.astype(jnp.bfloat16))

        kv_spread.each(h, use)
        total = total_ref[h]
        put_context(h, pair_rows(acc_ref[h] / total), 0, long)
        lse = top_ref[h] + jnp.log(total)
        lse_ref[h, 0:1, :long] = lse[:, :long]
        lse_ref[h, 1:2, :long] = lse[:, long:]
        return 0

    lax.fori_loop(0, pairs, other_part, 0)
    next_ref[...] = x + dot(context_ref[...], w_out_ref[...])
    q_spread.relay(0)
    q_spread.each(0, lambda block: None)
    q_spread.sent(0)
    for h in range(pairs):
        kv_spread.sent(h)


def spread_sems(n_dp, parts):
    return [
        pltpu.SemaphoreType.DMA((n_dp // 2, parts)),
        pltpu.SemaphoreType.DMA((n_dp, parts)),
        pltpu.SemaphoreType.DMA((n_dp, parts)),
    ]


def attention_forward(n_dp, collective_id, stream, norm_gain, norm_shift, weight_in, weight_out, doc_row, doc_col):
    rows, width = stream.shape
    long, short, pairs = LONG_DEV, rows - LONG_DEV, width // 128
    low = jnp.bfloat16
    outs = [
        jax.ShapeDtypeStruct((rows, width), jnp.float32),
        jax.ShapeDtypeStruct((width, rows), low),
        jax.ShapeDtypeStruct((rows, width), low),
        jax.ShapeDtypeStruct((width, rows), low),
        jax.ShapeDtypeStruct((n_dp, pairs, 2, long, 128), low),
        jax.ShapeDtypeStruct((n_dp, pairs, long, 128), low),
        jax.ShapeDtypeStruct((pairs, 2, short, 128), low),
        jax.ShapeDtypeStruct((pairs, short, 128), low),
        jax.ShapeDtypeStruct((pairs, 2, rows), jnp.float32),
    ]
    vmem = pl.BlockSpec(memory_space=pltpu.VMEM)
    return pl.pallas_call(
        functools.partial(attend_kernel, n_dp),
        out_shape=outs,
        in_specs=[vmem] * 7,
        out_specs=[vmem] * len(outs),
        scratch_shapes=[
            pltpu.VMEM((pairs, 128, 2 * long), jnp.float32),
            pltpu.VMEM((pairs, 1, 2 * long), jnp.float32),
            pltpu.VMEM((pairs, 1, 2 * long), jnp.float32),
        ]
        + spread_sems(n_dp, pairs)
        + spread_sems(n_dp, 1),
        compiler_params=pltpu.CompilerParams(
            collective_id=collective_id, has_side_effects=True, vmem_limit_bytes=48 * 1024 * 1024
        ),
        name="attention_forward",
    )(stream, norm_gain, norm_shift, weight_in, weight_out, doc_row, doc_col)


def attend_back_kernel(
    n_dp,
    up_ref, x_ref, gain_ref, w_in_ref, w_out_ref, doc_row_ref, doc_col_ref,
    context_ref, kv_ref, q_ref, short_kv_ref, short_q_ref, lse_ref,
    up_next_ref, up_low_ref, mixed_ref, sums_ref,
    do_ref, aux_ref, short_do_ref, short_aux_ref, dq_ref, dk_ref, dv_ref,
    do_far, do_near, do_recv, aux_far, aux_near, aux_recv,
):
    links = Links(n_dp)
    me = links.me
    pairs, long, width = kv_ref.shape[1], kv_ref.shape[3], x_ref.shape[1]
    scale = HEAD_DIM ** (-0.5)
    up = up_ref[...]
    up_low = up.astype(jnp.bfloat16)
    up_low_ref[...] = up_low
    grad_context = dot_rows(up_low, w_out_ref[...]).astype(jnp.bfloat16)
    lane = lax.broadcasted_iota(jnp.int32, (8, 128), 1) < HEAD_DIM
    head = lax.broadcasted_iota(jnp.int32, (8, 128), 0)
    picks = jnp.where(((head == 0) & lane) | ((head == 1) & ~lane), 1.0, 0.0)
    for h in range(pairs):
        at = slice(128 * h, 128 * h + 128)
        piece = grad_context[:, at]
        do_ref[me, h] = piece[:long]
        short_do_ref[h] = piece[long:]
        both = piece.astype(jnp.float32) * context_ref[:, at].astype(jnp.float32)
        delta = lax.dot_general(
            picks, both, (((1,), (1,)), ((), ())), precision=lax.Precision.HIGHEST, preferred_element_type=jnp.float32
        )
        aux_ref[me, h, 0:2] = lse_ref[h, :, :long]
        aux_ref[me, h, 2:4] = delta[0:2, :long]
        short_aux_ref[h, 0:2] = lse_ref[h, :, long:]
        short_aux_ref[h, 2:4] = delta[0:2, long:]
    links.greet()
    do_spread = Spread(links, lambda b, p: do_ref.at[b, p], pairs, False, do_far, do_near, do_recv)
    aux_spread = Spread(links, lambda b, p: aux_ref.at[b, p], pairs, False, aux_far, aux_near, aux_recv)
    for h in range(pairs):
        do_spread.send(h)
        aux_spread.send(h)

    def row_of(aux, first):
        return jnp.concatenate([aux[first : first + 1], aux[first + 1 : first + 2]], axis=1)

    def score_grads(keys, values, queries, grads, aux, seen):
        scores = dot_rows(keys, queries)
        probs = jnp.exp(scores - row_of(aux, 0))
        if seen is not None:
            probs = jnp.where(seen, probs, 0.0)
        grad_scores = probs * (dot_rows(values, grads) - row_of(aux, 2))
        return probs.astype(jnp.bfloat16), grad_scores.astype(jnp.bfloat16)

    def put(h, third, first, value):
        at = pl.ds(pl.multiple_of(third * width + 128 * h, 128), 128)
        mixed_ref[first : first + value.shape[0], at] = value.astype(jnp.bfloat16)

    def own_part(h, _):
        seen = short_seen(doc_row_ref[...], doc_col_ref[...])
        queries, grads = head_pair(short_q_ref[h]), head_pair(short_do_ref[h])
        keys = short_kv_ref[h, 0]
        probs, grad_scores = score_grads(keys, short_kv_ref[h, 1], queries, grads, short_aux_ref[h], seen)
        put(h, 0, long, (pair_rows(dot_columns(keys, grad_scores)) * scale).T)
        put(h, 1, long, dot(grad_scores, queries))
        put(h, 2, long, dot(probs, grads))
        queries, grads = head_pair(q_ref[me, h]), head_pair(do_ref[me, h])
        keys = kv_ref[me, h, 0]
        probs, grad_scores = score_grads(keys, kv_ref[me, h, 1], queries, grads, aux_ref[me, h], causal(long, long))
        dq_ref[h] = dot_columns(keys, grad_scores)
        dk_ref[h] = dot(grad_scores, queries)
        dv_ref[h] = dot(probs, grads)
        for block in range(n_dp - 1):

            @pl.when(block < me)
            def _():
                keys = kv_ref[block, h, 0]
                _, grad_scores = score_grads(keys, kv_ref[block, h, 1], queries, grads, aux_ref[me, h], None)
                dq_ref[h] += dot_columns(keys, grad_scores)

        put(h, 0, 0, (pair_rows(dq_ref[h]) * scale).T)
        return 0

    lax.fori_loop(0, pairs, own_part, 0)

    def other_part(h, _):
        do_spread.relay(h)
        aux_spread.relay(h)
        keys, values = kv_ref[me, h, 0], kv_ref[me, h, 1]

        def use(block):
            queries, grads = head_pair(q_ref[block, h]), head_pair(do_ref[block, h])
            probs, grad_scores = score_grads(keys, values, queries, grads, aux_ref[block, h], None)
            dk_ref[h] += dot(grad_scores, queries)
            dv_ref[h] += dot(probs, grads)

        aux_spread.each(h, lambda block: None)
        do_spread.each(h, use)
        put(h, 1, 0, dk_ref[h])
        put(h, 2, 0, dv_ref[h])
        return 0

    lax.fori_loop(0, pairs, other_part, 0)
    grad_normed = dot_rows(mixed_ref[...], w_in_ref[...])
    x = x_ref[...]
    center = x - jnp.mean(x, axis=-1, keepdims=True)
    inverse = lax.rsqrt(jnp.mean(center * center, axis=-1, keepdims=True) + epsilon)
    unit = center * inverse
    scaled = grad_normed * gain_ref[...]
    inner = (
        scaled - jnp.mean(scaled, axis=-1, keepdims=True) - unit * jnp.mean(scaled * unit, axis=-1, keepdims=True)
    )
    up_next_ref[...] = up + inverse * inner
    sums_ref[0:1] = jnp.sum(grad_normed * unit, axis=0, keepdims=True)
    sums_ref[1:2] = jnp.sum(grad_normed, axis=0, keepdims=True)
    for h in range(pairs):
        do_spread.sent(h)
        aux_spread.sent(h)


def attention_backward(n_dp, collective_id, upstream, stream, norm_gain, weight_in, weight_out, doc_row, doc_col, kept):
    rows, width = stream.shape
    long, short, pairs = LONG_DEV, rows - LONG_DEV, width // 128
    low = jnp.bfloat16
    outs = [
        jax.ShapeDtypeStruct((rows, width), jnp.float32),
        jax.ShapeDtypeStruct((rows, width), low),
        jax.ShapeDtypeStruct((rows, 3 * width), low),
        jax.ShapeDtypeStruct((2, width), jnp.float32),
    ]
    vmem = pl.BlockSpec(memory_space=pltpu.VMEM)
    return pl.pallas_call(
        functools.partial(attend_back_kernel, n_dp),
        out_shape=outs,
        in_specs=[vmem] * 13,
        out_specs=[vmem] * len(outs),
        scratch_shapes=[
            pltpu.VMEM((n_dp, pairs, long, 128), low),
            pltpu.VMEM((n_dp, pairs, 8, long), jnp.float32),
            pltpu.VMEM((pairs, short, 128), low),
            pltpu.VMEM((pairs, 8, short), jnp.float32),
            pltpu.VMEM((pairs, 128, 2 * long), jnp.float32),
            pltpu.VMEM((pairs, long, 128), jnp.float32),
            pltpu.VMEM((pairs, long, 128), jnp.float32),
        ]
        + spread_sems(n_dp, pairs)
        + spread_sems(n_dp, pairs),
        compiler_params=pltpu.CompilerParams(
            collective_id=collective_id, has_side_effects=True, vmem_limit_bytes=48 * 1024 * 1024
        ),
        name="attention_backward",
    )(upstream, stream, norm_gain, weight_in, weight_out, doc_row, doc_col, *kept)


def ffn_forward(stream, norm_gain, norm_shift, weight_in, weight_out):
    normed, unit_rows, inverse = norm_forward(stream, norm_gain, norm_shift)
    normed_low = normed.astype(jnp.bfloat16)
    hidden = jnp.dot(normed_low, weight_in, preferred_element_type=jnp.float32)
    active = exact_gelu(hidden).astype(jnp.bfloat16)
    stream_next = stream + jnp.dot(active, weight_out, preferred_element_type=jnp.float32)
    return (stream_next, (unit_rows, inverse, normed_low, hidden, active))


def ffn_backward(upstream, kept_state, norm_gain, weight_in, weight_out):
    unit_rows, inverse, normed_low, hidden, active = kept_state
    upstream_low = upstream.astype(jnp.bfloat16)
    grad_active = jnp.einsum(
        "td,fd->tf", upstream_low, weight_out, preferred_element_type=jnp.float32
    )
    grad_hidden = gelu_backward(hidden, grad_active).astype(jnp.bfloat16)
    grad_normed = jnp.einsum(
        "tf,df->td", grad_hidden, weight_in, preferred_element_type=jnp.float32
    )
    grad_stream, grad_gain, grad_shift = norm_backward(unit_rows, inverse, norm_gain, grad_normed)
    pairs = ((active, upstream_low), (normed_low, grad_hidden))
    return (upstream + grad_stream, pairs, grad_gain, grad_shift)


def mixture_forward(stream, norm_gain, norm_shift, router, expert_in, expert_out, assign_ids):
    normed, unit_rows, inverse = norm_forward(stream, norm_gain, norm_shift)
    normed_low = normed.astype(jnp.bfloat16)
    model_width = stream.shape[1]
    row_count = stream.shape[0]
    experts_all = router.shape[1]
    capacity = (5 * row_count + 4 * experts_all - 1) // (4 * experts_all)
    logits = jnp.dot(normed_low, router, preferred_element_type=jnp.float32)
    expert_numbers = jnp.arange(experts_all, dtype=jnp.int32)
    chosen_hot = (assign_ids[:, None] == expert_numbers[None, :]).astype(jnp.float32)
    gate_value = jax.nn.sigmoid(jnp.sum(logits * chosen_hot, axis=-1))
    counts = lax.psum(jnp.sum(chosen_hot, axis=0), ("dp", "expert"))
    gate_sums = lax.psum(jnp.sum(gate_value[:, None] * chosen_hot, axis=0), ("dp", "expert"))
    tokens_all = row_count * lax.axis_size("dp") * lax.axis_size("expert")
    token_share = counts / tokens_all
    balance = experts_all * jnp.sum((token_share - 1.0 / experts_all) * (gate_sums / tokens_all))
    hot_count = (assign_ids[:, None] == expert_numbers[None, :]).astype(jnp.int32)
    before = jnp.cumsum(hot_count, axis=0) - hot_count
    slot_place = jnp.sum(before * hot_count, axis=-1)
    slot_index = jnp.where(slot_place < capacity, assign_ids * capacity + slot_place, -1)
    dispatch = (
        slot_index[:, None] == jnp.arange(experts_all * capacity, dtype=jnp.int32)[None, :]
    ).astype(jnp.bfloat16)
    outgoing = jnp.einsum(
        "tc,td->cd", dispatch, normed_low, preferred_element_type=jnp.float32
    ).astype(jnp.bfloat16)
    outgoing = outgoing.reshape(experts_all, capacity, model_width)
    incoming = lax.all_to_all(outgoing, "expert", split_axis=0, concat_axis=0, tiled=True)
    slot_count = incoming.shape[1]
    grouped = incoming.reshape(-1, expert_in.shape[0], slot_count, model_width)
    hidden = jnp.einsum("sjcd,jdf->sjcf", grouped, expert_in, preferred_element_type=jnp.float32)
    active = exact_gelu(hidden).astype(jnp.bfloat16)
    result = jnp.einsum(
        "sjcf,jfd->sjcd", active, expert_out, preferred_element_type=jnp.float32
    ).astype(jnp.bfloat16)
    homeward = lax.all_to_all(
        result.reshape(incoming.shape), "expert", split_axis=0, concat_axis=0, tiled=True
    )
    gathered = jnp.dot(
        dispatch,
        homeward.reshape(experts_all * capacity, model_width),
        preferred_element_type=jnp.float32,
    )
    stream_next = stream + gate_value[:, None] * gathered
    kept_state = (
        unit_rows,
        inverse,
        normed_low,
        gate_value,
        token_share,
        tokens_all,
        chosen_hot,
        dispatch,
        gathered,
        incoming,
    )
    return (stream_next, balance, kept_state)


def mixture_backward(upstream, kept_state, norm_gain, router, expert_in, expert_out):
    (
        unit_rows,
        inverse,
        normed_low,
        gate_value,
        token_share,
        tokens_all,
        chosen_hot,
        dispatch,
        gathered,
        arrived,
    ) = kept_state
    model_width = upstream.shape[1]
    experts_all = router.shape[1]
    grad_gate = jnp.sum(upstream * gathered, axis=-1)
    grad_return = (gate_value[:, None] * upstream).astype(jnp.bfloat16)
    outgoing = jnp.einsum(
        "tc,td->cd", dispatch, grad_return, preferred_element_type=jnp.float32
    ).astype(jnp.bfloat16)
    outgoing = outgoing.reshape(experts_all, -1, model_width)
    incoming = lax.all_to_all(outgoing, "expert", split_axis=0, concat_axis=0, tiled=True)
    slot_count = incoming.shape[1]
    grouped_grad = incoming.reshape(-1, expert_in.shape[0], slot_count, model_width)
    grouped_rows = arrived.reshape(-1, expert_in.shape[0], slot_count, model_width)
    hidden = jnp.einsum(
        "sjcd,jdf->sjcf", grouped_rows, expert_in, preferred_element_type=jnp.float32
    )
    active = exact_gelu(hidden).astype(jnp.bfloat16)
    grad_out_weight = jnp.einsum(
        "sjcf,sjcd->jfd", active, grouped_grad, preferred_element_type=jnp.float32
    )
    grad_active = jnp.einsum(
        "sjcd,jfd->sjcf", grouped_grad, expert_out, preferred_element_type=jnp.float32
    )
    grad_hidden = gelu_backward(hidden, grad_active).astype(jnp.bfloat16)
    grad_in_weight = jnp.einsum(
        "sjcd,sjcf->jdf", grouped_rows, grad_hidden, preferred_element_type=jnp.float32
    )
    grad_rows = jnp.einsum(
        "sjcf,jdf->sjcd", grad_hidden, expert_in, preferred_element_type=jnp.float32
    ).astype(jnp.bfloat16)
    homeward = lax.all_to_all(
        grad_rows.reshape(incoming.shape), "expert", split_axis=0, concat_axis=0, tiled=True
    )
    grad_normed = jnp.dot(
        dispatch, homeward.reshape(-1, model_width), preferred_element_type=jnp.float32
    )
    share_weight = balance_weight * experts_all * (token_share - 1.0 / experts_all) / tokens_all
    grad_gate = grad_gate + jnp.sum(chosen_hot * share_weight[None, :], axis=-1)
    grad_chosen = grad_gate * gate_value * (1.0 - gate_value)
    grad_logits = grad_chosen[:, None] * chosen_hot
    router_float = router.astype(jnp.float32)
    grad_router = jnp.einsum(
        "td,te->de", normed_low.astype(jnp.float32), grad_logits, precision=lax.Precision.HIGHEST
    )
    grad_normed = grad_normed + jnp.einsum(
        "te,de->td", grad_logits, router_float, precision=lax.Precision.HIGHEST
    )
    grad_stream, grad_gain, grad_shift = norm_backward(unit_rows, inverse, norm_gain, grad_normed)
    return (
        upstream + grad_stream,
        grad_in_weight,
        grad_out_weight,
        grad_router,
        grad_gain,
        grad_shift,
    )


def shards(
    tokens,
    doc_lengths,
    assign,
    ln_gain,
    ln_bias,
    attn_in,
    attn_out,
    ffn_in,
    ffn_out,
    router,
    expert_in,
    expert_out,
    cotangent,
):
    n_dp, n_ex = lax.axis_size("dp"), lax.axis_size("expert")
    stream_first = tokens[0].astype(jnp.float32)
    row_count = stream_first.shape[0]
    doc_ends = jnp.cumsum(doc_lengths[0, 0])
    short_place = jnp.arange(row_count - LONG_DEV, dtype=jnp.int32)
    short_ids = jnp.sum((short_place[:, None] >= doc_ends[None, :]).astype(jnp.int32), axis=-1)
    doc_row, doc_col = short_ids[None, :], short_ids[:, None]
    weights_in, weights_out = lax.optimization_barrier((attn_in.transpose(1, 0, 2), attn_out.transpose(1, 0, 2)))
    gains, shifts = ln_gain.T, ln_bias.T
    stream_one, *kept_one = attention_forward(
        n_dp, 2, stream_first, gains[0:1], shifts[0:1], weights_in[0], weights_out[0], doc_row, doc_col
    )
    stream_two, kept_two = ffn_forward(stream_one, ln_gain[:, 1], ln_bias[:, 1], ffn_in, ffn_out)
    stream_three, *kept_three = attention_forward(
        n_dp, 3, stream_two, gains[2:3], shifts[2:3], weights_in[1], weights_out[1], doc_row, doc_col
    )
    stream_four, balance, kept_four = mixture_forward(
        stream_three, ln_gain[:, 3], ln_bias[:, 3], router, expert_in, expert_out, assign[0, :, 0]
    )
    output = stream_four.astype(jnp.bfloat16)[None]
    upstream = cotangent[0].astype(jnp.float32)
    upstream, expert_in_grad, expert_out_grad, router_grad, gain_three, shift_three = (
        mixture_backward(upstream, kept_four, ln_gain[:, 3], router, expert_in, expert_out)
    )
    upstream, second_low, second_mixed, second_sums = attention_backward(
        n_dp, 4, upstream, stream_two, gains[2:3], weights_in[1], weights_out[1], doc_row, doc_col,
        kept_three[1:2] + kept_three[3:],
    )
    upstream, dense_pairs, gain_one, shift_one = ffn_backward(upstream, kept_two, ln_gain[:, 1], ffn_in, ffn_out)
    upstream, first_low, first_mixed, first_sums = attention_backward(
        n_dp, 5, upstream, stream_first, gains[0:1], weights_in[0], weights_out[0], doc_row, doc_col,
        kept_one[1:2] + kept_one[3:],
    )
    grad_tokens = upstream.astype(jnp.bfloat16)[None]
    model_width = tokens.shape[2]
    rows = model_width // n_dp

    def blocks_of(acts):
        return acts.T.reshape(n_dp, -1, rows, row_count).astype(jnp.bfloat16)

    pairs = [(blocks_of(x), dy) for x, dy in dense_pairs]
    pairs = (
        [(kept_three[2].reshape(n_dp, 1, rows, row_count), second_low)]
        + [(kept_three[0].reshape(n_dp, 1, rows, row_count), second_mixed)]
        + pairs
        + [(kept_one[2].reshape(n_dp, 1, rows, row_count), first_low)]
        + [(kept_one[0].reshape(n_dp, 1, rows, row_count), first_mixed)]
    )
    chunks = reduce_grads(n_dp, n_ex, pairs, model_width).astype(jnp.float32)

    def wide(first, count):
        return chunks[first : first + count].transpose(1, 0, 2).reshape(rows, count * model_width)

    per_in = attn_in.shape[2] // model_width
    per_ffn = ffn_in.shape[1] // model_width
    at = 0
    second_out = chunks[0]
    second_in = wide(1, per_in)
    at = 1 + per_in
    ffn_out_sum = chunks[at : at + per_ffn].reshape(per_ffn * rows, model_width)
    ffn_in_sum = wide(at + per_ffn, per_ffn)
    at = at + 2 * per_ffn
    first_out = chunks[at]
    first_in = wide(at + 1, per_in)
    small = jnp.concatenate(
        [
            jnp.stack([first_sums[0], gain_one, second_sums[0], gain_three], axis=0),
            jnp.stack([first_sums[1], shift_one, second_sums[1], shift_three], axis=0),
            router_grad.T,
        ],
        axis=0,
    )
    small = lax.psum(small, ("dp", "expert"))
    small = lax.dynamic_slice_in_dim(small, lax.axis_index("dp") * rows, rows, 1).T
    summed = [
        jnp.stack([first_in, second_in], axis=1),
        jnp.stack([first_out, second_out], axis=1),
        ffn_in_sum,
        ffn_out_sum,
        small[:, 8:],
        small[:, :4],
        small[:, 4:8],
    ]
    expert_in_sum, expert_out_sum = (
        lax.psum_scatter(
            expert_in_grad.astype(jnp.bfloat16), "dp", scatter_dimension=1, tiled=True
        ).astype(jnp.float32),
        lax.psum_scatter(
            expert_out_grad.astype(jnp.bfloat16), "dp", scatter_dimension=1, tiled=True
        ).astype(jnp.float32),
    )
    return (
        output,
        balance,
        grad_tokens,
        summed[5],
        summed[6],
        summed[0],
        summed[1],
        summed[2],
        summed[3],
        summed[4],
        expert_in_sum,
        expert_out_sum,
    )


def solution(mesh):
    return jax.shard_map(
        shards,
        mesh=mesh,
        in_specs=(
            P("expert", "dp", None),
            P("expert", "dp", None),
            P("expert", "dp", None),
            P(),
            P(),
            P(),
            P(),
            P(),
            P(),
            P(),
            P("expert", None, None),
            P("expert", None, None),
            P("expert", "dp", None),
        ),
        out_specs=(
            P("expert", "dp", None),
            P(),
            P("expert", "dp", None),
            P("dp", None),
            P("dp", None),
            P("dp", None, None),
            P("dp", None, None),
            P("dp", None),
            P("dp", None),
            P("dp", None),
            P("expert", "dp", None),
            P("expert", "dp", None),
        ),
        check_vma=False,
    )
```

```python
import functools

import jax
import jax.numpy as jnp
from jax import lax
from jax.experimental import pallas as pl
from jax.experimental.pallas import tpu as pltpu
from jax.sharding import PartitionSpec as P

MESH = pl.DeviceIdType.MESH
HEADS = 12
HEAD_DIM = 64
LONG_DEV = 256


epsilon = 1e-05
balance_weight = 0.01
masked_score = -1e30


def bit_of(index, level):
    return (index // (1 << level)) % 2


def flip(index, level):
    return index + (1 << level) * (1 - 2 * bit_of(index, level))


def partner_index(index, mask, levels):
    total = 0
    for level in range(levels):
        own = bit_of(index, level)
        total = total + (1 << level) * (1 - own if (mask >> level) & 1 else own)
    return total


def reduce_plan(n_dp, n_ex, rows):
    dp_levels = n_dp.bit_length() - 1
    ex_levels = n_ex.bit_length() - 1
    halvings, piece = 0, rows
    while halvings < ex_levels and piece % 32 == 0:
        piece //= 2
        halvings += 1
    kinds = [("dp", b) for b in range(dp_levels)]
    kinds += [("half", b) for b in range(halvings)]
    kinds += [("both", b) for b in range(halvings, ex_levels)]
    kinds += [("back", b) for b in reversed(range(halvings))]
    return kinds, halvings, piece


def grad_kernel(n_dp, n_ex, rows, kinds, halvings, firsts, chunks, fin_slots, *refs):
    count, groups = len(kinds), len(firsts)
    x_refs, dy_refs = refs[:groups], refs[groups : 2 * groups]
    small_ref, out_ref, small_out_ref = refs[2 * groups : 2 * groups + 3]
    it = iter(refs[2 * groups + 3 :])
    send_bufs = [next(it) if k[0] != "back" else None for k in kinds]
    recv_bufs = [next(it) if k[0] != "back" else None for k in kinds]
    keep_bufs = [next(it) if k[0] != "back" else None for k in kinds]
    fin = next(it)
    send_sems = [next(it) for _ in kinds]
    recv_sems = [next(it) for _ in kinds]
    small_send, small_recv, small_send_sem, small_recv_sem = it
    t = pl.program_id(0)
    d, e = lax.axis_index("dp"), lax.axis_index("expert")
    dp_levels, ex_levels = n_dp.bit_length() - 1, n_ex.bit_length() - 1

    def peer(kind, level):
        return (flip(d, level), e) if kind == "dp" else (d, flip(e, level))

    @pl.when(t == 0)
    def _():
        barrier = pltpu.get_barrier_semaphore()
        for level in range(dp_levels):
            pl.semaphore_signal(barrier, inc=1, device_id=peer("dp", level), device_id_type=MESH)
        for level in range(ex_levels):
            pl.semaphore_signal(barrier, inc=1, device_id=peer("ex", level), device_id_type=MESH)
        pl.semaphore_wait(barrier, dp_levels + ex_levels)

    def kept_rows(depth):
        start = 0
        for b in range(depth):
            start = start + bit_of(e, b) * (rows >> (b + 1))
        return start

    def copy_of(s, c):
        kind, level = kinds[s]
        slot = lax.rem(c, 2)
        if kind == "back":
            span = rows >> (level + 1)
            at = pl.ds(pl.multiple_of(kept_rows(level + 1), span), span)
            src = fin.at[lax.rem(c, fin_slots), at]
            dst = src
        else:
            src, dst = send_bufs[s].at[slot], recv_bufs[s].at[slot]
        return pltpu.make_async_remote_copy(
            src_ref=src,
            dst_ref=dst,
            send_sem=send_sems[s].at[slot],
            recv_sem=recv_sems[s].at[slot],
            device_id=peer(kind, level),
            device_id_type=MESH,
        )

    def arrive(s, c):
        kind, level = kinds[s]
        copy_of(s, c).wait()
        slot = lax.rem(c, 2)
        if kind == "back":
            return None
        if kind == "dp":
            n = recv_bufs[s].shape[1]
            return [keep_bufs[s][slot, i] + recv_bufs[s][slot, i].astype(jnp.float32) for i in range(n)]
        return [keep_bufs[s][slot] + recv_bufs[s][slot].astype(jnp.float32)]

    def leave(s, c, values):
        kind, level = kinds[s]
        slot = lax.rem(c, 2)
        if kind == "dp":
            for i in range(len(values) // 2):
                send_bufs[s][slot, i] = values[2 * i + 1].astype(jnp.bfloat16)
        elif kind == "half":
            (value,) = values
            half = value.shape[0] // 2
            own = bit_of(e, level)
            top, low = value[:half], value[half:]
            send_bufs[s][slot] = jnp.where(own == 0, low, top).astype(jnp.bfloat16)
        elif kind == "both":
            (value,) = values
            send_bufs[s][slot] = value.astype(jnp.bfloat16)
        elif values is not None:
            (value,) = values
            span = value.shape[0]
            at = pl.ds(pl.multiple_of(kept_rows(halvings), span), span)
            fin[lax.rem(c, fin_slots), at] = value.astype(jnp.bfloat16)
        copy_of(s, c).start()
        if kind == "dp":
            for i in range(len(values) // 2):
                keep_bufs[s][slot, i] = values[2 * i]
        elif kind == "half":
            keep_bufs[s][slot] = jnp.where(own == 0, top, low)
        elif kind == "both":
            keep_bufs[s][slot] = value.astype(jnp.bfloat16).astype(jnp.float32)

    levels = [("dp", b) for b in range(dp_levels)] + [("ex", b) for b in range(ex_levels)]

    def small_copy(i):
        return pltpu.make_async_remote_copy(
            src_ref=small_send.at[i],
            dst_ref=small_recv.at[i],
            send_sem=small_send_sem.at[i],
            recv_sem=small_recv_sem.at[i],
            device_id=peer(*levels[i]),
            device_id_type=MESH,
        )

    for i in range(len(levels) + 1):

        @pl.when(t == i)
        def _(i=i):
            if i == 0:
                value = small_ref[...]
            else:
                small_copy(i - 1).wait()
                value = small_send[i - 1] + small_recv[i - 1]
            if i < len(levels):
                small_send[i] = value
                small_copy(i).start()
            else:
                small_out_ref[...] = value

    ends = list(firsts[1:]) + [chunks]
    for s in reversed(range(count + 1)):
        c = t - s
        if s == 0:
            for g in range(groups):

                @pl.when((c >= firsts[g]) & (c < ends[g]))
                def _(g=g):
                    dy = dy_refs[g][...]
                    slot = lax.rem(c, 2)

                    def piece(mask):
                        q = partner_index(d, mask, dp_levels)
                        return jnp.dot(x_refs[g][q], dy, preferred_element_type=jnp.float32)

                    for i in range(n_dp // 2):
                        send_bufs[0][slot, i] = piece(2 * i + 1).astype(jnp.bfloat16)
                    copy_of(0, c).start()
                    for i in range(n_dp // 2):
                        keep_bufs[0][slot, i] = piece(2 * i)

        else:

            @pl.when((c >= 0) & (c < chunks))
            def _(s=s, c=c):
                values = arrive(s - 1, c)
                if s < count:
                    leave(s, c, values)
                elif kinds[s - 1][0] == "back":
                    out_ref[...] = fin[lax.rem(c, fin_slots)]
                else:
                    out_ref[...] = values[0].astype(jnp.bfloat16)


def reduce_grads(n_dp, n_ex, pairs, small, width):
    _, _, rows, tokens = pairs[0][0].shape
    sizes = [x.shape[1] * (dy.shape[1] // width) for x, dy in pairs]
    firsts = [sum(sizes[:i]) for i in range(len(sizes))]
    chunks = sum(sizes)
    kinds, halvings, piece = reduce_plan(n_dp, n_ex, rows)
    count = len(kinds)
    fin_slots = max(1, halvings + 1)
    shapes = []
    for kind, level in kinds:
        if kind == "dp":
            shapes.append((n_dp >> (level + 1), rows, width))
        elif kind == "half":
            shapes.append((rows >> (level + 1), width))
        elif kind == "both":
            shapes.append((piece, width))
    scratch = [pltpu.VMEM((2,) + s, jnp.bfloat16) for s in shapes] * 2
    scratch += [pltpu.VMEM((2,) + s, jnp.float32) for s in shapes]
    scratch += [pltpu.VMEM((fin_slots, rows, width), jnp.bfloat16)]
    scratch += [pltpu.SemaphoreType.DMA((2,)) for _ in kinds] * 2
    hops = (n_dp * n_ex).bit_length() - 1
    scratch += [pltpu.VMEM((hops,) + small.shape, jnp.float32)] * 2
    scratch += [pltpu.SemaphoreType.DMA((hops,))] * 2
    in_specs = []
    for (x, dy), first, size in zip(pairs, firsts, sizes):
        many = x.shape[1] > 1

        def x_place(t, first=first, size=size, many=many):
            return (0, jnp.clip(t - first, 0, size - 1) if many else 0, 0, 0)

        in_specs.append(pl.BlockSpec((n_dp, None, rows, tokens), x_place))
    for (x, dy), first, size in zip(pairs, firsts, sizes):
        many = dy.shape[1] > width

        def dy_place(t, first=first, size=size, many=many):
            return (0, jnp.clip(t - first, 0, size - 1) if many else 0)

        in_specs.append(pl.BlockSpec((tokens, width), dy_place))
    return pl.pallas_call(
        functools.partial(grad_kernel, n_dp, n_ex, rows, kinds, halvings, firsts, chunks, fin_slots),
        grid=(chunks + count,),
        out_shape=[
            jax.ShapeDtypeStruct((chunks, rows, width), jnp.bfloat16),
            jax.ShapeDtypeStruct(small.shape, jnp.float32),
        ],
        in_specs=in_specs + [pl.BlockSpec(small.shape, lambda t: (0, 0))],
        out_specs=[
            pl.BlockSpec((None, rows, width), lambda t: (jnp.maximum(t - count, 0), 0, 0)),
            pl.BlockSpec(small.shape, lambda t: (0, 0)),
        ],
        scratch_shapes=scratch,
        compiler_params=pltpu.CompilerParams(
            collective_id=1, has_side_effects=True, vmem_limit_bytes=48 * 1024 * 1024
        ),
        name="dense_grads",
    )(*[x for x, _ in pairs], *[dy for _, dy in pairs], small)


def unpack_kernel(per_in, per_ffn, chunk_ref, in_ref, out_ref, ffn_in_ref, ffn_out_ref):
    width = chunk_ref.shape[2]
    at = 0
    for layer in (1, 0):
        out_ref[:, layer, :] = chunk_ref[at].astype(jnp.float32)
        for j in range(per_in):
            in_ref[:, layer, width * j : width * j + width] = chunk_ref[at + 1 + j].astype(jnp.float32)
        at += 1 + per_in
        if layer:
            for j in range(per_ffn):
                ffn_out_ref[j] = chunk_ref[at + j].astype(jnp.float32)
                ffn_in_ref[:, width * j : width * j + width] = chunk_ref[at + per_ffn + j].astype(jnp.float32)
            at += 2 * per_ffn


def unpack(chunks, per_in, per_ffn):
    count, rows, width = chunks.shape
    step = 48 if rows % 48 == 0 else rows
    wide = jnp.float32
    return pl.pallas_call(
        functools.partial(unpack_kernel, per_in, per_ffn),
        grid=(rows // step,),
        out_shape=[
            jax.ShapeDtypeStruct((rows, 2, per_in * width), wide),
            jax.ShapeDtypeStruct((rows, 2, width), wide),
            jax.ShapeDtypeStruct((rows, per_ffn * width), wide),
            jax.ShapeDtypeStruct((per_ffn, rows, width), wide),
        ],
        in_specs=[pl.BlockSpec((count, step, width), lambda i: (0, i, 0))],
        out_specs=[
            pl.BlockSpec((step, 2, per_in * width), lambda i: (i, 0, 0)),
            pl.BlockSpec((step, 2, width), lambda i: (i, 0, 0)),
            pl.BlockSpec((step, per_ffn * width), lambda i: (i, 0)),
            pl.BlockSpec((per_ffn, step, width), lambda i: (0, i, 0)),
        ],
        compiler_params=pltpu.CompilerParams(vmem_limit_bytes=40 * 1024 * 1024),
        name="unpack",
    )(chunks)


def dot(a, b):
    return jnp.dot(a, b, preferred_element_type=jnp.float32)


def dot_rows(a, b):
    return lax.dot_general(a, b, (((1,), (1,)), ((), ())), preferred_element_type=jnp.float32)


def dot_columns(a, b):
    return lax.dot_general(a, b, (((0,), (0,)), ((), ())), preferred_element_type=jnp.float32)


def gelu_parts(hidden):
    lower = 0.5 + 0.5 * lax.erf(hidden * 0.7071067811865476)
    slope = lower + hidden * jnp.exp(-0.5 * hidden * hidden) * 0.3989422804014327
    return hidden * lower, slope


def norm_parts(x):
    center = x - jnp.mean(x, axis=-1, keepdims=True)
    inverse = lax.rsqrt(jnp.mean(center * center, axis=-1, keepdims=True) + epsilon)
    return center * inverse, inverse


def norm_back(unit, inverse, gain, upstream):
    scaled = upstream * gain
    return inverse * (
        scaled - jnp.mean(scaled, axis=-1, keepdims=True) - unit * jnp.mean(scaled * unit, axis=-1, keepdims=True)
    )


def ffn_kernel(x_ref, gain_ref, shift_ref, w_in_ref, w_out_ref, next_ref, normed_t_ref, active_t_ref, slope_ref, normed_ref):
    @pl.when(pl.program_id(0) == 0)
    def _():
        x = x_ref[...]
        unit, _ = norm_parts(x)
        normed = (unit * gain_ref[...] + shift_ref[...]).astype(jnp.bfloat16)
        normed_ref[...] = normed
        normed_t_ref[...] = normed.T
        next_ref[...] = x

    active, slope = gelu_parts(dot(normed_ref[...], w_in_ref[...]))
    active = active.astype(jnp.bfloat16)
    slope_ref[...] = slope.astype(jnp.bfloat16)
    active_t_ref[...] = active.T
    next_ref[...] += dot(active, w_out_ref[...])


def ffn_forward(stream, norm_gain, norm_shift, weight_in, weight_out):
    rows, width = stream.shape
    hidden = weight_in.shape[1]
    low = jnp.bfloat16
    return pl.pallas_call(
        ffn_kernel,
        grid=(hidden // width,),
        out_shape=[
            jax.ShapeDtypeStruct((rows, width), jnp.float32),
            jax.ShapeDtypeStruct((width, rows), low),
            jax.ShapeDtypeStruct((hidden, rows), low),
            jax.ShapeDtypeStruct((rows, hidden), low),
        ],
        in_specs=[
            pl.BlockSpec((rows, width), lambda i: (0, 0)),
            pl.BlockSpec((1, width), lambda i: (0, 0)),
            pl.BlockSpec((1, width), lambda i: (0, 0)),
            pl.BlockSpec((width, width), lambda i: (0, i)),
            pl.BlockSpec((width, width), lambda i: (i, 0)),
        ],
        out_specs=[
            pl.BlockSpec((rows, width), lambda i: (0, 0)),
            pl.BlockSpec((width, rows), lambda i: (0, 0)),
            pl.BlockSpec((width, rows), lambda i: (i, 0)),
            pl.BlockSpec((rows, width), lambda i: (0, i)),
        ],
        scratch_shapes=[pltpu.VMEM((rows, width), low)],
        compiler_params=pltpu.CompilerParams(vmem_limit_bytes=48 * 1024 * 1024),
        name="ffn_forward",
    )(stream, norm_gain, norm_shift, weight_in, weight_out)


def ffn_back_kernel(steps, up_ref, x_ref, gain_ref, w_in_ref, w_out_ref, slope_ref, next_ref, low_ref, hidden_ref, sums_ref, acc_ref):
    i = pl.program_id(0)

    @pl.when(i == 0)
    def _():
        low_ref[...] = up_ref[...].astype(jnp.bfloat16)
        acc_ref[...] = jnp.zeros_like(acc_ref)

    grad = (dot_rows(low_ref[...], w_out_ref[...]) * slope_ref[...].astype(jnp.float32)).astype(jnp.bfloat16)
    hidden_ref[...] = grad
    acc_ref[...] += dot_rows(grad, w_in_ref[...])

    @pl.when(i == steps - 1)
    def _():
        unit, inverse = norm_parts(x_ref[...])
        grad_normed = acc_ref[...]
        next_ref[...] = up_ref[...] + norm_back(unit, inverse, gain_ref[...], grad_normed)
        sums_ref[0:1] = jnp.sum(grad_normed * unit, axis=0, keepdims=True)
        sums_ref[1:2] = jnp.sum(grad_normed, axis=0, keepdims=True)


def ffn_backward(upstream, stream, norm_gain, weight_in, weight_out, slope):
    rows, width = stream.shape
    hidden = weight_in.shape[1]
    low = jnp.bfloat16
    whole = pl.BlockSpec((rows, width), lambda i: (0, 0))
    return pl.pallas_call(
        functools.partial(ffn_back_kernel, hidden // width),
        grid=(hidden // width,),
        out_shape=[
            jax.ShapeDtypeStruct((rows, width), jnp.float32),
            jax.ShapeDtypeStruct((rows, width), low),
            jax.ShapeDtypeStruct((rows, hidden), low),
            jax.ShapeDtypeStruct((2, width), jnp.float32),
        ],
        in_specs=[
            whole,
            whole,
            pl.BlockSpec((1, width), lambda i: (0, 0)),
            pl.BlockSpec((width, width), lambda i: (0, i)),
            pl.BlockSpec((width, width), lambda i: (i, 0)),
            pl.BlockSpec((rows, width), lambda i: (0, i)),
        ],
        out_specs=[
            whole,
            whole,
            pl.BlockSpec((rows, width), lambda i: (0, i)),
            pl.BlockSpec((2, width), lambda i: (0, 0)),
        ],
        scratch_shapes=[pltpu.VMEM((rows, width), jnp.float32)],
        compiler_params=pltpu.CompilerParams(vmem_limit_bytes=48 * 1024 * 1024),
        name="ffn_backward",
    )(upstream, stream, norm_gain, weight_in, weight_out, slope)


def capacity_of(rows, experts):
    capacity = (5 * rows + 4 * experts - 1) // (4 * experts)
    return capacity, -(-capacity // 16) * 16


def chosen_rows(assign, experts):
    expert = lax.broadcasted_iota(jnp.int32, (experts, assign.shape[1]), 0)
    return jnp.where(assign == expert, 1.0, 0.0)


def dispatch_of(assign, experts):
    tokens = assign.shape[1]
    capacity, padded = capacity_of(tokens, experts)
    hot = chosen_rows(assign, experts)
    earlier = lax.broadcasted_iota(jnp.int32, (tokens, tokens), 0) < lax.broadcasted_iota(jnp.int32, (tokens, tokens), 1)
    before = dot(hot.astype(jnp.bfloat16), jnp.where(earlier, 1.0, 0.0).astype(jnp.bfloat16))
    place = jnp.sum(hot * before, axis=0, keepdims=True)
    slot = jnp.where(place < capacity, assign.astype(jnp.float32) * padded + place, -1.0)
    number = lax.broadcasted_iota(jnp.int32, (experts * padded, tokens), 0).astype(jnp.float32)
    return jnp.where(number == slot, 1.0, 0.0).astype(jnp.bfloat16)


class Across:
    def __init__(self, experts, out, into, send_sems, recv_sems):
        self.experts, self.out, self.into = experts, out, into
        self.send_sems, self.recv_sems = send_sems, recv_sems
        self.dp, self.me = lax.axis_index("dp"), lax.axis_index("expert")

    def copy(self, slab, place, to):
        return pltpu.make_async_remote_copy(
            src_ref=self.out.at[slab],
            dst_ref=self.into.at[place],
            send_sem=self.send_sems.at[slab],
            recv_sem=self.recv_sems.at[place],
            device_id=(self.dp, to),
            device_id_type=MESH,
        )

    def start(self, j):
        self.copy(j, self.me, j).start()

    def wait_from(self, j):
        self.copy(j, j, j).wait_recv()

    def wait_to(self, j):
        self.copy(j, self.me, j).wait_send()

    def others(self, use):
        def body(k, _):
            use(lax.rem(self.me + k, self.experts))
            return 0

        lax.fori_loop(1, self.experts, body, 0)

    def start_all(self):
        self.others(self.start)

    def wait_all(self):
        def both(j):
            self.wait_from(j)
            self.wait_to(j)

        self.others(both)


def greet(targets):
    barrier = pltpu.get_barrier_semaphore()
    for device in targets:
        pl.semaphore_signal(barrier, inc=1, device_id=device, device_id_type=MESH)
    pl.semaphore_wait(barrier, len(targets))


def across_peers(experts):
    d, e = lax.axis_index("dp"), lax.axis_index("expert")
    return [(d, lax.rem(e + k, experts)) for k in range(1, experts)]


def mixture_kernel(
    n_dp, n_ex,
    x_ref, gain_ref, shift_ref, router_ref, assign_ref, cot_ref, far_cot_ref, w_in_ref, w_out_ref,
    up_ref, sums_ref, router_grad_ref, rows_ref, back_ref, active_ref, hidden_ref, result_ref, gate_ref, stats_ref,
    send_ref, grad_ref, home_ref, dgate_ref, home_dgate_ref, stat_send, stat_recv, dispatch_ref, result_acc, grad_acc,
    x_send_sem, x_recv_sem, grad_send_sem, grad_recv_sem, dgate_send_sem, dgate_recv_sem, stat_send_sem, stat_recv_sem,
):
    d, e = lax.axis_index("dp"), lax.axis_index("expert")
    dp_levels, ex_levels = n_dp.bit_length() - 1, n_ex.bit_length() - 1
    tokens, width = x_ref.shape
    padded = send_ref.shape[1]
    group = min(4, n_ex)
    groups = n_ex // group
    exact = dict(precision=lax.Precision.HIGHEST, preferred_element_type=jnp.float32)
    hops = [(flip(d, b), e) for b in range(dp_levels)] + [(d, flip(e, b)) for b in range(ex_levels)]
    greet([(flip(d, b), e) for b in range(dp_levels)] + across_peers(n_ex))

    unit, inverse = norm_parts(x_ref[...])
    routed = (unit * gain_ref[...] + shift_ref[...]).astype(jnp.bfloat16)
    assign = assign_ref[...]
    dispatch = dispatch_of(assign, n_ex)
    dispatch_ref[...] = dispatch
    send_ref[...] = dot(dispatch, routed).astype(jnp.bfloat16).reshape(send_ref.shape)
    x_across = Across(n_ex, send_ref, rows_ref, x_send_sem, x_recv_sem)
    x_across.start_all()
    rows_ref[e] = send_ref[e]
    hot = chosen_rows(assign, n_ex)
    gate = jax.nn.sigmoid(jnp.sum(hot * dot_rows(router_ref[...], routed), axis=0, keepdims=True))
    gate_ref[...] = gate

    def stat_copy(i):
        return pltpu.make_async_remote_copy(
            src_ref=stat_send.at[i],
            dst_ref=stat_recv.at[i],
            send_sem=stat_send_sem.at[i],
            recv_sem=stat_recv_sem.at[i],
            device_id=hops[i],
            device_id_type=MESH,
        )

    lane = lax.broadcasted_iota(jnp.int32, stats_ref.shape, 1)
    stat_send[0] = jnp.where(
        lane == 0, jnp.sum(hot, axis=1, keepdims=True), jnp.sum(hot * gate, axis=1, keepdims=True)
    )
    stat_copy(0).start()

    def stat_step(i):
        stat_copy(i).wait()
        value = stat_send[i] + stat_recv[i]
        if i + 1 < len(hops):
            stat_send[i + 1] = value
            stat_copy(i + 1).start()
        else:
            stats_ref[...] = value

    grad_across = Across(n_ex, grad_ref, home_ref, grad_send_sem, grad_recv_sem)
    dgate_across = Across(n_ex, dgate_ref, home_dgate_ref, dgate_send_sem, dgate_recv_sem)
    step = 768 if w_in_ref.shape[1] % 768 == 0 else w_in_ref.shape[1]
    done = 0
    for k in range(groups):
        first = lax.rem(e // group + k, groups) * group
        for m in range(group):

            @pl.when(first + m != e)
            def _(m=m):
                x_across.wait_from(first + m)

        at = pl.ds(first, group)
        rows = rows_ref[at].reshape(group * padded, width)
        cot = far_cot_ref[at].reshape(group * padded, width).astype(jnp.float32)
        logits = dot_rows(rows, router_ref[...])
        own = lax.broadcasted_iota(jnp.int32, logits.shape, 1) == e
        slot_gate = jax.nn.sigmoid(jnp.sum(jnp.where(own, logits, 0.0), axis=1, keepdims=True))
        back = (slot_gate * cot).astype(jnp.bfloat16)
        back_ref[at] = back.reshape(group, padded, width)
        result_acc[...] = jnp.zeros_like(result_acc)
        grad_acc[...] = jnp.zeros_like(grad_acc)
        span = pl.ds(pl.multiple_of(first * padded, group * padded), group * padded)

        def block(i, _):
            cols = pl.ds(pl.multiple_of(i * step, step), step)
            active, slope = gelu_parts(dot(rows, w_in_ref[:, cols]))
            active = active.astype(jnp.bfloat16)
            hidden = (slope * dot_rows(back, w_out_ref[cols, :])).astype(jnp.bfloat16)
            active_ref[span, cols] = active
            hidden_ref[span, cols] = hidden
            result_acc[...] += dot(active, w_out_ref[cols, :])
            grad_acc[...] += dot_rows(hidden, w_in_ref[:, cols])
            return 0

        lax.fori_loop(0, w_in_ref.shape[1] // step, block, 0)
        grad_ref[at] = grad_acc[...].astype(jnp.bfloat16).reshape(group, padded, width)
        result = result_acc[...].astype(jnp.bfloat16)
        result_ref[at] = result.reshape(group, padded, width)
        dgate = lax.dot_general(
            jnp.ones((8, width), jnp.float32), cot * result.astype(jnp.float32), (((1,), (1,)), ((), ())), **exact
        )
        for m in range(group):
            dgate_ref[first + m, :, :padded] = dgate[:, m * padded : (m + 1) * padded]

            @pl.when(first + m != e)
            def _(m=m):
                grad_across.start(first + m)
                dgate_across.start(first + m)

            @pl.when(first + m == e)
            def _():
                home_ref[e] = grad_ref[e]
                home_dgate_ref[e] = dgate_ref[e]

        if done < len(hops):
            stat_step(done)
            done += 1

    for i in range(done, len(hops)):
        stat_step(i)
    x_across.others(x_across.wait_to)
    dgate_across.wait_all()
    dgate = jnp.zeros((8, tokens), jnp.float32)
    for j in range(n_ex):
        part = dispatch_ref[j * padded : (j + 1) * padded].astype(jnp.float32)
        dgate = dgate + jnp.dot(home_dgate_ref[j, :, :padded], part, **exact)
    everyone = tokens * n_dp * n_ex
    share = jnp.sum(jnp.where(lane == 0, stats_ref[...], 0.0), axis=1, keepdims=True) / everyone
    weight = balance_weight * n_ex * (share - 1.0 / n_ex) / everyone
    grad_gate = dgate[0:1] + jnp.sum(hot * weight, axis=0, keepdims=True)
    grad_logits = hot * (grad_gate * gate * (1.0 - gate))
    router_grad_ref[...] = jnp.dot(grad_logits, routed.astype(jnp.float32), **exact)
    grad_normed = lax.dot_general(
        grad_logits, router_ref[...].astype(jnp.float32), (((0,), (0,)), ((), ())), **exact
    )
    grad_across.wait_all()
    grad_normed = grad_normed + dot_columns(dispatch_ref[...], home_ref[...].reshape(n_ex * padded, width))
    up_ref[...] = cot_ref[...].astype(jnp.float32) + norm_back(unit, inverse, gain_ref[...], grad_normed)
    sums_ref[0:1] = jnp.sum(grad_normed * unit, axis=0, keepdims=True)
    sums_ref[1:2] = jnp.sum(grad_normed, axis=0, keepdims=True)


def mixture(n_dp, n_ex, collective_id, stream, norm_gain, norm_shift, router_t, assign, cot, far_cot, weight_in, weight_out):
    tokens, width = stream.shape
    hidden = weight_in.shape[1]
    _, padded = capacity_of(tokens, n_ex)
    slots = n_ex * padded
    group = min(4, n_ex) * padded
    low, wide = jnp.bfloat16, jnp.float32
    slab = (n_ex, padded, width)
    hops = (n_dp * n_ex).bit_length() - 1
    outs = [
        jax.ShapeDtypeStruct((tokens, width), wide),
        jax.ShapeDtypeStruct((2, width), wide),
        jax.ShapeDtypeStruct((n_ex, width), wide),
        jax.ShapeDtypeStruct(slab, low),
        jax.ShapeDtypeStruct(slab, low),
        jax.ShapeDtypeStruct((slots, hidden), low),
        jax.ShapeDtypeStruct((slots, hidden), low),
        jax.ShapeDtypeStruct(slab, low),
        jax.ShapeDtypeStruct((1, tokens), wide),
        jax.ShapeDtypeStruct((n_ex, 128), wide),
    ]
    vmem = pl.BlockSpec(memory_space=pltpu.VMEM)
    return pl.pallas_call(
        functools.partial(mixture_kernel, n_dp, n_ex),
        out_shape=outs,
        in_specs=[vmem] * 9,
        out_specs=[vmem] * len(outs),
        scratch_shapes=[
            pltpu.VMEM(slab, low),
            pltpu.VMEM(slab, low),
            pltpu.VMEM(slab, low),
            pltpu.VMEM((n_ex, 8, 128), wide),
            pltpu.VMEM((n_ex, 8, 128), wide),
            pltpu.VMEM((hops, n_ex, 128), wide),
            pltpu.VMEM((hops, n_ex, 128), wide),
            pltpu.VMEM((slots, tokens), low),
            pltpu.VMEM((group, width), wide),
            pltpu.VMEM((group, width), wide),
        ]
        + [pltpu.SemaphoreType.DMA((n_ex,)) for _ in range(6)]
        + [pltpu.SemaphoreType.DMA((hops,)) for _ in range(2)],
        compiler_params=pltpu.CompilerParams(
            collective_id=collective_id, has_side_effects=True, vmem_limit_bytes=56 * 1024 * 1024
        ),
        name="mixture",
    )(stream, norm_gain, norm_shift, router_t, assign, cot, far_cot, weight_in, weight_out)


def head_pair(rows):
    first = lax.broadcasted_iota(jnp.int32, rows.shape, 1) < HEAD_DIM
    zero = jnp.zeros_like(rows)
    return jnp.concatenate([jnp.where(first, rows, zero), jnp.where(first, zero, rows)], axis=0)


def pair_rows(both):
    n = both.shape[1] // 2
    return jnp.concatenate([both[:HEAD_DIM, :n], both[HEAD_DIM:, n:]], axis=0)


def causal(keys, queries):
    key = lax.broadcasted_iota(jnp.int32, (keys, 2 * queries), 0)
    query = lax.broadcasted_iota(jnp.int32, (keys, 2 * queries), 1)
    return key <= jnp.where(query >= queries, query - queries, query)


def short_seen(doc_row, doc_col):
    n = doc_row.shape[1]
    same = doc_col == jnp.concatenate([doc_row, doc_row], axis=1)
    return same & causal(n, n)


class Links:
    def __init__(self, n_dp):
        self.me, self.expert = lax.axis_index("dp"), lax.axis_index("expert")
        self.chips = n_dp // 2
        self.chip, self.core = self.me // 2, self.me % 2
        self.twin = self.me + 1 - 2 * self.core

    def peers(self):
        ring = [lax.rem(self.chip + k, self.chips) for k in range(1, self.chips)]
        return [(self.twin, self.expert)] + [(2 * other + self.core, self.expert) for other in ring]

    def copy(self, ref, send_sem, recv_sem, index):
        return pltpu.make_async_remote_copy(
            src_ref=ref,
            dst_ref=ref,
            send_sem=send_sem,
            recv_sem=recv_sem,
            device_id=(index, self.expert),
            device_id_type=MESH,
        )

    def before(self, later, other):
        return other > self.chip if later else other < self.chip


class Spread:
    def __init__(self, links, at, parts, later, far_sems, near_sems, recv_sems):
        self.links, self.at, self.later = links, at, later
        self.far_sems, self.near_sems, self.recv_sems = far_sems, near_sems, recv_sems

    def _far(self, other, p):
        k = self.links
        return k.copy(self.at(k.me, p), self.far_sems.at[other, p], self.recv_sems.at[k.me, p], 2 * other + k.core)

    def _near(self, block, p):
        k = self.links
        return k.copy(self.at(block, p), self.near_sems.at[block, p], self.recv_sems.at[block, p], k.twin)

    def _twin_needs(self):
        return self.links.core == (0 if self.later else 1)

    def send(self, p):
        k = self.links
        for other in range(k.chips):

            @pl.when(k.before(self.later, other))
            def _():
                self._far(other, p).start()

        @pl.when(self._twin_needs())
        def _():
            self._near(k.me, p).start()

    def sent(self, p):
        k = self.links
        for other in range(k.chips):

            @pl.when(k.before(self.later, other))
            def _():
                self._far(other, p).wait_send()

            @pl.when(k.before(not self.later, other))
            def _():
                self._near(2 * other + k.core, p).wait_send()

        @pl.when(self._twin_needs())
        def _():
            self._near(k.me, p).wait_send()

    def relay(self, p):
        k = self.links
        for other in range(k.chips):

            @pl.when(k.before(not self.later, other))
            def _():
                block = 2 * other + k.core
                copy = self._near(block, p)
                copy.wait_recv()
                copy.start()

    def each(self, p, use):
        k = self.links

        @pl.when(k.core == (1 if self.later else 0))
        def _():
            self._near(k.twin, p).wait_recv()
            use(k.twin)

        for other in range(k.chips):

            @pl.when(k.before(not self.later, other))
            def _():
                use(2 * other + k.core)
                block = 2 * other + 1 - k.core
                self._near(block, p).wait_recv()
                use(block)


def attend_kernel(
    n_dp, n_ex, inputs, *refs
):
    (x_ref, gain_ref, shift_ref, w_in_ref, w_out_ref, doc_row_ref, doc_col_ref), rest = refs[:7], refs[7:]
    if inputs > 7:
        (assign_ref, cot_ref), rest = rest[:2], rest[2:]
    (
        next_ref, normed_t_ref, context_ref, context_t_ref, kv_ref, q_ref, short_kv_ref, short_q_ref, lse_ref,
    ), rest = rest[:9], rest[9:]
    if inputs > 7:
        (far_cot_ref,), rest = rest[:1], rest[1:]
    (acc_ref, top_ref, total_ref, kv_far, kv_near, kv_recv, q_far, q_near, q_recv), rest = rest[:9], rest[9:]
    links = Links(n_dp)
    me = links.me
    pairs, long = kv_ref.shape[1], kv_ref.shape[3]
    width = x_ref.shape[1]
    x = x_ref[...]
    center = x - jnp.mean(x, axis=-1, keepdims=True)
    inverse = lax.rsqrt(jnp.mean(center * center, axis=-1, keepdims=True) + epsilon)
    normed = (center * inverse * gain_ref[...] + shift_ref[...]).astype(jnp.bfloat16)

    kv = dot(normed, w_in_ref[:, width:]).astype(jnp.bfloat16)
    for h in range(pairs):
        for part in range(2):
            piece = kv[:, part * width + 128 * h : part * width + 128 * h + 128]
            kv_ref[me, h, part] = piece[:long]
            short_kv_ref[h, part] = piece[long:]
    greet(links.peers() + (across_peers(n_ex) if inputs > 7 else []))
    kv_spread = Spread(links, lambda b, p: kv_ref.at[b, p], pairs, True, kv_far, kv_near, kv_recv)
    q_spread = Spread(links, lambda b, p: q_ref.at[b], 1, False, q_far, q_near, q_recv)
    for h in range(pairs):
        kv_spread.send(h)
    q = (dot(normed, w_in_ref[:, :width]).astype(jnp.bfloat16) * HEAD_DIM ** (-0.5)).astype(jnp.bfloat16)
    for h in range(pairs):
        piece = q[:, 128 * h : 128 * h + 128]
        q_ref[me, h] = piece[:long]
        short_q_ref[h] = piece[long:]
    q_spread.send(0)
    if inputs > 7:
        cot_send_ref, cot_send_sem, cot_recv_sem = rest
        cot_send_ref[...] = dot(dispatch_of(assign_ref[...], n_ex), cot_ref[...]).astype(jnp.bfloat16).reshape(
            cot_send_ref.shape
        )
        cot_across = Across(n_ex, cot_send_ref, far_cot_ref, cot_send_sem, cot_recv_sem)
        cot_across.start_all()
        far_cot_ref[links.expert] = cot_send_ref[links.expert]
    normed_t_ref[...] = normed.T

    def put_context(h, rows_t, first, count):
        at = pl.ds(pl.multiple_of(128 * h, 128), 128)
        context_t_ref[at, first : first + count] = rows_t.astype(jnp.bfloat16)
        context_ref[first : first + count, at] = rows_t.T.astype(jnp.bfloat16)

    def own_part(h, _):
        seen = short_seen(doc_row_ref[...], doc_col_ref[...])
        scores = jnp.where(seen, dot_rows(short_kv_ref[h, 0], head_pair(short_q_ref[h])), masked_score)
        top = jnp.max(scores, axis=0, keepdims=True)
        weights = jnp.exp(scores - top)
        total = jnp.sum(weights, axis=0, keepdims=True)
        rows_t = pair_rows(dot_columns(short_kv_ref[h, 1], weights.astype(jnp.bfloat16)) / total)
        short = rows_t.shape[1]
        put_context(h, rows_t, long, short)
        lse = top + jnp.log(total)
        lse_ref[h, 0:1, long:] = lse[:, :short]
        lse_ref[h, 1:2, long:] = lse[:, short:]
        scores = jnp.where(causal(long, long), dot_rows(kv_ref[me, h, 0], head_pair(q_ref[me, h])), masked_score)
        top = jnp.max(scores, axis=0, keepdims=True)
        weights = jnp.exp(scores - top)
        top_ref[h] = top
        total_ref[h] = jnp.sum(weights, axis=0, keepdims=True)
        acc_ref[h] = dot_columns(kv_ref[me, h, 1], weights.astype(jnp.bfloat16))
        return 0

    lax.fori_loop(0, pairs, own_part, 0)

    def other_part(h, _):
        kv_spread.relay(h)
        queries = head_pair(q_ref[me, h])

        def use(block):
            scores = dot_rows(kv_ref[block, h, 0], queries)
            old = top_ref[h]
            top = jnp.maximum(old, jnp.max(scores, axis=0, keepdims=True))
            factor = jnp.exp(old - top)
            weights = jnp.exp(scores - top)
            top_ref[h] = top
            total_ref[h] = total_ref[h] * factor + jnp.sum(weights, axis=0, keepdims=True)
            acc_ref[h] = acc_ref[h] * factor + dot_columns(kv_ref[block, h, 1], weights.astype(jnp.bfloat16))

        kv_spread.each(h, use)
        total = total_ref[h]
        put_context(h, pair_rows(acc_ref[h] / total), 0, long)
        lse = top_ref[h] + jnp.log(total)
        lse_ref[h, 0:1, :long] = lse[:, :long]
        lse_ref[h, 1:2, :long] = lse[:, long:]
        return 0

    lax.fori_loop(0, pairs, other_part, 0)
    next_ref[...] = x + dot(context_ref[...], w_out_ref[...])
    q_spread.relay(0)
    q_spread.each(0, lambda block: None)
    q_spread.sent(0)
    for h in range(pairs):
        kv_spread.sent(h)
    if inputs > 7:
        cot_across.wait_all()


def spread_sems(n_dp, parts):
    return [
        pltpu.SemaphoreType.DMA((n_dp // 2, parts)),
        pltpu.SemaphoreType.DMA((n_dp, parts)),
        pltpu.SemaphoreType.DMA((n_dp, parts)),
    ]


def attention_forward(
    n_dp, n_ex, collective_id, stream, norm_gain, norm_shift, weight_in, weight_out, doc_row, doc_col, routing=()
):
    rows, width = stream.shape
    long, short, pairs = LONG_DEV, rows - LONG_DEV, width // 128
    low = jnp.bfloat16
    outs = [
        jax.ShapeDtypeStruct((rows, width), jnp.float32),
        jax.ShapeDtypeStruct((width, rows), low),
        jax.ShapeDtypeStruct((rows, width), low),
        jax.ShapeDtypeStruct((width, rows), low),
        jax.ShapeDtypeStruct((n_dp, pairs, 2, long, 128), low),
        jax.ShapeDtypeStruct((n_dp, pairs, long, 128), low),
        jax.ShapeDtypeStruct((pairs, 2, short, 128), low),
        jax.ShapeDtypeStruct((pairs, short, 128), low),
        jax.ShapeDtypeStruct((pairs, 2, rows), jnp.float32),
    ]
    scratch = [
        pltpu.VMEM((pairs, 128, 2 * long), jnp.float32),
        pltpu.VMEM((pairs, 1, 2 * long), jnp.float32),
        pltpu.VMEM((pairs, 1, 2 * long), jnp.float32),
    ]
    scratch += spread_sems(n_dp, pairs) + spread_sems(n_dp, 1)
    if routing:
        slab = (n_ex, capacity_of(rows, n_ex)[1], width)
        outs += [jax.ShapeDtypeStruct(slab, low)]
        scratch += [pltpu.VMEM(slab, low)] + [pltpu.SemaphoreType.DMA((n_ex,))] * 2
    inputs = (stream, norm_gain, norm_shift, weight_in, weight_out, doc_row, doc_col) + tuple(routing)
    vmem = pl.BlockSpec(memory_space=pltpu.VMEM)
    return pl.pallas_call(
        functools.partial(attend_kernel, n_dp, n_ex, len(inputs)),
        out_shape=outs,
        in_specs=[vmem] * len(inputs),
        out_specs=[vmem] * len(outs),
        scratch_shapes=scratch,
        compiler_params=pltpu.CompilerParams(
            collective_id=collective_id, has_side_effects=True, vmem_limit_bytes=48 * 1024 * 1024
        ),
        name="attention_forward",
    )(*inputs)


def attend_back_kernel(n_dp, n_ex, inputs, *refs):
    (up_ref, x_ref, gain_ref, w_in_ref, w_out_ref, doc_row_ref, doc_col_ref), rest = refs[:7], refs[7:]
    (context_ref, kv_ref, q_ref, short_kv_ref, short_q_ref, lse_ref), rest = rest[:6], rest[6:]
    if inputs > 13:
        (assign_ref, gate_ref, stream_ref, result_ref), rest = rest[:4], rest[4:]
    (up_next_ref, up_low_ref, mixed_ref, sums_ref), rest = rest[:4], rest[4:]
    if inputs > 13:
        (output_ref,), rest = rest[:1], rest[1:]
    (do_ref, aux_ref, short_do_ref, short_aux_ref, dq_ref, dk_ref, dv_ref), rest = rest[:7], rest[7:]
    (do_far, do_near, do_recv, aux_far, aux_near, aux_recv), rest = rest[:6], rest[6:]
    links = Links(n_dp)
    me = links.me
    pairs, long, width = kv_ref.shape[1], kv_ref.shape[3], x_ref.shape[1]
    scale = HEAD_DIM ** (-0.5)
    up = up_ref[...]
    up_low = up.astype(jnp.bfloat16)
    up_low_ref[...] = up_low
    grad_context = dot_rows(up_low, w_out_ref[...]).astype(jnp.bfloat16)
    lane = lax.broadcasted_iota(jnp.int32, (8, 128), 1) < HEAD_DIM
    head = lax.broadcasted_iota(jnp.int32, (8, 128), 0)
    picks = jnp.where(((head == 0) & lane) | ((head == 1) & ~lane), 1.0, 0.0)
    for h in range(pairs):
        at = slice(128 * h, 128 * h + 128)
        piece = grad_context[:, at]
        do_ref[me, h] = piece[:long]
        short_do_ref[h] = piece[long:]
        both = piece.astype(jnp.float32) * context_ref[:, at].astype(jnp.float32)
        delta = lax.dot_general(
            picks, both, (((1,), (1,)), ((), ())), precision=lax.Precision.HIGHEST, preferred_element_type=jnp.float32
        )
        aux_ref[me, h, 0:2] = lse_ref[h, :, :long]
        aux_ref[me, h, 2:4] = delta[0:2, :long]
        short_aux_ref[h, 0:2] = lse_ref[h, :, long:]
        short_aux_ref[h, 2:4] = delta[0:2, long:]
    greet(links.peers() + (across_peers(n_ex) if inputs > 13 else []))
    do_spread = Spread(links, lambda b, p: do_ref.at[b, p], pairs, False, do_far, do_near, do_recv)
    aux_spread = Spread(links, lambda b, p: aux_ref.at[b, p], pairs, False, aux_far, aux_near, aux_recv)
    for h in range(pairs):
        do_spread.send(h)
        aux_spread.send(h)
    if inputs > 13:
        home_ref, result_send_sem, result_recv_sem = rest
        result_across = Across(n_ex, result_ref, home_ref, result_send_sem, result_recv_sem)
        result_across.start_all()
        home_ref[links.expert] = result_ref[links.expert]

    def row_of(aux, first):
        return jnp.concatenate([aux[first : first + 1], aux[first + 1 : first + 2]], axis=1)

    def score_grads(keys, values, queries, grads, aux, seen):
        scores = dot_rows(keys, queries)
        probs = jnp.exp(scores - row_of(aux, 0))
        if seen is not None:
            probs = jnp.where(seen, probs, 0.0)
        grad_scores = probs * (dot_rows(values, grads) - row_of(aux, 2))
        return probs.astype(jnp.bfloat16), grad_scores.astype(jnp.bfloat16)

    def put(h, third, first, value):
        at = pl.ds(pl.multiple_of(third * width + 128 * h, 128), 128)
        mixed_ref[first : first + value.shape[0], at] = value.astype(jnp.bfloat16)

    def own_part(h, _):
        seen = short_seen(doc_row_ref[...], doc_col_ref[...])
        queries, grads = head_pair(short_q_ref[h]), head_pair(short_do_ref[h])
        keys = short_kv_ref[h, 0]
        probs, grad_scores = score_grads(keys, short_kv_ref[h, 1], queries, grads, short_aux_ref[h], seen)
        put(h, 0, long, (pair_rows(dot_columns(keys, grad_scores)) * scale).T)
        put(h, 1, long, dot(grad_scores, queries))
        put(h, 2, long, dot(probs, grads))
        queries, grads = head_pair(q_ref[me, h]), head_pair(do_ref[me, h])
        keys = kv_ref[me, h, 0]
        probs, grad_scores = score_grads(keys, kv_ref[me, h, 1], queries, grads, aux_ref[me, h], causal(long, long))
        dq_ref[h] = dot_columns(keys, grad_scores)
        dk_ref[h] = dot(grad_scores, queries)
        dv_ref[h] = dot(probs, grads)
        for block in range(n_dp - 1):

            @pl.when(block < me)
            def _():
                keys = kv_ref[block, h, 0]
                _, grad_scores = score_grads(keys, kv_ref[block, h, 1], queries, grads, aux_ref[me, h], None)
                dq_ref[h] += dot_columns(keys, grad_scores)

        put(h, 0, 0, (pair_rows(dq_ref[h]) * scale).T)
        return 0

    lax.fori_loop(0, pairs, own_part, 0)

    def other_part(h, _):
        do_spread.relay(h)
        aux_spread.relay(h)
        keys, values = kv_ref[me, h, 0], kv_ref[me, h, 1]

        def use(block):
            queries, grads = head_pair(q_ref[block, h]), head_pair(do_ref[block, h])
            probs, grad_scores = score_grads(keys, values, queries, grads, aux_ref[block, h], None)
            dk_ref[h] += dot(grad_scores, queries)
            dv_ref[h] += dot(probs, grads)

        aux_spread.each(h, lambda block: None)
        do_spread.each(h, use)
        put(h, 1, 0, dk_ref[h])
        put(h, 2, 0, dv_ref[h])
        return 0

    lax.fori_loop(0, pairs, other_part, 0)
    grad_normed = dot_rows(mixed_ref[...], w_in_ref[...])
    x = x_ref[...]
    center = x - jnp.mean(x, axis=-1, keepdims=True)
    inverse = lax.rsqrt(jnp.mean(center * center, axis=-1, keepdims=True) + epsilon)
    unit = center * inverse
    scaled = grad_normed * gain_ref[...]
    inner = (
        scaled - jnp.mean(scaled, axis=-1, keepdims=True) - unit * jnp.mean(scaled * unit, axis=-1, keepdims=True)
    )
    up_next_ref[...] = up + inverse * inner
    sums_ref[0:1] = jnp.sum(grad_normed * unit, axis=0, keepdims=True)
    sums_ref[1:2] = jnp.sum(grad_normed, axis=0, keepdims=True)
    for h in range(pairs):
        do_spread.sent(h)
        aux_spread.sent(h)
    if inputs > 13:
        result_across.wait_all()
        dispatch = dispatch_of(assign_ref[...], n_ex)
        result = dot_columns(dispatch, home_ref[...].reshape(dispatch.shape[0], width))
        gate = jnp.broadcast_to(gate_ref[...], (128, gate_ref.shape[1])).T[:, 0:1]
        output_ref[...] = (stream_ref[...] + gate * result).astype(jnp.bfloat16)


def attention_backward(
    n_dp, n_ex, collective_id, upstream, stream, norm_gain, weight_in, weight_out, doc_row, doc_col, kept, routing=()
):
    rows, width = stream.shape
    long, short, pairs = LONG_DEV, rows - LONG_DEV, width // 128
    low = jnp.bfloat16
    outs = [
        jax.ShapeDtypeStruct((rows, width), jnp.float32),
        jax.ShapeDtypeStruct((rows, width), low),
        jax.ShapeDtypeStruct((rows, 3 * width), low),
        jax.ShapeDtypeStruct((2, width), jnp.float32),
    ]
    scratch = [
        pltpu.VMEM((n_dp, pairs, long, 128), low),
        pltpu.VMEM((n_dp, pairs, 8, long), jnp.float32),
        pltpu.VMEM((pairs, short, 128), low),
        pltpu.VMEM((pairs, 8, short), jnp.float32),
        pltpu.VMEM((pairs, 128, 2 * long), jnp.float32),
        pltpu.VMEM((pairs, long, 128), jnp.float32),
        pltpu.VMEM((pairs, long, 128), jnp.float32),
    ]
    scratch += spread_sems(n_dp, pairs) + spread_sems(n_dp, pairs)
    if routing:
        outs += [jax.ShapeDtypeStruct((rows, width), low)]
        scratch += [pltpu.VMEM(routing[3].shape, low)] + [pltpu.SemaphoreType.DMA((n_ex,))] * 2
    inputs = (upstream, stream, norm_gain, weight_in, weight_out, doc_row, doc_col) + tuple(kept) + tuple(routing)
    vmem = pl.BlockSpec(memory_space=pltpu.VMEM)
    return pl.pallas_call(
        functools.partial(attend_back_kernel, n_dp, n_ex, len(inputs)),
        out_shape=outs,
        in_specs=[vmem] * len(inputs),
        out_specs=[vmem] * len(outs),
        scratch_shapes=scratch,
        compiler_params=pltpu.CompilerParams(
            collective_id=collective_id, has_side_effects=True, vmem_limit_bytes=56 * 1024 * 1024
        ),
        name="attention_backward",
    )(*inputs)


def shards(
    tokens,
    doc_lengths,
    assign,
    ln_gain,
    ln_bias,
    attn_in,
    attn_out,
    ffn_in,
    ffn_out,
    router,
    expert_in,
    expert_out,
    cotangent,
):
    n_dp, n_ex = lax.axis_size("dp"), lax.axis_size("expert")
    stream_first = tokens[0].astype(jnp.float32)
    row_count = stream_first.shape[0]
    doc_ends = jnp.cumsum(doc_lengths[0, 0])
    short_place = jnp.arange(row_count - LONG_DEV, dtype=jnp.int32)
    short_ids = jnp.sum((short_place[:, None] >= doc_ends[None, :]).astype(jnp.int32), axis=-1)
    doc_row, doc_col = short_ids[None, :], short_ids[:, None]
    weights_in, weights_out = lax.optimization_barrier((attn_in.transpose(1, 0, 2), attn_out.transpose(1, 0, 2)))
    gains, shifts = ln_gain.T, ln_bias.T
    assign_row = assign[0].T
    stream_one, *kept_one = attention_forward(
        n_dp, n_ex, 2, stream_first, gains[0:1], shifts[0:1], weights_in[0], weights_out[0], doc_row, doc_col
    )
    stream_two, dense_normed_t, active_t, slope = ffn_forward(stream_one, gains[1:2], shifts[1:2], ffn_in, ffn_out)
    stream_three, *kept_three, far_cot = attention_forward(
        n_dp, n_ex, 3, stream_two, gains[2:3], shifts[2:3], weights_in[1], weights_out[1], doc_row, doc_col,
        (assign_row, cotangent[0]),
    )
    (
        upstream, fourth_sums, router_grad, expert_rows, expert_back, expert_active, expert_hidden, result, gate, stats
    ) = mixture(
        n_dp, n_ex, 6, stream_three, gains[3:4], shifts[3:4], router.T, assign_row, cotangent[0], far_cot,
        expert_in[0], expert_out[0],
    )
    everyone = row_count * n_dp * n_ex
    balance = n_ex * jnp.sum((stats[:, 0] / everyone - 1.0 / n_ex) * (stats[:, 1] / everyone))
    expert_slots = expert_active.shape[0]
    expert_in_grad = jnp.einsum(
        "sd,sf->df", expert_rows.reshape(expert_slots, -1), expert_hidden, preferred_element_type=jnp.float32
    )[None]
    expert_out_grad = jnp.einsum(
        "sf,sd->fd", expert_active, expert_back.reshape(expert_slots, -1), preferred_element_type=jnp.float32
    )[None]
    upstream, second_low, second_mixed, second_sums, output = attention_backward(
        n_dp, n_ex, 4, upstream, stream_two, gains[2:3], weights_in[1], weights_out[1], doc_row, doc_col,
        kept_three[1:2] + kept_three[3:], (assign_row, gate, stream_three, result),
    )
    output = output[None]
    upstream, dense_low, dense_hidden, dense_sums = ffn_backward(
        upstream, stream_one, gains[1:2], ffn_in, ffn_out, slope
    )
    upstream, first_low, first_mixed, first_sums = attention_backward(
        n_dp, n_ex, 5, upstream, stream_first, gains[0:1], weights_in[0], weights_out[0], doc_row, doc_col,
        kept_one[1:2] + kept_one[3:],
    )
    grad_tokens = upstream.astype(jnp.bfloat16)[None]
    model_width = tokens.shape[2]
    rows = model_width // n_dp

    def blocks_of(rows_t):
        return rows_t.reshape(n_dp, -1, rows, row_count)

    pairs = [
        (blocks_of(kept_three[2]), second_low),
        (blocks_of(kept_three[0]), second_mixed),
        (blocks_of(active_t), dense_low),
        (blocks_of(dense_normed_t), dense_hidden),
        (blocks_of(kept_one[2]), first_low),
        (blocks_of(kept_one[0]), first_mixed),
    ]
    small = jnp.concatenate(
        [
            first_sums[0:1], dense_sums[0:1], second_sums[0:1], fourth_sums[0:1],
            first_sums[1:2], dense_sums[1:2], second_sums[1:2], fourth_sums[1:2],
            router_grad,
        ],
        axis=0,
    )
    chunks, small = reduce_grads(n_dp, n_ex, pairs, small, model_width)
    attn_in_sum, attn_out_sum, ffn_in_sum, ffn_out_sum = unpack(
        chunks, attn_in.shape[2] // model_width, ffn_in.shape[1] // model_width
    )
    small = lax.dynamic_slice_in_dim(small, lax.axis_index("dp") * rows, rows, 1).T
    summed = [
        attn_in_sum,
        attn_out_sum,
        ffn_in_sum,
        ffn_out_sum.reshape(-1, model_width),
        small[:, 8:],
        small[:, :4],
        small[:, 4:8],
    ]
    expert_in_sum, expert_out_sum = (
        lax.psum_scatter(
            expert_in_grad.astype(jnp.bfloat16), "dp", scatter_dimension=1, tiled=True
        ).astype(jnp.float32),
        lax.psum_scatter(
            expert_out_grad.astype(jnp.bfloat16), "dp", scatter_dimension=1, tiled=True
        ).astype(jnp.float32),
    )
    return (
        output,
        balance,
        grad_tokens,
        summed[5],
        summed[6],
        summed[0],
        summed[1],
        summed[2],
        summed[3],
        summed[4],
        expert_in_sum,
        expert_out_sum,
    )


def solution(mesh):
    return jax.shard_map(
        shards,
        mesh=mesh,
        in_specs=(
            P("expert", "dp", None),
            P("expert", "dp", None),
            P("expert", "dp", None),
            P(),
            P(),
            P(),
            P(),
            P(),
            P(),
            P(),
            P("expert", None, None),
            P("expert", None, None),
            P("expert", "dp", None),
        ),
        out_specs=(
            P("expert", "dp", None),
            P(),
            P("expert", "dp", None),
            P("dp", None),
            P("dp", None),
            P("dp", None, None),
            P("dp", None, None),
            P("dp", None),
            P("dp", None),
            P("dp", None),
            P("expert", "dp", None),
            P("expert", "dp", None),
        ),
        check_vma=False,
    )
```

```python
import functools

import jax
import jax.numpy as jnp
from jax import lax
from jax.experimental import pallas as pl
from jax.experimental.pallas import tpu as pltpu
from jax.sharding import PartitionSpec as P

MESH = pl.DeviceIdType.MESH
HEADS = 12
HEAD_DIM = 64
LONG_DEV = 256


epsilon = 1e-05
balance_weight = 0.01
masked_score = -1e30


def bit_of(index, level):
    return (index // (1 << level)) % 2


def flip(index, level):
    return index + (1 << level) * (1 - 2 * bit_of(index, level))


def partner_index(index, mask, levels):
    total = 0
    for level in range(levels):
        own = bit_of(index, level)
        total = total + (1 << level) * (1 - own if (mask >> level) & 1 else own)
    return total


def unpack_kernel(
    per_in, per_ffn, chunk_ref, expert_ref, in_ref, out_ref, ffn_in_ref, ffn_out_ref, expert_in_ref, expert_out_ref
):
    per_expert = expert_ref.shape[0] // 2
    width = chunk_ref.shape[2]
    at = 0
    for layer in (1, 0):
        out_ref[:, layer, :] = chunk_ref[at].astype(jnp.float32)
        for j in range(per_in):
            in_ref[:, layer, width * j : width * j + width] = chunk_ref[at + 1 + j].astype(jnp.float32)
        at += 1 + per_in
        if layer:
            for j in range(per_ffn):
                ffn_out_ref[j] = chunk_ref[at + j].astype(jnp.float32)
                ffn_in_ref[:, width * j : width * j + width] = chunk_ref[at + per_ffn + j].astype(jnp.float32)
            at += 2 * per_ffn
    for j in range(per_expert):
        expert_in_ref[:, width * j : width * j + width] = expert_ref[j].astype(jnp.float32)
        expert_out_ref[j] = expert_ref[per_expert + j].astype(jnp.float32)


def unpack(chunks, expert_chunks, per_in, per_ffn):
    count, rows, width = chunks.shape
    experts = expert_chunks.shape[0]
    step = 48 if rows % 48 == 0 else rows
    wide = jnp.float32
    return pl.pallas_call(
        functools.partial(unpack_kernel, per_in, per_ffn),
        grid=(rows // step,),
        out_shape=[
            jax.ShapeDtypeStruct((rows, 2, per_in * width), wide),
            jax.ShapeDtypeStruct((rows, 2, width), wide),
            jax.ShapeDtypeStruct((rows, per_ffn * width), wide),
            jax.ShapeDtypeStruct((per_ffn, rows, width), wide),
            jax.ShapeDtypeStruct((rows, experts // 2 * width), wide),
            jax.ShapeDtypeStruct((experts // 2, rows, width), wide),
        ],
        in_specs=[
            pl.BlockSpec((count, step, width), lambda i: (0, i, 0)),
            pl.BlockSpec((experts, step, width), lambda i: (0, i, 0)),
        ],
        out_specs=[
            pl.BlockSpec((step, 2, per_in * width), lambda i: (i, 0, 0)),
            pl.BlockSpec((step, 2, width), lambda i: (i, 0, 0)),
            pl.BlockSpec((step, per_ffn * width), lambda i: (i, 0)),
            pl.BlockSpec((per_ffn, step, width), lambda i: (0, i, 0)),
            pl.BlockSpec((step, experts // 2 * width), lambda i: (i, 0)),
            pl.BlockSpec((experts // 2, step, width), lambda i: (0, i, 0)),
        ],
        compiler_params=pltpu.CompilerParams(vmem_limit_bytes=40 * 1024 * 1024),
        name="unpack",
    )(chunks, expert_chunks)


def dot(a, b):
    return jnp.dot(a, b, preferred_element_type=jnp.float32)


def dot_rows(a, b):
    return lax.dot_general(a, b, (((1,), (1,)), ((), ())), preferred_element_type=jnp.float32)


def dot_columns(a, b):
    return lax.dot_general(a, b, (((0,), (0,)), ((), ())), preferred_element_type=jnp.float32)


def gelu_parts(hidden):
    lower = 0.5 + 0.5 * lax.erf(hidden * 0.7071067811865476)
    slope = lower + hidden * jnp.exp(-0.5 * hidden * hidden) * 0.3989422804014327
    return hidden * lower, slope


def norm_parts(x):
    center = x - jnp.mean(x, axis=-1, keepdims=True)
    inverse = lax.rsqrt(jnp.mean(center * center, axis=-1, keepdims=True) + epsilon)
    return center * inverse, inverse


def norm_back(unit, inverse, gain, upstream):
    scaled = upstream * gain
    return inverse * (
        scaled - jnp.mean(scaled, axis=-1, keepdims=True) - unit * jnp.mean(scaled * unit, axis=-1, keepdims=True)
    )


def ffn_kernel(x_ref, gain_ref, shift_ref, w_in_ref, w_out_ref, next_ref, normed_t_ref, active_t_ref, slope_ref, normed_ref):
    @pl.when(pl.program_id(0) == 0)
    def _():
        x = x_ref[...]
        unit, _ = norm_parts(x)
        normed = (unit * gain_ref[...] + shift_ref[...]).astype(jnp.bfloat16)
        normed_ref[...] = normed
        normed_t_ref[...] = normed.T
        next_ref[...] = x

    active, slope = gelu_parts(dot(normed_ref[...], w_in_ref[...]))
    active = active.astype(jnp.bfloat16)
    slope_ref[...] = slope.astype(jnp.bfloat16)
    active_t_ref[...] = active.T
    next_ref[...] += dot(active, w_out_ref[...])


def ffn_forward(stream, norm_gain, norm_shift, weight_in, weight_out):
    rows, width = stream.shape
    hidden = weight_in.shape[1]
    low = jnp.bfloat16
    return pl.pallas_call(
        ffn_kernel,
        grid=(hidden // width,),
        out_shape=[
            jax.ShapeDtypeStruct((rows, width), jnp.float32),
            jax.ShapeDtypeStruct((width, rows), low),
            jax.ShapeDtypeStruct((hidden, rows), low),
            jax.ShapeDtypeStruct((rows, hidden), low),
        ],
        in_specs=[
            pl.BlockSpec((rows, width), lambda i: (0, 0)),
            pl.BlockSpec((1, width), lambda i: (0, 0)),
            pl.BlockSpec((1, width), lambda i: (0, 0)),
            pl.BlockSpec((width, width), lambda i: (0, i)),
            pl.BlockSpec((width, width), lambda i: (i, 0)),
        ],
        out_specs=[
            pl.BlockSpec((rows, width), lambda i: (0, 0)),
            pl.BlockSpec((width, rows), lambda i: (0, 0)),
            pl.BlockSpec((width, rows), lambda i: (i, 0)),
            pl.BlockSpec((rows, width), lambda i: (0, i)),
        ],
        scratch_shapes=[pltpu.VMEM((rows, width), low)],
        compiler_params=pltpu.CompilerParams(vmem_limit_bytes=48 * 1024 * 1024),
        name="ffn_forward",
    )(stream, norm_gain, norm_shift, weight_in, weight_out)


def capacity_of(rows, experts):
    capacity = (5 * rows + 4 * experts - 1) // (4 * experts)
    return capacity, -(-capacity // 16) * 16


def chosen_rows(assign, experts):
    expert = lax.broadcasted_iota(jnp.int32, (experts, assign.shape[1]), 0)
    return jnp.where(assign == expert, 1.0, 0.0)


def dispatch_of(assign, experts):
    tokens = assign.shape[1]
    capacity, padded = capacity_of(tokens, experts)
    hot = chosen_rows(assign, experts)
    earlier = lax.broadcasted_iota(jnp.int32, (tokens, tokens), 0) < lax.broadcasted_iota(jnp.int32, (tokens, tokens), 1)
    before = dot(hot.astype(jnp.bfloat16), jnp.where(earlier, 1.0, 0.0).astype(jnp.bfloat16))
    place = jnp.sum(hot * before, axis=0, keepdims=True)
    slot = jnp.where(place < capacity, assign.astype(jnp.float32) * padded + place, -1.0)
    number = lax.broadcasted_iota(jnp.int32, (experts * padded, tokens), 0).astype(jnp.float32)
    return jnp.where(number == slot, 1.0, 0.0).astype(jnp.bfloat16)


class Across:
    def __init__(self, experts, out, into, send_sems, recv_sems):
        self.experts, self.out, self.into = experts, out, into
        self.send_sems, self.recv_sems = send_sems, recv_sems
        self.dp, self.me = lax.axis_index("dp"), lax.axis_index("expert")

    def copy(self, slab, place, to):
        return pltpu.make_async_remote_copy(
            src_ref=self.out.at[slab],
            dst_ref=self.into.at[place],
            send_sem=self.send_sems.at[slab],
            recv_sem=self.recv_sems.at[place],
            device_id=(self.dp, to),
            device_id_type=MESH,
        )

    def start(self, j):
        self.copy(j, self.me, j).start()

    def wait_from(self, j):
        self.copy(j, j, j).wait_recv()

    def wait_to(self, j):
        self.copy(j, self.me, j).wait_send()

    def others(self, use):
        def body(k, _):
            use(lax.rem(self.me + k, self.experts))
            return 0

        lax.fori_loop(1, self.experts, body, 0)

    def start_all(self):
        self.others(self.start)

    def wait_all(self):
        def both(j):
            self.wait_from(j)
            self.wait_to(j)

        self.others(both)


def greet(targets):
    barrier = pltpu.get_barrier_semaphore()
    for device in targets:
        pl.semaphore_signal(barrier, inc=1, device_id=device, device_id_type=MESH)
    pl.semaphore_wait(barrier, len(targets))


def across_peers(experts):
    d, e = lax.axis_index("dp"), lax.axis_index("expert")
    return [(d, lax.rem(e + k, experts)) for k in range(1, experts)]


def mixture_kernel(
    n_dp, n_ex,
    x_ref, gain_ref, shift_ref, router_ref, assign_ref, cot_ref, far_cot_ref, w_in_ref, w_out_ref,
    up_ref, sums_ref, router_grad_ref, rows_t_ref, back_ref, active_t_ref, hidden_ref, result_ref, gate_ref, stats_ref,
    rows_ref, send_ref, grad_ref, home_ref, dgate_ref, home_dgate_ref, stat_send, stat_recv, dispatch_ref, result_acc, grad_acc,
    x_send_sem, x_recv_sem, grad_send_sem, grad_recv_sem, dgate_send_sem, dgate_recv_sem, stat_send_sem, stat_recv_sem,
):
    d, e = lax.axis_index("dp"), lax.axis_index("expert")
    dp_levels, ex_levels = n_dp.bit_length() - 1, n_ex.bit_length() - 1
    tokens, width = x_ref.shape
    padded = send_ref.shape[1]
    group = min(max(4, 128 // padded), n_ex)
    groups = n_ex // group
    exact = dict(precision=lax.Precision.HIGHEST, preferred_element_type=jnp.float32)
    hops = [(flip(d, b), e) for b in range(dp_levels)] + [(d, flip(e, b)) for b in range(ex_levels)]
    greet([(flip(d, b), e) for b in range(dp_levels)] + across_peers(n_ex))

    unit, inverse = norm_parts(x_ref[...])
    routed = (unit * gain_ref[...] + shift_ref[...]).astype(jnp.bfloat16)
    assign = assign_ref[...]
    dispatch = dispatch_of(assign, n_ex)
    dispatch_ref[...] = dispatch
    send_ref[...] = dot(dispatch, routed).astype(jnp.bfloat16).reshape(send_ref.shape)
    x_across = Across(n_ex, send_ref, rows_ref, x_send_sem, x_recv_sem)
    x_across.start_all()
    rows_ref[e] = send_ref[e]
    hot = chosen_rows(assign, n_ex)
    gate = jax.nn.sigmoid(jnp.sum(hot * dot_rows(router_ref[...], routed), axis=0, keepdims=True))
    gate_ref[...] = gate

    def stat_copy(i):
        return pltpu.make_async_remote_copy(
            src_ref=stat_send.at[i],
            dst_ref=stat_recv.at[i],
            send_sem=stat_send_sem.at[i],
            recv_sem=stat_recv_sem.at[i],
            device_id=hops[i],
            device_id_type=MESH,
        )

    lane = lax.broadcasted_iota(jnp.int32, stats_ref.shape, 1)
    stat_send[0] = jnp.where(
        lane == 0, jnp.sum(hot, axis=1, keepdims=True), jnp.sum(hot * gate, axis=1, keepdims=True)
    )
    stat_copy(0).start()

    def stat_step(i):
        stat_copy(i).wait()
        value = stat_send[i] + stat_recv[i]
        if i + 1 < len(hops):
            stat_send[i + 1] = value
            stat_copy(i + 1).start()
        else:
            stats_ref[...] = value

    grad_across = Across(n_ex, grad_ref, home_ref, grad_send_sem, grad_recv_sem)
    dgate_across = Across(n_ex, dgate_ref, home_dgate_ref, dgate_send_sem, dgate_recv_sem)
    step = 768 if w_in_ref.shape[1] % 768 == 0 else w_in_ref.shape[1]
    done = 0
    for k in range(groups):
        first = lax.rem(e // group + k, groups) * group
        for m in range(group):

            @pl.when(first + m != e)
            def _(m=m):
                x_across.wait_from(first + m)

        at = pl.ds(first, group)
        rows = rows_ref[at].reshape(group * padded, width)
        cot = far_cot_ref[at].reshape(group * padded, width).astype(jnp.float32)
        logits = dot_rows(rows, router_ref[...])
        own = lax.broadcasted_iota(jnp.int32, logits.shape, 1) == e
        slot_gate = jax.nn.sigmoid(jnp.sum(jnp.where(own, logits, 0.0), axis=1, keepdims=True))
        back = (slot_gate * cot).astype(jnp.bfloat16)
        back_ref[at] = back.reshape(group, padded, width)
        span = pl.ds(pl.multiple_of(first * padded, group * padded), group * padded)
        rows_t_ref[:, span] = rows.T
        result_acc[...] = jnp.zeros_like(result_acc)
        grad_acc[...] = jnp.zeros_like(grad_acc)

        def block(i, _):
            cols = pl.ds(pl.multiple_of(i * step, step), step)
            active, slope = gelu_parts(dot(rows, w_in_ref[:, cols]))
            active = active.astype(jnp.bfloat16)
            hidden = (slope * dot_rows(back, w_out_ref[cols, :])).astype(jnp.bfloat16)
            active_t_ref[cols, span] = active.T
            hidden_ref[span, cols] = hidden
            result_acc[...] += dot(active, w_out_ref[cols, :])
            grad_acc[...] += dot_rows(hidden, w_in_ref[:, cols])
            return 0

        lax.fori_loop(0, w_in_ref.shape[1] // step, block, 0)
        grad_ref[at] = grad_acc[...].astype(jnp.bfloat16).reshape(group, padded, width)
        result = result_acc[...].astype(jnp.bfloat16)
        result_ref[at] = result.reshape(group, padded, width)
        dgate = lax.dot_general(
            jnp.ones((8, width), jnp.float32), cot * result.astype(jnp.float32), (((1,), (1,)), ((), ())), **exact
        )
        for m in range(group):
            dgate_ref[first + m, :, :padded] = dgate[:, m * padded : (m + 1) * padded]

            @pl.when(first + m != e)
            def _(m=m):
                grad_across.start(first + m)
                dgate_across.start(first + m)

            @pl.when(first + m == e)
            def _():
                home_ref[e] = grad_ref[e]
                home_dgate_ref[e] = dgate_ref[e]

        if done < len(hops):
            stat_step(done)
            done += 1

    for i in range(done, len(hops)):
        stat_step(i)
    x_across.others(x_across.wait_to)
    dgate_across.wait_all()
    dgate = jnp.zeros((8, tokens), jnp.float32)
    for j in range(n_ex):
        part = dispatch_ref[j * padded : (j + 1) * padded].astype(jnp.float32)
        dgate = dgate + jnp.dot(home_dgate_ref[j, :, :padded], part, **exact)
    everyone = tokens * n_dp * n_ex
    share = jnp.sum(jnp.where(lane == 0, stats_ref[...], 0.0), axis=1, keepdims=True) / everyone
    weight = balance_weight * n_ex * (share - 1.0 / n_ex) / everyone
    grad_gate = dgate[0:1] + jnp.sum(hot * weight, axis=0, keepdims=True)
    grad_logits = hot * (grad_gate * gate * (1.0 - gate))
    router_grad_ref[...] = jnp.dot(grad_logits, routed.astype(jnp.float32), **exact)
    grad_normed = lax.dot_general(
        grad_logits, router_ref[...].astype(jnp.float32), (((0,), (0,)), ((), ())), **exact
    )
    grad_across.wait_all()
    grad_normed = grad_normed + dot_columns(dispatch_ref[...], home_ref[...].reshape(n_ex * padded, width))
    up_ref[...] = cot_ref[...].astype(jnp.float32) + norm_back(unit, inverse, gain_ref[...], grad_normed)
    sums_ref[0:1] = jnp.sum(grad_normed * unit, axis=0, keepdims=True)
    sums_ref[1:2] = jnp.sum(grad_normed, axis=0, keepdims=True)


def mixture(n_dp, n_ex, collective_id, stream, norm_gain, norm_shift, router_t, assign, cot, far_cot, weight_in, weight_out):
    tokens, width = stream.shape
    hidden = weight_in.shape[1]
    _, padded = capacity_of(tokens, n_ex)
    slots = n_ex * padded
    group = min(max(4, 128 // padded), n_ex) * padded
    low, wide = jnp.bfloat16, jnp.float32
    slab = (n_ex, padded, width)
    hops = (n_dp * n_ex).bit_length() - 1
    outs = [
        jax.ShapeDtypeStruct((tokens, width), wide),
        jax.ShapeDtypeStruct((2, width), wide),
        jax.ShapeDtypeStruct((n_ex, width), wide),
        jax.ShapeDtypeStruct((width, slots), low),
        jax.ShapeDtypeStruct(slab, low),
        jax.ShapeDtypeStruct((hidden, slots), low),
        jax.ShapeDtypeStruct((slots, hidden), low),
        jax.ShapeDtypeStruct(slab, low),
        jax.ShapeDtypeStruct((1, tokens), wide),
        jax.ShapeDtypeStruct((n_ex, 128), wide),
    ]
    vmem = pl.BlockSpec(memory_space=pltpu.VMEM)
    return pl.pallas_call(
        functools.partial(mixture_kernel, n_dp, n_ex),
        out_shape=outs,
        in_specs=[vmem] * 9,
        out_specs=[vmem] * len(outs),
        scratch_shapes=[
            pltpu.VMEM(slab, low),
            pltpu.VMEM(slab, low),
            pltpu.VMEM(slab, low),
            pltpu.VMEM(slab, low),
            pltpu.VMEM((n_ex, 8, 128), wide),
            pltpu.VMEM((n_ex, 8, 128), wide),
            pltpu.VMEM((hops, n_ex, 128), wide),
            pltpu.VMEM((hops, n_ex, 128), wide),
            pltpu.VMEM((slots, tokens), low),
            pltpu.VMEM((group, width), wide),
            pltpu.VMEM((group, width), wide),
        ]
        + [pltpu.SemaphoreType.DMA((n_ex,)) for _ in range(6)]
        + [pltpu.SemaphoreType.DMA((hops,)) for _ in range(2)],
        compiler_params=pltpu.CompilerParams(
            collective_id=collective_id, has_side_effects=True, vmem_limit_bytes=56 * 1024 * 1024
        ),
        name="mixture",
    )(stream, norm_gain, norm_shift, router_t, assign, cot, far_cot, weight_in, weight_out)


def head_pair(rows):
    first = lax.broadcasted_iota(jnp.int32, rows.shape, 1) < HEAD_DIM
    zero = jnp.zeros_like(rows)
    return jnp.concatenate([jnp.where(first, rows, zero), jnp.where(first, zero, rows)], axis=0)


def pair_rows(both):
    n = both.shape[1] // 2
    return jnp.concatenate([both[:HEAD_DIM, :n], both[HEAD_DIM:, n:]], axis=0)


def causal(keys, queries):
    key = lax.broadcasted_iota(jnp.int32, (keys, 2 * queries), 0)
    query = lax.broadcasted_iota(jnp.int32, (keys, 2 * queries), 1)
    return key <= jnp.where(query >= queries, query - queries, query)


def short_seen(doc_row, doc_col):
    n = doc_row.shape[1]
    same = doc_col == jnp.concatenate([doc_row, doc_row], axis=1)
    return same & causal(n, n)


class Links:
    def __init__(self, n_dp):
        self.me, self.expert = lax.axis_index("dp"), lax.axis_index("expert")
        self.chips = n_dp // 2
        self.chip, self.core = self.me // 2, self.me % 2
        self.twin = self.me + 1 - 2 * self.core

    def peers(self):
        ring = [lax.rem(self.chip + k, self.chips) for k in range(1, self.chips)]
        return [(self.twin, self.expert)] + [(2 * other + self.core, self.expert) for other in ring]

    def copy(self, ref, send_sem, recv_sem, index):
        return pltpu.make_async_remote_copy(
            src_ref=ref,
            dst_ref=ref,
            send_sem=send_sem,
            recv_sem=recv_sem,
            device_id=(index, self.expert),
            device_id_type=MESH,
        )

    def before(self, later, other):
        return other > self.chip if later else other < self.chip


class Spread:
    def __init__(self, links, at, parts, later, far_sems, near_sems, recv_sems):
        self.links, self.at, self.later = links, at, later
        self.far_sems, self.near_sems, self.recv_sems = far_sems, near_sems, recv_sems

    def _far(self, other, p):
        k = self.links
        return k.copy(self.at(k.me, p), self.far_sems.at[other, p], self.recv_sems.at[k.me, p], 2 * other + k.core)

    def _near(self, block, p):
        k = self.links
        return k.copy(self.at(block, p), self.near_sems.at[block, p], self.recv_sems.at[block, p], k.twin)

    def _twin_needs(self):
        return self.links.core == (0 if self.later else 1)

    def send(self, p):
        k = self.links
        for other in range(k.chips):

            @pl.when(k.before(self.later, other))
            def _():
                self._far(other, p).start()

        @pl.when(self._twin_needs())
        def _():
            self._near(k.me, p).start()

    def sent(self, p):
        k = self.links
        for other in range(k.chips):

            @pl.when(k.before(self.later, other))
            def _():
                self._far(other, p).wait_send()

            @pl.when(k.before(not self.later, other))
            def _():
                self._near(2 * other + k.core, p).wait_send()

        @pl.when(self._twin_needs())
        def _():
            self._near(k.me, p).wait_send()

    def relay(self, p):
        k = self.links
        for other in range(k.chips):

            @pl.when(k.before(not self.later, other))
            def _():
                block = 2 * other + k.core
                copy = self._near(block, p)
                copy.wait_recv()
                copy.start()

    def each(self, p, use):
        k = self.links

        @pl.when(k.core == (1 if self.later else 0))
        def _():
            self._near(k.twin, p).wait_recv()
            use(k.twin)

        for other in range(k.chips):

            @pl.when(k.before(not self.later, other))
            def _():
                use(2 * other + k.core)
                block = 2 * other + 1 - k.core
                self._near(block, p).wait_recv()
                use(block)


def attend_kernel(
    n_dp, n_ex, inputs, *refs
):
    (x_ref, gain_ref, shift_ref, w_in_ref, w_out_ref, doc_row_ref, doc_col_ref), rest = refs[:7], refs[7:]
    if inputs > 7:
        (assign_ref, cot_ref), rest = rest[:2], rest[2:]
    (
        next_ref, normed_t_ref, context_ref, context_t_ref, kv_ref, q_ref, short_kv_ref, short_q_ref, lse_ref,
    ), rest = rest[:9], rest[9:]
    if inputs > 7:
        (far_cot_ref,), rest = rest[:1], rest[1:]
    (acc_ref, top_ref, total_ref, kv_far, kv_near, kv_recv, q_far, q_near, q_recv), rest = rest[:9], rest[9:]
    links = Links(n_dp)
    me = links.me
    pairs, long = kv_ref.shape[1], kv_ref.shape[3]
    width = x_ref.shape[1]
    x = x_ref[...]
    center = x - jnp.mean(x, axis=-1, keepdims=True)
    inverse = lax.rsqrt(jnp.mean(center * center, axis=-1, keepdims=True) + epsilon)
    normed = (center * inverse * gain_ref[...] + shift_ref[...]).astype(jnp.bfloat16)

    kv = dot(normed, w_in_ref[:, width:]).astype(jnp.bfloat16)
    for h in range(pairs):
        for part in range(2):
            piece = kv[:, part * width + 128 * h : part * width + 128 * h + 128]
            kv_ref[me, h, part] = piece[:long]
            short_kv_ref[h, part] = piece[long:]
    greet(links.peers() + (across_peers(n_ex) if inputs > 7 else []))
    kv_spread = Spread(links, lambda b, p: kv_ref.at[b, p], pairs, True, kv_far, kv_near, kv_recv)
    q_spread = Spread(links, lambda b, p: q_ref.at[b], 1, False, q_far, q_near, q_recv)
    for h in range(pairs):
        kv_spread.send(h)
    q = (dot(normed, w_in_ref[:, :width]).astype(jnp.bfloat16) * HEAD_DIM ** (-0.5)).astype(jnp.bfloat16)
    for h in range(pairs):
        piece = q[:, 128 * h : 128 * h + 128]
        q_ref[me, h] = piece[:long]
        short_q_ref[h] = piece[long:]
    q_spread.send(0)
    if inputs > 7:
        cot_send_ref, cot_send_sem, cot_recv_sem = rest
        cot_send_ref[...] = dot(dispatch_of(assign_ref[...], n_ex), cot_ref[...]).astype(jnp.bfloat16).reshape(
            cot_send_ref.shape
        )
        cot_across = Across(n_ex, cot_send_ref, far_cot_ref, cot_send_sem, cot_recv_sem)
        cot_across.start_all()
        far_cot_ref[links.expert] = cot_send_ref[links.expert]
    normed_t_ref[...] = normed.T

    def put_context(h, rows_t, first, count):
        at = pl.ds(pl.multiple_of(128 * h, 128), 128)
        context_t_ref[at, first : first + count] = rows_t.astype(jnp.bfloat16)
        context_ref[first : first + count, at] = rows_t.T.astype(jnp.bfloat16)

    def own_part(h, _):
        seen = short_seen(doc_row_ref[...], doc_col_ref[...])
        scores = jnp.where(seen, dot_rows(short_kv_ref[h, 0], head_pair(short_q_ref[h])), masked_score)
        top = jnp.max(scores, axis=0, keepdims=True)
        weights = jnp.exp(scores - top)
        total = jnp.sum(weights, axis=0, keepdims=True)
        rows_t = pair_rows(dot_columns(short_kv_ref[h, 1], weights.astype(jnp.bfloat16)) / total)
        short = rows_t.shape[1]
        put_context(h, rows_t, long, short)
        lse = top + jnp.log(total)
        lse_ref[h, 0:1, long:] = lse[:, :short]
        lse_ref[h, 1:2, long:] = lse[:, short:]
        scores = jnp.where(causal(long, long), dot_rows(kv_ref[me, h, 0], head_pair(q_ref[me, h])), masked_score)
        top = jnp.max(scores, axis=0, keepdims=True)
        weights = jnp.exp(scores - top)
        top_ref[h] = top
        total_ref[h] = jnp.sum(weights, axis=0, keepdims=True)
        acc_ref[h] = dot_columns(kv_ref[me, h, 1], weights.astype(jnp.bfloat16))
        return 0

    lax.fori_loop(0, pairs, own_part, 0)

    def other_part(h, _):
        kv_spread.relay(h)
        queries = head_pair(q_ref[me, h])

        def use(block):
            scores = dot_rows(kv_ref[block, h, 0], queries)
            old = top_ref[h]
            top = jnp.maximum(old, jnp.max(scores, axis=0, keepdims=True))
            factor = jnp.exp(old - top)
            weights = jnp.exp(scores - top)
            top_ref[h] = top
            total_ref[h] = total_ref[h] * factor + jnp.sum(weights, axis=0, keepdims=True)
            acc_ref[h] = acc_ref[h] * factor + dot_columns(kv_ref[block, h, 1], weights.astype(jnp.bfloat16))

        kv_spread.each(h, use)
        total = total_ref[h]
        put_context(h, pair_rows(acc_ref[h] / total), 0, long)
        lse = top_ref[h] + jnp.log(total)
        lse_ref[h, 0:1, :long] = lse[:, :long]
        lse_ref[h, 1:2, :long] = lse[:, long:]
        return 0

    lax.fori_loop(0, pairs, other_part, 0)
    next_ref[...] = x + dot(context_ref[...], w_out_ref[...])
    q_spread.relay(0)
    q_spread.each(0, lambda block: None)
    q_spread.sent(0)
    for h in range(pairs):
        kv_spread.sent(h)
    if inputs > 7:
        cot_across.wait_all()


def spread_sems(n_dp, parts):
    return [
        pltpu.SemaphoreType.DMA((n_dp // 2, parts)),
        pltpu.SemaphoreType.DMA((n_dp, parts)),
        pltpu.SemaphoreType.DMA((n_dp, parts)),
    ]


def attention_forward(
    n_dp, n_ex, collective_id, stream, norm_gain, norm_shift, weight_in, weight_out, doc_row, doc_col, routing=()
):
    rows, width = stream.shape
    long, short, pairs = LONG_DEV, rows - LONG_DEV, width // 128
    low = jnp.bfloat16
    outs = [
        jax.ShapeDtypeStruct((rows, width), jnp.float32),
        jax.ShapeDtypeStruct((width, rows), low),
        jax.ShapeDtypeStruct((rows, width), low),
        jax.ShapeDtypeStruct((width, rows), low),
        jax.ShapeDtypeStruct((n_dp, pairs, 2, long, 128), low),
        jax.ShapeDtypeStruct((n_dp, pairs, long, 128), low),
        jax.ShapeDtypeStruct((pairs, 2, short, 128), low),
        jax.ShapeDtypeStruct((pairs, short, 128), low),
        jax.ShapeDtypeStruct((pairs, 2, rows), jnp.float32),
    ]
    scratch = [
        pltpu.VMEM((pairs, 128, 2 * long), jnp.float32),
        pltpu.VMEM((pairs, 1, 2 * long), jnp.float32),
        pltpu.VMEM((pairs, 1, 2 * long), jnp.float32),
    ]
    scratch += spread_sems(n_dp, pairs) + spread_sems(n_dp, 1)
    if routing:
        slab = (n_ex, capacity_of(rows, n_ex)[1], width)
        outs += [jax.ShapeDtypeStruct(slab, low)]
        scratch += [pltpu.VMEM(slab, low)] + [pltpu.SemaphoreType.DMA((n_ex,))] * 2
    inputs = (stream, norm_gain, norm_shift, weight_in, weight_out, doc_row, doc_col) + tuple(routing)
    vmem = pl.BlockSpec(memory_space=pltpu.VMEM)
    return pl.pallas_call(
        functools.partial(attend_kernel, n_dp, n_ex, len(inputs)),
        out_shape=outs,
        in_specs=[vmem] * len(inputs),
        out_specs=[vmem] * len(outs),
        scratch_shapes=scratch,
        compiler_params=pltpu.CompilerParams(
            collective_id=collective_id, has_side_effects=True, vmem_limit_bytes=48 * 1024 * 1024
        ),
        name="attention_forward",
    )(*inputs)


def share_context(context, lse, grad_context, do_ref, aux_ref, short_do_ref, short_aux_ref, me, long):
    lane = lax.broadcasted_iota(jnp.int32, (8, 128), 1) < HEAD_DIM
    head = lax.broadcasted_iota(jnp.int32, (8, 128), 0)
    picks = jnp.where(((head == 0) & lane) | ((head == 1) & ~lane), 1.0, 0.0)
    for h in range(do_ref.shape[1]):
        at = slice(128 * h, 128 * h + 128)
        piece = grad_context[:, at]
        do_ref[me, h] = piece[:long]
        short_do_ref[h] = piece[long:]
        both = piece.astype(jnp.float32) * context[:, at].astype(jnp.float32)
        delta = lax.dot_general(
            picks, both, (((1,), (1,)), ((), ())), precision=lax.Precision.HIGHEST, preferred_element_type=jnp.float32
        )
        aux_ref[me, h, 0:2] = lse[h, :, :long]
        aux_ref[me, h, 2:4] = delta[0:2, :long]
        short_aux_ref[h, 0:2] = lse[h, :, long:]
        short_aux_ref[h, 2:4] = delta[0:2, long:]


def attend_back_pair(n_dp, me, width, r, do_spread, aux_spread, h):
    scale = HEAD_DIM ** (-0.5)
    mixed_ref = r["mixed"]
    long = r["kv"].shape[3]

    def row_of(aux, first):
        return jnp.concatenate([aux[first : first + 1], aux[first + 1 : first + 2]], axis=1)

    def score_grads(keys, values, queries, grads, aux, seen):
        scores = dot_rows(keys, queries)
        probs = jnp.exp(scores - row_of(aux, 0))
        if seen is not None:
            probs = jnp.where(seen, probs, 0.0)
        grad_scores = probs * (dot_rows(values, grads) - row_of(aux, 2))
        return probs.astype(jnp.bfloat16), grad_scores.astype(jnp.bfloat16)

    def put(third, first, value):
        at = pl.ds(pl.multiple_of(third * width + 128 * h, 128), 128)
        mixed_ref[first : first + value.shape[0], at] = value.astype(jnp.bfloat16)

    seen = short_seen(r["doc_row"][...], r["doc_col"][...])
    queries, grads = head_pair(r["short_q"][h]), head_pair(r["short_do"][h])
    keys = r["short_kv"][h, 0]
    probs, grad_scores = score_grads(keys, r["short_kv"][h, 1], queries, grads, r["short_aux"][h], seen)
    put(0, long, (pair_rows(dot_columns(keys, grad_scores)) * scale).T)
    put(1, long, dot(grad_scores, queries))
    put(2, long, dot(probs, grads))
    queries, grads = head_pair(r["q"][me, h]), head_pair(r["do"][me, h])
    own_keys, own_values = r["kv"][me, h, 0], r["kv"][me, h, 1]
    probs, grad_scores = score_grads(own_keys, own_values, queries, grads, r["aux"][me, h], causal(long, long))
    r["dq"][...] = dot_columns(own_keys, grad_scores)
    r["dk"][...] = dot(grad_scores, queries)
    r["dv"][...] = dot(probs, grads)
    for block in range(n_dp - 1):

        @pl.when(block < me)
        def _():
            keys = r["kv"][block, h, 0]
            _, grad_scores = score_grads(keys, r["kv"][block, h, 1], queries, grads, r["aux"][me, h], None)
            r["dq"][...] += dot_columns(keys, grad_scores)

    put(0, 0, (pair_rows(r["dq"][...]) * scale).T)
    do_spread.relay(h)
    aux_spread.relay(h)

    def use(block):
        queries, grads = head_pair(r["q"][block, h]), head_pair(r["do"][block, h])
        probs, grad_scores = score_grads(own_keys, own_values, queries, grads, r["aux"][block, h], None)
        r["dk"][...] += dot(grad_scores, queries)
        r["dv"][...] += dot(probs, grads)

    aux_spread.each(h, lambda block: None)
    do_spread.each(h, use)
    put(1, 0, r["dk"][...])
    put(2, 0, r["dv"][...])


def back_scratch(n_dp, pairs, long, short):
    return (
        [
            pltpu.VMEM((n_dp, pairs, long, 128), jnp.bfloat16),
            pltpu.VMEM((n_dp, pairs, 8, long), jnp.float32),
            pltpu.VMEM((pairs, short, 128), jnp.bfloat16),
            pltpu.VMEM((pairs, 8, short), jnp.float32),
            pltpu.VMEM((128, 2 * long), jnp.float32),
            pltpu.VMEM((long, 128), jnp.float32),
            pltpu.VMEM((long, 128), jnp.float32),
        ]
        + spread_sems(n_dp, pairs)
        + spread_sems(n_dp, pairs)
    )


def lane_plan(n_dp, n_ex, rows, order):
    dp_levels = [("dp", b) for b in range(n_dp.bit_length() - 1)]
    ex_levels = n_ex.bit_length() - 1
    halved, piece = [], rows
    for level in ((0, 1), (1, 0))[order]:
        if level < ex_levels and piece % 32 == 0:
            halved.append(level)
            piece //= 2
    halves = [("half", b) for b in halved]
    if order:
        kinds = dp_levels[:1] + halves[:1] + dp_levels[1:] + halves[1:]
    else:
        kinds = dp_levels + halves
    kinds += [("both", b) for b in range(ex_levels) if b not in halved]
    kinds += [("back", b) for b in reversed(halved)]
    return kinds, halved


class Lane:
    def __init__(self, n_dp, n_ex, rows, columns, order, refs):
        self.rows, self.columns = rows, columns
        self.kinds, self.halved = lane_plan(n_dp, n_ex, rows, order)
        self.count = len(self.kinds)
        moving = [k[0] != "back" for k in self.kinds]
        self.send = [next(refs) if m else None for m in moving]
        self.recv = [next(refs) if m else None for m in moving]
        self.keep = [next(refs) if m else None for m in moving]
        self.fin = next(refs)
        self.send_sems = [next(refs) for _ in moving]
        self.recv_sems = [next(refs) for _ in moving]
        self.d, self.e = lax.axis_index("dp"), lax.axis_index("expert")

    @staticmethod
    def scratch(n_dp, n_ex, rows, columns, order):
        kinds, halved = lane_plan(n_dp, n_ex, rows, order)
        width, pieces, height, shapes = columns[1] - columns[0], n_dp, rows, []
        for kind, _ in kinds:
            if kind == "dp":
                pieces //= 2
            elif kind == "half":
                height //= 2
            if kind != "back":
                shapes.append((pieces, height, width))
        scratch = [pltpu.VMEM((2,) + s, jnp.bfloat16) for s in shapes]
        scratch += [pltpu.VMEM((4,) + s, jnp.bfloat16) for s in shapes]
        scratch += [pltpu.VMEM((2,) + s, jnp.float32) for s in shapes]
        scratch += [pltpu.VMEM((len(halved) + 3, rows, width), jnp.bfloat16)]
        return scratch + [pltpu.SemaphoreType.DMA((4,)) for _ in kinds] * 2

    def peer(self, kind, level):
        return (flip(self.d, level), self.e) if kind == "dp" else (self.d, flip(self.e, level))

    def kept_rows(self, depth):
        start = 0
        for i, level in enumerate(self.halved[:depth]):
            start = start + bit_of(self.e, level) * (self.rows >> (i + 1))
        return start

    def copy_of(self, s, c):
        kind, level = self.kinds[s]
        slot, place = lax.rem(c, 2), lax.rem(c, 4)
        if kind == "back":
            depth = self.halved.index(level) + 1
            span = self.rows >> depth
            at = pl.ds(pl.multiple_of(self.kept_rows(depth), span), span)
            src = self.fin.at[lax.rem(c, len(self.halved) + 3), at]
            dst = src
        else:
            src, dst = self.send[s].at[slot], self.recv[s].at[place]
        return pltpu.make_async_remote_copy(
            src_ref=src,
            dst_ref=dst,
            send_sem=self.send_sems[s].at[place],
            recv_sem=self.recv_sems[s].at[place],
            device_id=self.peer(kind, level),
            device_id_type=MESH,
        )

    def arrive(self, s, c):
        self.copy_of(s, c).wait()
        slot, place = lax.rem(c, 2), lax.rem(c, 4)
        if self.kinds[s][0] == "back":
            return None
        return [
            self.keep[s][slot, i] + self.recv[s][place, i].astype(jnp.float32) for i in range(self.keep[s].shape[1])
        ]

    def leave(self, s, c, values):
        kind, level = self.kinds[s]
        slot = lax.rem(c, 2)
        kept = None
        if kind == "dp":
            sent, kept = values[1::2], values[0::2]
        elif kind == "half":
            half = values[0].shape[0] // 2
            own = bit_of(self.e, level)
            sent = [jnp.where(own == 0, v[half:], v[:half]) for v in values]
            kept = [jnp.where(own == 0, v[:half], v[half:]) for v in values]
        elif kind == "both":
            sent = values
            kept = [v.astype(jnp.bfloat16).astype(jnp.float32) for v in values]
        elif values is not None:
            span = values[0].shape[0]
            at = pl.ds(pl.multiple_of(self.kept_rows(len(self.halved)), span), span)
            self.fin[lax.rem(c, len(self.halved) + 3), at] = values[0].astype(jnp.bfloat16)
        if kept is not None:
            for i, v in enumerate(sent):
                self.send[s][slot, i] = v.astype(jnp.bfloat16)
        self.copy_of(s, c).start()
        if kept is not None:
            for i, v in enumerate(kept):
                self.keep[s][slot, i] = v

    def final(self, c):
        values = self.arrive(self.count - 1, c)
        if values is None:
            return self.fin[lax.rem(c, len(self.halved) + 3)]
        return values[0].astype(jnp.bfloat16)


class Reduction:
    def __init__(self, n_dp, n_ex, rows, groups, lanes, refs):
        self.n_dp, self.rows, self.groups = n_dp, rows, groups
        refs = iter(refs)
        self.lanes = [Lane(n_dp, n_ex, rows, columns, order, refs) for columns, order in lanes]
        self.stage_ref, self.stage_sem, self.out = next(refs), next(refs), next(refs)
        self.count = self.lanes[0].count
        self.chunks = sum(g[0] for g in groups)
        self.firsts = [sum(g[0] for g in groups[:i]) for i in range(len(groups))]
        self.ticks = self.chunks + self.count
        self.d = lax.axis_index("dp")
        self.peer = self.lanes[0].peer

    @staticmethod
    def scratch(n_dp, n_ex, rows, width, lanes):
        scratch = []
        for columns, order in lanes:
            scratch += Lane.scratch(n_dp, n_ex, rows, columns, order)
        return scratch + [pltpu.VMEM((2, rows, width), jnp.bfloat16), pltpu.SemaphoreType.DMA((2,))]

    def out_copy(self, c):
        slot = lax.rem(c, 2)
        return pltpu.make_async_copy(self.stage_ref.at[slot], self.out.at[c], self.stage_sem.at[slot])

    def first(self, g, c):
        _, piece, factor = self.groups[g]
        j = c - self.firsts[g]
        dy = factor(j)
        slot = lax.rem(c, 2)
        levels = self.n_dp.bit_length() - 1
        half = self.n_dp // 2

        def products(odd):
            parts = [piece(j, partner_index(self.d, 2 * i + odd, levels)) for i in range(half)]
            return dot(jnp.concatenate(parts, axis=0), dy)

        value = products(1)
        for lane in self.lanes:
            for i in range(half):
                part = value[i * self.rows : (i + 1) * self.rows, slice(*lane.columns)]
                lane.send[0][slot, i] = part.astype(jnp.bfloat16)
            lane.copy_of(0, c).start()
        value = products(0)
        for lane in self.lanes:
            for i in range(half):
                lane.keep[0][slot, i] = value[i * self.rows : (i + 1) * self.rows, slice(*lane.columns)]

    def last(self, c):
        slot = lax.rem(c, 2)

        @pl.when(c >= 2)
        def _():
            self.out_copy(c - 2).wait()

        for lane in self.lanes:
            self.stage_ref[slot, :, slice(*lane.columns)] = lane.final(c)
        self.out_copy(c).start()

    def tick(self, t, low, high):
        for s in range(self.count + 1):
            if high - s <= 0 or low - s >= self.chunks:
                continue
            c = t - s
            if s > 0:

                @pl.when((c >= 0) & (c < self.chunks))
                def _(s=s, c=c):
                    if s < self.count:
                        for lane in self.lanes:
                            lane.leave(s, c, lane.arrive(s - 1, c))
                    else:
                        self.last(c)

                continue
            for g, (size, _, _) in enumerate(self.groups):
                begin, end = self.firsts[g], self.firsts[g] + size
                if high <= begin or low >= end:
                    continue

                @pl.when((c >= begin) & (c < end))
                def _(g=g):
                    self.first(g, c)

    def finish(self):
        for c in range(max(0, self.chunks - 2), self.chunks):
            self.out_copy(c).wait()


def dense_lanes(width):
    cut = width // 768 * 640
    return [((0, cut), 0), ((cut, width), 1)]


def attend_back_kernel(n_dp, n_ex, *refs):
    (up_ref, x_ref, gain_ref, w_in_ref, w_out_ref, doc_row_ref, doc_col_ref), rest = refs[:7], refs[7:]
    (context_ref, kv_ref, q_ref, short_kv_ref, short_q_ref, lse_ref), rest = rest[:6], rest[6:]
    (assign_ref, gate_ref, stream_ref, result_ref), rest = rest[:4], rest[4:]
    (rows_t_ref, hidden_ref, active_t_ref, back_ref), rest = rest[:4], rest[4:]
    (up_next_ref, up_low_ref, mixed_ref, sums_ref, output_ref, chunks_ref), rest = rest[:6], rest[6:]
    (do_ref, aux_ref, short_do_ref, short_aux_ref, dq_ref, dk_ref, dv_ref), rest = rest[:7], rest[7:]
    (do_far, do_near, do_recv, aux_far, aux_near, aux_recv), rest = rest[:6], rest[6:]
    (home_ref, result_send_sem, result_recv_sem), rest = rest[:3], rest[3:]
    links = Links(n_dp)
    me = links.me
    pairs, long, width = kv_ref.shape[1], kv_ref.shape[3], x_ref.shape[1]
    up = up_ref[...]
    up_low = up.astype(jnp.bfloat16)
    up_low_ref[...] = up_low
    grad_context = dot_rows(up_low, w_out_ref[...]).astype(jnp.bfloat16)
    share_context(context_ref, lse_ref, grad_context, do_ref, aux_ref, short_do_ref, short_aux_ref, me, long)
    blocks = hidden_ref.shape[1] // width
    groups = [
        (blocks, lambda j, q: rows_t_ref[q, 0], lambda j: hidden_ref[:, pl.ds(pl.multiple_of(j * width, width), width)]),
        (blocks, lambda j, q: active_t_ref[q, j], lambda j: back_ref[...]),
    ]
    red = Reduction(n_dp, 1, width // n_dp, groups, [((0, width), 0)], list(rest) + [chunks_ref])
    greet(links.peers() + across_peers(n_ex))
    do_spread = Spread(links, lambda b, p: do_ref.at[b, p], pairs, False, do_far, do_near, do_recv)
    aux_spread = Spread(links, lambda b, p: aux_ref.at[b, p], pairs, False, aux_far, aux_near, aux_recv)
    for h in range(pairs):
        do_spread.send(h)
        aux_spread.send(h)
    result_across = Across(n_ex, result_ref, home_ref, result_send_sem, result_recv_sem)
    result_across.start_all()
    home_ref[links.expert] = result_ref[links.expert]
    red.tick(0, 0, 1)
    sequence = dict(
        doc_row=doc_row_ref, doc_col=doc_col_ref, kv=kv_ref, q=q_ref, short_kv=short_kv_ref, short_q=short_q_ref,
        do=do_ref, aux=aux_ref, short_do=short_do_ref, short_aux=short_aux_ref, dq=dq_ref, dk=dk_ref, dv=dv_ref,
        mixed=mixed_ref,
    )

    def pair(h, _):
        attend_back_pair(n_dp, me, width, sequence, do_spread, aux_spread, h)
        red.tick(1 + h, 1, 1 + pairs)
        return 0

    lax.fori_loop(0, pairs, pair, 0)
    grad_normed = dot_rows(mixed_ref[...], w_in_ref[...])
    unit, inverse = norm_parts(x_ref[...])
    up_next_ref[...] = up + norm_back(unit, inverse, gain_ref[...], grad_normed)
    sums_ref[0:1] = jnp.sum(grad_normed * unit, axis=0, keepdims=True)
    sums_ref[1:2] = jnp.sum(grad_normed, axis=0, keepdims=True)
    red.tick(1 + pairs, 1 + pairs, 2 + pairs)
    result_across.wait_all()
    dispatch = dispatch_of(assign_ref[...], n_ex)
    result = dot_columns(dispatch, home_ref[...].reshape(dispatch.shape[0], width))
    gate = jnp.broadcast_to(gate_ref[...], (128, gate_ref.shape[1])).T[:, 0:1]
    output_ref[...] = (stream_ref[...] + gate * result).astype(jnp.bfloat16)

    def rest_tick(t, _):
        red.tick(t, 2 + pairs, red.ticks)
        return 0

    lax.fori_loop(2 + pairs, red.ticks, rest_tick, 0)
    red.finish()
    for h in range(pairs):
        do_spread.sent(h)
        aux_spread.sent(h)


def attention_backward(
    n_dp, n_ex, collective_id, upstream, stream, norm_gain, weight_in, weight_out, doc_row, doc_col, kept, routing
):
    rows, width = stream.shape
    long, short, pairs = LONG_DEV, rows - LONG_DEV, width // 128
    low = jnp.bfloat16
    outs = [
        jax.ShapeDtypeStruct((rows, width), jnp.float32),
        jax.ShapeDtypeStruct((rows, width), low),
        jax.ShapeDtypeStruct((rows, 3 * width), low),
        jax.ShapeDtypeStruct((2, width), jnp.float32),
        jax.ShapeDtypeStruct((rows, width), low),
        jax.ShapeDtypeStruct((2 * (routing[5].shape[1] // width), width // n_dp, width), low),
    ]
    scratch = back_scratch(n_dp, pairs, long, short)
    scratch += [pltpu.VMEM(routing[3].shape, low)] + [pltpu.SemaphoreType.DMA((n_ex,))] * 2
    scratch += Reduction.scratch(n_dp, 1, width // n_dp, width, [((0, width), 0)])
    inputs = (upstream, stream, norm_gain, weight_in, weight_out, doc_row, doc_col) + tuple(kept) + tuple(routing)
    vmem = pl.BlockSpec(memory_space=pltpu.VMEM)
    return pl.pallas_call(
        functools.partial(attend_back_kernel, n_dp, n_ex),
        out_shape=outs,
        in_specs=[vmem] * len(inputs),
        out_specs=[vmem] * (len(outs) - 1) + [pl.BlockSpec(memory_space=pl.ANY)],
        scratch_shapes=scratch,
        compiler_params=pltpu.CompilerParams(
            collective_id=collective_id, has_side_effects=True, vmem_limit_bytes=56 * 1024 * 1024
        ),
        name="attention_backward",
    )(*inputs)


def tail_kernel(n_dp, n_ex, names, staged, *refs):
    r = dict(zip(names, refs))
    extra = iter(refs[len(names) :])
    loads = {}
    for name in staged:
        buffer, sem = next(extra), next(extra)
        loads[name] = pltpu.make_async_copy(r[name], buffer, sem)
        r[name] = buffer
    weights_in, weights_out, slopes, weight_sem = (next(extra) for _ in range(4))
    first_sem = next(extra)
    up_ref, acc_ref, dense_low_ref, dense_hidden_ref, first_low_ref, mixed_ref = (next(extra) for _ in range(6))
    do_ref, aux_ref, short_do_ref, short_aux_ref, dq_ref, dk_ref, dv_ref = (next(extra) for _ in range(7))
    do_far, do_near, do_recv, aux_far, aux_near, aux_recv = (next(extra) for _ in range(6))
    small_send, small_recv, small_send_sem, small_recv_sem = (next(extra) for _ in range(4))
    links = Links(n_dp)
    me = links.me
    width = up_ref.shape[1]
    rows = width // n_dp
    pairs, long = r["kv"].shape[1], r["kv"].shape[3]
    blocks = r["dense_in"].shape[1] // width
    per_in = mixed_ref.shape[1] // width

    def block_loads(i):
        slot = lax.rem(i, 2)
        at = pl.ds(pl.multiple_of(i * width, width), width)
        return [
            pltpu.make_async_copy(r["dense_out"].at[at, :], weights_out.at[slot], weight_sem.at[slot, 0]),
            pltpu.make_async_copy(r["dense_in"].at[:, at], weights_in.at[slot], weight_sem.at[slot, 1]),
            pltpu.make_async_copy(r["slope"].at[:, at], slopes.at[slot], weight_sem.at[slot, 2]),
        ]

    for i in range(min(2, blocks)):
        for load in block_loads(i):
            load.start()
    for name in staged:
        loads[name].start()
    free, busy = blocks % 2, (blocks - 1) % 2
    out_load = pltpu.make_async_copy(r["attn_out"].at[0], weights_out.at[free], first_sem.at[0])
    thirds = [weights_in.at[free], weights_in.at[busy], weights_out.at[busy]]
    in_loads = [
        pltpu.make_async_copy(r["attn_in"].at[0, :, pl.ds(i * width, width)], third, first_sem.at[1 + i])
        for i, third in enumerate(thirds)
    ]

    def columns(ref):
        return lambda j: ref[:, pl.ds(pl.multiple_of(j * width, width), width)]

    def one(ref):
        return lambda j, q: ref[q, 0]

    groups = [
        (1, one(r["second_context_t"]), columns(r["second_low"])),
        (per_in, one(r["second_normed_t"]), columns(r["second_mixed"])),
        (blocks, lambda j, q: r["active_t"][q, j], lambda j: dense_low_ref[...]),
        (blocks, one(r["dense_normed_t"]), columns(dense_hidden_ref)),
        (1, one(r["first_context_t"]), columns(first_low_ref)),
        (per_in, one(r["first_normed_t"]), columns(mixed_ref)),
    ]
    red_refs = list(extra) + [r["chunks"]]
    red = Reduction(n_dp, n_ex, rows, groups, dense_lanes(width), red_refs)
    levels = [("dp", b) for b in range(n_dp.bit_length() - 1)] + [("ex", b) for b in range(n_ex.bit_length() - 1)]
    greet([red.peer(*level) for level in levels] + (links.peers()[1:] if links.chips > 2 else []))

    up = r["up"][...]
    dense_low_ref[...] = up.astype(jnp.bfloat16)
    acc_ref[...] = jnp.zeros_like(acc_ref)
    for name in ("second_context_t", "second_low", "second_normed_t", "second_mixed"):
        loads[name].wait()

    def dense(i, _):
        slot = lax.rem(i, 2)
        for load in block_loads(i):
            load.wait()
        grad = dot_rows(dense_low_ref[...], weights_out[slot]) * slopes[slot].astype(jnp.float32)
        grad = grad.astype(jnp.bfloat16)
        dense_hidden_ref[:, pl.ds(pl.multiple_of(i * width, width), width)] = grad
        acc_ref[...] += dot_rows(grad, weights_in[slot])

        @pl.when(i + 2 < blocks)
        def _():
            for load in block_loads(i + 2):
                load.start()

        @pl.when(i == blocks - 2)
        def _():
            out_load.start()
            in_loads[0].start()

        @pl.when(lax.rem(i, 2) == 1)
        def _():
            red.tick(i // 2, 0, 2)

        return 0

    lax.fori_loop(0, blocks, dense, 0)
    for load in in_loads[1:]:
        load.start()
    for name in staged:
        if not name.startswith("second"):
            loads[name].wait()
    unit, inverse = norm_parts(r["dense_x"][...])
    grad_normed = acc_ref[...]
    up = up + norm_back(unit, inverse, r["dense_gain"][...], grad_normed)
    up_ref[...] = up
    small_send[0] = r["small"][...]
    small_send[0, 1:2] = jnp.sum(grad_normed * unit, axis=0, keepdims=True)
    small_send[0, 5:6] = jnp.sum(grad_normed, axis=0, keepdims=True)
    at_tick = blocks // 2

    scale = HEAD_DIM ** (-0.5)
    up_low = up.astype(jnp.bfloat16)
    first_low_ref[...] = up_low
    out_load.wait()
    grad_context = dot_rows(up_low, weights_out[free]).astype(jnp.bfloat16)
    share_context(r["context"], r["lse"], grad_context, do_ref, aux_ref, short_do_ref, short_aux_ref, me, long)
    do_spread = Spread(links, lambda b, p: do_ref.at[b, p], pairs, False, do_far, do_near, do_recv)
    aux_spread = Spread(links, lambda b, p: aux_ref.at[b, p], pairs, False, aux_far, aux_near, aux_recv)
    for h in range(pairs):
        do_spread.send(h)
        aux_spread.send(h)
    red.tick(at_tick, at_tick, at_tick + 1)
    at_tick += 1
    sequence = dict(
        doc_row=r["doc_row"], doc_col=r["doc_col"], kv=r["kv"], q=r["q"], short_kv=r["short_kv"], short_q=r["short_q"],
        do=do_ref, aux=aux_ref, short_do=short_do_ref, short_aux=short_aux_ref, dq=dq_ref, dk=dk_ref, dv=dv_ref,
        mixed=mixed_ref,
    )

    def pair(h, _):
        attend_back_pair(n_dp, me, width, sequence, do_spread, aux_spread, h)
        red.tick(at_tick + h, at_tick, at_tick + pairs)
        return 0

    lax.fori_loop(0, pairs, pair, 0)
    at_tick += pairs
    grad_normed = jnp.zeros((up_ref.shape[0], width), jnp.float32)
    for i, third in enumerate(thirds):
        in_loads[i].wait()
        grad_normed = grad_normed + dot_rows(mixed_ref[:, i * width : (i + 1) * width], third[...])
    unit, inverse = norm_parts(r["first_x"][...].astype(jnp.float32))
    r["grad_tokens"][...] = (
        up_ref[...] + norm_back(unit, inverse, r["first_gain"][...], grad_normed)
    ).astype(jnp.bfloat16)
    small_send[0, 0:1] = jnp.sum(grad_normed * unit, axis=0, keepdims=True)
    small_send[0, 4:5] = jnp.sum(grad_normed, axis=0, keepdims=True)

    def small_copy(i):
        return pltpu.make_async_remote_copy(
            src_ref=small_send.at[i],
            dst_ref=small_recv.at[i],
            send_sem=small_send_sem.at[i],
            recv_sem=small_recv_sem.at[i],
            device_id=red.peer(*levels[i]),
            device_id_type=MESH,
        )

    small_copy(0).start()

    def rest(t, _):
        red.tick(t, at_tick, red.ticks)
        for i in range(1, len(levels) + 1):

            @pl.when(t == at_tick + i)
            def _(i=i):
                small_copy(i - 1).wait()
                value = small_send[i - 1] + small_recv[i - 1]
                if i < len(levels):
                    small_send[i] = value
                    small_copy(i).start()
                else:
                    r["small_sum"][...] = value

        return 0

    lax.fori_loop(at_tick, red.ticks, rest, 0)
    red.finish()
    for h in range(pairs):
        do_spread.sent(h)
        aux_spread.sent(h)


def tail(n_dp, n_ex, collective_id, arrays):
    staged = (
        "second_context_t", "second_low", "second_normed_t", "second_mixed", "active_t", "dense_normed_t", "dense_x",
        "kv", "q", "short_kv", "short_q", "context", "first_x", "first_context_t", "first_normed_t",
    )
    far = staged + ("dense_in", "dense_out", "slope", "attn_in", "attn_out")
    low, wide = jnp.bfloat16, jnp.float32
    tokens, width = arrays["up"].shape
    hidden = arrays["dense_in"].shape[1]
    mixed = arrays["attn_in"].shape[2]
    rows = width // n_dp
    long, short, pairs = LONG_DEV, tokens - LONG_DEV, width // 128
    chunks = 2 * (hidden // width) + 2 * (1 + mixed // width)
    small = arrays["small"].shape
    outs = dict(
        chunks=jax.ShapeDtypeStruct((chunks, rows, width), low),
        grad_tokens=jax.ShapeDtypeStruct((tokens, width), low),
        small_sum=jax.ShapeDtypeStruct(small, wide),
    )
    scratch = []
    for name in staged:
        scratch += [pltpu.VMEM(arrays[name].shape, arrays[name].dtype), pltpu.SemaphoreType.DMA]
    scratch += [pltpu.VMEM((2, width, width), low)] * 2
    scratch += [pltpu.VMEM((2, tokens, width), low), pltpu.SemaphoreType.DMA((2, 3))]
    scratch += [pltpu.SemaphoreType.DMA((4,))]
    scratch += [pltpu.VMEM((tokens, width), wide)] * 2
    scratch += [pltpu.VMEM((tokens, n), low) for n in (width, hidden, width, mixed)]
    scratch += back_scratch(n_dp, pairs, long, short)
    hops = (n_dp * n_ex).bit_length() - 1
    scratch += [pltpu.VMEM((hops,) + small, wide)] * 2 + [pltpu.SemaphoreType.DMA((hops,))] * 2
    scratch += Reduction.scratch(n_dp, n_ex, rows, width, dense_lanes(width))
    vmem, anywhere = pl.BlockSpec(memory_space=pltpu.VMEM), pl.BlockSpec(memory_space=pl.ANY)
    names = tuple(arrays) + tuple(outs)
    return pl.pallas_call(
        functools.partial(tail_kernel, n_dp, n_ex, names, staged),
        out_shape=list(outs.values()),
        in_specs=[anywhere if name in far else vmem for name in arrays],
        out_specs=[anywhere if name == "chunks" else vmem for name in outs],
        scratch_shapes=scratch,
        compiler_params=pltpu.CompilerParams(
            collective_id=collective_id, has_side_effects=True, vmem_limit_bytes=61 * 1024 * 1024
        ),
        name="tail",
    )(*arrays.values())


def shards(
    tokens,
    doc_lengths,
    assign,
    ln_gain,
    ln_bias,
    attn_in,
    attn_out,
    ffn_in,
    ffn_out,
    router,
    expert_in,
    expert_out,
    cotangent,
):
    n_dp, n_ex = lax.axis_size("dp"), lax.axis_size("expert")
    stream_first = tokens[0].astype(jnp.float32)
    row_count = stream_first.shape[0]
    doc_ends = jnp.cumsum(doc_lengths[0, 0])
    short_place = jnp.arange(row_count - LONG_DEV, dtype=jnp.int32)
    short_ids = jnp.sum((short_place[:, None] >= doc_ends[None, :]).astype(jnp.int32), axis=-1)
    doc_row, doc_col = short_ids[None, :], short_ids[:, None]
    weights_in, weights_out = lax.optimization_barrier((attn_in.transpose(1, 0, 2), attn_out.transpose(1, 0, 2)))
    gains, shifts = ln_gain.T, ln_bias.T
    assign_row = assign[0].T
    stream_one, *kept_one = attention_forward(
        n_dp, n_ex, 2, stream_first, gains[0:1], shifts[0:1], weights_in[0], weights_out[0], doc_row, doc_col
    )
    stream_two, dense_normed_t, active_t, slope = ffn_forward(stream_one, gains[1:2], shifts[1:2], ffn_in, ffn_out)
    stream_three, *kept_three, far_cot = attention_forward(
        n_dp, n_ex, 3, stream_two, gains[2:3], shifts[2:3], weights_in[1], weights_out[1], doc_row, doc_col,
        (assign_row, cotangent[0]),
    )
    (
        upstream, fourth_sums, router_grad, rows_t, expert_back, expert_active_t, expert_hidden, result, gate, stats
    ) = mixture(
        n_dp, n_ex, 6, stream_three, gains[3:4], shifts[3:4], router.T, assign_row, cotangent[0], far_cot,
        expert_in[0], expert_out[0],
    )
    everyone = row_count * n_dp * n_ex
    balance = n_ex * jnp.sum((stats[:, 0] / everyone - 1.0 / n_ex) * (stats[:, 1] / everyone))
    model_width = tokens.shape[2]
    rows = model_width // n_dp
    expert_factors = (
        rows_t.reshape(n_dp, 1, rows, -1),
        expert_hidden,
        expert_active_t.reshape(n_dp, -1, rows, expert_hidden.shape[0]),
        expert_back.reshape(-1, model_width),
    )
    upstream, second_low, second_mixed, second_sums, output, expert_chunks = attention_backward(
        n_dp, n_ex, 4, upstream, stream_two, gains[2:3], weights_in[1], weights_out[1], doc_row, doc_col,
        kept_three[1:2] + kept_three[3:], (assign_row, gate, stream_three, result) + expert_factors,
    )
    output = output[None]

    def blocks_of(rows_t):
        return rows_t.reshape(n_dp, -1, rows, row_count)

    none = jnp.zeros((2, model_width), jnp.float32)
    small = jnp.concatenate(
        [none, second_sums[0:1], fourth_sums[0:1], none, second_sums[1:2], fourth_sums[1:2], router_grad], axis=0
    )
    chunks, grad_tokens, small = tail(
        n_dp,
        n_ex,
        5,
        dict(
            up=upstream,
            dense_x=stream_one,
            dense_gain=gains[1:2],
            first_gain=gains[0:1],
            dense_in=ffn_in,
            dense_out=ffn_out,
            slope=slope,
            first_x=tokens[0],
            attn_in=weights_in,
            attn_out=weights_out,
            doc_row=doc_row,
            doc_col=doc_col,
            context=kept_one[1],
            kv=kept_one[3],
            q=kept_one[4],
            short_kv=kept_one[5],
            short_q=kept_one[6],
            lse=kept_one[7],
            second_context_t=blocks_of(kept_three[2]),
            second_normed_t=blocks_of(kept_three[0]),
            active_t=blocks_of(active_t),
            dense_normed_t=blocks_of(dense_normed_t),
            first_context_t=blocks_of(kept_one[2]),
            first_normed_t=blocks_of(kept_one[0]),
            second_low=second_low,
            second_mixed=second_mixed,
            small=small,
        ),
    )
    grad_tokens = grad_tokens[None]
    attn_in_sum, attn_out_sum, ffn_in_sum, ffn_out_sum, expert_in_sum, expert_out_sum = unpack(
        chunks, expert_chunks, attn_in.shape[2] // model_width, ffn_in.shape[1] // model_width
    )
    small = lax.dynamic_slice_in_dim(small, lax.axis_index("dp") * rows, rows, 1).T
    summed = [
        attn_in_sum,
        attn_out_sum,
        ffn_in_sum,
        ffn_out_sum.reshape(-1, model_width),
        small[:, 8:],
        small[:, :4],
        small[:, 4:8],
    ]
    return (
        output,
        balance,
        grad_tokens,
        summed[5],
        summed[6],
        summed[0],
        summed[1],
        summed[2],
        summed[3],
        summed[4],
        expert_in_sum[None],
        expert_out_sum.reshape(1, -1, model_width),
    )


def solution(mesh):
    return jax.shard_map(
        shards,
        mesh=mesh,
        in_specs=(
            P("expert", "dp", None),
            P("expert", "dp", None),
            P("expert", "dp", None),
            P(),
            P(),
            P(),
            P(),
            P(),
            P(),
            P(),
            P("expert", None, None),
            P("expert", None, None),
            P("expert", "dp", None),
        ),
        out_specs=(
            P("expert", "dp", None),
            P(),
            P("expert", "dp", None),
            P("dp", None),
            P("dp", None),
            P("dp", None, None),
            P("dp", None, None),
            P("dp", None),
            P("dp", None),
            P("dp", None),
            P("expert", "dp", None),
            P("expert", "dp", None),
        ),
        check_vma=False,
    )
```

```python
import functools
import types

import jax
import jax.numpy as jnp
from jax import lax
from jax.experimental import pallas as pl
from jax.experimental.pallas import tpu as pltpu
from jax.sharding import PartitionSpec as P

MESH = pl.DeviceIdType.MESH
HEADS = 12
HEAD_DIM = 64
LONG_DEV = 256


epsilon = 1e-05
balance_weight = 0.01
masked_score = -1e30


def bit_of(index, level):
    return (index // (1 << level)) % 2


def flip(index, level):
    return index + (1 << level) * (1 - 2 * bit_of(index, level))


def partner_index(index, mask, levels):
    total = 0
    for level in range(levels):
        own = bit_of(index, level)
        total = total + (1 << level) * (1 - own if (mask >> level) & 1 else own)
    return total


def unpack_kernel(
    per_in, per_ffn, chunk_ref, expert_ref, in_ref, out_ref, ffn_in_ref, ffn_out_ref, expert_in_ref, expert_out_ref
):
    per_expert = expert_ref.shape[0] // 2
    width = chunk_ref.shape[2]
    at = 0
    for layer in (1, 0):
        out_ref[:, layer, :] = chunk_ref[at].astype(jnp.float32)
        for j in range(per_in):
            in_ref[:, layer, width * j : width * j + width] = chunk_ref[at + 1 + j].astype(jnp.float32)
        at += 1 + per_in
        if layer:
            for j in range(per_ffn):
                ffn_out_ref[j] = chunk_ref[at + j].astype(jnp.float32)
                ffn_in_ref[:, width * j : width * j + width] = chunk_ref[at + per_ffn + j].astype(jnp.float32)
            at += 2 * per_ffn
    for j in range(per_expert):
        expert_in_ref[:, width * j : width * j + width] = expert_ref[j].astype(jnp.float32)
        expert_out_ref[j] = expert_ref[per_expert + j].astype(jnp.float32)


def unpack(chunks, expert_chunks, per_in, per_ffn):
    count, rows, width = chunks.shape
    experts = expert_chunks.shape[0]
    step = 48 if rows % 48 == 0 else rows
    wide = jnp.float32
    return pl.pallas_call(
        functools.partial(unpack_kernel, per_in, per_ffn),
        grid=(rows // step,),
        out_shape=[
            jax.ShapeDtypeStruct((rows, 2, per_in * width), wide),
            jax.ShapeDtypeStruct((rows, 2, width), wide),
            jax.ShapeDtypeStruct((rows, per_ffn * width), wide),
            jax.ShapeDtypeStruct((per_ffn, rows, width), wide),
            jax.ShapeDtypeStruct((rows, experts // 2 * width), wide),
            jax.ShapeDtypeStruct((experts // 2, rows, width), wide),
        ],
        in_specs=[
            pl.BlockSpec((count, step, width), lambda i: (0, i, 0)),
            pl.BlockSpec((experts, step, width), lambda i: (0, i, 0)),
        ],
        out_specs=[
            pl.BlockSpec((step, 2, per_in * width), lambda i: (i, 0, 0)),
            pl.BlockSpec((step, 2, width), lambda i: (i, 0, 0)),
            pl.BlockSpec((step, per_ffn * width), lambda i: (i, 0)),
            pl.BlockSpec((per_ffn, step, width), lambda i: (0, i, 0)),
            pl.BlockSpec((step, experts // 2 * width), lambda i: (i, 0)),
            pl.BlockSpec((experts // 2, step, width), lambda i: (0, i, 0)),
        ],
        compiler_params=pltpu.CompilerParams(vmem_limit_bytes=40 * 1024 * 1024),
        name="unpack",
    )(chunks, expert_chunks)


def dot(a, b):
    return jnp.dot(a, b, preferred_element_type=jnp.float32)


def dot_rows(a, b):
    return lax.dot_general(a, b, (((1,), (1,)), ((), ())), preferred_element_type=jnp.float32)


def dot_columns(a, b):
    return lax.dot_general(a, b, (((0,), (0,)), ((), ())), preferred_element_type=jnp.float32)


def gelu_parts(hidden):
    lower = 0.5 + 0.5 * lax.erf(hidden * 0.7071067811865476)
    slope = lower + hidden * jnp.exp(-0.5 * hidden * hidden) * 0.3989422804014327
    return hidden * lower, slope


def norm_parts(x):
    center = x - jnp.mean(x, axis=-1, keepdims=True)
    inverse = lax.rsqrt(jnp.mean(center * center, axis=-1, keepdims=True) + epsilon)
    return center * inverse, inverse


def norm_back(unit, inverse, gain, upstream):
    scaled = upstream * gain
    return inverse * (
        scaled - jnp.mean(scaled, axis=-1, keepdims=True) - unit * jnp.mean(scaled * unit, axis=-1, keepdims=True)
    )


def ffn_kernel(x_ref, gain_ref, shift_ref, w_in_ref, w_out_ref, next_ref, normed_t_ref, active_t_ref, slope_ref, normed_ref):
    @pl.when(pl.program_id(0) == 0)
    def _():
        x = x_ref[...]
        unit, _ = norm_parts(x)
        normed = (unit * gain_ref[...] + shift_ref[...]).astype(jnp.bfloat16)
        normed_ref[...] = normed
        normed_t_ref[...] = normed.T
        next_ref[...] = x

    active, slope = gelu_parts(dot(normed_ref[...], w_in_ref[...]))
    active = active.astype(jnp.bfloat16)
    slope_ref[...] = slope.astype(jnp.bfloat16)
    active_t_ref[...] = active.T
    next_ref[...] += dot(active, w_out_ref[...])


def ffn_forward(stream, norm_gain, norm_shift, weight_in, weight_out):
    rows, width = stream.shape
    hidden = weight_in.shape[1]
    low = jnp.bfloat16
    return pl.pallas_call(
        ffn_kernel,
        grid=(hidden // width,),
        out_shape=[
            jax.ShapeDtypeStruct((rows, width), jnp.float32),
            jax.ShapeDtypeStruct((width, rows), low),
            jax.ShapeDtypeStruct((hidden, rows), low),
            jax.ShapeDtypeStruct((rows, hidden), low),
        ],
        in_specs=[
            pl.BlockSpec((rows, width), lambda i: (0, 0)),
            pl.BlockSpec((1, width), lambda i: (0, 0)),
            pl.BlockSpec((1, width), lambda i: (0, 0)),
            pl.BlockSpec((width, width), lambda i: (0, i)),
            pl.BlockSpec((width, width), lambda i: (i, 0)),
        ],
        out_specs=[
            pl.BlockSpec((rows, width), lambda i: (0, 0)),
            pl.BlockSpec((width, rows), lambda i: (0, 0)),
            pl.BlockSpec((width, rows), lambda i: (i, 0)),
            pl.BlockSpec((rows, width), lambda i: (0, i)),
        ],
        scratch_shapes=[pltpu.VMEM((rows, width), low)],
        compiler_params=pltpu.CompilerParams(vmem_limit_bytes=48 * 1024 * 1024),
        name="ffn_forward",
    )(stream, norm_gain, norm_shift, weight_in, weight_out)


def capacity_of(rows, experts):
    capacity = (5 * rows + 4 * experts - 1) // (4 * experts)
    return capacity, -(-capacity // 16) * 16


def chosen_rows(assign, experts):
    expert = lax.broadcasted_iota(jnp.int32, (experts, assign.shape[1]), 0)
    return jnp.where(assign == expert, 1.0, 0.0)


def dispatch_of(assign, experts):
    tokens = assign.shape[1]
    capacity, padded = capacity_of(tokens, experts)
    hot = chosen_rows(assign, experts)
    earlier = lax.broadcasted_iota(jnp.int32, (tokens, tokens), 0) < lax.broadcasted_iota(jnp.int32, (tokens, tokens), 1)
    before = dot(hot.astype(jnp.bfloat16), jnp.where(earlier, 1.0, 0.0).astype(jnp.bfloat16))
    place = jnp.sum(hot * before, axis=0, keepdims=True)
    slot = jnp.where(place < capacity, assign.astype(jnp.float32) * padded + place, -1.0)
    number = lax.broadcasted_iota(jnp.int32, (experts * padded, tokens), 0).astype(jnp.float32)
    return jnp.where(number == slot, 1.0, 0.0).astype(jnp.bfloat16)


class Across:
    def __init__(self, experts, out, into, send_sems, recv_sems):
        self.experts, self.out, self.into = experts, out, into
        self.send_sems, self.recv_sems = send_sems, recv_sems
        self.dp, self.me = lax.axis_index("dp"), lax.axis_index("expert")

    def copy(self, slab, place, to):
        return pltpu.make_async_remote_copy(
            src_ref=self.out.at[slab],
            dst_ref=self.into.at[place],
            send_sem=self.send_sems.at[slab],
            recv_sem=self.recv_sems.at[place],
            device_id=(self.dp, to),
            device_id_type=MESH,
        )

    def start(self, j):
        self.copy(j, self.me, j).start()

    def wait_from(self, j):
        self.copy(j, j, j).wait_recv()

    def wait_to(self, j):
        self.copy(j, self.me, j).wait_send()

    def others(self, use):
        def body(k, _):
            use(lax.rem(self.me + k, self.experts))
            return 0

        lax.fori_loop(1, self.experts, body, 0)

    def start_all(self):
        self.others(self.start)

    def wait_all(self):
        def both(j):
            self.wait_from(j)
            self.wait_to(j)

        self.others(both)


def greet(targets):
    barrier = pltpu.get_barrier_semaphore()
    for device in targets:
        pl.semaphore_signal(barrier, inc=1, device_id=device, device_id_type=MESH)
    pl.semaphore_wait(barrier, len(targets))


def across_peers(experts):
    d, e = lax.axis_index("dp"), lax.axis_index("expert")
    return [(d, lax.rem(e + k, experts)) for k in range(1, experts)]


def head_pair(rows):
    first = lax.broadcasted_iota(jnp.int32, rows.shape, 1) < HEAD_DIM
    zero = jnp.zeros_like(rows)
    return jnp.concatenate([jnp.where(first, rows, zero), jnp.where(first, zero, rows)], axis=0)


def pair_rows(both):
    n = both.shape[1] // 2
    return jnp.concatenate([both[:HEAD_DIM, :n], both[HEAD_DIM:, n:]], axis=0)


def causal(keys, queries):
    key = lax.broadcasted_iota(jnp.int32, (keys, 2 * queries), 0)
    query = lax.broadcasted_iota(jnp.int32, (keys, 2 * queries), 1)
    return key <= jnp.where(query >= queries, query - queries, query)


def short_seen(doc_row, doc_col):
    n = doc_row.shape[1]
    same = doc_col == jnp.concatenate([doc_row, doc_row], axis=1)
    return same & causal(n, n)


class Links:
    def __init__(self, n_dp):
        self.me, self.expert = lax.axis_index("dp"), lax.axis_index("expert")
        self.chips = n_dp // 2
        self.chip, self.core = self.me // 2, self.me % 2
        self.twin = self.me + 1 - 2 * self.core

    def peers(self):
        ring = [lax.rem(self.chip + k, self.chips) for k in range(1, self.chips)]
        return [(self.twin, self.expert)] + [(2 * other + self.core, self.expert) for other in ring]

    def copy(self, ref, send_sem, recv_sem, index):
        return pltpu.make_async_remote_copy(
            src_ref=ref,
            dst_ref=ref,
            send_sem=send_sem,
            recv_sem=recv_sem,
            device_id=(index, self.expert),
            device_id_type=MESH,
        )

    def before(self, later, other):
        return other > self.chip if later else other < self.chip


class Spread:
    def __init__(self, links, at, parts, later, far_sems, near_sems, recv_sems):
        self.links, self.at, self.later = links, at, later
        self.far_sems, self.near_sems, self.recv_sems = far_sems, near_sems, recv_sems

    def _far(self, other, p):
        k = self.links
        return k.copy(self.at(k.me, p), self.far_sems.at[other, p], self.recv_sems.at[k.me, p], 2 * other + k.core)

    def _near(self, block, p):
        k = self.links
        return k.copy(self.at(block, p), self.near_sems.at[block, p], self.recv_sems.at[block, p], k.twin)

    def _twin_needs(self):
        return self.links.core == (0 if self.later else 1)

    def send(self, p):
        k = self.links
        for other in range(k.chips):

            @pl.when(k.before(self.later, other))
            def _():
                self._far(other, p).start()

        @pl.when(self._twin_needs())
        def _():
            self._near(k.me, p).start()

    def sent(self, p):
        k = self.links
        for other in range(k.chips):

            @pl.when(k.before(self.later, other))
            def _():
                self._far(other, p).wait_send()

            @pl.when(k.before(not self.later, other))
            def _():
                self._near(2 * other + k.core, p).wait_send()

        @pl.when(self._twin_needs())
        def _():
            self._near(k.me, p).wait_send()

    def relay(self, p):
        k = self.links
        for other in range(k.chips):

            @pl.when(k.before(not self.later, other))
            def _():
                block = 2 * other + k.core
                copy = self._near(block, p)
                copy.wait_recv()
                copy.start()

    def each(self, p, use):
        k = self.links

        @pl.when(k.core == (1 if self.later else 0))
        def _():
            self._near(k.twin, p).wait_recv()
            use(k.twin)

        for other in range(k.chips):

            @pl.when(k.before(not self.later, other))
            def _():
                use(2 * other + k.core)
                block = 2 * other + 1 - k.core
                self._near(block, p).wait_recv()
                use(block)


def attend_kernel(
    n_dp, n_ex, inputs, *refs
):
    (x_ref, gain_ref, shift_ref, w_in_ref, w_out_ref, doc_row_ref, doc_col_ref), rest = refs[:7], refs[7:]
    if inputs > 7:
        (assign_ref, cot_ref), rest = rest[:2], rest[2:]
    (
        next_ref, normed_t_ref, context_ref, context_t_ref, kv_ref, q_ref, short_kv_ref, short_q_ref, lse_ref,
    ), rest = rest[:9], rest[9:]
    if inputs > 7:
        (far_cot_ref,), rest = rest[:1], rest[1:]
    (acc_ref, top_ref, total_ref, kv_far, kv_near, kv_recv, q_far, q_near, q_recv), rest = rest[:9], rest[9:]
    links = Links(n_dp)
    me = links.me
    pairs, long = kv_ref.shape[1], kv_ref.shape[3]
    width = x_ref.shape[1]
    x = x_ref[...]
    center = x - jnp.mean(x, axis=-1, keepdims=True)
    inverse = lax.rsqrt(jnp.mean(center * center, axis=-1, keepdims=True) + epsilon)
    normed = (center * inverse * gain_ref[...] + shift_ref[...]).astype(jnp.bfloat16)

    kv = dot(normed, w_in_ref[:, width:]).astype(jnp.bfloat16)
    for h in range(pairs):
        for part in range(2):
            piece = kv[:, part * width + 128 * h : part * width + 128 * h + 128]
            kv_ref[me, h, part] = piece[:long]
            short_kv_ref[h, part] = piece[long:]
    greet(links.peers() + (across_peers(n_ex) if inputs > 7 else []))
    kv_spread = Spread(links, lambda b, p: kv_ref.at[b, p], pairs, True, kv_far, kv_near, kv_recv)
    q_spread = Spread(links, lambda b, p: q_ref.at[b], 1, False, q_far, q_near, q_recv)
    for h in range(pairs):
        kv_spread.send(h)
    q = (dot(normed, w_in_ref[:, :width]).astype(jnp.bfloat16) * HEAD_DIM ** (-0.5)).astype(jnp.bfloat16)
    for h in range(pairs):
        piece = q[:, 128 * h : 128 * h + 128]
        q_ref[me, h] = piece[:long]
        short_q_ref[h] = piece[long:]
    q_spread.send(0)
    if inputs > 7:
        cot_send_ref, cot_send_sem, cot_recv_sem = rest
        cot_send_ref[...] = dot(dispatch_of(assign_ref[...], n_ex), cot_ref[...]).astype(jnp.bfloat16).reshape(
            cot_send_ref.shape
        )
        cot_across = Across(n_ex, cot_send_ref, far_cot_ref, cot_send_sem, cot_recv_sem)
        cot_across.start_all()
        far_cot_ref[links.expert] = cot_send_ref[links.expert]
    normed_t_ref[...] = normed.T

    def put_context(h, rows_t, first, count):
        at = pl.ds(pl.multiple_of(128 * h, 128), 128)
        context_t_ref[at, first : first + count] = rows_t.astype(jnp.bfloat16)
        context_ref[first : first + count, at] = rows_t.T.astype(jnp.bfloat16)

    def own_part(h, _):
        seen = short_seen(doc_row_ref[...], doc_col_ref[...])
        scores = jnp.where(seen, dot_rows(short_kv_ref[h, 0], head_pair(short_q_ref[h])), masked_score)
        top = jnp.max(scores, axis=0, keepdims=True)
        weights = jnp.exp(scores - top)
        total = jnp.sum(weights, axis=0, keepdims=True)
        rows_t = pair_rows(dot_columns(short_kv_ref[h, 1], weights.astype(jnp.bfloat16)) / total)
        short = rows_t.shape[1]
        put_context(h, rows_t, long, short)
        lse = top + jnp.log(total)
        lse_ref[h, 0:1, long:] = lse[:, :short]
        lse_ref[h, 1:2, long:] = lse[:, short:]
        scores = jnp.where(causal(long, long), dot_rows(kv_ref[me, h, 0], head_pair(q_ref[me, h])), masked_score)
        top = jnp.max(scores, axis=0, keepdims=True)
        weights = jnp.exp(scores - top)
        top_ref[h] = top
        total_ref[h] = jnp.sum(weights, axis=0, keepdims=True)
        acc_ref[h] = dot_columns(kv_ref[me, h, 1], weights.astype(jnp.bfloat16))
        return 0

    lax.fori_loop(0, pairs, own_part, 0)

    def other_part(h, _):
        kv_spread.relay(h)
        queries = head_pair(q_ref[me, h])

        def use(block):
            scores = dot_rows(kv_ref[block, h, 0], queries)
            old = top_ref[h]
            top = jnp.maximum(old, jnp.max(scores, axis=0, keepdims=True))
            factor = jnp.exp(old - top)
            weights = jnp.exp(scores - top)
            top_ref[h] = top
            total_ref[h] = total_ref[h] * factor + jnp.sum(weights, axis=0, keepdims=True)
            acc_ref[h] = acc_ref[h] * factor + dot_columns(kv_ref[block, h, 1], weights.astype(jnp.bfloat16))

        kv_spread.each(h, use)
        total = total_ref[h]
        put_context(h, pair_rows(acc_ref[h] / total), 0, long)
        lse = top_ref[h] + jnp.log(total)
        lse_ref[h, 0:1, :long] = lse[:, :long]
        lse_ref[h, 1:2, :long] = lse[:, long:]
        return 0

    lax.fori_loop(0, pairs, other_part, 0)
    next_ref[...] = x + dot(context_ref[...], w_out_ref[...])
    q_spread.relay(0)
    q_spread.each(0, lambda block: None)
    q_spread.sent(0)
    for h in range(pairs):
        kv_spread.sent(h)
    if inputs > 7:
        cot_across.wait_all()


def spread_sems(n_dp, parts):
    return [
        pltpu.SemaphoreType.DMA((n_dp // 2, parts)),
        pltpu.SemaphoreType.DMA((n_dp, parts)),
        pltpu.SemaphoreType.DMA((n_dp, parts)),
    ]


def attention_forward(
    n_dp, n_ex, collective_id, stream, norm_gain, norm_shift, weight_in, weight_out, doc_row, doc_col, routing=()
):
    rows, width = stream.shape
    long, short, pairs = LONG_DEV, rows - LONG_DEV, width // 128
    low = jnp.bfloat16
    outs = [
        jax.ShapeDtypeStruct((rows, width), jnp.float32),
        jax.ShapeDtypeStruct((width, rows), low),
        jax.ShapeDtypeStruct((rows, width), low),
        jax.ShapeDtypeStruct((width, rows), low),
        jax.ShapeDtypeStruct((n_dp, pairs, 2, long, 128), low),
        jax.ShapeDtypeStruct((n_dp, pairs, long, 128), low),
        jax.ShapeDtypeStruct((pairs, 2, short, 128), low),
        jax.ShapeDtypeStruct((pairs, short, 128), low),
        jax.ShapeDtypeStruct((pairs, 2, rows), jnp.float32),
    ]
    scratch = [
        pltpu.VMEM((pairs, 128, 2 * long), jnp.float32),
        pltpu.VMEM((pairs, 1, 2 * long), jnp.float32),
        pltpu.VMEM((pairs, 1, 2 * long), jnp.float32),
    ]
    scratch += spread_sems(n_dp, pairs) + spread_sems(n_dp, 1)
    if routing:
        slab = (n_ex, capacity_of(rows, n_ex)[1], width)
        outs += [jax.ShapeDtypeStruct(slab, low)]
        scratch += [pltpu.VMEM(slab, low)] + [pltpu.SemaphoreType.DMA((n_ex,))] * 2
    inputs = (stream, norm_gain, norm_shift, weight_in, weight_out, doc_row, doc_col) + tuple(routing)
    vmem = pl.BlockSpec(memory_space=pltpu.VMEM)
    return pl.pallas_call(
        functools.partial(attend_kernel, n_dp, n_ex, len(inputs)),
        out_shape=outs,
        in_specs=[vmem] * len(inputs),
        out_specs=[vmem] * len(outs),
        scratch_shapes=scratch,
        compiler_params=pltpu.CompilerParams(
            collective_id=collective_id, has_side_effects=True, vmem_limit_bytes=48 * 1024 * 1024
        ),
        name="attention_forward",
    )(*inputs)


def share_context(context, lse, grad_context, do_ref, aux_ref, short_do_ref, short_aux_ref, me, long):
    lane = lax.broadcasted_iota(jnp.int32, (8, 128), 1) < HEAD_DIM
    head = lax.broadcasted_iota(jnp.int32, (8, 128), 0)
    picks = jnp.where(((head == 0) & lane) | ((head == 1) & ~lane), 1.0, 0.0)
    for h in range(do_ref.shape[1]):
        at = slice(128 * h, 128 * h + 128)
        piece = grad_context[:, at]
        do_ref[me, h] = piece[:long]
        short_do_ref[h] = piece[long:]
        both = piece.astype(jnp.float32) * context[:, at].astype(jnp.float32)
        delta = lax.dot_general(
            picks, both, (((1,), (1,)), ((), ())), precision=lax.Precision.HIGHEST, preferred_element_type=jnp.float32
        )
        aux_ref[me, h, 0:2] = lse[h, :, :long]
        aux_ref[me, h, 2:4] = delta[0:2, :long]
        short_aux_ref[h, 0:2] = lse[h, :, long:]
        short_aux_ref[h, 2:4] = delta[0:2, long:]


def attend_back_pair(n_dp, me, width, r, do_spread, aux_spread, h):
    scale = HEAD_DIM ** (-0.5)
    mixed_ref = r.mixed
    long = r.kv.shape[3]

    def row_of(aux, first):
        return jnp.concatenate([aux[first : first + 1], aux[first + 1 : first + 2]], axis=1)

    def score_grads(keys, values, queries, grads, aux, seen):
        scores = dot_rows(keys, queries)
        probs = jnp.exp(scores - row_of(aux, 0))
        if seen is not None:
            probs = jnp.where(seen, probs, 0.0)
        grad_scores = probs * (dot_rows(values, grads) - row_of(aux, 2))
        return probs.astype(jnp.bfloat16), grad_scores.astype(jnp.bfloat16)

    def put(third, first, value):
        at = pl.ds(pl.multiple_of(third * width + 128 * h, 128), 128)
        mixed_ref[first : first + value.shape[0], at] = value.astype(jnp.bfloat16)

    seen = short_seen(r.doc_row[...], r.doc_col[...])
    queries, grads = head_pair(r.short_q[h]), head_pair(r.short_do[h])
    keys = r.short_kv[h, 0]
    probs, grad_scores = score_grads(keys, r.short_kv[h, 1], queries, grads, r.short_aux[h], seen)
    put(0, long, (pair_rows(dot_columns(keys, grad_scores)) * scale).T)
    put(1, long, dot(grad_scores, queries))
    put(2, long, dot(probs, grads))
    queries, grads = head_pair(r.q[me, h]), head_pair(r.do[me, h])
    own_keys, own_values = r.kv[me, h, 0], r.kv[me, h, 1]
    probs, grad_scores = score_grads(own_keys, own_values, queries, grads, r.aux[me, h], causal(long, long))
    r.dq[...] = dot_columns(own_keys, grad_scores)
    r.dk[...] = dot(grad_scores, queries)
    r.dv[...] = dot(probs, grads)
    for block in range(n_dp - 1):

        @pl.when(block < me)
        def _():
            keys = r.kv[block, h, 0]
            _, grad_scores = score_grads(keys, r.kv[block, h, 1], queries, grads, r.aux[me, h], None)
            r.dq[...] += dot_columns(keys, grad_scores)

    put(0, 0, (pair_rows(r.dq[...]) * scale).T)
    do_spread.relay(h)
    aux_spread.relay(h)

    def use(block):
        queries, grads = head_pair(r.q[block, h]), head_pair(r.do[block, h])
        probs, grad_scores = score_grads(own_keys, own_values, queries, grads, r.aux[block, h], None)
        r.dk[...] += dot(grad_scores, queries)
        r.dv[...] += dot(probs, grads)

    aux_spread.each(h, lambda block: None)
    do_spread.each(h, use)
    put(1, 0, r.dk[...])
    put(2, 0, r.dv[...])


def back_scratch(n_dp, pairs, long, short):
    return (
        [
            pltpu.VMEM((n_dp, pairs, long, 128), jnp.bfloat16),
            pltpu.VMEM((n_dp, pairs, 8, long), jnp.float32),
            pltpu.VMEM((pairs, short, 128), jnp.bfloat16),
            pltpu.VMEM((pairs, 8, short), jnp.float32),
            pltpu.VMEM((128, 2 * long), jnp.float32),
            pltpu.VMEM((long, 128), jnp.float32),
            pltpu.VMEM((long, 128), jnp.float32),
        ]
        + spread_sems(n_dp, pairs)
        + spread_sems(n_dp, pairs)
    )


def lane_plan(n_dp, n_ex, rows, order):
    dp_levels = [("dp", b) for b in range(n_dp.bit_length() - 1)]
    ex_levels = n_ex.bit_length() - 1
    halved, piece = [], rows
    for level in ((0, 1), (1, 0))[order]:
        if level < ex_levels and piece % 32 == 0:
            halved.append(level)
            piece //= 2
    halves = [("half", b) for b in halved]
    if order:
        kinds = dp_levels[:1] + halves[:1] + dp_levels[1:] + halves[1:]
    else:
        kinds = dp_levels + halves
    kinds += [("both", b) for b in range(ex_levels) if b not in halved]
    kinds += [("back", b) for b in reversed(halved)]
    return kinds, halved


class Lane:
    def __init__(self, n_dp, n_ex, rows, columns, order, refs):
        self.rows, self.columns = rows, columns
        self.kinds, self.halved = lane_plan(n_dp, n_ex, rows, order)
        self.count = len(self.kinds)
        moving = [k[0] != "back" for k in self.kinds]
        self.send = [next(refs) if m else None for m in moving]
        self.recv = [next(refs) if m else None for m in moving]
        self.keep = [next(refs) if m else None for m in moving]
        self.fin = next(refs)
        self.send_sems = [next(refs) for _ in moving]
        self.recv_sems = [next(refs) for _ in moving]
        self.d, self.e = lax.axis_index("dp"), lax.axis_index("expert")

    @staticmethod
    def scratch(n_dp, n_ex, rows, columns, order):
        kinds, halved = lane_plan(n_dp, n_ex, rows, order)
        width, pieces, height, shapes = columns[1] - columns[0], n_dp, rows, []
        for kind, _ in kinds:
            if kind == "dp":
                pieces //= 2
            elif kind == "half":
                height //= 2
            if kind != "back":
                shapes.append((pieces, height, width))
        scratch = [pltpu.VMEM((2,) + s, jnp.bfloat16) for s in shapes]
        scratch += [pltpu.VMEM((4,) + s, jnp.bfloat16) for s in shapes]
        scratch += [pltpu.VMEM((2,) + s, jnp.float32) for s in shapes]
        scratch += [pltpu.VMEM((len(halved) + 3, rows, width), jnp.bfloat16)]
        return scratch + [pltpu.SemaphoreType.DMA((4,)) for _ in kinds] * 2

    def peer(self, kind, level):
        return (flip(self.d, level), self.e) if kind == "dp" else (self.d, flip(self.e, level))

    def kept_rows(self, depth):
        start = 0
        for i, level in enumerate(self.halved[:depth]):
            start = start + bit_of(self.e, level) * (self.rows >> (i + 1))
        return start

    def copy_of(self, s, c):
        kind, level = self.kinds[s]
        slot, place = lax.rem(c, 2), lax.rem(c, 4)
        if kind == "back":
            depth = self.halved.index(level) + 1
            span = self.rows >> depth
            at = pl.ds(pl.multiple_of(self.kept_rows(depth), span), span)
            src = self.fin.at[lax.rem(c, len(self.halved) + 3), at]
            dst = src
        else:
            src, dst = self.send[s].at[slot], self.recv[s].at[place]
        return pltpu.make_async_remote_copy(
            src_ref=src,
            dst_ref=dst,
            send_sem=self.send_sems[s].at[place],
            recv_sem=self.recv_sems[s].at[place],
            device_id=self.peer(kind, level),
            device_id_type=MESH,
        )

    def arrive(self, s, c):
        self.copy_of(s, c).wait()
        slot, place = lax.rem(c, 2), lax.rem(c, 4)
        if self.kinds[s][0] == "back":
            return None
        return [
            self.keep[s][slot, i] + self.recv[s][place, i].astype(jnp.float32) for i in range(self.keep[s].shape[1])
        ]

    def leave(self, s, c, values):
        kind, level = self.kinds[s]
        slot = lax.rem(c, 2)
        kept = None
        if kind == "dp":
            sent, kept = values[1::2], values[0::2]
        elif kind == "half":
            half = values[0].shape[0] // 2
            own = bit_of(self.e, level)
            sent = [jnp.where(own == 0, v[half:], v[:half]) for v in values]
            kept = [jnp.where(own == 0, v[:half], v[half:]) for v in values]
        elif kind == "both":
            sent = values
            kept = [v.astype(jnp.bfloat16).astype(jnp.float32) for v in values]
        elif values is not None:
            span = values[0].shape[0]
            at = pl.ds(pl.multiple_of(self.kept_rows(len(self.halved)), span), span)
            self.fin[lax.rem(c, len(self.halved) + 3), at] = values[0].astype(jnp.bfloat16)
        if kept is not None:
            for i, v in enumerate(sent):
                self.send[s][slot, i] = v.astype(jnp.bfloat16)
        self.copy_of(s, c).start()
        if kept is not None:
            for i, v in enumerate(kept):
                self.keep[s][slot, i] = v

    def final(self, c):
        values = self.arrive(self.count - 1, c)
        if values is None:
            return self.fin[lax.rem(c, len(self.halved) + 3)]
        return values[0].astype(jnp.bfloat16)


class Reduction:
    def __init__(self, n_dp, n_ex, rows, groups, lanes, refs):
        self.n_dp, self.rows, self.groups = n_dp, rows, groups
        refs = iter(refs)
        self.lanes = [Lane(n_dp, n_ex, rows, columns, order, refs) for columns, order in lanes]
        self.stage_ref, self.stage_sem, self.out = next(refs), next(refs), next(refs)
        self.count = self.lanes[0].count
        self.chunks = sum(g[0] for g in groups)
        self.firsts = [sum(g[0] for g in groups[:i]) for i in range(len(groups))]
        self.ticks = self.chunks + self.count
        self.d = lax.axis_index("dp")
        self.peer = self.lanes[0].peer

    @staticmethod
    def scratch(n_dp, n_ex, rows, width, lanes):
        scratch = []
        for columns, order in lanes:
            scratch += Lane.scratch(n_dp, n_ex, rows, columns, order)
        return scratch + [pltpu.VMEM((2, rows, width), jnp.bfloat16), pltpu.SemaphoreType.DMA((2,))]

    def out_copy(self, c):
        slot = lax.rem(c, 2)
        return pltpu.make_async_copy(self.stage_ref.at[slot], self.out.at[c], self.stage_sem.at[slot])

    def first(self, g, c):
        _, piece, factor = self.groups[g]
        j = c - self.firsts[g]
        dy = factor(j)
        slot = lax.rem(c, 2)
        levels = self.n_dp.bit_length() - 1
        half = self.n_dp // 2

        def products(odd):
            parts = [piece(j, partner_index(self.d, 2 * i + odd, levels)) for i in range(half)]
            return dot(jnp.concatenate(parts, axis=0), dy)

        value = products(1)
        for lane in self.lanes:
            for i in range(half):
                part = value[i * self.rows : (i + 1) * self.rows, slice(*lane.columns)]
                lane.send[0][slot, i] = part.astype(jnp.bfloat16)
            lane.copy_of(0, c).start()
        value = products(0)
        for lane in self.lanes:
            for i in range(half):
                lane.keep[0][slot, i] = value[i * self.rows : (i + 1) * self.rows, slice(*lane.columns)]

    def last(self, c):
        slot = lax.rem(c, 2)

        @pl.when(c >= 2)
        def _():
            self.out_copy(c - 2).wait()

        for lane in self.lanes:
            self.stage_ref[slot, :, slice(*lane.columns)] = lane.final(c)
        self.out_copy(c).start()

    def tick(self, t, low, high):
        for s in range(self.count + 1):
            if high - s <= 0 or low - s >= self.chunks:
                continue
            c = t - s
            if s > 0:

                @pl.when((c >= 0) & (c < self.chunks))
                def _(s=s, c=c):
                    if s < self.count:
                        for lane in self.lanes:
                            lane.leave(s, c, lane.arrive(s - 1, c))
                    else:
                        self.last(c)

                continue
            for g, (size, _, _) in enumerate(self.groups):
                begin, end = self.firsts[g], self.firsts[g] + size
                if high <= begin or low >= end:
                    continue

                @pl.when((c >= begin) & (c < end))
                def _(g=g):
                    self.first(g, c)

    def finish(self):
        for c in range(max(0, self.chunks - 2), self.chunks):
            self.out_copy(c).wait()


def dense_lanes(width):
    cut = width // 768 * 640
    return [((0, cut), 0), ((cut, width), 1)]


def middle_kernel(n_dp, n_ex, names, staged, *refs):
    r = types.SimpleNamespace(**dict(zip(names, refs)))
    extra = iter(refs[len(names) :])
    loads = types.SimpleNamespace()
    for name in staged:
        buffer, sem = next(extra), next(extra)
        setattr(loads, name, pltpu.make_async_copy(getattr(r, name), buffer, sem))
        setattr(r, name, buffer)
    w_in_ref, w_out_ref, weight_sem = (next(extra) for _ in range(3))
    rows_ref, send_ref, grad_ref, home_ref, result_ref, result_home_ref = (next(extra) for _ in range(6))
    rows_t_ref, back_ref, active_t_ref, hidden_ref, dispatch_ref, gate_ref = (next(extra) for _ in range(6))
    dgate_ref, home_dgate_ref, stat_send, stat_recv, result_acc, grad_acc = (next(extra) for _ in range(6))
    (
        x_send_sem, x_recv_sem, grad_send_sem, grad_recv_sem, dgate_send_sem, dgate_recv_sem,
        result_send_sem, result_recv_sem, stat_send_sem, stat_recv_sem,
    ) = (next(extra) for _ in range(10))
    do_ref, aux_ref, short_do_ref, short_aux_ref, dq_ref, dk_ref, dv_ref = (next(extra) for _ in range(7))
    do_far, do_near, do_recv, aux_far, aux_near, aux_recv = (next(extra) for _ in range(6))
    links = Links(n_dp)
    d, e, me = links.me, links.expert, links.me
    dp_levels, ex_levels = n_dp.bit_length() - 1, n_ex.bit_length() - 1
    tokens, width = r.stream.shape
    padded = send_ref.shape[1]
    blocks = r.expert_in.shape[1] // width
    pairs, long = r.kv.shape[1], r.kv.shape[3]
    group = min(max(4, 128 // padded), n_ex)
    groups = n_ex // group
    exact = dict(precision=lax.Precision.HIGHEST, preferred_element_type=jnp.float32)
    hops = [(flip(d, b), e) for b in range(dp_levels)] + [(d, flip(e, b)) for b in range(ex_levels)]

    def column(i):
        return pl.ds(i * width, width)

    expert_loads = [
        (
            pltpu.make_async_copy(r.expert_in.at[:, column(i)], w_in_ref.at[i], weight_sem.at[0, i]),
            pltpu.make_async_copy(r.expert_out.at[column(i), :], w_out_ref.at[i], weight_sem.at[1, i]),
        )
        for i in range(blocks)
    ]
    for both in expert_loads:
        for load in both:
            load.start()
    for name in staged:
        getattr(loads, name).start()
    greet(links.peers() + across_peers(n_ex))

    unit, inverse = norm_parts(r.stream[...])
    routed = (unit * r.gain[...] + r.shift[...]).astype(jnp.bfloat16)
    assign = r.assign[...]
    dispatch = dispatch_of(assign, n_ex)
    dispatch_ref[...] = dispatch
    send_ref[...] = dot(dispatch, routed).astype(jnp.bfloat16).reshape(send_ref.shape)
    x_across = Across(n_ex, send_ref, rows_ref, x_send_sem, x_recv_sem)

    def place(k, i):
        return lax.rem(e // group + k, groups) * group + lax.rem(e + i, group)

    def source(k, i):
        return lax.rem(e // group + k, groups) * group + lax.rem(e + group - i, group)

    for i in range(group):
        if i:
            x_across.start(place(0, i))
        for k in range(1, groups):
            x_across.start(place(k, i))
    rows_ref[e] = send_ref[e]
    router = r.router[...]
    hot = chosen_rows(assign, n_ex)
    gate = jax.nn.sigmoid(jnp.sum(hot * dot_rows(router, routed), axis=0, keepdims=True))
    gate_ref[...] = gate

    def stat_copy(i):
        return pltpu.make_async_remote_copy(
            src_ref=stat_send.at[i],
            dst_ref=stat_recv.at[i],
            send_sem=stat_send_sem.at[i],
            recv_sem=stat_recv_sem.at[i],
            device_id=hops[i],
            device_id_type=MESH,
        )

    lane = lax.broadcasted_iota(jnp.int32, r.stats.shape, 1)
    stat_send[0] = jnp.where(
        lane == 0, jnp.sum(hot, axis=1, keepdims=True), jnp.sum(hot * gate, axis=1, keepdims=True)
    )
    stat_copy(0).start()

    def stat_step(i):
        stat_copy(i).wait()
        value = stat_send[i] + stat_recv[i]
        if i + 1 < len(hops):
            stat_send[i + 1] = value
            stat_copy(i + 1).start()
        else:
            r.stats[...] = value

    grad_across = Across(n_ex, grad_ref, home_ref, grad_send_sem, grad_recv_sem)
    dgate_across = Across(n_ex, dgate_ref, home_dgate_ref, dgate_send_sem, dgate_recv_sem)
    steps = [[(0, i) for i in range(group)]]
    cut = group // 2 if (group // 2) * padded % 128 == 0 else group
    for k in range(1, groups):
        steps += [[(k, i) for i in range(first, first + cut)] for first in range(0, group, cut)]
    done, at = 0, 0
    for number, members in enumerate(steps):
        count = len(members) * padded
        sources = [source(k, i) for k, i in members]
        for (k, i), j in zip(members, sources):
            if (k, i) != (0, 0):
                x_across.wait_from(j)
        rows = jnp.concatenate([rows_ref[j] for j in sources], axis=0)
        cot = jnp.concatenate([r.far_cot[j] for j in sources], axis=0).astype(jnp.float32)
        logits = dot_rows(rows, router)
        own = lax.broadcasted_iota(jnp.int32, logits.shape, 1) == e
        slot_gate = jax.nn.sigmoid(jnp.sum(jnp.where(own, logits, 0.0), axis=1, keepdims=True))
        back = (slot_gate * cot).astype(jnp.bfloat16)
        span = slice(at, at + count)
        back_ref[span] = back
        rows_t_ref[:, span] = rows.T
        result_acc[:count] = jnp.zeros((count, width), jnp.float32)
        grad_acc[:count] = jnp.zeros((count, width), jnp.float32)

        def block(i, _, rows=rows, back=back, span=span, count=count):
            cols = pl.ds(pl.multiple_of(i * width, width), width)
            active, slope = gelu_parts(dot(rows, w_in_ref[i]))
            active = active.astype(jnp.bfloat16)
            hidden = (slope * dot_rows(back, w_out_ref[i])).astype(jnp.bfloat16)
            active_t_ref[cols, span] = active.T
            hidden_ref[span, cols] = hidden
            result_acc[:count] += dot(active, w_out_ref[i])
            grad_acc[:count] += dot_rows(hidden, w_in_ref[i])
            return 0

        if number == 0:
            for both in expert_loads:
                for load in both:
                    load.wait()
        lax.fori_loop(0, blocks, block, 0)
        grad = grad_acc[:count].astype(jnp.bfloat16)
        result = result_acc[:count].astype(jnp.bfloat16)
        dgate = lax.dot_general(
            jnp.ones((8, width), jnp.float32), cot * result.astype(jnp.float32), (((1,), (1,)), ((), ())), **exact
        )
        for m, (k, i) in enumerate(members):
            j, part = sources[m], slice(m * padded, (m + 1) * padded)
            grad_ref[j] = grad[part]
            result_ref[j] = result[part]
            dgate_ref[j, :, :padded] = dgate[:, part]
            if (k, i) == (0, 0):
                home_ref[e] = grad_ref[e]
                home_dgate_ref[e] = dgate_ref[e]
            else:
                grad_across.start(j)
                dgate_across.start(j)
        at += count
        if done < len(hops):
            stat_step(done)
            done += 1

    thirds = [w_in_ref.at[i] for i in range(3)]
    in_loads = [
        pltpu.make_async_copy(r.attn_in.at[1, :, column(i)], third, weight_sem.at[0, i])
        for i, third in enumerate(thirds)
    ]
    out_load = pltpu.make_async_copy(r.attn_out.at[1], w_out_ref.at[0], weight_sem.at[1, 0])
    for load in in_loads + [out_load]:
        load.start()
    rows = width // n_dp

    def rows_of(ref, j, q):
        return ref[pl.ds(pl.multiple_of((q * (ref.shape[0] // width) + j) * rows, rows), rows), :]

    factors = [
        (blocks, lambda j, q: rows_of(rows_t_ref, 0, q), lambda j: hidden_ref[:, pl.ds(pl.multiple_of(j * width, width), width)]),
        (blocks, lambda j, q: rows_of(active_t_ref, j, q), lambda j: back_ref[...]),
    ]
    red = Reduction(n_dp, 1, rows, factors, [((0, width), 0)], list(extra) + [r.chunks])
    red.tick(0, 0, 1)
    early = 1
    while done < len(hops):
        stat_step(done)
        done += 1
    x_across.others(x_across.wait_to)
    red.tick(1, 1, 2)
    early += 1
    dgate_across.wait_all()
    dgate = jnp.zeros((8, tokens), jnp.float32)
    for j in range(n_ex):
        part = dispatch_ref[j * padded : (j + 1) * padded].astype(jnp.float32)
        dgate = dgate + jnp.dot(home_dgate_ref[j, :, :padded], part, **exact)
    everyone = tokens * n_dp * n_ex
    share = jnp.sum(jnp.where(lane == 0, r.stats[...], 0.0), axis=1, keepdims=True) / everyone
    weight = balance_weight * n_ex * (share - 1.0 / n_ex) / everyone
    gate = gate_ref[...]
    grad_gate = dgate[0:1] + jnp.sum(hot * weight, axis=0, keepdims=True)
    grad_logits = hot * (grad_gate * gate * (1.0 - gate))
    r.router_grad[...] = jnp.dot(grad_logits, routed.astype(jnp.float32), **exact)
    grad_normed = lax.dot_general(grad_logits, router.astype(jnp.float32), (((0,), (0,)), ((), ())), **exact)
    red.tick(2, 2, 3)
    early += 1
    grad_across.wait_all()
    grad_normed = grad_normed + dot_columns(dispatch_ref[...], home_ref[...].reshape(n_ex * padded, width))
    unit, inverse = norm_parts(r.stream[...])
    up = r.cot[...].astype(jnp.float32) + norm_back(unit, inverse, r.gain[...], grad_normed)
    r.sums[0:1] = jnp.sum(grad_normed * unit, axis=0, keepdims=True)
    r.sums[1:2] = jnp.sum(grad_normed, axis=0, keepdims=True)

    r.up_next[...] = up
    up_low = up.astype(jnp.bfloat16)
    r.up_low[...] = up_low
    out_load.wait()
    for name in staged:
        getattr(loads, name).wait()
    grad_context = dot_rows(up_low, w_out_ref[0]).astype(jnp.bfloat16)
    share_context(r.context, r.lse, grad_context, do_ref, aux_ref, short_do_ref, short_aux_ref, me, long)
    do_spread = Spread(links, lambda b, p: do_ref.at[b, p], pairs, False, do_far, do_near, do_recv)
    aux_spread = Spread(links, lambda b, p: aux_ref.at[b, p], pairs, False, aux_far, aux_near, aux_recv)
    for h in range(pairs):
        do_spread.send(h)
        aux_spread.send(h)
    result_across = Across(n_ex, result_ref, result_home_ref, result_send_sem, result_recv_sem)
    result_across.start_all()
    result_home_ref[e] = result_ref[e]
    sequence = types.SimpleNamespace(
        doc_row=r.doc_row, doc_col=r.doc_col, kv=r.kv, q=r.q, short_kv=r.short_kv, short_q=r.short_q,
        do=do_ref, aux=aux_ref, short_do=short_do_ref, short_aux=short_aux_ref, dq=dq_ref, dk=dk_ref, dv=dv_ref,
        mixed=r.mixed,
    )

    def pair(h, _):
        attend_back_pair(n_dp, me, width, sequence, do_spread, aux_spread, h)
        red.tick(early + h, early, early + pairs)
        return 0

    lax.fori_loop(0, pairs, pair, 0)
    grad_normed = jnp.zeros((tokens, width), jnp.float32)
    for i, third in enumerate(thirds):
        in_loads[i].wait()
        grad_normed = grad_normed + dot_rows(r.mixed[:, i * width : (i + 1) * width], third[...])
    unit, inverse = norm_parts(r.attn_x[...])
    r.up_next[...] += norm_back(unit, inverse, r.attn_gain[...], grad_normed)
    r.attn_sums[0:1] = jnp.sum(grad_normed * unit, axis=0, keepdims=True)
    r.attn_sums[1:2] = jnp.sum(grad_normed, axis=0, keepdims=True)

    def rest(t, _):
        red.tick(t, early + pairs, red.ticks)
        return 0

    lax.fori_loop(early + pairs, red.ticks, rest, 0)
    result_across.wait_all()
    result = dot_columns(dispatch_ref[...], result_home_ref[...].reshape(n_ex * padded, width))
    gate = jnp.broadcast_to(gate_ref[...], (128, tokens)).T[:, 0:1]
    r.output[...] = (r.stream[...] + gate * result).astype(jnp.bfloat16)
    red.finish()
    for h in range(pairs):
        do_spread.sent(h)
        aux_spread.sent(h)


def middle(n_dp, n_ex, collective_id, near, staged, far):
    arrays = {**near, **staged, **far}
    a = types.SimpleNamespace(**arrays)
    low, wide = jnp.bfloat16, jnp.float32
    tokens, width = a.stream.shape
    hidden = a.expert_in.shape[1]
    mixed = a.attn_in.shape[2]
    blocks, rows = hidden // width, width // n_dp
    long, short, pairs = LONG_DEV, tokens - LONG_DEV, width // 128
    _, padded = capacity_of(tokens, n_ex)
    slots = n_ex * padded
    group = min(max(4, 128 // padded), n_ex) * padded
    slab = (n_ex, padded, width)
    hops = (n_dp * n_ex).bit_length() - 1
    outs = dict(
        up_next=jax.ShapeDtypeStruct((tokens, width), wide),
        up_low=jax.ShapeDtypeStruct((tokens, width), low),
        mixed=jax.ShapeDtypeStruct((tokens, mixed), low),
        sums=jax.ShapeDtypeStruct((2, width), wide),
        attn_sums=jax.ShapeDtypeStruct((2, width), wide),
        router_grad=jax.ShapeDtypeStruct((n_ex, width), wide),
        stats=jax.ShapeDtypeStruct((n_ex, 128), wide),
        output=jax.ShapeDtypeStruct((tokens, width), low),
        chunks=jax.ShapeDtypeStruct((2 * blocks, rows, width), low),
    )
    scratch = []
    for name in staged:
        scratch += [pltpu.VMEM(arrays[name].shape, arrays[name].dtype), pltpu.SemaphoreType.DMA]
    scratch += [pltpu.VMEM((blocks, width, width), low)] * 2 + [pltpu.SemaphoreType.DMA((2, blocks))]
    scratch += [pltpu.VMEM(slab, low)] * 6
    scratch += [
        pltpu.VMEM((width, slots), low),
        pltpu.VMEM((slots, width), low),
        pltpu.VMEM((hidden, slots), low),
        pltpu.VMEM((slots, hidden), low),
        pltpu.VMEM((slots, tokens), low),
        pltpu.VMEM((1, tokens), wide),
        pltpu.VMEM((n_ex, 8, 128), wide),
        pltpu.VMEM((n_ex, 8, 128), wide),
        pltpu.VMEM((hops, n_ex, 128), wide),
        pltpu.VMEM((hops, n_ex, 128), wide),
        pltpu.VMEM((group, width), wide),
        pltpu.VMEM((group, width), wide),
    ]
    scratch += [pltpu.SemaphoreType.DMA((n_ex,))] * 8 + [pltpu.SemaphoreType.DMA((hops,))] * 2
    scratch += back_scratch(n_dp, pairs, long, short)
    scratch += Reduction.scratch(n_dp, 1, rows, width, [((0, width), 0)])
    vmem, anywhere = pl.BlockSpec(memory_space=pltpu.VMEM), pl.BlockSpec(memory_space=pl.ANY)
    names = tuple(arrays) + tuple(outs)
    values = pl.pallas_call(
        functools.partial(middle_kernel, n_dp, n_ex, names, tuple(staged)),
        out_shape=list(outs.values()),
        in_specs=[vmem] * len(near) + [anywhere] * (len(staged) + len(far)),
        out_specs=[vmem] * (len(outs) - 1) + [anywhere],
        scratch_shapes=scratch,
        compiler_params=pltpu.CompilerParams(
            collective_id=collective_id, has_side_effects=True, vmem_limit_bytes=61 * 1024 * 1024
        ),
        name="middle",
    )(*arrays.values())
    return types.SimpleNamespace(**dict(zip(outs, values)))


def tail_kernel(n_dp, n_ex, names, staged, *refs):
    r = types.SimpleNamespace(**dict(zip(names, refs)))
    extra = iter(refs[len(names) :])
    loads = types.SimpleNamespace()
    for name in staged:
        buffer, sem = next(extra), next(extra)
        setattr(loads, name, pltpu.make_async_copy(getattr(r, name), buffer, sem))
        setattr(r, name, buffer)
    weights_in, weights_out, slopes, weight_sem = (next(extra) for _ in range(4))
    first_sem = next(extra)
    up_ref, acc_ref, dense_low_ref, dense_hidden_ref, first_low_ref, mixed_ref = (next(extra) for _ in range(6))
    do_ref, aux_ref, short_do_ref, short_aux_ref, dq_ref, dk_ref, dv_ref = (next(extra) for _ in range(7))
    do_far, do_near, do_recv, aux_far, aux_near, aux_recv = (next(extra) for _ in range(6))
    small_send, small_recv, small_send_sem, small_recv_sem = (next(extra) for _ in range(4))
    links = Links(n_dp)
    me = links.me
    width = up_ref.shape[1]
    rows = width // n_dp
    pairs, long = r.kv.shape[1], r.kv.shape[3]
    blocks = r.dense_in.shape[1] // width
    per_in = mixed_ref.shape[1] // width

    def block_loads(i):
        slot = lax.rem(i, 2)
        at = pl.ds(pl.multiple_of(i * width, width), width)
        return [
            pltpu.make_async_copy(r.dense_out.at[at, :], weights_out.at[slot], weight_sem.at[slot, 0]),
            pltpu.make_async_copy(r.dense_in.at[:, at], weights_in.at[slot], weight_sem.at[slot, 1]),
            pltpu.make_async_copy(r.slope.at[:, at], slopes.at[slot], weight_sem.at[slot, 2]),
        ]

    for i in range(min(2, blocks)):
        for load in block_loads(i):
            load.start()
    for name in staged:
        getattr(loads, name).start()
    free, busy = blocks % 2, (blocks - 1) % 2
    out_load = pltpu.make_async_copy(r.attn_out.at[0], weights_out.at[free], first_sem.at[0])
    thirds = [weights_in.at[free], weights_in.at[busy], weights_out.at[busy]]
    in_loads = [
        pltpu.make_async_copy(r.attn_in.at[0, :, pl.ds(i * width, width)], third, first_sem.at[1 + i])
        for i, third in enumerate(thirds)
    ]

    def columns(ref):
        return lambda j: ref[:, pl.ds(pl.multiple_of(j * width, width), width)]

    def one(ref):
        return lambda j, q: ref[q, 0]

    groups = [
        (1, one(r.second_context_t), columns(r.second_low)),
        (per_in, one(r.second_normed_t), columns(r.second_mixed)),
        (blocks, lambda j, q: r.active_t[q, j], lambda j: dense_low_ref[...]),
        (blocks, one(r.dense_normed_t), columns(dense_hidden_ref)),
        (1, one(r.first_context_t), columns(first_low_ref)),
        (per_in, one(r.first_normed_t), columns(mixed_ref)),
    ]
    red_refs = list(extra) + [r.chunks]
    red = Reduction(n_dp, n_ex, rows, groups, dense_lanes(width), red_refs)
    levels = [("dp", b) for b in range(n_dp.bit_length() - 1)] + [("ex", b) for b in range(n_ex.bit_length() - 1)]
    greet([red.peer(*level) for level in levels] + (links.peers()[1:] if links.chips > 2 else []))

    up = r.up[...]
    dense_low_ref[...] = up.astype(jnp.bfloat16)
    acc_ref[...] = jnp.zeros_like(acc_ref)
    ready = (loads.second_context_t, loads.second_low, loads.second_normed_t, loads.second_mixed)
    for load in ready:
        load.wait()

    def dense(i, _):
        slot = lax.rem(i, 2)
        for load in block_loads(i):
            load.wait()
        grad = dot_rows(dense_low_ref[...], weights_out[slot]) * slopes[slot].astype(jnp.float32)
        grad = grad.astype(jnp.bfloat16)
        dense_hidden_ref[:, pl.ds(pl.multiple_of(i * width, width), width)] = grad
        acc_ref[...] += dot_rows(grad, weights_in[slot])

        @pl.when(i + 2 < blocks)
        def _():
            for load in block_loads(i + 2):
                load.start()

        @pl.when(i == blocks - 2)
        def _():
            out_load.start()
            in_loads[0].start()

        @pl.when(lax.rem(i, 2) == 1)
        def _():
            red.tick(i // 2, 0, 2)

        return 0

    lax.fori_loop(0, blocks, dense, 0)
    for load in in_loads[1:]:
        load.start()
    for name in staged:
        if all(getattr(loads, name) is not load for load in ready):
            getattr(loads, name).wait()
    unit, inverse = norm_parts(r.dense_x[...])
    grad_normed = acc_ref[...]
    up = up + norm_back(unit, inverse, r.dense_gain[...], grad_normed)
    up_ref[...] = up
    small_send[0] = r.small[...]
    small_send[0, 1:2] = jnp.sum(grad_normed * unit, axis=0, keepdims=True)
    small_send[0, 5:6] = jnp.sum(grad_normed, axis=0, keepdims=True)
    at_tick = blocks // 2

    scale = HEAD_DIM ** (-0.5)
    up_low = up.astype(jnp.bfloat16)
    first_low_ref[...] = up_low
    out_load.wait()
    grad_context = dot_rows(up_low, weights_out[free]).astype(jnp.bfloat16)
    share_context(r.context, r.lse, grad_context, do_ref, aux_ref, short_do_ref, short_aux_ref, me, long)
    do_spread = Spread(links, lambda b, p: do_ref.at[b, p], pairs, False, do_far, do_near, do_recv)
    aux_spread = Spread(links, lambda b, p: aux_ref.at[b, p], pairs, False, aux_far, aux_near, aux_recv)
    for h in range(pairs):
        do_spread.send(h)
        aux_spread.send(h)
    red.tick(at_tick, at_tick, at_tick + 1)
    at_tick += 1
    sequence = types.SimpleNamespace(
        doc_row=r.doc_row, doc_col=r.doc_col, kv=r.kv, q=r.q, short_kv=r.short_kv, short_q=r.short_q,
        do=do_ref, aux=aux_ref, short_do=short_do_ref, short_aux=short_aux_ref, dq=dq_ref, dk=dk_ref, dv=dv_ref,
        mixed=mixed_ref,
    )

    def pair(h, _):
        attend_back_pair(n_dp, me, width, sequence, do_spread, aux_spread, h)
        red.tick(at_tick + h, at_tick, at_tick + pairs)
        return 0

    lax.fori_loop(0, pairs, pair, 0)
    at_tick += pairs
    grad_normed = jnp.zeros((up_ref.shape[0], width), jnp.float32)
    for i, third in enumerate(thirds):
        in_loads[i].wait()
        grad_normed = grad_normed + dot_rows(mixed_ref[:, i * width : (i + 1) * width], third[...])
    unit, inverse = norm_parts(r.first_x[...].astype(jnp.float32))
    r.grad_tokens[...] = (
        up_ref[...] + norm_back(unit, inverse, r.first_gain[...], grad_normed)
    ).astype(jnp.bfloat16)
    small_send[0, 0:1] = jnp.sum(grad_normed * unit, axis=0, keepdims=True)
    small_send[0, 4:5] = jnp.sum(grad_normed, axis=0, keepdims=True)

    def small_copy(i):
        return pltpu.make_async_remote_copy(
            src_ref=small_send.at[i],
            dst_ref=small_recv.at[i],
            send_sem=small_send_sem.at[i],
            recv_sem=small_recv_sem.at[i],
            device_id=red.peer(*levels[i]),
            device_id_type=MESH,
        )

    small_copy(0).start()

    def rest(t, _):
        red.tick(t, at_tick, red.ticks)
        for i in range(1, len(levels) + 1):

            @pl.when(t == at_tick + i)
            def _(i=i):
                small_copy(i - 1).wait()
                value = small_send[i - 1] + small_recv[i - 1]
                if i < len(levels):
                    small_send[i] = value
                    small_copy(i).start()
                else:
                    r.small_sum[...] = value

        return 0

    lax.fori_loop(at_tick, red.ticks, rest, 0)
    red.finish()
    for h in range(pairs):
        do_spread.sent(h)
        aux_spread.sent(h)


def tail(n_dp, n_ex, collective_id, near, staged, far):
    arrays = {**near, **staged, **far}
    a = types.SimpleNamespace(**arrays)
    low, wide = jnp.bfloat16, jnp.float32
    tokens, width = a.up.shape
    hidden = a.dense_in.shape[1]
    mixed = a.attn_in.shape[2]
    rows = width // n_dp
    long, short, pairs = LONG_DEV, tokens - LONG_DEV, width // 128
    chunks = 2 * (hidden // width) + 2 * (1 + mixed // width)
    small = a.small.shape
    outs = dict(
        grad_tokens=jax.ShapeDtypeStruct((tokens, width), low),
        small_sum=jax.ShapeDtypeStruct(small, wide),
        chunks=jax.ShapeDtypeStruct((chunks, rows, width), low),
    )
    scratch = []
    for name in staged:
        scratch += [pltpu.VMEM(arrays[name].shape, arrays[name].dtype), pltpu.SemaphoreType.DMA]
    scratch += [pltpu.VMEM((2, width, width), low)] * 2
    scratch += [pltpu.VMEM((2, tokens, width), low), pltpu.SemaphoreType.DMA((2, 3))]
    scratch += [pltpu.SemaphoreType.DMA((4,))]
    scratch += [pltpu.VMEM((tokens, width), wide)] * 2
    scratch += [pltpu.VMEM((tokens, n), low) for n in (width, hidden, width, mixed)]
    scratch += back_scratch(n_dp, pairs, long, short)
    hops = (n_dp * n_ex).bit_length() - 1
    scratch += [pltpu.VMEM((hops,) + small, wide)] * 2 + [pltpu.SemaphoreType.DMA((hops,))] * 2
    scratch += Reduction.scratch(n_dp, n_ex, rows, width, dense_lanes(width))
    vmem, anywhere = pl.BlockSpec(memory_space=pltpu.VMEM), pl.BlockSpec(memory_space=pl.ANY)
    names = tuple(arrays) + tuple(outs)
    return pl.pallas_call(
        functools.partial(tail_kernel, n_dp, n_ex, names, tuple(staged)),
        out_shape=list(outs.values()),
        in_specs=[vmem] * len(near) + [anywhere] * (len(staged) + len(far)),
        out_specs=[vmem] * (len(outs) - 1) + [anywhere],
        scratch_shapes=scratch,
        compiler_params=pltpu.CompilerParams(
            collective_id=collective_id, has_side_effects=True, vmem_limit_bytes=61 * 1024 * 1024
        ),
        name="tail",
    )(*arrays.values())


def shards(
    tokens,
    doc_lengths,
    assign,
    ln_gain,
    ln_bias,
    attn_in,
    attn_out,
    ffn_in,
    ffn_out,
    router,
    expert_in,
    expert_out,
    cotangent,
):
    n_dp, n_ex = lax.axis_size("dp"), lax.axis_size("expert")
    stream_first = tokens[0].astype(jnp.float32)
    row_count = stream_first.shape[0]
    doc_ends = jnp.cumsum(doc_lengths[0, 0])
    short_place = jnp.arange(row_count - LONG_DEV, dtype=jnp.int32)
    short_ids = jnp.sum((short_place[:, None] >= doc_ends[None, :]).astype(jnp.int32), axis=-1)
    doc_row, doc_col = short_ids[None, :], short_ids[:, None]
    weights_in, weights_out = lax.optimization_barrier((attn_in.transpose(1, 0, 2), attn_out.transpose(1, 0, 2)))
    gains, shifts = ln_gain.T, ln_bias.T
    assign_row = assign[0].T
    stream_one, *kept_one = attention_forward(
        n_dp, n_ex, 2, stream_first, gains[0:1], shifts[0:1], weights_in[0], weights_out[0], doc_row, doc_col
    )
    stream_two, dense_normed_t, active_t, slope = ffn_forward(stream_one, gains[1:2], shifts[1:2], ffn_in, ffn_out)
    stream_three, *kept_three, far_cot = attention_forward(
        n_dp, n_ex, 3, stream_two, gains[2:3], shifts[2:3], weights_in[1], weights_out[1], doc_row, doc_col,
        (assign_row, cotangent[0]),
    )
    model_width = tokens.shape[2]
    rows = model_width // n_dp
    mid = middle(
        n_dp,
        n_ex,
        4,
        dict(
            stream=stream_three,
            gain=gains[3:4],
            shift=shifts[3:4],
            router=router.T,
            assign=assign_row,
            cot=cotangent[0],
            far_cot=far_cot,
            attn_gain=gains[2:3],
            doc_row=doc_row,
            doc_col=doc_col,
            lse=kept_three[7],
        ),
        dict(
            attn_x=stream_two,
            context=kept_three[1],
            kv=kept_three[3],
            q=kept_three[4],
            short_kv=kept_three[5],
            short_q=kept_three[6],
        ),
        dict(
            expert_in=expert_in[0],
            expert_out=expert_out[0],
            attn_in=weights_in,
            attn_out=weights_out,
        ),
    )
    everyone = row_count * n_dp * n_ex
    stats = mid.stats
    balance = n_ex * jnp.sum((stats[:, 0] / everyone - 1.0 / n_ex) * (stats[:, 1] / everyone))
    output = mid.output[None]
    second_sums, fourth_sums = mid.attn_sums, mid.sums

    def blocks_of(rows_t):
        return rows_t.reshape(n_dp, -1, rows, row_count)

    none = jnp.zeros((2, model_width), jnp.float32)
    small = jnp.concatenate(
        [none, second_sums[0:1], fourth_sums[0:1], none, second_sums[1:2], fourth_sums[1:2], mid.router_grad], axis=0
    )
    grad_tokens, small, chunks = tail(
        n_dp,
        n_ex,
        5,
        dict(
            up=mid.up_next,
            dense_gain=gains[1:2],
            first_gain=gains[0:1],
            doc_row=doc_row,
            doc_col=doc_col,
            lse=kept_one[7],
            small=small,
        ),
        dict(
            dense_x=stream_one,
            first_x=tokens[0],
            context=kept_one[1],
            kv=kept_one[3],
            q=kept_one[4],
            short_kv=kept_one[5],
            short_q=kept_one[6],
            second_context_t=blocks_of(kept_three[2]),
            second_normed_t=blocks_of(kept_three[0]),
            active_t=blocks_of(active_t),
            dense_normed_t=blocks_of(dense_normed_t),
            first_context_t=blocks_of(kept_one[2]),
            first_normed_t=blocks_of(kept_one[0]),
            second_low=mid.up_low,
            second_mixed=mid.mixed,
        ),
        dict(
            dense_in=ffn_in,
            dense_out=ffn_out,
            slope=slope,
            attn_in=weights_in,
            attn_out=weights_out,
        ),
    )
    grad_tokens = grad_tokens[None]
    attn_in_sum, attn_out_sum, ffn_in_sum, ffn_out_sum, expert_in_sum, expert_out_sum = unpack(
        chunks, mid.chunks, attn_in.shape[2] // model_width, ffn_in.shape[1] // model_width
    )
    small = lax.dynamic_slice_in_dim(small, lax.axis_index("dp") * rows, rows, 1).T
    summed = [
        attn_in_sum,
        attn_out_sum,
        ffn_in_sum,
        ffn_out_sum.reshape(-1, model_width),
        small[:, 8:],
        small[:, :4],
        small[:, 4:8],
    ]
    return (
        output,
        balance,
        grad_tokens,
        summed[5],
        summed[6],
        summed[0],
        summed[1],
        summed[2],
        summed[3],
        summed[4],
        expert_in_sum[None],
        expert_out_sum.reshape(1, -1, model_width),
    )


def solution(mesh):
    return jax.shard_map(
        shards,
        mesh=mesh,
        in_specs=(
            P("expert", "dp", None),
            P("expert", "dp", None),
            P("expert", "dp", None),
            P(),
            P(),
            P(),
            P(),
            P(),
            P(),
            P(),
            P("expert", None, None),
            P("expert", None, None),
            P("expert", "dp", None),
        ),
        out_specs=(
            P("expert", "dp", None),
            P(),
            P("expert", "dp", None),
            P("dp", None),
            P("dp", None),
            P("dp", None, None),
            P("dp", None, None),
            P("dp", None),
            P("dp", None),
            P("dp", None),
            P("expert", "dp", None),
            P("expert", "dp", None),
        ),
        check_vma=False,
    )
```

```python
import functools
import types

import jax
import jax.numpy as jnp
from jax import lax
from jax.experimental import pallas as pl
from jax.experimental.pallas import tpu as pltpu
from jax.sharding import PartitionSpec as P

MESH = pl.DeviceIdType.MESH
HEADS = 12
HEAD_DIM = 64
LONG_DEV = 256


epsilon = 1e-05
balance_weight = 0.01
masked_score = -1e30


def bit_of(index, level):
    return (index // (1 << level)) % 2


def flip(index, level):
    return index + (1 << level) * (1 - 2 * bit_of(index, level))


def partner_index(index, mask, levels):
    total = 0
    for level in range(levels):
        own = bit_of(index, level)
        total = total + (1 << level) * (1 - own if (mask >> level) & 1 else own)
    return total


def unpack_kernel(
    per_in, per_ffn, chunk_ref, expert_ref, in_ref, out_ref, ffn_in_ref, ffn_out_ref, expert_in_ref, expert_out_ref
):
    per_expert = expert_ref.shape[0] // 2
    width = chunk_ref.shape[2]
    at = 0
    for layer in (1, 0):
        out_ref[:, layer, :] = chunk_ref[at].astype(jnp.float32)
        for j in range(per_in):
            in_ref[:, layer, width * j : width * j + width] = chunk_ref[at + 1 + j].astype(jnp.float32)
        at += 1 + per_in
        if layer:
            for j in range(per_ffn):
                ffn_out_ref[j] = chunk_ref[at + j].astype(jnp.float32)
                ffn_in_ref[:, width * j : width * j + width] = chunk_ref[at + per_ffn + j].astype(jnp.float32)
            at += 2 * per_ffn
    for j in range(per_expert):
        expert_in_ref[:, width * j : width * j + width] = expert_ref[j].astype(jnp.float32)
        expert_out_ref[j] = expert_ref[per_expert + j].astype(jnp.float32)


def unpack(chunks, expert_chunks, per_in, per_ffn):
    count, rows, width = chunks.shape
    experts = expert_chunks.shape[0]
    step = 48 if rows % 48 == 0 else rows
    wide = jnp.float32
    return pl.pallas_call(
        functools.partial(unpack_kernel, per_in, per_ffn),
        grid=(rows // step,),
        out_shape=[
            jax.ShapeDtypeStruct((rows, 2, per_in * width), wide),
            jax.ShapeDtypeStruct((rows, 2, width), wide),
            jax.ShapeDtypeStruct((rows, per_ffn * width), wide),
            jax.ShapeDtypeStruct((per_ffn, rows, width), wide),
            jax.ShapeDtypeStruct((rows, experts // 2 * width), wide),
            jax.ShapeDtypeStruct((experts // 2, rows, width), wide),
        ],
        in_specs=[
            pl.BlockSpec((count, step, width), lambda i: (0, i, 0)),
            pl.BlockSpec((experts, step, width), lambda i: (0, i, 0)),
        ],
        out_specs=[
            pl.BlockSpec((step, 2, per_in * width), lambda i: (i, 0, 0)),
            pl.BlockSpec((step, 2, width), lambda i: (i, 0, 0)),
            pl.BlockSpec((step, per_ffn * width), lambda i: (i, 0)),
            pl.BlockSpec((per_ffn, step, width), lambda i: (0, i, 0)),
            pl.BlockSpec((step, experts // 2 * width), lambda i: (i, 0)),
            pl.BlockSpec((experts // 2, step, width), lambda i: (0, i, 0)),
        ],
        compiler_params=pltpu.CompilerParams(vmem_limit_bytes=40 * 1024 * 1024),
        name="unpack",
    )(chunks, expert_chunks)


def dot(a, b):
    return jnp.dot(a, b, preferred_element_type=jnp.float32)


def dot_rows(a, b):
    return lax.dot_general(a, b, (((1,), (1,)), ((), ())), preferred_element_type=jnp.float32)


def dot_columns(a, b):
    return lax.dot_general(a, b, (((0,), (0,)), ((), ())), preferred_element_type=jnp.float32)


def gelu_parts(hidden):
    lower = 0.5 + 0.5 * lax.erf(hidden * 0.7071067811865476)
    slope = lower + hidden * jnp.exp(-0.5 * hidden * hidden) * 0.3989422804014327
    return hidden * lower, slope


def norm_parts(x):
    center = x - jnp.mean(x, axis=-1, keepdims=True)
    inverse = lax.rsqrt(jnp.mean(center * center, axis=-1, keepdims=True) + epsilon)
    return center * inverse, inverse


def norm_back(unit, inverse, gain, upstream):
    scaled = upstream * gain
    return inverse * (
        scaled - jnp.mean(scaled, axis=-1, keepdims=True) - unit * jnp.mean(scaled * unit, axis=-1, keepdims=True)
    )


def capacity_of(rows, experts):
    capacity = (5 * rows + 4 * experts - 1) // (4 * experts)
    return capacity, -(-capacity // 16) * 16


def chosen_rows(assign, experts):
    expert = lax.broadcasted_iota(jnp.int32, (experts, assign.shape[1]), 0)
    return jnp.where(assign == expert, 1.0, 0.0)


def dispatch_of(assign, experts):
    tokens = assign.shape[1]
    capacity, padded = capacity_of(tokens, experts)
    hot = chosen_rows(assign, experts)
    earlier = lax.broadcasted_iota(jnp.int32, (tokens, tokens), 0) < lax.broadcasted_iota(jnp.int32, (tokens, tokens), 1)
    before = dot(hot.astype(jnp.bfloat16), jnp.where(earlier, 1.0, 0.0).astype(jnp.bfloat16))
    place = jnp.sum(hot * before, axis=0, keepdims=True)
    slot = jnp.where(place < capacity, assign.astype(jnp.float32) * padded + place, -1.0)
    number = lax.broadcasted_iota(jnp.int32, (experts * padded, tokens), 0).astype(jnp.float32)
    return jnp.where(number == slot, 1.0, 0.0).astype(jnp.bfloat16)


class Across:
    def __init__(self, experts, out, into, send_sems, recv_sems):
        self.experts, self.out, self.into = experts, out, into
        self.send_sems, self.recv_sems = send_sems, recv_sems
        self.dp, self.me = lax.axis_index("dp"), lax.axis_index("expert")

    def copy(self, slab, place, to):
        return pltpu.make_async_remote_copy(
            src_ref=self.out.at[slab],
            dst_ref=self.into.at[place],
            send_sem=self.send_sems.at[slab],
            recv_sem=self.recv_sems.at[place],
            device_id=(self.dp, to),
            device_id_type=MESH,
        )

    def start(self, j):
        self.copy(j, self.me, j).start()

    def wait_from(self, j):
        self.copy(j, j, j).wait_recv()

    def wait_to(self, j):
        self.copy(j, self.me, j).wait_send()

    def others(self, use):
        def body(k, _):
            use(lax.rem(self.me + k, self.experts))
            return 0

        lax.fori_loop(1, self.experts, body, 0)

    def start_all(self):
        self.others(self.start)

    def wait_all(self):
        def both(j):
            self.wait_from(j)
            self.wait_to(j)

        self.others(both)


def greet(targets):
    barrier = pltpu.get_barrier_semaphore()
    for device in targets:
        pl.semaphore_signal(barrier, inc=1, device_id=device, device_id_type=MESH)
    pl.semaphore_wait(barrier, len(targets))


def across_peers(experts):
    d, e = lax.axis_index("dp"), lax.axis_index("expert")
    return [(d, lax.rem(e + k, experts)) for k in range(1, experts)]


def head_pair(rows):
    first = lax.broadcasted_iota(jnp.int32, rows.shape, 1) < HEAD_DIM
    zero = jnp.zeros_like(rows)
    return jnp.concatenate([jnp.where(first, rows, zero), jnp.where(first, zero, rows)], axis=0)


def pair_rows(both):
    n = both.shape[1] // 2
    return jnp.concatenate([both[:HEAD_DIM, :n], both[HEAD_DIM:, n:]], axis=0)


def causal(keys, queries):
    key = lax.broadcasted_iota(jnp.int32, (keys, 2 * queries), 0)
    query = lax.broadcasted_iota(jnp.int32, (keys, 2 * queries), 1)
    return key <= jnp.where(query >= queries, query - queries, query)


def short_seen(doc_row, doc_col):
    n = doc_row.shape[1]
    same = doc_col == jnp.concatenate([doc_row, doc_row], axis=1)
    return same & causal(n, n)


class Links:
    def __init__(self, n_dp):
        self.me, self.expert = lax.axis_index("dp"), lax.axis_index("expert")
        self.chips = n_dp // 2
        self.chip, self.core = self.me // 2, self.me % 2
        self.twin = self.me + 1 - 2 * self.core

    def peers(self):
        ring = [lax.rem(self.chip + k, self.chips) for k in range(1, self.chips)]
        return [(self.twin, self.expert)] + [(2 * other + self.core, self.expert) for other in ring]

    def copy(self, ref, send_sem, recv_sem, index):
        return pltpu.make_async_remote_copy(
            src_ref=ref,
            dst_ref=ref,
            send_sem=send_sem,
            recv_sem=recv_sem,
            device_id=(index, self.expert),
            device_id_type=MESH,
        )

    def before(self, later, other):
        return other > self.chip if later else other < self.chip


class Spread:
    def __init__(self, links, at, parts, later, far_sems, near_sems, recv_sems):
        self.links, self.at, self.later = links, at, later
        self.far_sems, self.near_sems, self.recv_sems = far_sems, near_sems, recv_sems

    def _far(self, other, p):
        k = self.links
        return k.copy(self.at(k.me, p), self.far_sems.at[other, p], self.recv_sems.at[k.me, p], 2 * other + k.core)

    def _near(self, block, p):
        k = self.links
        return k.copy(self.at(block, p), self.near_sems.at[block, p], self.recv_sems.at[block, p], k.twin)

    def _twin_needs(self):
        return self.links.core == (0 if self.later else 1)

    def send(self, p):
        k = self.links
        for other in range(k.chips):

            @pl.when(k.before(self.later, other))
            def _():
                self._far(other, p).start()

        @pl.when(self._twin_needs())
        def _():
            self._near(k.me, p).start()

    def sent(self, p):
        k = self.links
        for other in range(k.chips):

            @pl.when(k.before(self.later, other))
            def _():
                self._far(other, p).wait_send()

            @pl.when(k.before(not self.later, other))
            def _():
                self._near(2 * other + k.core, p).wait_send()

        @pl.when(self._twin_needs())
        def _():
            self._near(k.me, p).wait_send()

    def relay(self, p):
        k = self.links
        for other in range(k.chips):

            @pl.when(k.before(not self.later, other))
            def _():
                block = 2 * other + k.core
                copy = self._near(block, p)
                copy.wait_recv()
                copy.start()

    def each(self, p, use):
        k = self.links

        @pl.when(k.core == (1 if self.later else 0))
        def _():
            self._near(k.twin, p).wait_recv()
            use(k.twin)

        for other in range(k.chips):

            @pl.when(k.before(not self.later, other))
            def _():
                use(2 * other + k.core)
                block = 2 * other + 1 - k.core
                self._near(block, p).wait_recv()
                use(block)


def spread_sems(n_dp, parts):
    return [
        pltpu.SemaphoreType.DMA((n_dp // 2, parts)),
        pltpu.SemaphoreType.DMA((n_dp, parts)),
        pltpu.SemaphoreType.DMA((n_dp, parts)),
    ]


def attend(n_dp, links, s, x, gain, shift, w_in, w_out, doc_row, doc_col, ready, between):
    me = links.me
    pairs, long, width = s.kv.shape[1], s.kv.shape[3], x.shape[1]
    unit, _ = norm_parts(x)
    normed = (unit * gain + shift).astype(jnp.bfloat16)
    ready(0)
    kv = dot(normed, w_in[:, width:]).astype(jnp.bfloat16)
    for h in range(pairs):
        for part in range(2):
            piece = kv[:, part * width + 128 * h : part * width + 128 * h + 128]
            s.kv[me, h, part] = piece[:long]
            s.short_kv[h, part] = piece[long:]
    kv_spread = Spread(links, lambda b, p: s.kv.at[b, p], pairs, True, *s.kv_sems)
    q_spread = Spread(links, lambda b, p: s.q.at[b], 1, False, *s.q_sems)
    for h in range(pairs):
        kv_spread.send(h)
    ready(1)
    q = (dot(normed, w_in[:, :width]).astype(jnp.bfloat16) * HEAD_DIM ** (-0.5)).astype(jnp.bfloat16)
    for h in range(pairs):
        piece = q[:, 128 * h : 128 * h + 128]
        s.q[me, h] = piece[:long]
        s.short_q[h] = piece[long:]
    q_spread.send(0)
    between()
    s.normed_t[...] = normed.T

    def put_context(h, rows_t, first, count):
        at = pl.ds(pl.multiple_of(128 * h, 128), 128)
        s.context_t[at, first : first + count] = rows_t.astype(jnp.bfloat16)
        s.context[first : first + count, at] = rows_t.T.astype(jnp.bfloat16)

    def own_part(h, _):
        seen = short_seen(doc_row, doc_col)
        scores = jnp.where(seen, dot_rows(s.short_kv[h, 0], head_pair(s.short_q[h])), masked_score)
        top = jnp.max(scores, axis=0, keepdims=True)
        weights = jnp.exp(scores - top)
        total = jnp.sum(weights, axis=0, keepdims=True)
        rows_t = pair_rows(dot_columns(s.short_kv[h, 1], weights.astype(jnp.bfloat16)) / total)
        short = rows_t.shape[1]
        put_context(h, rows_t, long, short)
        lse = top + jnp.log(total)
        s.lse[h, 0:1, long:] = lse[:, :short]
        s.lse[h, 1:2, long:] = lse[:, short:]
        scores = jnp.where(causal(long, long), dot_rows(s.kv[me, h, 0], head_pair(s.q[me, h])), masked_score)
        top = jnp.max(scores, axis=0, keepdims=True)
        weights = jnp.exp(scores - top)
        s.top[h] = top
        s.total[h] = jnp.sum(weights, axis=0, keepdims=True)
        s.acc[h] = dot_columns(s.kv[me, h, 1], weights.astype(jnp.bfloat16))
        return 0

    lax.fori_loop(0, pairs, own_part, 0)

    def other_part(h, _):
        kv_spread.relay(h)
        queries = head_pair(s.q[me, h])

        def use(block):
            scores = dot_rows(s.kv[block, h, 0], queries)
            old = s.top[h]
            top = jnp.maximum(old, jnp.max(scores, axis=0, keepdims=True))
            factor = jnp.exp(old - top)
            weights = jnp.exp(scores - top)
            s.top[h] = top
            s.total[h] = s.total[h] * factor + jnp.sum(weights, axis=0, keepdims=True)
            s.acc[h] = s.acc[h] * factor + dot_columns(s.kv[block, h, 1], weights.astype(jnp.bfloat16))

        kv_spread.each(h, use)
        total = s.total[h]
        put_context(h, pair_rows(s.acc[h] / total), 0, long)
        lse = s.top[h] + jnp.log(total)
        s.lse[h, 0:1, :long] = lse[:, :long]
        s.lse[h, 1:2, :long] = lse[:, long:]
        return 0

    lax.fori_loop(0, pairs, other_part, 0)
    ready(2)
    following = x + dot(s.context[...], w_out[...])

    def settle():
        q_spread.relay(0)
        q_spread.each(0, lambda block: None)
        q_spread.sent(0)
        for h in range(pairs):
            kv_spread.sent(h)

    return following, settle


def front_kernel(n_dp, n_ex, names, saved, *refs):
    r = types.SimpleNamespace(**dict(zip(names, refs)))
    extra = iter(refs[len(names) :])
    buffers = []
    for layer in range(2):
        s = types.SimpleNamespace()
        for name in saved:
            setattr(s, name, next(extra))
        s.acc, s.top, s.total = next(extra), next(extra), next(extra)
        s.kv_sems = [next(extra) for _ in range(3)]
        s.q_sems = [next(extra) for _ in range(3)]
        s.stored = next(extra)
        buffers.append(s)
    w_in, w_out, w_sem, dense_in, dense_out, dense_sem = (next(extra) for _ in range(6))
    stream_ref, dense_normed, active_ref, slope_ref, dense_normed_t, far_cot = (next(extra) for _ in range(6))
    stored, cot_send, cot_send_sem, cot_recv_sem = (next(extra) for _ in range(4))
    links = Links(n_dp)
    tokens, width = r.tokens.shape
    blocks = r.dense_in.shape[1] // width
    low = jnp.bfloat16

    def block_loads(i):
        slot = lax.rem(i, 2)
        at = pl.ds(pl.multiple_of(i * width, width), width)
        return [
            pltpu.make_async_copy(r.dense_in.at[:, at], dense_in.at[slot], dense_sem.at[slot, 0]),
            pltpu.make_async_copy(r.dense_out.at[at, :], dense_out.at[slot], dense_sem.at[slot, 1]),
        ]

    def weight_loads(layer):
        return [
            pltpu.make_async_copy(
                r.attn_in.at[layer, :, pl.ds(width, 2 * width)], w_in.at[layer, :, pl.ds(width, 2 * width)], w_sem.at[layer, 0]
            ),
            pltpu.make_async_copy(
                r.attn_in.at[layer, :, pl.ds(0, width)], w_in.at[layer, :, pl.ds(0, width)], w_sem.at[layer, 1]
            ),
            pltpu.make_async_copy(r.attn_out.at[layer], w_out.at[layer], w_sem.at[layer, 2]),
        ]

    loads = [weight_loads(0), weight_loads(1)]
    for load in loads[0]:
        load.start()
    for i in range(min(2, blocks)):
        for load in block_loads(i):
            load.start()
    for load in loads[1]:
        load.start()
    greet(links.peers() + across_peers(n_ex))
    writes = []

    def write(source, target, sem):
        copy = pltpu.make_async_copy(source, target, sem)
        copy.start()
        writes.append(copy)

    def layer(number, x, between):
        s = buffers[number]
        column = 2 * number
        following, settle = attend(
            n_dp, links, s, x, r.gains[column : column + 1], r.shifts[column : column + 1], w_in.at[number], w_out.at[number],
            r.doc_row[...], r.doc_col[...], lambda i: loads[number][i].wait(), between,
        )
        return following, settle

    def save(number, settle):
        s = buffers[number]
        settle()
        for i, name in enumerate(saved):
            write(getattr(s, name), getattr(r, name + str(number)), s.stored.at[i])

    x, settle = layer(0, r.tokens[...].astype(jnp.float32), lambda: None)
    r.stream0[...] = x
    stream_ref[...] = x
    unit, _ = norm_parts(x)
    normed = (unit * r.gains[1:2] + r.shifts[1:2]).astype(low)
    dense_normed[...] = normed
    save(0, settle)
    dense_normed_t[...] = normed.T

    def dense(i, _):
        slot = lax.rem(i, 2)
        for load in block_loads(i):
            load.wait()
        active, slope = gelu_parts(dot(dense_normed[...], dense_in[slot]))
        active = active.astype(low)
        at = pl.ds(pl.multiple_of(i * width, width), width)
        slope_ref[:, at] = slope.astype(low)
        active_ref[at, :] = active.T
        stream_ref[...] += dot(active, dense_out[slot])

        @pl.when(i + 2 < blocks)
        def _():
            for load in block_loads(i + 2):
                load.start()

        return 0

    lax.fori_loop(0, blocks, dense, 0)
    write(dense_normed_t, r.dense_normed_t, stored.at[0])
    write(active_ref, r.active_t, stored.at[1])
    write(slope_ref, r.slope, stored.at[2])
    x = stream_ref[...]
    r.stream1[...] = x

    cot_across = Across(n_ex, cot_send, far_cot, cot_send_sem, cot_recv_sem)

    def send_cotangent():
        cot_send[...] = dot(dispatch_of(r.assign[...], n_ex), r.cot[...]).astype(low).reshape(cot_send.shape)
        cot_across.start_all()
        far_cot[links.expert] = cot_send[links.expert]

    x, settle = layer(1, x, send_cotangent)
    r.stream2[...] = x
    save(1, settle)
    cot_across.wait_all()
    write(far_cot, r.far_cot, stored.at[3])
    for copy in writes:
        copy.wait()


def front(n_dp, n_ex, collective_id, near, far):
    arrays = {**near, **far}
    a = types.SimpleNamespace(**arrays)
    low, wide = jnp.bfloat16, jnp.float32
    tokens, width = a.tokens.shape
    hidden, mixed = a.dense_in.shape[1], a.attn_in.shape[2]
    long, short, pairs = LONG_DEV, tokens - LONG_DEV, width // 128
    slab = (n_ex, capacity_of(tokens, n_ex)[1], width)
    saved = dict(
        normed_t=jax.ShapeDtypeStruct((width, tokens), low),
        context=jax.ShapeDtypeStruct((tokens, width), low),
        context_t=jax.ShapeDtypeStruct((width, tokens), low),
        kv=jax.ShapeDtypeStruct((n_dp, pairs, 2, long, 128), low),
        q=jax.ShapeDtypeStruct((n_dp, pairs, long, 128), low),
        short_kv=jax.ShapeDtypeStruct((pairs, 2, short, 128), low),
        short_q=jax.ShapeDtypeStruct((pairs, short, 128), low),
        lse=jax.ShapeDtypeStruct((pairs, 2, tokens), wide),
    )
    stream = jax.ShapeDtypeStruct((tokens, width), wide)
    outs = dict(stream0=stream, stream1=stream, stream2=stream)
    direct = len(outs)
    for layer in range(2):
        for name, shape in saved.items():
            outs[name + str(layer)] = shape
    outs.update(
        dense_normed_t=jax.ShapeDtypeStruct((width, tokens), low),
        active_t=jax.ShapeDtypeStruct((hidden, tokens), low),
        slope=jax.ShapeDtypeStruct((tokens, hidden), low),
        far_cot=jax.ShapeDtypeStruct(slab, low),
    )
    scratch = []
    for layer in range(2):
        scratch += [pltpu.VMEM(shape.shape, shape.dtype) for shape in saved.values()]
        scratch += [
            pltpu.VMEM((pairs, 128, 2 * long), wide),
            pltpu.VMEM((pairs, 1, 2 * long), wide),
            pltpu.VMEM((pairs, 1, 2 * long), wide),
        ]
        scratch += spread_sems(n_dp, pairs) + spread_sems(n_dp, 1)
        scratch += [pltpu.SemaphoreType.DMA((len(saved),))]
    scratch += [pltpu.VMEM((2, width, mixed), low), pltpu.VMEM((2, width, width), low), pltpu.SemaphoreType.DMA((2, 3))]
    scratch += [pltpu.VMEM((2, width, width), low)] * 2 + [pltpu.SemaphoreType.DMA((2, 2))]
    scratch += [
        pltpu.VMEM((tokens, width), wide),
        pltpu.VMEM((tokens, width), low),
        pltpu.VMEM((hidden, tokens), low),
        pltpu.VMEM((tokens, hidden), low),
        pltpu.VMEM((width, tokens), low),
        pltpu.VMEM(slab, low),
        pltpu.SemaphoreType.DMA((4,)),
        pltpu.VMEM(slab, low),
        pltpu.SemaphoreType.DMA((n_ex,)),
        pltpu.SemaphoreType.DMA((n_ex,)),
    ]
    vmem, anywhere = pl.BlockSpec(memory_space=pltpu.VMEM), pl.BlockSpec(memory_space=pl.ANY)
    names = tuple(arrays) + tuple(outs)
    values = pl.pallas_call(
        functools.partial(front_kernel, n_dp, n_ex, names, tuple(saved)),
        out_shape=list(outs.values()),
        in_specs=[vmem] * len(near) + [anywhere] * len(far),
        out_specs=[vmem] * direct + [anywhere] * (len(outs) - direct),
        scratch_shapes=scratch,
        compiler_params=pltpu.CompilerParams(
            collective_id=collective_id, has_side_effects=True, vmem_limit_bytes=61 * 1024 * 1024
        ),
        name="front",
    )(*arrays.values())
    return types.SimpleNamespace(**dict(zip(outs, values)))


def share_context(context, lse, grad_context, do_ref, aux_ref, short_do_ref, short_aux_ref, me, long):
    lane = lax.broadcasted_iota(jnp.int32, (8, 128), 1) < HEAD_DIM
    head = lax.broadcasted_iota(jnp.int32, (8, 128), 0)
    picks = jnp.where(((head == 0) & lane) | ((head == 1) & ~lane), 1.0, 0.0)
    for h in range(do_ref.shape[1]):
        at = slice(128 * h, 128 * h + 128)
        piece = grad_context[:, at]
        do_ref[me, h] = piece[:long]
        short_do_ref[h] = piece[long:]
        both = piece.astype(jnp.float32) * context[:, at].astype(jnp.float32)
        delta = lax.dot_general(
            picks, both, (((1,), (1,)), ((), ())), precision=lax.Precision.HIGHEST, preferred_element_type=jnp.float32
        )
        aux_ref[me, h, 0:2] = lse[h, :, :long]
        aux_ref[me, h, 2:4] = delta[0:2, :long]
        short_aux_ref[h, 0:2] = lse[h, :, long:]
        short_aux_ref[h, 2:4] = delta[0:2, long:]


def attend_back_pair(n_dp, me, width, r, do_spread, aux_spread, h):
    scale = HEAD_DIM ** (-0.5)
    mixed_ref = r.mixed
    long = r.kv.shape[3]

    def row_of(aux, first):
        return jnp.concatenate([aux[first : first + 1], aux[first + 1 : first + 2]], axis=1)

    def score_grads(keys, values, queries, grads, aux, seen):
        scores = dot_rows(keys, queries)
        probs = jnp.exp(scores - row_of(aux, 0))
        if seen is not None:
            probs = jnp.where(seen, probs, 0.0)
        grad_scores = probs * (dot_rows(values, grads) - row_of(aux, 2))
        return probs.astype(jnp.bfloat16), grad_scores.astype(jnp.bfloat16)

    def put(third, first, value):
        at = pl.ds(pl.multiple_of(third * width + 128 * h, 128), 128)
        mixed_ref[first : first + value.shape[0], at] = value.astype(jnp.bfloat16)

    seen = short_seen(r.doc_row[...], r.doc_col[...])
    queries, grads = head_pair(r.short_q[h]), head_pair(r.short_do[h])
    keys = r.short_kv[h, 0]
    probs, grad_scores = score_grads(keys, r.short_kv[h, 1], queries, grads, r.short_aux[h], seen)
    put(0, long, (pair_rows(dot_columns(keys, grad_scores)) * scale).T)
    put(1, long, dot(grad_scores, queries))
    put(2, long, dot(probs, grads))
    queries, grads = head_pair(r.q[me, h]), head_pair(r.do[me, h])
    own_keys, own_values = r.kv[me, h, 0], r.kv[me, h, 1]
    probs, grad_scores = score_grads(own_keys, own_values, queries, grads, r.aux[me, h], causal(long, long))
    r.dq[...] = dot_columns(own_keys, grad_scores)
    r.dk[...] = dot(grad_scores, queries)
    r.dv[...] = dot(probs, grads)
    for block in range(n_dp - 1):

        @pl.when(block < me)
        def _():
            keys = r.kv[block, h, 0]
            _, grad_scores = score_grads(keys, r.kv[block, h, 1], queries, grads, r.aux[me, h], None)
            r.dq[...] += dot_columns(keys, grad_scores)

    put(0, 0, (pair_rows(r.dq[...]) * scale).T)
    do_spread.relay(h)
    aux_spread.relay(h)

    def use(block):
        queries, grads = head_pair(r.q[block, h]), head_pair(r.do[block, h])
        probs, grad_scores = score_grads(own_keys, own_values, queries, grads, r.aux[block, h], None)
        r.dk[...] += dot(grad_scores, queries)
        r.dv[...] += dot(probs, grads)

    aux_spread.each(h, lambda block: None)
    do_spread.each(h, use)
    put(1, 0, r.dk[...])
    put(2, 0, r.dv[...])


def back_scratch(n_dp, pairs, long, short):
    return (
        [
            pltpu.VMEM((n_dp, pairs, long, 128), jnp.bfloat16),
            pltpu.VMEM((n_dp, pairs, 8, long), jnp.float32),
            pltpu.VMEM((pairs, short, 128), jnp.bfloat16),
            pltpu.VMEM((pairs, 8, short), jnp.float32),
            pltpu.VMEM((128, 2 * long), jnp.float32),
            pltpu.VMEM((long, 128), jnp.float32),
            pltpu.VMEM((long, 128), jnp.float32),
        ]
        + spread_sems(n_dp, pairs)
        + spread_sems(n_dp, pairs)
    )


def lane_plan(n_dp, n_ex, rows, order):
    dp_levels = [("dp", b) for b in range(n_dp.bit_length() - 1)]
    ex_levels = n_ex.bit_length() - 1
    halved, piece = [], rows
    for level in ((0, 1), (1, 0))[order]:
        if level < ex_levels and piece % 32 == 0:
            halved.append(level)
            piece //= 2
    halves = [("half", b) for b in halved]
    if order:
        kinds = dp_levels[:1] + halves[:1] + dp_levels[1:] + halves[1:]
    else:
        kinds = dp_levels + halves
    kinds += [("both", b) for b in range(ex_levels) if b not in halved]
    kinds += [("back", b) for b in reversed(halved)]
    return kinds, halved


class Lane:
    def __init__(self, n_dp, n_ex, rows, columns, order, refs):
        self.rows, self.columns = rows, columns
        self.kinds, self.halved = lane_plan(n_dp, n_ex, rows, order)
        self.count = len(self.kinds)
        moving = [k[0] != "back" for k in self.kinds]
        self.send = [next(refs) if m else None for m in moving]
        self.recv = [next(refs) if m else None for m in moving]
        self.keep = [next(refs) if m else None for m in moving]
        self.fin = next(refs)
        self.send_sems = [next(refs) for _ in moving]
        self.recv_sems = [next(refs) for _ in moving]
        self.d, self.e = lax.axis_index("dp"), lax.axis_index("expert")

    @staticmethod
    def scratch(n_dp, n_ex, rows, columns, order):
        kinds, halved = lane_plan(n_dp, n_ex, rows, order)
        width, pieces, height, shapes = columns[1] - columns[0], n_dp, rows, []
        for kind, _ in kinds:
            if kind == "dp":
                pieces //= 2
            elif kind == "half":
                height //= 2
            if kind != "back":
                shapes.append((pieces, height, width))
        scratch = [pltpu.VMEM((2,) + s, jnp.bfloat16) for s in shapes]
        scratch += [pltpu.VMEM((4,) + s, jnp.bfloat16) for s in shapes]
        scratch += [pltpu.VMEM((2,) + s, jnp.float32) for s in shapes]
        scratch += [pltpu.VMEM((len(halved) + 3, rows, width), jnp.bfloat16)]
        return scratch + [pltpu.SemaphoreType.DMA((4,)) for _ in kinds] * 2

    def peer(self, kind, level):
        return (flip(self.d, level), self.e) if kind == "dp" else (self.d, flip(self.e, level))

    def kept_rows(self, depth):
        start = 0
        for i, level in enumerate(self.halved[:depth]):
            start = start + bit_of(self.e, level) * (self.rows >> (i + 1))
        return start

    def copy_of(self, s, c):
        kind, level = self.kinds[s]
        slot, place = lax.rem(c, 2), lax.rem(c, 4)
        if kind == "back":
            depth = self.halved.index(level) + 1
            span = self.rows >> depth
            at = pl.ds(pl.multiple_of(self.kept_rows(depth), span), span)
            src = self.fin.at[lax.rem(c, len(self.halved) + 3), at]
            dst = src
        else:
            src, dst = self.send[s].at[slot], self.recv[s].at[place]
        return pltpu.make_async_remote_copy(
            src_ref=src,
            dst_ref=dst,
            send_sem=self.send_sems[s].at[place],
            recv_sem=self.recv_sems[s].at[place],
            device_id=self.peer(kind, level),
            device_id_type=MESH,
        )

    def arrive(self, s, c):
        self.copy_of(s, c).wait()
        slot, place = lax.rem(c, 2), lax.rem(c, 4)
        if self.kinds[s][0] == "back":
            return None
        return [
            self.keep[s][slot, i] + self.recv[s][place, i].astype(jnp.float32) for i in range(self.keep[s].shape[1])
        ]

    def leave(self, s, c, values):
        kind, level = self.kinds[s]
        slot = lax.rem(c, 2)
        kept = None
        if kind == "dp":
            sent, kept = values[1::2], values[0::2]
        elif kind == "half":
            half = values[0].shape[0] // 2
            own = bit_of(self.e, level)
            sent = [jnp.where(own == 0, v[half:], v[:half]) for v in values]
            kept = [jnp.where(own == 0, v[:half], v[half:]) for v in values]
        elif kind == "both":
            sent = values
            kept = [v.astype(jnp.bfloat16).astype(jnp.float32) for v in values]
        elif values is not None:
            span = values[0].shape[0]
            at = pl.ds(pl.multiple_of(self.kept_rows(len(self.halved)), span), span)
            self.fin[lax.rem(c, len(self.halved) + 3), at] = values[0].astype(jnp.bfloat16)
        if kept is not None:
            for i, v in enumerate(sent):
                self.send[s][slot, i] = v.astype(jnp.bfloat16)
        self.copy_of(s, c).start()
        if kept is not None:
            for i, v in enumerate(kept):
                self.keep[s][slot, i] = v

    def final(self, c):
        values = self.arrive(self.count - 1, c)
        if values is None:
            return self.fin[lax.rem(c, len(self.halved) + 3)]
        return values[0].astype(jnp.bfloat16)


class Reduction:
    def __init__(self, n_dp, n_ex, rows, groups, lanes, refs):
        self.n_dp, self.rows, self.groups = n_dp, rows, groups
        refs = iter(refs)
        self.lanes = [Lane(n_dp, n_ex, rows, columns, order, refs) for columns, order in lanes]
        self.stage_ref, self.stage_sem, self.out = next(refs), next(refs), next(refs)
        self.count = self.lanes[0].count
        self.chunks = sum(g[0] for g in groups)
        self.firsts = [sum(g[0] for g in groups[:i]) for i in range(len(groups))]
        self.ticks = self.chunks + self.count
        self.d = lax.axis_index("dp")
        self.peer = self.lanes[0].peer

    @staticmethod
    def scratch(n_dp, n_ex, rows, width, lanes):
        scratch = []
        for columns, order in lanes:
            scratch += Lane.scratch(n_dp, n_ex, rows, columns, order)
        return scratch + [pltpu.VMEM((2, rows, width), jnp.bfloat16), pltpu.SemaphoreType.DMA((2,))]

    def out_copy(self, c):
        slot = lax.rem(c, 2)
        return pltpu.make_async_copy(self.stage_ref.at[slot], self.out.at[c], self.stage_sem.at[slot])

    def first(self, g, c):
        _, piece, factor = self.groups[g]
        j = c - self.firsts[g]
        dy = factor(j)
        slot = lax.rem(c, 2)
        levels = self.n_dp.bit_length() - 1
        half = self.n_dp // 2

        def products(odd):
            parts = [piece(j, partner_index(self.d, 2 * i + odd, levels)) for i in range(half)]
            return dot(jnp.concatenate(parts, axis=0), dy)

        value = products(1)
        for lane in self.lanes:
            for i in range(half):
                part = value[i * self.rows : (i + 1) * self.rows, slice(*lane.columns)]
                lane.send[0][slot, i] = part.astype(jnp.bfloat16)
            lane.copy_of(0, c).start()
        value = products(0)
        for lane in self.lanes:
            for i in range(half):
                lane.keep[0][slot, i] = value[i * self.rows : (i + 1) * self.rows, slice(*lane.columns)]

    def last(self, c):
        slot = lax.rem(c, 2)

        @pl.when(c >= 2)
        def _():
            self.out_copy(c - 2).wait()

        for lane in self.lanes:
            self.stage_ref[slot, :, slice(*lane.columns)] = lane.final(c)
        self.out_copy(c).start()

    def tick(self, t, low, high):
        for s in range(self.count + 1):
            if high - s <= 0 or low - s >= self.chunks:
                continue
            c = t - s
            if s > 0:

                @pl.when((c >= 0) & (c < self.chunks))
                def _(s=s, c=c):
                    if s < self.count:
                        for lane in self.lanes:
                            lane.leave(s, c, lane.arrive(s - 1, c))
                    else:
                        self.last(c)

                continue
            for g, (size, _, _) in enumerate(self.groups):
                begin, end = self.firsts[g], self.firsts[g] + size
                if high <= begin or low >= end:
                    continue

                @pl.when((c >= begin) & (c < end))
                def _(g=g):
                    self.first(g, c)

    def finish(self):
        for c in range(max(0, self.chunks - 2), self.chunks):
            self.out_copy(c).wait()


def dense_lanes(width):
    cut = width // 768 * 640
    return [((0, cut), 0), ((cut, width), 1)]


def middle_kernel(n_dp, n_ex, names, staged, *refs):
    r = types.SimpleNamespace(**dict(zip(names, refs)))
    extra = iter(refs[len(names) :])
    loads = types.SimpleNamespace()
    for name in staged:
        buffer, sem = next(extra), next(extra)
        setattr(loads, name, pltpu.make_async_copy(getattr(r, name), buffer, sem))
        setattr(r, name, buffer)
    w_in_ref, w_out_ref, weight_sem = (next(extra) for _ in range(3))
    rows_ref, send_ref, grad_ref, home_ref, result_ref, result_home_ref = (next(extra) for _ in range(6))
    rows_t_ref, back_ref, active_t_ref, hidden_ref, dispatch_ref, gate_ref = (next(extra) for _ in range(6))
    dgate_ref, home_dgate_ref, stat_send, stat_recv, result_acc, grad_acc = (next(extra) for _ in range(6))
    (
        x_send_sem, x_recv_sem, grad_send_sem, grad_recv_sem, dgate_send_sem, dgate_recv_sem,
        result_send_sem, result_recv_sem, stat_send_sem, stat_recv_sem,
    ) = (next(extra) for _ in range(10))
    do_ref, aux_ref, short_do_ref, short_aux_ref, dq_ref, dk_ref, dv_ref = (next(extra) for _ in range(7))
    do_far, do_near, do_recv, aux_far, aux_near, aux_recv = (next(extra) for _ in range(6))
    links = Links(n_dp)
    d, e, me = links.me, links.expert, links.me
    shared = links.chips == 2
    if shared:
        peer_rows_ref, peer_cot_ref, peer_row_sems, peer_cot_sems = (next(extra) for _ in range(4))
    dp_levels, ex_levels = n_dp.bit_length() - 1, n_ex.bit_length() - 1
    tokens, width = r.stream.shape
    padded = send_ref.shape[1]
    blocks = r.expert_in.shape[1] // width
    pairs, long = r.kv.shape[1], r.kv.shape[3]
    group = min(max(4, 128 // padded), n_ex)
    groups = n_ex // group
    exact = dict(precision=lax.Precision.HIGHEST, preferred_element_type=jnp.float32)
    hops = [(flip(d, b), e) for b in range(dp_levels)] + [(d, flip(e, b)) for b in range(ex_levels)]

    def column(i):
        return pl.ds(i * width, width)

    expert_loads = [
        (
            pltpu.make_async_copy(r.expert_in.at[:, column(i)], w_in_ref.at[i], weight_sem.at[0, i]),
            pltpu.make_async_copy(r.expert_out.at[column(i), :], w_out_ref.at[i], weight_sem.at[1, i]),
        )
        for i in range(blocks)
    ]
    for both in expert_loads:
        for load in both:
            load.start()
    for name in staged:
        getattr(loads, name).start()
    greet(links.peers() + across_peers(n_ex))

    def peer_copy(source, target, sems):
        return pltpu.make_async_remote_copy(
            src_ref=source,
            dst_ref=target,
            send_sem=sems.at[0],
            recv_sem=sems.at[1],
            device_id=(flip(d, 1), e),
            device_id_type=MESH,
        )

    def row_copy(j):
        return peer_copy(rows_ref.at[j], peer_rows_ref.at[j], peer_row_sems.at[j])

    if shared:
        cot_copy = peer_copy(r.far_cot, peer_cot_ref, peer_cot_sems)
        cot_copy.start()

    unit, inverse = norm_parts(r.stream[...])
    routed = (unit * r.gain[...] + r.shift[...]).astype(jnp.bfloat16)
    assign = r.assign[...]
    dispatch = dispatch_of(assign, n_ex)
    dispatch_ref[...] = dispatch
    send_ref[...] = dot(dispatch, routed).astype(jnp.bfloat16).reshape(send_ref.shape)
    x_across = Across(n_ex, send_ref, rows_ref, x_send_sem, x_recv_sem)

    def place(k, i):
        return lax.rem(e // group + k, groups) * group + lax.rem(e + i, group)

    def source(k, i):
        return lax.rem(e // group + k, groups) * group + lax.rem(e + group - i, group)

    for i in range(group):
        if i:
            x_across.start(place(0, i))
        for k in range(1, groups):
            x_across.start(place(k, i))
    rows_ref[e] = send_ref[e]
    router = r.router[...]
    hot = chosen_rows(assign, n_ex)
    gate = jax.nn.sigmoid(jnp.sum(hot * dot_rows(router, routed), axis=0, keepdims=True))
    gate_ref[...] = gate

    def stat_copy(i):
        return pltpu.make_async_remote_copy(
            src_ref=stat_send.at[i],
            dst_ref=stat_recv.at[i],
            send_sem=stat_send_sem.at[i],
            recv_sem=stat_recv_sem.at[i],
            device_id=hops[i],
            device_id_type=MESH,
        )

    lane = lax.broadcasted_iota(jnp.int32, r.stats.shape, 1)
    stat_send[0] = jnp.where(
        lane == 0, jnp.sum(hot, axis=1, keepdims=True), jnp.sum(hot * gate, axis=1, keepdims=True)
    )
    stat_copy(0).start()

    def stat_step(i):
        stat_copy(i).wait()
        value = stat_send[i] + stat_recv[i]
        if i + 1 < len(hops):
            stat_send[i + 1] = value
            stat_copy(i + 1).start()
        else:
            r.stats[...] = value

    grad_across = Across(n_ex, grad_ref, home_ref, grad_send_sem, grad_recv_sem)
    dgate_across = Across(n_ex, dgate_ref, home_dgate_ref, dgate_send_sem, dgate_recv_sem)
    steps = [[(0, i) for i in range(group)]]
    cut = group // 2 if (group // 2) * padded % 128 == 0 else group
    for k in range(1, groups):
        steps += [[(k, i) for i in range(first, first + cut)] for first in range(0, group, cut)]
    def expert_rows(rows, cot, at, whole):
        count = rows.shape[0]
        logits = dot_rows(rows, router)
        own = lax.broadcasted_iota(jnp.int32, logits.shape, 1) == e
        slot_gate = jax.nn.sigmoid(jnp.sum(jnp.where(own, logits, 0.0), axis=1, keepdims=True))
        back = (slot_gate * cot).astype(jnp.bfloat16)
        span = slice(at, at + count)
        back_ref[span] = back
        rows_t_ref[:, span] = rows.T
        if whole:
            result_acc[:count] = jnp.zeros((count, width), jnp.float32)
            grad_acc[:count] = jnp.zeros((count, width), jnp.float32)

        def block(i, _):
            cols = pl.ds(pl.multiple_of(i * width, width), width)
            active, slope = gelu_parts(dot(rows, w_in_ref[i]))
            active = active.astype(jnp.bfloat16)
            hidden = (slope * dot_rows(back, w_out_ref[i])).astype(jnp.bfloat16)
            active_t_ref[cols, span] = active.T
            hidden_ref[span, cols] = hidden
            if whole:
                result_acc[:count] += dot(active, w_out_ref[i])
                grad_acc[:count] += dot_rows(hidden, w_in_ref[i])
            return 0

        lax.fori_loop(0, blocks, block, 0)

    done, at = 0, 0
    for number, members in enumerate(steps):
        count = len(members) * padded
        sources = [source(k, i) for k, i in members]
        for (k, i), j in zip(members, sources):
            if (k, i) != (0, 0):
                x_across.wait_from(j)
            if shared:
                row_copy(j).start()
        rows = jnp.concatenate([rows_ref[j] for j in sources], axis=0)
        cot = jnp.concatenate([r.far_cot[j] for j in sources], axis=0).astype(jnp.float32)
        if number == 0:
            for both in expert_loads:
                for load in both:
                    load.wait()
        expert_rows(rows, cot, at, True)
        grad = grad_acc[:count].astype(jnp.bfloat16)
        result = result_acc[:count].astype(jnp.bfloat16)
        dgate = lax.dot_general(
            jnp.ones((8, width), jnp.float32), cot * result.astype(jnp.float32), (((1,), (1,)), ((), ())), **exact
        )
        for m, (k, i) in enumerate(members):
            j, part = sources[m], slice(m * padded, (m + 1) * padded)
            grad_ref[j] = grad[part]
            result_ref[j] = result[part]
            dgate_ref[j, :, :padded] = dgate[:, part]
            if (k, i) == (0, 0):
                home_ref[e] = grad_ref[e]
                home_dgate_ref[e] = dgate_ref[e]
            else:
                grad_across.start(j)
                dgate_across.start(j)
        at += count
        if done < len(hops):
            stat_step(done)
            done += 1

    if shared:
        cot_copy.wait()
        for k in range(groups):
            sources = [source(k, i) for i in range(group)]
            for j in sources:
                row_copy(j).wait()
            rows = jnp.concatenate([peer_rows_ref[j] for j in sources], axis=0)
            cot = jnp.concatenate([peer_cot_ref[j] for j in sources], axis=0).astype(jnp.float32)
            expert_rows(rows, cot, at, False)
            at += group * padded
            if done < len(hops):
                stat_step(done)
                done += 1

    thirds = [w_in_ref.at[i] for i in range(3)]
    in_loads = [
        pltpu.make_async_copy(r.attn_in.at[1, :, column(i)], third, weight_sem.at[0, i])
        for i, third in enumerate(thirds)
    ]
    out_load = pltpu.make_async_copy(r.attn_out.at[1], w_out_ref.at[0], weight_sem.at[1, 0])
    for load in in_loads + [out_load]:
        load.start()
    rows = width // n_dp

    def rows_of(ref, j, q):
        return ref[pl.ds(pl.multiple_of((q * (ref.shape[0] // width) + j) * rows, rows), rows), :]

    base = 2 * links.chip if shared else 0
    factors = [
        (blocks, lambda j, q: rows_of(rows_t_ref, 0, base + q), lambda j: hidden_ref[:, pl.ds(pl.multiple_of(j * width, width), width)]),
        (blocks, lambda j, q: rows_of(active_t_ref, j, base + q), lambda j: back_ref[...]),
    ]
    red = Reduction(2 if shared else n_dp, 1, rows, factors, [((0, width), 0)], list(extra) + [r.chunks])
    red.tick(0, 0, 1)
    early = 1
    while done < len(hops):
        stat_step(done)
        done += 1
    x_across.others(x_across.wait_to)
    red.tick(1, 1, 2)
    early += 1
    dgate_across.wait_all()
    dgate = jnp.zeros((8, tokens), jnp.float32)
    for j in range(n_ex):
        part = dispatch_ref[j * padded : (j + 1) * padded].astype(jnp.float32)
        dgate = dgate + jnp.dot(home_dgate_ref[j, :, :padded], part, **exact)
    everyone = tokens * n_dp * n_ex
    share = jnp.sum(jnp.where(lane == 0, r.stats[...], 0.0), axis=1, keepdims=True) / everyone
    weight = balance_weight * n_ex * (share - 1.0 / n_ex) / everyone
    gate = gate_ref[...]
    grad_gate = dgate[0:1] + jnp.sum(hot * weight, axis=0, keepdims=True)
    grad_logits = hot * (grad_gate * gate * (1.0 - gate))
    r.router_grad[...] = jnp.dot(grad_logits, routed.astype(jnp.float32), **exact)
    grad_normed = lax.dot_general(grad_logits, router.astype(jnp.float32), (((0,), (0,)), ((), ())), **exact)
    red.tick(2, 2, 3)
    early += 1
    grad_across.wait_all()
    grad_normed = grad_normed + dot_columns(dispatch_ref[...], home_ref[...].reshape(n_ex * padded, width))
    unit, inverse = norm_parts(r.stream[...])
    up = r.cot[...].astype(jnp.float32) + norm_back(unit, inverse, r.gain[...], grad_normed)
    r.sums[0:1] = jnp.sum(grad_normed * unit, axis=0, keepdims=True)
    r.sums[1:2] = jnp.sum(grad_normed, axis=0, keepdims=True)

    r.up_next[...] = up
    up_low = up.astype(jnp.bfloat16)
    r.up_low[...] = up_low
    out_load.wait()
    for name in staged:
        getattr(loads, name).wait()
    grad_context = dot_rows(up_low, w_out_ref[0]).astype(jnp.bfloat16)
    share_context(r.context, r.lse, grad_context, do_ref, aux_ref, short_do_ref, short_aux_ref, me, long)
    do_spread = Spread(links, lambda b, p: do_ref.at[b, p], pairs, False, do_far, do_near, do_recv)
    aux_spread = Spread(links, lambda b, p: aux_ref.at[b, p], pairs, False, aux_far, aux_near, aux_recv)
    for h in range(pairs):
        do_spread.send(h)
        aux_spread.send(h)
    result_across = Across(n_ex, result_ref, result_home_ref, result_send_sem, result_recv_sem)
    result_across.start_all()
    result_home_ref[e] = result_ref[e]
    sequence = types.SimpleNamespace(
        doc_row=r.doc_row, doc_col=r.doc_col, kv=r.kv, q=r.q, short_kv=r.short_kv, short_q=r.short_q,
        do=do_ref, aux=aux_ref, short_do=short_do_ref, short_aux=short_aux_ref, dq=dq_ref, dk=dk_ref, dv=dv_ref,
        mixed=r.mixed,
    )

    def pair(h, _):
        attend_back_pair(n_dp, me, width, sequence, do_spread, aux_spread, h)
        red.tick(early + h, early, early + pairs)
        return 0

    lax.fori_loop(0, pairs, pair, 0)
    grad_normed = jnp.zeros((tokens, width), jnp.float32)
    for i, third in enumerate(thirds):
        in_loads[i].wait()
        grad_normed = grad_normed + dot_rows(r.mixed[:, i * width : (i + 1) * width], third[...])
    unit, inverse = norm_parts(r.attn_x[...])
    r.up_next[...] += norm_back(unit, inverse, r.attn_gain[...], grad_normed)
    r.attn_sums[0:1] = jnp.sum(grad_normed * unit, axis=0, keepdims=True)
    r.attn_sums[1:2] = jnp.sum(grad_normed, axis=0, keepdims=True)

    def rest(t, _):
        red.tick(t, early + pairs, red.ticks)
        return 0

    lax.fori_loop(early + pairs, red.ticks, rest, 0)
    result_across.wait_all()
    result = dot_columns(dispatch_ref[...], result_home_ref[...].reshape(n_ex * padded, width))
    gate = jnp.broadcast_to(gate_ref[...], (128, tokens)).T[:, 0:1]
    r.output[...] = (r.stream[...] + gate * result).astype(jnp.bfloat16)
    red.finish()
    for h in range(pairs):
        do_spread.sent(h)
        aux_spread.sent(h)


def middle(n_dp, n_ex, collective_id, near, staged, far):
    arrays = {**near, **staged, **far}
    a = types.SimpleNamespace(**arrays)
    low, wide = jnp.bfloat16, jnp.float32
    tokens, width = a.stream.shape
    hidden = a.expert_in.shape[1]
    mixed = a.attn_in.shape[2]
    blocks, rows = hidden // width, width // n_dp
    long, short, pairs = LONG_DEV, tokens - LONG_DEV, width // 128
    _, padded = capacity_of(tokens, n_ex)
    slots = n_ex * padded
    group = min(max(4, 128 // padded), n_ex) * padded
    slab = (n_ex, padded, width)
    hops = (n_dp * n_ex).bit_length() - 1
    outs = dict(
        up_next=jax.ShapeDtypeStruct((tokens, width), wide),
        up_low=jax.ShapeDtypeStruct((tokens, width), low),
        mixed=jax.ShapeDtypeStruct((tokens, mixed), low),
        sums=jax.ShapeDtypeStruct((2, width), wide),
        attn_sums=jax.ShapeDtypeStruct((2, width), wide),
        router_grad=jax.ShapeDtypeStruct((n_ex, width), wide),
        stats=jax.ShapeDtypeStruct((n_ex, 128), wide),
        output=jax.ShapeDtypeStruct((tokens, width), low),
        chunks=jax.ShapeDtypeStruct((2 * blocks, rows, width), low),
    )
    scratch = []
    for name in staged:
        scratch += [pltpu.VMEM(arrays[name].shape, arrays[name].dtype), pltpu.SemaphoreType.DMA]
    scratch += [pltpu.VMEM((blocks, width, width), low)] * 2 + [pltpu.SemaphoreType.DMA((2, blocks))]
    scratch += [pltpu.VMEM(slab, low)] * 6
    shared = n_dp == 4
    known = 2 * slots if shared else slots
    scratch += [
        pltpu.VMEM((width, known), low),
        pltpu.VMEM((known, width), low),
        pltpu.VMEM((hidden, known), low),
        pltpu.VMEM((known, hidden), low),
        pltpu.VMEM((slots, tokens), low),
        pltpu.VMEM((1, tokens), wide),
        pltpu.VMEM((n_ex, 8, 128), wide),
        pltpu.VMEM((n_ex, 8, 128), wide),
        pltpu.VMEM((hops, n_ex, 128), wide),
        pltpu.VMEM((hops, n_ex, 128), wide),
        pltpu.VMEM((group, width), wide),
        pltpu.VMEM((group, width), wide),
    ]
    scratch += [pltpu.SemaphoreType.DMA((n_ex,))] * 8 + [pltpu.SemaphoreType.DMA((hops,))] * 2
    scratch += back_scratch(n_dp, pairs, long, short)
    if shared:
        scratch += [pltpu.VMEM(slab, low)] * 2 + [pltpu.SemaphoreType.DMA((n_ex, 2)), pltpu.SemaphoreType.DMA((2,))]
    scratch += Reduction.scratch(2 if shared else n_dp, 1, rows, width, [((0, width), 0)])
    vmem, anywhere = pl.BlockSpec(memory_space=pltpu.VMEM), pl.BlockSpec(memory_space=pl.ANY)
    names = tuple(arrays) + tuple(outs)
    values = pl.pallas_call(
        functools.partial(middle_kernel, n_dp, n_ex, names, tuple(staged)),
        out_shape=list(outs.values()),
        in_specs=[vmem] * len(near) + [anywhere] * (len(staged) + len(far)),
        out_specs=[vmem] * (len(outs) - 1) + [anywhere],
        scratch_shapes=scratch,
        compiler_params=pltpu.CompilerParams(
            collective_id=collective_id, has_side_effects=True, vmem_limit_bytes=61 * 1024 * 1024
        ),
        name="middle",
    )(*arrays.values())
    return types.SimpleNamespace(**dict(zip(outs, values)))


def tail_kernel(n_dp, n_ex, names, staged, *refs):
    r = types.SimpleNamespace(**dict(zip(names, refs)))
    extra = iter(refs[len(names) :])
    loads = types.SimpleNamespace()
    for name in staged:
        buffer, sem = next(extra), next(extra)
        setattr(loads, name, pltpu.make_async_copy(getattr(r, name), buffer, sem))
        setattr(r, name, buffer)
    weights_in, weights_out, slopes, weight_sem = (next(extra) for _ in range(4))
    first_sem = next(extra)
    up_ref, acc_ref, dense_low_ref, dense_hidden_ref, first_low_ref, mixed_ref = (next(extra) for _ in range(6))
    do_ref, aux_ref, short_do_ref, short_aux_ref, dq_ref, dk_ref, dv_ref = (next(extra) for _ in range(7))
    do_far, do_near, do_recv, aux_far, aux_near, aux_recv = (next(extra) for _ in range(6))
    small_send, small_recv, small_send_sem, small_recv_sem = (next(extra) for _ in range(4))
    links = Links(n_dp)
    me = links.me
    width = up_ref.shape[1]
    rows = width // n_dp
    pairs, long = r.kv.shape[1], r.kv.shape[3]
    blocks = r.dense_in.shape[1] // width
    per_in = mixed_ref.shape[1] // width

    def block_loads(i):
        slot = lax.rem(i, 2)
        at = pl.ds(pl.multiple_of(i * width, width), width)
        return [
            pltpu.make_async_copy(r.dense_out.at[at, :], weights_out.at[slot], weight_sem.at[slot, 0]),
            pltpu.make_async_copy(r.dense_in.at[:, at], weights_in.at[slot], weight_sem.at[slot, 1]),
            pltpu.make_async_copy(r.slope.at[:, at], slopes.at[slot], weight_sem.at[slot, 2]),
        ]

    ready = (loads.second_context_t, loads.second_low, loads.second_normed_t, loads.second_mixed)
    for load in ready:
        load.start()
    for i in range(min(2, blocks)):
        for load in block_loads(i):
            load.start()
    loads.active_t.start()
    for name in staged:
        if all(getattr(loads, name) is not load for load in ready + (loads.active_t,)):
            getattr(loads, name).start()
    free, busy = blocks % 2, (blocks - 1) % 2
    out_load = pltpu.make_async_copy(r.attn_out.at[0], weights_out.at[free], first_sem.at[0])
    thirds = [weights_in.at[free], weights_in.at[busy], weights_out.at[busy]]
    in_loads = [
        pltpu.make_async_copy(r.attn_in.at[0, :, pl.ds(i * width, width)], third, first_sem.at[1 + i])
        for i, third in enumerate(thirds)
    ]

    def columns(ref):
        return lambda j: ref[:, pl.ds(pl.multiple_of(j * width, width), width)]

    def one(ref):
        return lambda j, q: ref[q, 0]

    groups = [
        (1, one(r.second_context_t), columns(r.second_low)),
        (per_in, one(r.second_normed_t), columns(r.second_mixed)),
        (blocks, lambda j, q: r.active_t[q, j], lambda j: dense_low_ref[...]),
        (blocks, one(r.dense_normed_t), columns(dense_hidden_ref)),
        (1, one(r.first_context_t), columns(first_low_ref)),
        (per_in, one(r.first_normed_t), columns(mixed_ref)),
    ]
    red_refs = list(extra) + [r.chunks]
    red = Reduction(n_dp, n_ex, rows, groups, dense_lanes(width), red_refs)
    levels = [("dp", b) for b in range(n_dp.bit_length() - 1)] + [("ex", b) for b in range(n_ex.bit_length() - 1)]
    greet([red.peer(*level) for level in levels] + (links.peers()[1:] if links.chips > 2 else []))

    up = r.up[...]
    dense_low_ref[...] = up.astype(jnp.bfloat16)
    acc_ref[...] = jnp.zeros_like(acc_ref)
    for load in ready:
        load.wait()
    red.tick(0, 0, 1)
    loads.active_t.wait()

    def dense(i, _):
        slot = lax.rem(i, 2)
        for load in block_loads(i):
            load.wait()
        grad = dot_rows(dense_low_ref[...], weights_out[slot]) * slopes[slot].astype(jnp.float32)
        grad = grad.astype(jnp.bfloat16)
        dense_hidden_ref[:, pl.ds(pl.multiple_of(i * width, width), width)] = grad
        acc_ref[...] += dot_rows(grad, weights_in[slot])

        @pl.when(i + 2 < blocks)
        def _():
            for load in block_loads(i + 2):
                load.start()

        @pl.when(i == blocks - 2)
        def _():
            out_load.start()
            in_loads[0].start()

        red.tick(1 + i, 1, 1 + blocks)
        return 0

    lax.fori_loop(0, blocks, dense, 0)
    for load in in_loads[1:]:
        load.start()
    for name in staged:
        if all(getattr(loads, name) is not load for load in ready + (loads.active_t,)):
            getattr(loads, name).wait()
    unit, inverse = norm_parts(r.dense_x[...])
    grad_normed = acc_ref[...]
    up = up + norm_back(unit, inverse, r.dense_gain[...], grad_normed)
    up_ref[...] = up
    small_send[0] = r.small[...]
    small_send[0, 1:2] = jnp.sum(grad_normed * unit, axis=0, keepdims=True)
    small_send[0, 5:6] = jnp.sum(grad_normed, axis=0, keepdims=True)
    at_tick = 1 + blocks

    scale = HEAD_DIM ** (-0.5)
    up_low = up.astype(jnp.bfloat16)
    first_low_ref[...] = up_low
    out_load.wait()
    grad_context = dot_rows(up_low, weights_out[free]).astype(jnp.bfloat16)
    share_context(r.context, r.lse, grad_context, do_ref, aux_ref, short_do_ref, short_aux_ref, me, long)
    do_spread = Spread(links, lambda b, p: do_ref.at[b, p], pairs, False, do_far, do_near, do_recv)
    aux_spread = Spread(links, lambda b, p: aux_ref.at[b, p], pairs, False, aux_far, aux_near, aux_recv)
    for h in range(pairs):
        do_spread.send(h)
        aux_spread.send(h)
    red.tick(at_tick, at_tick, at_tick + 1)
    at_tick += 1
    sequence = types.SimpleNamespace(
        doc_row=r.doc_row, doc_col=r.doc_col, kv=r.kv, q=r.q, short_kv=r.short_kv, short_q=r.short_q,
        do=do_ref, aux=aux_ref, short_do=short_do_ref, short_aux=short_aux_ref, dq=dq_ref, dk=dk_ref, dv=dv_ref,
        mixed=mixed_ref,
    )

    def pair(h, _):
        attend_back_pair(n_dp, me, width, sequence, do_spread, aux_spread, h)
        red.tick(at_tick + h, at_tick, at_tick + pairs)
        return 0

    lax.fori_loop(0, pairs, pair, 0)
    at_tick += pairs
    grad_normed = jnp.zeros((up_ref.shape[0], width), jnp.float32)
    for i, third in enumerate(thirds):
        in_loads[i].wait()
        grad_normed = grad_normed + dot_rows(mixed_ref[:, i * width : (i + 1) * width], third[...])
    unit, inverse = norm_parts(r.first_x[...].astype(jnp.float32))
    r.grad_tokens[...] = (
        up_ref[...] + norm_back(unit, inverse, r.first_gain[...], grad_normed)
    ).astype(jnp.bfloat16)
    small_send[0, 0:1] = jnp.sum(grad_normed * unit, axis=0, keepdims=True)
    small_send[0, 4:5] = jnp.sum(grad_normed, axis=0, keepdims=True)

    def small_copy(i):
        return pltpu.make_async_remote_copy(
            src_ref=small_send.at[i],
            dst_ref=small_recv.at[i],
            send_sem=small_send_sem.at[i],
            recv_sem=small_recv_sem.at[i],
            device_id=red.peer(*levels[i]),
            device_id_type=MESH,
        )

    small_copy(0).start()

    def rest(t, _):
        red.tick(t, at_tick, red.ticks)
        for i in range(1, len(levels) + 1):

            @pl.when(t == at_tick + i)
            def _(i=i):
                small_copy(i - 1).wait()
                value = small_send[i - 1] + small_recv[i - 1]
                if i < len(levels):
                    small_send[i] = value
                    small_copy(i).start()
                else:
                    r.small_sum[...] = value

        return 0

    lax.fori_loop(at_tick, red.ticks, rest, 0)
    red.finish()
    for h in range(pairs):
        do_spread.sent(h)
        aux_spread.sent(h)


def tail(n_dp, n_ex, collective_id, near, staged, far):
    arrays = {**near, **staged, **far}
    a = types.SimpleNamespace(**arrays)
    low, wide = jnp.bfloat16, jnp.float32
    tokens, width = a.up.shape
    hidden = a.dense_in.shape[1]
    mixed = a.attn_in.shape[2]
    rows = width // n_dp
    long, short, pairs = LONG_DEV, tokens - LONG_DEV, width // 128
    chunks = 2 * (hidden // width) + 2 * (1 + mixed // width)
    small = a.small.shape
    outs = dict(
        grad_tokens=jax.ShapeDtypeStruct((tokens, width), low),
        small_sum=jax.ShapeDtypeStruct(small, wide),
        chunks=jax.ShapeDtypeStruct((chunks, rows, width), low),
    )
    scratch = []
    for name in staged:
        scratch += [pltpu.VMEM(arrays[name].shape, arrays[name].dtype), pltpu.SemaphoreType.DMA]
    scratch += [pltpu.VMEM((2, width, width), low)] * 2
    scratch += [pltpu.VMEM((2, tokens, width), low), pltpu.SemaphoreType.DMA((2, 3))]
    scratch += [pltpu.SemaphoreType.DMA((4,))]
    scratch += [pltpu.VMEM((tokens, width), wide)] * 2
    scratch += [pltpu.VMEM((tokens, n), low) for n in (width, hidden, width, mixed)]
    scratch += back_scratch(n_dp, pairs, long, short)
    hops = (n_dp * n_ex).bit_length() - 1
    scratch += [pltpu.VMEM((hops,) + small, wide)] * 2 + [pltpu.SemaphoreType.DMA((hops,))] * 2
    scratch += Reduction.scratch(n_dp, n_ex, rows, width, dense_lanes(width))
    vmem, anywhere = pl.BlockSpec(memory_space=pltpu.VMEM), pl.BlockSpec(memory_space=pl.ANY)
    names = tuple(arrays) + tuple(outs)
    return pl.pallas_call(
        functools.partial(tail_kernel, n_dp, n_ex, names, tuple(staged)),
        out_shape=list(outs.values()),
        in_specs=[vmem] * len(near) + [anywhere] * (len(staged) + len(far)),
        out_specs=[vmem] * (len(outs) - 1) + [anywhere],
        scratch_shapes=scratch,
        compiler_params=pltpu.CompilerParams(
            collective_id=collective_id, has_side_effects=True, vmem_limit_bytes=61 * 1024 * 1024
        ),
        name="tail",
    )(*arrays.values())


def shards(
    tokens,
    doc_lengths,
    assign,
    ln_gain,
    ln_bias,
    attn_in,
    attn_out,
    ffn_in,
    ffn_out,
    router,
    expert_in,
    expert_out,
    cotangent,
):
    n_dp, n_ex = lax.axis_size("dp"), lax.axis_size("expert")
    row_count = tokens.shape[1]
    doc_ends = jnp.cumsum(doc_lengths[0, 0])
    short_place = jnp.arange(row_count - LONG_DEV, dtype=jnp.int32)
    short_ids = jnp.sum((short_place[:, None] >= doc_ends[None, :]).astype(jnp.int32), axis=-1)
    doc_row, doc_col = short_ids[None, :], short_ids[:, None]
    weights_in, weights_out = lax.optimization_barrier((attn_in.transpose(1, 0, 2), attn_out.transpose(1, 0, 2)))
    gains, shifts = ln_gain.T, ln_bias.T
    assign_row = assign[0].T
    fore = front(
        n_dp,
        n_ex,
        2,
        dict(
            tokens=tokens[0],
            gains=gains,
            shifts=shifts,
            doc_row=doc_row,
            doc_col=doc_col,
            assign=assign_row,
            cot=cotangent[0],
        ),
        dict(attn_in=weights_in, attn_out=weights_out, dense_in=ffn_in, dense_out=ffn_out),
    )
    model_width = tokens.shape[2]
    rows = model_width // n_dp
    mid = middle(
        n_dp,
        n_ex,
        4,
        dict(
            stream=fore.stream2,
            gain=gains[3:4],
            shift=shifts[3:4],
            router=router.T,
            assign=assign_row,
            cot=cotangent[0],
            far_cot=fore.far_cot,
            attn_gain=gains[2:3],
            doc_row=doc_row,
            doc_col=doc_col,
            lse=fore.lse1,
        ),
        dict(
            attn_x=fore.stream1,
            context=fore.context1,
            kv=fore.kv1,
            q=fore.q1,
            short_kv=fore.short_kv1,
            short_q=fore.short_q1,
        ),
        dict(
            expert_in=expert_in[0],
            expert_out=expert_out[0],
            attn_in=weights_in,
            attn_out=weights_out,
        ),
    )
    everyone = row_count * n_dp * n_ex
    stats = mid.stats
    balance = n_ex * jnp.sum((stats[:, 0] / everyone - 1.0 / n_ex) * (stats[:, 1] / everyone))
    output = mid.output[None]
    second_sums, fourth_sums = mid.attn_sums, mid.sums

    def blocks_of(rows_t):
        return rows_t.reshape(n_dp, -1, rows, row_count)

    none = jnp.zeros((2, model_width), jnp.float32)
    small = jnp.concatenate(
        [none, second_sums[0:1], fourth_sums[0:1], none, second_sums[1:2], fourth_sums[1:2], mid.router_grad], axis=0
    )
    grad_tokens, small, chunks = tail(
        n_dp,
        n_ex,
        5,
        dict(
            up=mid.up_next,
            dense_gain=gains[1:2],
            first_gain=gains[0:1],
            doc_row=doc_row,
            doc_col=doc_col,
            lse=fore.lse0,
            small=small,
        ),
        dict(
            dense_x=fore.stream0,
            first_x=tokens[0],
            context=fore.context0,
            kv=fore.kv0,
            q=fore.q0,
            short_kv=fore.short_kv0,
            short_q=fore.short_q0,
            second_context_t=blocks_of(fore.context_t1),
            second_normed_t=blocks_of(fore.normed_t1),
            active_t=blocks_of(fore.active_t),
            dense_normed_t=blocks_of(fore.dense_normed_t),
            first_context_t=blocks_of(fore.context_t0),
            first_normed_t=blocks_of(fore.normed_t0),
            second_low=mid.up_low,
            second_mixed=mid.mixed,
        ),
        dict(
            dense_in=ffn_in,
            dense_out=ffn_out,
            slope=fore.slope,
            attn_in=weights_in,
            attn_out=weights_out,
        ),
    )
    grad_tokens = grad_tokens[None]
    attn_in_sum, attn_out_sum, ffn_in_sum, ffn_out_sum, expert_in_sum, expert_out_sum = unpack(
        chunks, mid.chunks, attn_in.shape[2] // model_width, ffn_in.shape[1] // model_width
    )
    small = lax.dynamic_slice_in_dim(small, lax.axis_index("dp") * rows, rows, 1).T
    summed = [
        attn_in_sum,
        attn_out_sum,
        ffn_in_sum,
        ffn_out_sum.reshape(-1, model_width),
        small[:, 8:],
        small[:, :4],
        small[:, 4:8],
    ]
    return (
        output,
        balance,
        grad_tokens,
        summed[5],
        summed[6],
        summed[0],
        summed[1],
        summed[2],
        summed[3],
        summed[4],
        expert_in_sum[None],
        expert_out_sum.reshape(1, -1, model_width),
    )


def solution(mesh):
    return jax.shard_map(
        shards,
        mesh=mesh,
        in_specs=(
            P("expert", "dp", None),
            P("expert", "dp", None),
            P("expert", "dp", None),
            P(),
            P(),
            P(),
            P(),
            P(),
            P(),
            P(),
            P("expert", None, None),
            P("expert", None, None),
            P("expert", "dp", None),
        ),
        out_specs=(
            P("expert", "dp", None),
            P(),
            P("expert", "dp", None),
            P("dp", None),
            P("dp", None),
            P("dp", None, None),
            P("dp", None, None),
            P("dp", None),
            P("dp", None),
            P("dp", None),
            P("expert", "dp", None),
            P("expert", "dp", None),
        ),
        check_vma=False,
    )
```

```python
import functools
import types

import jax
import jax.numpy as jnp
from jax import lax
from jax.experimental import pallas as pl
from jax.experimental.pallas import tpu as pltpu
from jax.sharding import PartitionSpec as P

MESH = pl.DeviceIdType.MESH
HEADS = 12
HEAD_DIM = 64
LONG_DEV = 256


epsilon = 1e-05
balance_weight = 0.01
masked_score = -1e30


def bit_of(index, level):
    return (index // (1 << level)) % 2


def flip(index, level):
    return index + (1 << level) * (1 - 2 * bit_of(index, level))


def partner_index(index, mask, levels):
    total = 0
    for level in range(levels):
        own = bit_of(index, level)
        total = total + (1 << level) * (1 - own if (mask >> level) & 1 else own)
    return total


def unpack_kernel(
    per_in, per_ffn,
    chunk_ref, expert_ref, small_ref, tokens_ref, output_ref,
    in_ref, out_ref, ffn_in_ref, ffn_out_ref, expert_in_ref, expert_out_ref,
    gain_ref, shift_ref, router_ref, tokens_out_ref, output_out_ref,
):
    per_expert = expert_ref.shape[0] // 2
    width = chunk_ref.shape[2]
    at = 0
    for layer in (1, 0):
        out_ref[:, layer, :] = chunk_ref[at].astype(jnp.float32)
        for j in range(per_in):
            in_ref[:, layer, width * j : width * j + width] = chunk_ref[at + 1 + j].astype(jnp.float32)
        at += 1 + per_in
        if layer:
            for j in range(per_ffn):
                ffn_out_ref[j] = chunk_ref[at + j].astype(jnp.float32)
                ffn_in_ref[:, width * j : width * j + width] = chunk_ref[at + per_ffn + j].astype(jnp.float32)
            at += 2 * per_ffn
    for j in range(per_expert):
        expert_in_ref[:, width * j : width * j + width] = expert_ref[j].astype(jnp.float32)
        expert_out_ref[j] = expert_ref[per_expert + j].astype(jnp.float32)
    gain_ref[...] = small_ref[0:4]
    shift_ref[...] = small_ref[4:8]
    router_ref[...] = small_ref[8:]
    tokens_out_ref[...] = tokens_ref[...]
    output_out_ref[...] = output_ref[...]


def unpack(chunks, expert_chunks, small, grad_tokens, output, per_in, per_ffn):
    count, rows, width = chunks.shape
    experts = expert_chunks.shape[0]
    tokens = output.shape[0]
    step = 48 if rows % 48 == 0 else rows
    wide, low = jnp.float32, jnp.bfloat16
    token_spec = pl.BlockSpec((tokens // (rows // step), width), lambda i: (i, 0))

    def fixed(shape):
        return pl.BlockSpec(shape, lambda i: (0, 0))

    return pl.pallas_call(
        functools.partial(unpack_kernel, per_in, per_ffn),
        grid=(rows // step,),
        out_shape=[
            jax.ShapeDtypeStruct((rows, 2, per_in * width), wide),
            jax.ShapeDtypeStruct((rows, 2, width), wide),
            jax.ShapeDtypeStruct((rows, per_ffn * width), wide),
            jax.ShapeDtypeStruct((per_ffn, rows, width), wide),
            jax.ShapeDtypeStruct((rows, experts // 2 * width), wide),
            jax.ShapeDtypeStruct((experts // 2, rows, width), wide),
            jax.ShapeDtypeStruct((4, rows), wide),
            jax.ShapeDtypeStruct((4, rows), wide),
            jax.ShapeDtypeStruct((small.shape[0] - 8, rows), wide),
            jax.ShapeDtypeStruct((tokens, width), low),
            jax.ShapeDtypeStruct((tokens, width), low),
        ],
        in_specs=[
            pl.BlockSpec((count, step, width), lambda i: (0, i, 0)),
            pl.BlockSpec((experts, step, width), lambda i: (0, i, 0)),
            fixed(small.shape),
            token_spec,
            token_spec,
        ],
        out_specs=[
            pl.BlockSpec((step, 2, per_in * width), lambda i: (i, 0, 0)),
            pl.BlockSpec((step, 2, width), lambda i: (i, 0, 0)),
            pl.BlockSpec((step, per_ffn * width), lambda i: (i, 0)),
            pl.BlockSpec((per_ffn, step, width), lambda i: (0, i, 0)),
            pl.BlockSpec((step, experts // 2 * width), lambda i: (i, 0)),
            pl.BlockSpec((experts // 2, step, width), lambda i: (0, i, 0)),
            fixed((4, rows)),
            fixed((4, rows)),
            fixed((small.shape[0] - 8, rows)),
            token_spec,
            token_spec,
        ],
        compiler_params=pltpu.CompilerParams(vmem_limit_bytes=62 * 1024 * 1024),
        name="unpack",
    )(chunks, expert_chunks, small, grad_tokens, output)


def dot(a, b):
    return jnp.dot(a, b, preferred_element_type=jnp.float32)


def dot_rows(a, b):
    return lax.dot_general(a, b, (((1,), (1,)), ((), ())), preferred_element_type=jnp.float32)


def dot_columns(a, b):
    return lax.dot_general(a, b, (((0,), (0,)), ((), ())), preferred_element_type=jnp.float32)


def gelu_parts(hidden):
    lower = 0.5 + 0.5 * lax.erf(hidden * 0.7071067811865476)
    slope = lower + hidden * jnp.exp(-0.5 * hidden * hidden) * 0.3989422804014327
    return hidden * lower, slope


def split(value):
    high = value.astype(jnp.bfloat16)
    rest = value - high.astype(jnp.float32)
    middle_part = rest.astype(jnp.bfloat16)
    low = (rest - middle_part.astype(jnp.float32)).astype(jnp.bfloat16)
    return jnp.concatenate([high, middle_part, low], axis=0)


def norm_parts(x):
    center = x - jnp.mean(x, axis=-1, keepdims=True)
    inverse = lax.rsqrt(jnp.mean(center * center, axis=-1, keepdims=True) + epsilon)
    return center * inverse, inverse


def norm_back(unit, inverse, gain, upstream):
    scaled = upstream * gain
    return inverse * (
        scaled - jnp.mean(scaled, axis=-1, keepdims=True) - unit * jnp.mean(scaled * unit, axis=-1, keepdims=True)
    )


def capacity_of(rows, experts):
    capacity = (5 * rows + 4 * experts - 1) // (4 * experts)
    return capacity, -(-capacity // 16) * 16


def chosen_rows(assign, experts):
    expert = lax.broadcasted_iota(jnp.int32, (experts, assign.shape[1]), 0)
    return jnp.where(assign == expert, 1.0, 0.0)


def dispatch_of(assign, experts):
    tokens = assign.shape[1]
    capacity, padded = capacity_of(tokens, experts)
    hot = chosen_rows(assign, experts)
    earlier = lax.broadcasted_iota(jnp.int32, (tokens, tokens), 0) < lax.broadcasted_iota(jnp.int32, (tokens, tokens), 1)
    before = dot(hot.astype(jnp.bfloat16), jnp.where(earlier, 1.0, 0.0).astype(jnp.bfloat16))
    place = jnp.sum(hot * before, axis=0, keepdims=True)
    slot = jnp.where(place < capacity, assign.astype(jnp.float32) * padded + place, -1.0)
    number = lax.broadcasted_iota(jnp.int32, (experts * padded, tokens), 0).astype(jnp.float32)
    return jnp.where(number == slot, 1.0, 0.0).astype(jnp.bfloat16)


class Across:
    def __init__(self, experts, out, into, send_sems, recv_sems):
        self.experts, self.out, self.into = experts, out, into
        self.send_sems, self.recv_sems = send_sems, recv_sems
        self.dp, self.me = lax.axis_index("dp"), lax.axis_index("expert")

    def copy(self, slab, place, to):
        return pltpu.make_async_remote_copy(
            src_ref=self.out.at[slab],
            dst_ref=self.into.at[place],
            send_sem=self.send_sems.at[slab],
            recv_sem=self.recv_sems.at[place],
            device_id=(self.dp, to),
            device_id_type=MESH,
        )

    def start(self, j):
        self.copy(j, self.me, j).start()

    def wait_from(self, j):
        self.copy(j, j, j).wait_recv()

    def wait_to(self, j):
        self.copy(j, self.me, j).wait_send()

    def others(self, use):
        def body(k, _):
            use(lax.rem(self.me + k, self.experts))
            return 0

        lax.fori_loop(1, self.experts, body, 0)

    def start_all(self):
        self.others(self.start)

    def wait_all(self):
        def both(j):
            self.wait_from(j)
            self.wait_to(j)

        self.others(both)


def greet(targets):
    barrier = pltpu.get_barrier_semaphore()
    for device in targets:
        pl.semaphore_signal(barrier, inc=1, device_id=device, device_id_type=MESH)
    pl.semaphore_wait(barrier, len(targets))


def across_peers(experts):
    d, e = lax.axis_index("dp"), lax.axis_index("expert")
    return [(d, lax.rem(e + k, experts)) for k in range(1, experts)]


def head_pair(rows):
    first = lax.broadcasted_iota(jnp.int32, rows.shape, 1) < HEAD_DIM
    zero = jnp.zeros_like(rows)
    return jnp.concatenate([jnp.where(first, rows, zero), jnp.where(first, zero, rows)], axis=0)


def pair_rows(both):
    n = both.shape[1] // 2
    return jnp.concatenate([both[:HEAD_DIM, :n], both[HEAD_DIM:, n:]], axis=0)


def causal(keys, queries):
    key = lax.broadcasted_iota(jnp.int32, (keys, 2 * queries), 0)
    query = lax.broadcasted_iota(jnp.int32, (keys, 2 * queries), 1)
    return key <= jnp.where(query >= queries, query - queries, query)


def short_seen(doc_row):
    n = doc_row.shape[1]
    doc_col = jnp.broadcast_to(doc_row, (n, n)).T
    same = jnp.concatenate([doc_col, doc_col], axis=1) == jnp.concatenate([doc_row, doc_row], axis=1)
    return same & causal(n, n)


class Links:
    def __init__(self, n_dp):
        self.me, self.expert = lax.axis_index("dp"), lax.axis_index("expert")
        self.chips = n_dp // 2
        self.chip, self.core = self.me // 2, self.me % 2
        self.twin = self.me + 1 - 2 * self.core

    def peers(self):
        ring = [lax.rem(self.chip + k, self.chips) for k in range(1, self.chips)]
        return [(self.twin, self.expert)] + [(2 * other + self.core, self.expert) for other in ring]

    def copy(self, ref, send_sem, recv_sem, index):
        return pltpu.make_async_remote_copy(
            src_ref=ref,
            dst_ref=ref,
            send_sem=send_sem,
            recv_sem=recv_sem,
            device_id=(index, self.expert),
            device_id_type=MESH,
        )

    def before(self, later, other):
        return other > self.chip if later else other < self.chip


class Spread:
    def __init__(self, links, at, parts, later, far_sems, near_sems, recv_sems):
        self.links, self.at, self.later = links, at, later
        self.far_sems, self.near_sems, self.recv_sems = far_sems, near_sems, recv_sems

    def _far(self, other, p):
        k = self.links
        return k.copy(self.at(k.me, p), self.far_sems.at[other, p], self.recv_sems.at[k.me, p], 2 * other + k.core)

    def _near(self, block, p):
        k = self.links
        return k.copy(self.at(block, p), self.near_sems.at[block, p], self.recv_sems.at[block, p], k.twin)

    def _twin_needs(self):
        return self.links.core == (0 if self.later else 1)

    def send(self, p):
        k = self.links
        for other in range(k.chips):

            @pl.when(k.before(self.later, other))
            def _():
                self._far(other, p).start()

        @pl.when(self._twin_needs())
        def _():
            self._near(k.me, p).start()

    def sent(self, p):
        k = self.links
        for other in range(k.chips):

            @pl.when(k.before(self.later, other))
            def _():
                self._far(other, p).wait_send()

            @pl.when(k.before(not self.later, other))
            def _():
                self._near(2 * other + k.core, p).wait_send()

        @pl.when(self._twin_needs())
        def _():
            self._near(k.me, p).wait_send()

    def relay(self, p):
        k = self.links
        for other in range(k.chips):

            @pl.when(k.before(not self.later, other))
            def _():
                block = 2 * other + k.core
                copy = self._near(block, p)
                copy.wait_recv()
                copy.start()

    def each(self, p, use):
        k = self.links

        @pl.when(k.core == (1 if self.later else 0))
        def _():
            self._near(k.twin, p).wait_recv()
            use(k.twin)

        for other in range(k.chips):

            @pl.when(k.before(not self.later, other))
            def _():
                use(2 * other + k.core)
                block = 2 * other + 1 - k.core
                self._near(block, p).wait_recv()
                use(block)


def spread_sems(n_dp, parts):
    return [
        pltpu.SemaphoreType.DMA((n_dp // 2, parts)),
        pltpu.SemaphoreType.DMA((n_dp, parts)),
        pltpu.SemaphoreType.DMA((n_dp, parts)),
    ]


def attend(n_dp, links, s, x, gain, shift, w_in, w_out, doc_row, ready, between):
    me = links.me
    pairs, long, width = s.kv.shape[1], s.kv.shape[3], x.shape[1]
    unit, _ = norm_parts(x)
    normed = (unit * gain + shift).astype(jnp.bfloat16)
    ready(0)
    kv = dot(normed, w_in[:, width:]).astype(jnp.bfloat16)
    for h in range(pairs):
        for part in range(2):
            piece = kv[:, part * width + 128 * h : part * width + 128 * h + 128]
            s.kv[me, h, part] = piece[:long]
            s.short_kv[h, part] = piece[long:]
    kv_spread = Spread(links, lambda b, p: s.kv.at[b, p], pairs, True, *s.kv_sems)
    q_spread = Spread(links, lambda b, p: s.q.at[b], 1, False, *s.q_sems)
    for h in range(pairs):
        kv_spread.send(h)
    ready(1)
    q = (dot(normed, w_in[:, :width]).astype(jnp.bfloat16) * HEAD_DIM ** (-0.5)).astype(jnp.bfloat16)
    for h in range(pairs):
        piece = q[:, 128 * h : 128 * h + 128]
        s.q[me, h] = piece[:long]
        s.short_q[h] = piece[long:]
    q_spread.send(0)
    between()
    s.normed_t[...] = normed.T

    def put_context(h, rows_t, first, count):
        at = pl.ds(pl.multiple_of(128 * h, 128), 128)
        s.context_t[at, first : first + count] = rows_t.astype(jnp.bfloat16)
        s.context[first : first + count, at] = rows_t.T.astype(jnp.bfloat16)

    def own_part(h, _):
        seen = short_seen(doc_row)
        scores = jnp.where(seen, dot_rows(s.short_kv[h, 0], head_pair(s.short_q[h])), masked_score)
        top = jnp.max(scores, axis=0, keepdims=True)
        weights = jnp.exp(scores - top)
        total = jnp.sum(weights, axis=0, keepdims=True)
        rows_t = pair_rows(dot_columns(s.short_kv[h, 1], weights.astype(jnp.bfloat16)) / total)
        short = rows_t.shape[1]
        put_context(h, rows_t, long, short)
        lse = top + jnp.log(total)
        s.lse[h, 0:1, long:] = lse[:, :short]
        s.lse[h, 1:2, long:] = lse[:, short:]
        scores = jnp.where(causal(long, long), dot_rows(s.kv[me, h, 0], head_pair(s.q[me, h])), masked_score)
        top = jnp.max(scores, axis=0, keepdims=True)
        weights = jnp.exp(scores - top)
        s.top[h] = top
        s.total[h] = jnp.sum(weights, axis=0, keepdims=True)
        s.acc[h] = dot_columns(s.kv[me, h, 1], weights.astype(jnp.bfloat16))
        return 0

    lax.fori_loop(0, pairs, own_part, 0)

    def other_part(h, _):
        kv_spread.relay(h)
        queries = head_pair(s.q[me, h])

        def use(block):
            scores = dot_rows(s.kv[block, h, 0], queries)
            old = s.top[h]
            top = jnp.maximum(old, jnp.max(scores, axis=0, keepdims=True))
            factor = jnp.exp(old - top)
            weights = jnp.exp(scores - top)
            s.top[h] = top
            s.total[h] = s.total[h] * factor + jnp.sum(weights, axis=0, keepdims=True)
            s.acc[h] = s.acc[h] * factor + dot_columns(s.kv[block, h, 1], weights.astype(jnp.bfloat16))

        kv_spread.each(h, use)
        total = s.total[h]
        put_context(h, pair_rows(s.acc[h] / total), 0, long)
        lse = s.top[h] + jnp.log(total)
        s.lse[h, 0:1, :long] = lse[:, :long]
        s.lse[h, 1:2, :long] = lse[:, long:]
        return 0

    lax.fori_loop(0, pairs, other_part, 0)
    ready(2)
    following = x + dot(s.context[...], w_out[...])

    def settle():
        q_spread.relay(0)
        q_spread.each(0, lambda block: None)
        q_spread.sent(0)
        for h in range(pairs):
            kv_spread.sent(h)

    return following, settle


def front_kernel(n_dp, n_ex, names, saved, *refs):
    r = types.SimpleNamespace(**dict(zip(names, refs)))
    extra = iter(refs[len(names) :])
    buffers = []
    for layer in range(2):
        s = types.SimpleNamespace()
        for name in saved:
            setattr(s, name, next(extra))
        s.acc, s.top, s.total = next(extra), next(extra), next(extra)
        s.kv_sems = [next(extra) for _ in range(3)]
        s.q_sems = [next(extra) for _ in range(3)]
        s.stored = next(extra)
        buffers.append(s)
    w_in, w_out, w_sem, dense_in, dense_out, dense_sem = (next(extra) for _ in range(6))
    stream_ref, dense_normed, active_ref, slope_ref, dense_normed_t, far_cot = (next(extra) for _ in range(6))
    stored, cot_send, cot_send_sem, cot_recv_sem = (next(extra) for _ in range(4))
    links = Links(n_dp)
    tokens, width = r.tokens.shape
    blocks = r.dense_in.shape[1] // width
    low = jnp.bfloat16

    def block_loads(i):
        slot = lax.rem(i, 2)
        at = pl.ds(pl.multiple_of(i * width, width), width)
        return [
            pltpu.make_async_copy(r.dense_in.at[:, at], dense_in.at[slot], dense_sem.at[slot, 0]),
            pltpu.make_async_copy(r.dense_out.at[at, :], dense_out.at[slot], dense_sem.at[slot, 1]),
        ]

    def weight_loads(layer):
        return [
            pltpu.make_async_copy(
                r.attn_in.at[layer, :, pl.ds(width, 2 * width)], w_in.at[layer, :, pl.ds(width, 2 * width)], w_sem.at[layer, 0]
            ),
            pltpu.make_async_copy(
                r.attn_in.at[layer, :, pl.ds(0, width)], w_in.at[layer, :, pl.ds(0, width)], w_sem.at[layer, 1]
            ),
            pltpu.make_async_copy(r.attn_out.at[layer], w_out.at[layer], w_sem.at[layer, 2]),
        ]

    loads = [weight_loads(0), weight_loads(1)]
    for load in loads[0]:
        load.start()
    for i in range(min(2, blocks)):
        for load in block_loads(i):
            load.start()
    for load in loads[1]:
        load.start()
    greet(links.peers() + across_peers(n_ex))
    writes = []

    def write(source, target, sem):
        copy = pltpu.make_async_copy(source, target, sem)
        copy.start()
        writes.append(copy)

    def layer(number, x, between):
        s = buffers[number]
        column = 2 * number
        following, settle = attend(
            n_dp, links, s, x, r.gains[column : column + 1], r.shifts[column : column + 1], w_in.at[number], w_out.at[number],
            r.doc_row[...], lambda i: loads[number][i].wait(), between,
        )
        return following, settle

    def save(number, settle):
        s = buffers[number]
        settle()
        for i, name in enumerate(saved):
            write(getattr(s, name), getattr(r, name + str(number)), s.stored.at[i])

    x, settle = layer(0, r.tokens[...].astype(jnp.float32), lambda: None)
    r.stream0[...] = x
    stream_ref[...] = x
    unit, _ = norm_parts(x)
    normed = (unit * r.gains[1:2] + r.shifts[1:2]).astype(low)
    dense_normed[...] = normed
    save(0, settle)
    dense_normed_t[...] = normed.T

    def dense(i, _):
        slot = lax.rem(i, 2)
        for load in block_loads(i):
            load.wait()
        active, slope = gelu_parts(dot(dense_normed[...], dense_in[slot]))
        active = active.astype(low)
        at = pl.ds(pl.multiple_of(i * width, width), width)
        slope_ref[:, at] = slope.astype(low)
        active_ref[at, :] = active.T
        stream_ref[...] += dot(active, dense_out[slot])

        @pl.when(i + 2 < blocks)
        def _():
            for load in block_loads(i + 2):
                load.start()

        return 0

    lax.fori_loop(0, blocks, dense, 0)
    write(dense_normed_t, r.dense_normed_t, stored.at[0])
    write(active_ref, r.active_t, stored.at[1])
    write(slope_ref, r.slope, stored.at[2])
    x = stream_ref[...]
    r.stream1[...] = x

    cot_across = Across(n_ex, cot_send, far_cot, cot_send_sem, cot_recv_sem)

    def send_cotangent():
        cot_send[...] = dot(dispatch_of(r.assign[...], n_ex), r.cot[...]).astype(low).reshape(cot_send.shape)
        cot_across.start_all()
        far_cot[links.expert] = cot_send[links.expert]

    x, settle = layer(1, x, send_cotangent)
    r.stream2[...] = x
    save(1, settle)
    cot_across.wait_all()
    write(far_cot, r.far_cot, stored.at[3])
    for copy in writes:
        copy.wait()


def front(n_dp, n_ex, collective_id, near, far):
    arrays = {**near, **far}
    a = types.SimpleNamespace(**arrays)
    low, wide = jnp.bfloat16, jnp.float32
    tokens, width = a.tokens.shape
    hidden, mixed = a.dense_in.shape[1], a.attn_in.shape[2]
    long, short, pairs = LONG_DEV, tokens - LONG_DEV, width // 128
    slab = (n_ex, capacity_of(tokens, n_ex)[1], width)
    saved = dict(
        normed_t=jax.ShapeDtypeStruct((width, tokens), low),
        context=jax.ShapeDtypeStruct((tokens, width), low),
        context_t=jax.ShapeDtypeStruct((width, tokens), low),
        kv=jax.ShapeDtypeStruct((n_dp, pairs, 2, long, 128), low),
        q=jax.ShapeDtypeStruct((n_dp, pairs, long, 128), low),
        short_kv=jax.ShapeDtypeStruct((pairs, 2, short, 128), low),
        short_q=jax.ShapeDtypeStruct((pairs, short, 128), low),
        lse=jax.ShapeDtypeStruct((pairs, 2, tokens), wide),
    )
    stream = jax.ShapeDtypeStruct((tokens, width), wide)
    outs = dict(stream0=stream, stream1=stream, stream2=stream)
    direct = len(outs)
    for layer in range(2):
        for name, shape in saved.items():
            outs[name + str(layer)] = shape
    outs.update(
        dense_normed_t=jax.ShapeDtypeStruct((width, tokens), low),
        active_t=jax.ShapeDtypeStruct((hidden, tokens), low),
        slope=jax.ShapeDtypeStruct((tokens, hidden), low),
        far_cot=jax.ShapeDtypeStruct(slab, low),
    )
    scratch = []
    for layer in range(2):
        scratch += [pltpu.VMEM(shape.shape, shape.dtype) for shape in saved.values()]
        scratch += [
            pltpu.VMEM((pairs, 128, 2 * long), wide),
            pltpu.VMEM((pairs, 1, 2 * long), wide),
            pltpu.VMEM((pairs, 1, 2 * long), wide),
        ]
        scratch += spread_sems(n_dp, pairs) + spread_sems(n_dp, 1)
        scratch += [pltpu.SemaphoreType.DMA((len(saved),))]
    scratch += [pltpu.VMEM((2, width, mixed), low), pltpu.VMEM((2, width, width), low), pltpu.SemaphoreType.DMA((2, 3))]
    scratch += [pltpu.VMEM((2, width, width), low)] * 2 + [pltpu.SemaphoreType.DMA((2, 2))]
    scratch += [
        pltpu.VMEM((tokens, width), wide),
        pltpu.VMEM((tokens, width), low),
        pltpu.VMEM((hidden, tokens), low),
        pltpu.VMEM((tokens, hidden), low),
        pltpu.VMEM((width, tokens), low),
        pltpu.VMEM(slab, low),
        pltpu.SemaphoreType.DMA((4,)),
        pltpu.VMEM(slab, low),
        pltpu.SemaphoreType.DMA((n_ex,)),
        pltpu.SemaphoreType.DMA((n_ex,)),
    ]
    vmem, anywhere = pl.BlockSpec(memory_space=pltpu.VMEM), pl.BlockSpec(memory_space=pl.ANY)
    names = tuple(arrays) + tuple(outs)
    values = pl.pallas_call(
        functools.partial(front_kernel, n_dp, n_ex, names, tuple(saved)),
        out_shape=list(outs.values()),
        in_specs=[vmem] * len(near) + [anywhere] * len(far),
        out_specs=[vmem] * direct + [anywhere] * (len(outs) - direct),
        scratch_shapes=scratch,
        compiler_params=pltpu.CompilerParams(
            collective_id=collective_id, has_side_effects=True, vmem_limit_bytes=62 * 1024 * 1024
        ),
        name="front",
    )(*arrays.values())
    return types.SimpleNamespace(**dict(zip(outs, values)))


def runs(most, count, use):
    for first in range(0, most, 3):
        for size in range(1, min(3, most - first) + 1):
            exactly = count - first == size if size < 3 else count - first >= size

            @pl.when(exactly)
            def _():
                use(first, size)


def put_context_grads(grad_context, do_ref, short_do_ref, me, long):
    for h in range(do_ref.shape[1]):
        piece = grad_context[:, 128 * h : 128 * h + 128]
        do_ref[me, h] = piece[:long]
        short_do_ref[h] = piece[long:]


def put_row_terms(context, lse, grad_context, aux_ref, short_aux_ref, me, long):
    width = grad_context.shape[1]
    rows = (width // HEAD_DIM + 15) // 16 * 16
    lane = lax.broadcasted_iota(jnp.int32, (rows, width), 1)
    head = lax.broadcasted_iota(jnp.int32, (rows, width), 0) * HEAD_DIM
    picks = jnp.where((lane >= head) & (lane < head + HEAD_DIM), 1.0, 0.0).astype(jnp.bfloat16)
    both = grad_context.astype(jnp.float32) * context[...].astype(jnp.float32)
    high = both.astype(jnp.bfloat16)
    delta = dot_rows(picks, high) + dot_rows(picks, (both - high.astype(jnp.float32)).astype(jnp.bfloat16))
    for h in range(aux_ref.shape[1]):
        aux_ref[me, h, 0:2] = lse[h, :, :long]
        aux_ref[me, h, 2:4] = delta[2 * h : 2 * h + 2, :long]
        short_aux_ref[h, 0:2] = lse[h, :, long:]
        short_aux_ref[h, 2:4] = delta[2 * h : 2 * h + 2, long:]


def attend_back_pair(n_dp, me, width, r, do_spread, aux_spread, h):
    scale = HEAD_DIM ** (-0.5)
    mixed_ref = r.mixed
    long = r.kv.shape[3]

    def row_of(aux):
        return [jnp.concatenate([aux[i : i + 1], aux[i + 1 : i + 2]], axis=1) for i in (0, 2)]

    def score_grads(keys, values, queries, grads, rows, seen):
        scores = dot_rows(keys, queries)
        probs = jnp.exp(scores - rows[0])
        if seen is not None:
            probs = jnp.where(seen, probs, 0.0)
        grad_scores = probs * (dot_rows(values, grads) - rows[1])
        return probs.astype(jnp.bfloat16), grad_scores.astype(jnp.bfloat16)

    def put(third, first, value):
        at = pl.ds(pl.multiple_of(third * width + 128 * h, 128), 128)
        mixed_ref[first : first + value.shape[0], at] = value.astype(jnp.bfloat16)

    seen = short_seen(r.doc_row[...])
    queries, grads = head_pair(r.short_q[h]), head_pair(r.short_do[h])
    keys = r.short_kv[h, 0]
    probs, grad_scores = score_grads(keys, r.short_kv[h, 1], queries, grads, row_of(r.short_aux[h]), seen)
    put(0, long, (pair_rows(dot_columns(keys, grad_scores)) * scale).T)
    put(1, long, dot(grad_scores, queries))
    put(2, long, dot(probs, grads))
    queries, grads = head_pair(r.q[me, h]), head_pair(r.do[me, h])
    own_keys, own_values = r.kv[me, h, 0], r.kv[me, h, 1]
    probs, grad_scores = score_grads(own_keys, own_values, queries, grads, row_of(r.aux[me, h]), causal(long, long))
    r.dq[...] = dot_columns(own_keys, grad_scores)
    r.dk[...] = dot(grad_scores, queries)
    r.dv[...] = dot(probs, grads)

    def earlier(first, size):
        at = pl.ds(first, size)
        keys = r.kv[at, h, 0].reshape(size * long, 128)
        values = r.kv[at, h, 1].reshape(size * long, 128)
        _, grad_scores = score_grads(keys, values, queries, grads, row_of(r.aux[me, h]), None)
        r.dq[...] += dot_columns(keys, grad_scores)

    runs(n_dp - 1, me, earlier)
    put(0, 0, (pair_rows(r.dq[...]) * scale).T)
    do_spread.relay(h)
    aux_spread.relay(h)

    def later(first, size):
        blocks = [me + 1 + first + i for i in range(size)]
        queries = jnp.concatenate([head_pair(r.q[block, h]) for block in blocks], axis=0)
        grads = jnp.concatenate([head_pair(r.do[block, h]) for block in blocks], axis=0)
        rows = [row_of(r.aux[block, h]) for block in blocks]
        rows = [jnp.concatenate([row[i] for row in rows], axis=1) for i in range(2)]
        probs, grad_scores = score_grads(own_keys, own_values, queries, grads, rows, None)
        r.dk[...] += dot(grad_scores, queries)
        r.dv[...] += dot(probs, grads)

    aux_spread.each(h, lambda block: None)
    do_spread.each(h, lambda block: None)
    runs(n_dp - 1, n_dp - 1 - me, later)
    put(1, 0, r.dk[...])
    put(2, 0, r.dv[...])


def back_scratch(n_dp, pairs, long, short):
    return (
        [
            pltpu.VMEM((n_dp, pairs, long, 128), jnp.bfloat16),
            pltpu.VMEM((n_dp, pairs, 8, long), jnp.float32),
            pltpu.VMEM((pairs, short, 128), jnp.bfloat16),
            pltpu.VMEM((pairs, 8, short), jnp.float32),
            pltpu.VMEM((128, 2 * long), jnp.float32),
            pltpu.VMEM((long, 128), jnp.float32),
            pltpu.VMEM((long, 128), jnp.float32),
        ]
        + spread_sems(n_dp, pairs)
        + spread_sems(n_dp, pairs)
    )


def lane_plan(n_dp, n_ex, rows, order):
    dp_levels = [("dp", b) for b in range(n_dp.bit_length() - 1)]
    ex_levels = n_ex.bit_length() - 1
    halved, piece = [], rows
    for level in ((0, 1), (1, 0))[order]:
        if level < ex_levels and piece % 32 == 0:
            halved.append(level)
            piece //= 2
    halves = [("half", b) for b in halved]
    if order:
        kinds = dp_levels[:1] + halves[:1] + dp_levels[1:] + halves[1:]
    else:
        kinds = dp_levels + halves
    kinds += [("both", b) for b in range(ex_levels) if b not in halved]
    kinds += [("back", b) for b in reversed(halved)]
    return kinds, halved


class Lane:
    def __init__(self, n_dp, n_ex, rows, columns, order, refs):
        self.rows, self.columns = rows, columns
        self.kinds, self.halved = lane_plan(n_dp, n_ex, rows, order)
        self.count = len(self.kinds)
        moving = [k[0] != "back" for k in self.kinds]
        self.send = [next(refs) if m else None for m in moving]
        self.recv = [next(refs) if m else None for m in moving]
        self.keep = [next(refs) if m else None for m in moving]
        self.fin = next(refs)
        self.send_sems = [next(refs) for _ in moving]
        self.recv_sems = [next(refs) for _ in moving]
        self.d, self.e = lax.axis_index("dp"), lax.axis_index("expert")

    @staticmethod
    def scratch(n_dp, n_ex, rows, columns, order):
        kinds, halved = lane_plan(n_dp, n_ex, rows, order)
        width, pieces, height, shapes = columns[1] - columns[0], n_dp, rows, []
        for kind, _ in kinds:
            if kind == "dp":
                pieces //= 2
            elif kind == "half":
                height //= 2
            if kind != "back":
                shapes.append((pieces, height, width))
        scratch = [pltpu.VMEM((2,) + s, jnp.bfloat16) for s in shapes]
        scratch += [pltpu.VMEM((4,) + s, jnp.bfloat16) for s in shapes]
        scratch += [pltpu.VMEM((2,) + s, jnp.float32) for s in shapes]
        scratch += [pltpu.VMEM((len(halved) + 3, rows, width) if halved else (1, 16, 128), jnp.bfloat16)]
        return scratch + [pltpu.SemaphoreType.DMA((4,)) for _ in kinds] * 2

    def peer(self, kind, level):
        return (flip(self.d, level), self.e) if kind == "dp" else (self.d, flip(self.e, level))

    def kept_rows(self, depth):
        start = 0
        for i, level in enumerate(self.halved[:depth]):
            start = start + bit_of(self.e, level) * (self.rows >> (i + 1))
        return start

    def copy_of(self, s, c):
        kind, level = self.kinds[s]
        slot, place = lax.rem(c, 2), lax.rem(c, 4)
        if kind == "back":
            depth = self.halved.index(level) + 1
            span = self.rows >> depth
            at = pl.ds(pl.multiple_of(self.kept_rows(depth), span), span)
            src = self.fin.at[lax.rem(c, len(self.halved) + 3), at]
            dst = src
        else:
            src, dst = self.send[s].at[slot], self.recv[s].at[place]
        return pltpu.make_async_remote_copy(
            src_ref=src,
            dst_ref=dst,
            send_sem=self.send_sems[s].at[place],
            recv_sem=self.recv_sems[s].at[place],
            device_id=self.peer(kind, level),
            device_id_type=MESH,
        )

    def arrive(self, s, c):
        self.copy_of(s, c).wait()
        slot, place = lax.rem(c, 2), lax.rem(c, 4)
        if self.kinds[s][0] == "back":
            return None
        return [
            self.keep[s][slot, i] + self.recv[s][place, i].astype(jnp.float32) for i in range(self.keep[s].shape[1])
        ]

    def leave(self, s, c, values):
        kind, level = self.kinds[s]
        slot = lax.rem(c, 2)
        kept = None
        if kind == "dp":
            sent, kept = values[1::2], values[0::2]
        elif kind == "half":
            half = values[0].shape[0] // 2
            own = bit_of(self.e, level)
            sent = [jnp.where(own == 0, v[half:], v[:half]) for v in values]
            kept = [jnp.where(own == 0, v[:half], v[half:]) for v in values]
        elif kind == "both":
            sent = values
            kept = [v.astype(jnp.bfloat16).astype(jnp.float32) for v in values]
        elif values is not None:
            span = values[0].shape[0]
            at = pl.ds(pl.multiple_of(self.kept_rows(len(self.halved)), span), span)
            self.fin[lax.rem(c, len(self.halved) + 3), at] = values[0].astype(jnp.bfloat16)
        if kept is not None:
            for i, v in enumerate(sent):
                self.send[s][slot, i] = v.astype(jnp.bfloat16)
        self.copy_of(s, c).start()
        if kept is not None:
            for i, v in enumerate(kept):
                self.keep[s][slot, i] = v

    def final(self, c):
        values = self.arrive(self.count - 1, c)
        if values is None:
            return self.fin[lax.rem(c, len(self.halved) + 3)]
        return values[0].astype(jnp.bfloat16)


class Reduction:
    def __init__(self, n_dp, n_ex, rows, groups, lanes, refs, out):
        self.n_dp, self.rows, self.groups = n_dp, rows, groups
        self.lanes = [Lane(n_dp, n_ex, rows, columns, order, refs) for columns, order in lanes]
        self.stage_ref, self.stage_sem, self.out = next(refs), next(refs), out
        self.count = self.lanes[0].count
        self.chunks = sum(g[0] for g in groups)
        self.firsts = [sum(g[0] for g in groups[:i]) for i in range(len(groups))]
        self.ticks = self.chunks + self.count
        self.d = lax.axis_index("dp")
        self.peer = self.lanes[0].peer

    @staticmethod
    def scratch(n_dp, n_ex, rows, width, lanes):
        scratch = []
        for columns, order in lanes:
            scratch += Lane.scratch(n_dp, n_ex, rows, columns, order)
        return scratch + [pltpu.VMEM((2, rows, width), jnp.bfloat16), pltpu.SemaphoreType.DMA((2,))]

    def out_copy(self, c):
        slot = lax.rem(c, 2)
        return pltpu.make_async_copy(self.stage_ref.at[slot], self.out.at[c], self.stage_sem.at[slot])

    def first(self, g, c):
        _, piece, factor = self.groups[g]
        j = c - self.firsts[g]
        dy = factor(j)
        slot = lax.rem(c, 2)
        levels = self.n_dp.bit_length() - 1
        half = self.n_dp // 2

        def products(odd):
            parts = [piece(j, partner_index(self.d, 2 * i + odd, levels)) for i in range(half)]
            return dot(jnp.concatenate(parts, axis=0), dy)

        value = products(1)
        for lane in self.lanes:
            for i in range(half):
                part = value[i * self.rows : (i + 1) * self.rows, slice(*lane.columns)]
                lane.send[0][slot, i] = part.astype(jnp.bfloat16)
            lane.copy_of(0, c).start()
        value = products(0)
        for lane in self.lanes:
            for i in range(half):
                lane.keep[0][slot, i] = value[i * self.rows : (i + 1) * self.rows, slice(*lane.columns)]

    def last(self, c):
        slot = lax.rem(c, 2)

        @pl.when(c >= 2)
        def _():
            self.out_copy(c - 2).wait()

        for lane in self.lanes:
            self.stage_ref[slot, :, slice(*lane.columns)] = lane.final(c)
        self.out_copy(c).start()

    def tick(self, t, low, high):
        for s in range(self.count + 1):
            if high - s <= 0 or low - s >= self.chunks:
                continue
            c = t - s
            if s > 0:

                @pl.when((c >= 0) & (c < self.chunks))
                def _(s=s, c=c):
                    if s < self.count:
                        for lane in self.lanes:
                            lane.leave(s, c, lane.arrive(s - 1, c))
                    else:
                        self.last(c)

                continue
            for g, (size, _, _) in enumerate(self.groups):
                begin, end = self.firsts[g], self.firsts[g] + size
                if high <= begin or low >= end:
                    continue

                @pl.when((c >= begin) & (c < end))
                def _(g=g):
                    self.first(g, c)

    def finish(self):
        for c in range(max(0, self.chunks - 2), self.chunks):
            self.out_copy(c).wait()


def dense_lanes(width):
    cut = width // 768 * 640
    return [((0, cut), 0), ((cut, width), 1)]


def middle_kernel(n_dp, n_ex, names, staged, *refs):
    r = types.SimpleNamespace(**dict(zip(names, refs)))
    extra = iter(refs[len(names) :])
    loads = types.SimpleNamespace()
    for name in staged:
        buffer, sem = next(extra), next(extra)
        setattr(loads, name, pltpu.make_async_copy(getattr(r, name), buffer, sem))
        setattr(r, name, buffer)
    w_in_ref, w_out_ref, weight_sem, factor_sem = (next(extra) for _ in range(4))
    rows_ref, send_ref, grad_ref, home_ref, result_ref = (next(extra) for _ in range(5))
    rows_t_ref, back_ref, active_t_ref, hidden_ref = (next(extra) for _ in range(4))
    dgate_ref, home_dgate_ref, stat_send, stat_recv, result_acc, grad_acc = (next(extra) for _ in range(6))
    (
        x_send_sem, x_recv_sem, grad_send_sem, grad_recv_sem, dgate_send_sem, dgate_recv_sem,
        result_send_sem, result_recv_sem, stat_send_sem, stat_recv_sem,
    ) = (next(extra) for _ in range(10))
    do_ref, aux_ref, short_do_ref, short_aux_ref, dq_ref, dk_ref, dv_ref = (next(extra) for _ in range(7))
    do_far, do_near, do_recv, aux_far, aux_near, aux_recv = (next(extra) for _ in range(6))
    links = Links(n_dp)
    d, e, me = links.me, links.expert, links.me
    shared = links.chips == 2
    if shared:
        peer_rows_ref, peer_cot_ref, peer_row_sems, peer_cot_sems = (next(extra) for _ in range(4))
    dp_levels, ex_levels = n_dp.bit_length() - 1, n_ex.bit_length() - 1
    tokens, width = r.stream.shape
    padded = send_ref.shape[1]
    blocks = r.expert_in.shape[1] // width
    pairs, long = r.kv.shape[1], r.kv.shape[3]
    group = min(max(4, 128 // padded), n_ex)
    groups = n_ex // group
    hops = [(flip(d, b), e) for b in range(dp_levels)] + [(d, flip(e, b)) for b in range(ex_levels)]

    def column(i):
        return pl.ds(i * width, width)

    expert_loads = [
        (
            pltpu.make_async_copy(r.expert_in.at[:, column(i)], w_in_ref.at[i], weight_sem.at[0, i]),
            pltpu.make_async_copy(r.expert_out.at[column(i), :], w_out_ref.at[i], weight_sem.at[1, i]),
        )
        for i in range(blocks)
    ]
    for both in expert_loads:
        for load in both:
            load.start()
    for name in staged:
        getattr(loads, name).start()
    greet(links.peers() + across_peers(n_ex))

    def peer_copy(source, target, sems):
        return pltpu.make_async_remote_copy(
            src_ref=source,
            dst_ref=target,
            send_sem=sems.at[0],
            recv_sem=sems.at[1],
            device_id=(flip(d, 1), e),
            device_id_type=MESH,
        )

    def row_copy(j):
        return peer_copy(rows_ref.at[j], peer_rows_ref.at[j], peer_row_sems.at[j])

    if shared:
        cot_copy = peer_copy(r.far_cot, peer_cot_ref, peer_cot_sems)
        cot_copy.start()

    unit, inverse = norm_parts(r.stream[...])
    routed = (unit * r.gains[3:4] + r.shifts[3:4]).astype(jnp.bfloat16)
    assign = r.assign[...]
    dispatch = dispatch_of(assign, n_ex)
    r.dispatch[...] = dispatch
    send_ref[...] = dot(dispatch, routed).astype(jnp.bfloat16).reshape(send_ref.shape)
    x_across = Across(n_ex, send_ref, rows_ref, x_send_sem, x_recv_sem)

    def place(k, i):
        return lax.rem(e // group + k, groups) * group + lax.rem(e + i, group)

    def source(k, i):
        return lax.rem(e // group + k, groups) * group + lax.rem(e + group - i, group)

    for i in range(group):
        if i:
            x_across.start(place(0, i))
        for k in range(1, groups):
            x_across.start(place(k, i))
    rows_ref[e] = send_ref[e]
    router = r.router[...]
    hot = chosen_rows(assign, n_ex)
    gate = jax.nn.sigmoid(jnp.sum(hot * dot_rows(router, routed), axis=0, keepdims=True))
    r.gate[...] = gate

    def stat_copy(i):
        return pltpu.make_async_remote_copy(
            src_ref=stat_send.at[i],
            dst_ref=stat_recv.at[i],
            send_sem=stat_send_sem.at[i],
            recv_sem=stat_recv_sem.at[i],
            device_id=hops[i],
            device_id_type=MESH,
        )

    lane = lax.broadcasted_iota(jnp.int32, r.stats.shape, 1)
    stat_send[0] = jnp.where(
        lane == 0, jnp.sum(hot, axis=1, keepdims=True), jnp.sum(hot * gate, axis=1, keepdims=True)
    )
    stat_copy(0).start()

    def stat_step(i):
        stat_copy(i).wait()
        value = stat_send[i] + stat_recv[i]
        if i + 1 < len(hops):
            stat_send[i + 1] = value
            stat_copy(i + 1).start()
        else:
            r.stats[...] = value

    grad_across = Across(n_ex, grad_ref, home_ref, grad_send_sem, grad_recv_sem)
    dgate_across = Across(n_ex, dgate_ref, home_dgate_ref, dgate_send_sem, dgate_recv_sem)
    steps = [[(0, i) for i in range(group)]]
    cut = group // 2 if (group // 2) * padded % 128 == 0 else group
    for k in range(1, groups):
        steps += [[(k, i) for i in range(first, first + cut)] for first in range(0, group, cut)]
    def expert_rows(rows, cot, at, whole):
        count = rows.shape[0]
        logits = dot_rows(rows, router)
        own = lax.broadcasted_iota(jnp.int32, logits.shape, 1) == e
        slot_gate = jax.nn.sigmoid(jnp.sum(jnp.where(own, logits, 0.0), axis=1, keepdims=True))
        back = (slot_gate * cot).astype(jnp.bfloat16)
        span = slice(at, at + count)
        back_ref[span] = back
        rows_t_ref[:, span] = rows.T
        if whole:
            result_acc[:count] = jnp.zeros((count, width), jnp.float32)
            grad_acc[:count] = jnp.zeros((count, width), jnp.float32)

        def block(i, _):
            cols = pl.ds(pl.multiple_of(i * width, width), width)
            active, slope = gelu_parts(dot(rows, w_in_ref[i]))
            active = active.astype(jnp.bfloat16)
            hidden = (slope * dot_rows(back, w_out_ref[i])).astype(jnp.bfloat16)
            active_t_ref[cols, span] = active.T
            hidden_ref[span, cols] = hidden
            if whole:
                result_acc[:count] += dot(active, w_out_ref[i])
                grad_acc[:count] += dot_rows(hidden, w_in_ref[i])
            return 0

        lax.fori_loop(0, blocks, block, 0)

    done, at = 0, 0
    for number, members in enumerate(steps):
        count = len(members) * padded
        sources = [source(k, i) for k, i in members]
        for (k, i), j in zip(members, sources):
            if (k, i) != (0, 0):
                x_across.wait_from(j)
            if shared:
                row_copy(j).start()
        rows = jnp.concatenate([rows_ref[j] for j in sources], axis=0)
        cot = jnp.concatenate([r.far_cot[j] for j in sources], axis=0).astype(jnp.float32)
        if number == 0:
            for both in expert_loads:
                for load in both:
                    load.wait()
        expert_rows(rows, cot, at, True)
        grad = grad_acc[:count].astype(jnp.bfloat16)
        result = result_acc[:count].astype(jnp.bfloat16)
        both = cot * result.astype(jnp.float32)
        high = both.astype(jnp.bfloat16)
        rest = both - high.astype(jnp.float32)
        ones = jnp.ones((16, width), jnp.bfloat16)
        dgate = dot_rows(ones, high) + dot_rows(ones, rest.astype(jnp.bfloat16))
        for m, (k, i) in enumerate(members):
            j, part = sources[m], slice(m * padded, (m + 1) * padded)
            grad_ref[j] = grad[part]
            result_ref[j] = result[part]
            dgate_ref[j, :, :padded] = dgate[:8, part]
            if (k, i) == (0, 0):
                home_ref[e] = grad_ref[e]
                home_dgate_ref[e] = dgate_ref[e]
            else:
                grad_across.start(j)
                dgate_across.start(j)
        at += count
        if done < len(hops):
            stat_step(done)
            done += 1

    if shared:
        cot_copy.wait()
        for k in range(groups):
            sources = [source(k, i) for i in range(group)]
            for j in sources:
                row_copy(j).wait()
            rows = jnp.concatenate([peer_rows_ref[j] for j in sources], axis=0)
            cot = jnp.concatenate([peer_cot_ref[j] for j in sources], axis=0).astype(jnp.float32)
            expert_rows(rows, cot, at, False)
            at += group * padded
            if done < len(hops):
                stat_step(done)
                done += 1

    thirds = [w_in_ref.at[i] for i in range(3)]
    in_loads = [
        pltpu.make_async_copy(r.attn_in.at[1, :, column(i)], third, weight_sem.at[0, i])
        for i, third in enumerate(thirds)
    ]
    out_load = pltpu.make_async_copy(r.attn_out.at[1], w_out_ref.at[0], weight_sem.at[1, 0])
    for load in in_loads + [out_load]:
        load.start()
    rows = width // n_dp

    def rows_of(ref, j, q):
        return ref[pl.ds(pl.multiple_of((q * (ref.shape[0] // width) + j) * rows, rows), rows), :]

    red, writes = None, []
    if shared:
        factors = ((rows_t_ref, r.rows_t), (back_ref, r.back), (active_t_ref, r.expert_active_t), (hidden_ref, r.expert_hidden))
        writes = [pltpu.make_async_copy(here, there, factor_sem.at[i]) for i, (here, there) in enumerate(factors)]
        for write in writes:
            write.start()
    else:
        factors = [
            (blocks, lambda j, q: rows_of(rows_t_ref, 0, q), lambda j: hidden_ref[:, pl.ds(pl.multiple_of(j * width, width), width)]),
            (blocks, lambda j, q: rows_of(active_t_ref, j, q), lambda j: back_ref[...]),
        ]
        red = Reduction(n_dp, 1, rows, factors, [((0, width), 0)], extra, r.chunks)
    early = 0
    if red:
        red.tick(0, 0, 1)
        early = 1
    while done < len(hops):
        stat_step(done)
        done += 1
    x_across.others(x_across.wait_to)
    if red:
        red.tick(1, 1, 2)
        early = 2
    dgate_across.wait_all()
    slot_grads = jnp.concatenate([home_dgate_ref[j, :, :padded] for j in range(n_ex)], axis=1)
    dgate = dot(split(slot_grads), r.dispatch[...])
    dgate = dgate[0:8] + dgate[8:16] + dgate[16:24]
    everyone = tokens * n_dp * n_ex
    share = jnp.sum(jnp.where(lane == 0, r.stats[...], 0.0), axis=1, keepdims=True) / everyone
    weight = balance_weight * n_ex * (share - 1.0 / n_ex) / everyone
    mean_gate = jnp.sum(jnp.where(lane == 1, r.stats[...], 0.0), axis=1, keepdims=True) / everyone
    balance = n_ex * jnp.sum((share - 1.0 / n_ex) * mean_gate, axis=0, keepdims=True)
    r.balance[...] = jnp.broadcast_to(balance, r.balance.shape)
    grad_gate = dgate[0:1] + jnp.sum(hot * weight, axis=0, keepdims=True)
    grad_logits = hot * (grad_gate * gate * (1.0 - gate))
    parts = split(grad_logits)
    product = dot(parts, routed)
    r.router_grad[...] = product[:n_ex] + product[n_ex : 2 * n_ex] + product[2 * n_ex :]
    grad_normed = dot_columns(parts, jnp.concatenate([router] * 3, axis=0))
    if red:
        red.tick(2, 2, 3)
        early = 3
    grad_across.wait_all()
    grad_normed = grad_normed + dot_columns(r.dispatch[...], home_ref[...].reshape(n_ex * padded, width))
    unit, inverse = norm_parts(r.stream[...])
    up = r.cot[...].astype(jnp.float32) + norm_back(unit, inverse, r.gains[3:4], grad_normed)
    r.sums[0:1] = jnp.sum(grad_normed * unit, axis=0, keepdims=True)
    r.sums[1:2] = jnp.sum(grad_normed, axis=0, keepdims=True)

    r.up_next[...] = up
    up_low = up.astype(jnp.bfloat16)
    r.up_low[...] = up_low
    out_load.wait()
    for name in staged:
        getattr(loads, name).wait()
    grad_context = dot_rows(up_low, w_out_ref[0]).astype(jnp.bfloat16)
    put_context_grads(grad_context, do_ref, short_do_ref, me, long)
    do_spread = Spread(links, lambda b, p: do_ref.at[b, p], pairs, False, do_far, do_near, do_recv)
    aux_spread = Spread(links, lambda b, p: aux_ref.at[b, p], pairs, False, aux_far, aux_near, aux_recv)
    put_row_terms(r.context, r.lse, grad_context, aux_ref, short_aux_ref, me, long)
    for h in range(pairs):
        do_spread.send(h)
        aux_spread.send(h)
    result_across = Across(n_ex, result_ref, r.result_home, result_send_sem, result_recv_sem)
    result_across.start_all()
    r.result_home[e] = result_ref[e]
    sequence = types.SimpleNamespace(
        doc_row=r.doc_row, kv=r.kv, q=r.q, short_kv=r.short_kv, short_q=r.short_q,
        do=do_ref, aux=aux_ref, short_do=short_do_ref, short_aux=short_aux_ref, dq=dq_ref, dk=dk_ref, dv=dv_ref,
        mixed=r.mixed,
    )

    def pair(h, _):
        attend_back_pair(n_dp, me, width, sequence, do_spread, aux_spread, h)
        if red:
            red.tick(early + h, early, early + pairs)
        return 0

    lax.fori_loop(0, pairs, pair, 0)
    grad_normed = jnp.zeros((tokens, width), jnp.float32)
    for i, third in enumerate(thirds):
        in_loads[i].wait()
        grad_normed = grad_normed + dot_rows(r.mixed[:, i * width : (i + 1) * width], third[...])
    unit, inverse = norm_parts(r.attn_x[...])
    r.up_next[...] += norm_back(unit, inverse, r.gains[2:3], grad_normed)
    r.attn_sums[0:1] = jnp.sum(grad_normed * unit, axis=0, keepdims=True)
    r.attn_sums[1:2] = jnp.sum(grad_normed, axis=0, keepdims=True)

    if red:

        def rest(t, _):
            red.tick(t, early + pairs, red.ticks)
            return 0

        lax.fori_loop(early + pairs, red.ticks, rest, 0)
        red.finish()
    result_across.wait_all()
    for write in writes:
        write.wait()
    for h in range(pairs):
        do_spread.sent(h)
        aux_spread.sent(h)


def middle(n_dp, n_ex, collective_id, near, staged, far):
    arrays = {**near, **staged, **far}
    a = types.SimpleNamespace(**arrays)
    low, wide = jnp.bfloat16, jnp.float32
    tokens, width = a.stream.shape
    hidden = a.expert_in.shape[1]
    mixed = a.attn_in.shape[2]
    blocks, rows = hidden // width, width // n_dp
    long, short, pairs = LONG_DEV, tokens - LONG_DEV, width // 128
    _, padded = capacity_of(tokens, n_ex)
    slots = n_ex * padded
    group = min(max(4, 128 // padded), n_ex) * padded
    slab = (n_ex, padded, width)
    hops = (n_dp * n_ex).bit_length() - 1
    outs = dict(
        up_next=jax.ShapeDtypeStruct((tokens, width), wide),
        up_low=jax.ShapeDtypeStruct((tokens, width), low),
        mixed=jax.ShapeDtypeStruct((tokens, mixed), low),
        sums=jax.ShapeDtypeStruct((2, width), wide),
        attn_sums=jax.ShapeDtypeStruct((2, width), wide),
        router_grad=jax.ShapeDtypeStruct((n_ex, width), wide),
        stats=jax.ShapeDtypeStruct((n_ex, 128), wide),
        balance=jax.ShapeDtypeStruct((1, 128), wide),
        result_home=jax.ShapeDtypeStruct(slab, low),
        gate=jax.ShapeDtypeStruct((1, tokens), wide),
        dispatch=jax.ShapeDtypeStruct((slots, tokens), low),
    )
    direct, shared = len(outs), n_dp == 4
    known = 2 * slots if shared else slots
    if shared:
        outs.update(
            rows_t=jax.ShapeDtypeStruct((width, known), low),
            back=jax.ShapeDtypeStruct((known, width), low),
            expert_active_t=jax.ShapeDtypeStruct((hidden, known), low),
            expert_hidden=jax.ShapeDtypeStruct((known, hidden), low),
        )
    else:
        outs.update(chunks=jax.ShapeDtypeStruct((2 * blocks, rows, width), low))
    scratch = []
    for name in staged:
        scratch += [pltpu.VMEM(arrays[name].shape, arrays[name].dtype), pltpu.SemaphoreType.DMA]
    scratch += [pltpu.VMEM((blocks, width, width), low)] * 2 + [pltpu.SemaphoreType.DMA((2, blocks)), pltpu.SemaphoreType.DMA((4,))]
    scratch += [pltpu.VMEM(slab, low)] * 5
    scratch += [
        pltpu.VMEM((width, known), low),
        pltpu.VMEM((known, width), low),
        pltpu.VMEM((hidden, known), low),
        pltpu.VMEM((known, hidden), low),
        pltpu.VMEM((n_ex, 8, 128), wide),
        pltpu.VMEM((n_ex, 8, 128), wide),
        pltpu.VMEM((hops, n_ex, 128), wide),
        pltpu.VMEM((hops, n_ex, 128), wide),
        pltpu.VMEM((group, width), wide),
        pltpu.VMEM((group, width), wide),
    ]
    scratch += [pltpu.SemaphoreType.DMA((n_ex,))] * 8 + [pltpu.SemaphoreType.DMA((hops,))] * 2
    scratch += back_scratch(n_dp, pairs, long, short)
    if shared:
        scratch += [pltpu.VMEM(slab, low)] * 2 + [pltpu.SemaphoreType.DMA((n_ex, 2)), pltpu.SemaphoreType.DMA((2,))]
    else:
        scratch += Reduction.scratch(n_dp, 1, rows, width, [((0, width), 0)])
    vmem, anywhere = pl.BlockSpec(memory_space=pltpu.VMEM), pl.BlockSpec(memory_space=pl.ANY)
    names = tuple(arrays) + tuple(outs)
    values = pl.pallas_call(
        functools.partial(middle_kernel, n_dp, n_ex, names, tuple(staged)),
        out_shape=list(outs.values()),
        in_specs=[vmem] * len(near) + [anywhere] * (len(staged) + len(far)),
        out_specs=[vmem] * direct + [anywhere] * (len(outs) - direct),
        scratch_shapes=scratch,
        compiler_params=pltpu.CompilerParams(
            collective_id=collective_id, has_side_effects=True, vmem_limit_bytes=62 * 1024 * 1024
        ),
        name="middle",
    )(*arrays.values())
    return types.SimpleNamespace(**dict(zip(outs, values)))


def tail_kernel(n_dp, n_ex, names, staged, *refs):
    r = types.SimpleNamespace(**dict(zip(names, refs)))
    extra = iter(refs[len(names) :])
    loads = types.SimpleNamespace()
    for name in staged:
        buffer, sem = next(extra), next(extra)
        setattr(loads, name, pltpu.make_async_copy(getattr(r, name), buffer, sem))
        setattr(r, name, buffer)
    weights_in, weights_out, slopes, weight_sem = (next(extra) for _ in range(4))
    first_sem = next(extra)
    acc_ref, dense_low_ref, dense_hidden_ref = (next(extra) for _ in range(3))
    up_ref, first_low_ref, mixed_ref = acc_ref, r.second_low, r.second_mixed
    do_ref, aux_ref, short_do_ref, short_aux_ref, dq_ref, dk_ref, dv_ref = (next(extra) for _ in range(7))
    do_far, do_near, do_recv, aux_far, aux_near, aux_recv = (next(extra) for _ in range(6))
    small_send, small_recv, small_send_sem, small_recv_sem = (next(extra) for _ in range(4))
    shared = n_dp == 4
    if shared:
        expert_x, expert_y, expert_sem = (next(extra) for _ in range(3))
    links = Links(n_dp)
    me = links.me
    width = up_ref.shape[1]
    rows = width // n_dp
    pairs, long = r.kv.shape[1], r.kv.shape[3]
    blocks = r.dense_in.shape[1] // width
    per_in = mixed_ref.shape[1] // width

    def block_loads(i):
        slot = lax.rem(i, 2)
        at = pl.ds(pl.multiple_of(i * width, width), width)
        return [
            pltpu.make_async_copy(r.dense_out.at[at, :], weights_out.at[slot], weight_sem.at[slot, 0]),
            pltpu.make_async_copy(r.dense_in.at[:, at], weights_in.at[slot], weight_sem.at[slot, 1]),
            pltpu.make_async_copy(r.slope.at[:, at], slopes.at[slot], weight_sem.at[slot, 2]),
        ]

    ready = (loads.second_context_t, loads.second_low, loads.second_normed_t, loads.second_mixed)
    for load in ready:
        load.start()
    for i in range(min(2, blocks)):
        for load in block_loads(i):
            load.start()
    loads.active_t.start()
    for name in staged:
        if all(getattr(loads, name) is not load for load in ready + (loads.active_t,)):
            getattr(loads, name).start()
    free, busy = blocks % 2, (blocks - 1) % 2
    out_load = pltpu.make_async_copy(r.attn_out.at[0], weights_out.at[free], first_sem.at[0])
    thirds = [weights_in.at[free], weights_in.at[busy], weights_out.at[busy]]
    in_loads = [
        pltpu.make_async_copy(r.attn_in.at[0, :, pl.ds(i * width, width)], third, first_sem.at[1 + i])
        for i, third in enumerate(thirds)
    ]

    def columns(ref):
        return lambda j: ref[:, pl.ds(pl.multiple_of(j * width, width), width)]

    def one(ref):
        return lambda j, q: ref[q, 0]

    groups = [
        (1, one(r.second_context_t), columns(r.second_low)),
        (per_in, one(r.second_normed_t), columns(r.second_mixed)),
        (blocks, lambda j, q: r.active_t[q, j], lambda j: dense_low_ref[...]),
        (blocks, one(r.dense_normed_t), columns(dense_hidden_ref)),
        (1, one(r.first_context_t), columns(first_low_ref)),
        (per_in, one(r.first_normed_t), columns(mixed_ref)),
    ]
    red = Reduction(n_dp, n_ex, rows, groups, dense_lanes(width), extra, r.chunks)
    if shared:
        expert_blocks = r.expert_hidden.shape[1] // width
        base = 2 * links.chip

        def expert_loads(c, act):
            slot = lax.rem(c, 2)

            def load(rows_t, at, per, factor):
                for q in range(2):
                    row = pl.multiple_of(((base + q) * per + at) * rows, rows)
                    act(pltpu.make_async_copy(rows_t.at[pl.ds(row, rows), :], expert_x.at[slot, q], expert_sem.at[slot, q]))
                act(pltpu.make_async_copy(factor, expert_y.at[slot], expert_sem.at[slot, 2]))

            @pl.when(c < expert_blocks)
            def _():
                load(r.rows_t, 0, 1, r.expert_hidden.at[:, pl.ds(pl.multiple_of(c * width, width), width)])

            @pl.when((c >= expert_blocks) & (c < 2 * expert_blocks))
            def _():
                load(r.expert_active_t, c - expert_blocks, expert_blocks, r.back)

        def expert_part(j, q):
            return expert_x[lax.rem(j, 2), q]

        expert_groups = [(2 * expert_blocks, expert_part, lambda j: expert_y[lax.rem(j, 2)])]
        expert_red = Reduction(2, 1, rows, expert_groups, [((0, width), 0)], extra, r.expert_chunks)
    levels = [("dp", b) for b in range(n_dp.bit_length() - 1)] + [("ex", b) for b in range(n_ex.bit_length() - 1)]
    greet([red.peer(*level) for level in levels] + (links.peers()[1:] if links.chips > 2 else []))

    up = r.up[...]
    dense_low_ref[...] = up.astype(jnp.bfloat16)
    acc_ref[...] = jnp.zeros_like(acc_ref)
    for load in ready:
        load.wait()
    red.tick(0, 0, 1)
    loads.active_t.wait()

    def dense(i, _):
        slot = lax.rem(i, 2)
        for load in block_loads(i):
            load.wait()
        grad = dot_rows(dense_low_ref[...], weights_out[slot]) * slopes[slot].astype(jnp.float32)
        grad = grad.astype(jnp.bfloat16)
        dense_hidden_ref[:, pl.ds(pl.multiple_of(i * width, width), width)] = grad
        acc_ref[...] += dot_rows(grad, weights_in[slot])

        @pl.when(i + 2 < blocks)
        def _():
            for load in block_loads(i + 2):
                load.start()

        @pl.when(i == blocks - 2)
        def _():
            out_load.start()
            in_loads[0].start()

        red.tick(1 + i, 1, 1 + blocks)
        return 0

    lax.fori_loop(0, blocks, dense, 0)
    for load in in_loads[1:]:
        load.start()
    for name in staged:
        if all(getattr(loads, name) is not load for load in ready + (loads.active_t,)):
            getattr(loads, name).wait()
    unit, inverse = norm_parts(r.dense_x[...])
    grad_normed = acc_ref[...]
    up = up + norm_back(unit, inverse, r.gains[1:2], grad_normed)
    up_ref[...] = up
    for first, sums in ((2, r.second_sums), (3, r.last_sums)):
        small_send[0, first : first + 1] = sums[0:1]
        small_send[0, first + 4 : first + 5] = sums[1:2]
    small_send[0, 8:] = r.router_grad[...]
    small_send[0, 1:2] = jnp.sum(grad_normed * unit, axis=0, keepdims=True)
    small_send[0, 5:6] = jnp.sum(grad_normed, axis=0, keepdims=True)
    at_tick = 1 + blocks

    scale = HEAD_DIM ** (-0.5)
    up_low = up.astype(jnp.bfloat16)
    first_low_ref[...] = up_low
    out_load.wait()
    grad_context = dot_rows(up_low, weights_out[free]).astype(jnp.bfloat16)
    red.tick(at_tick, at_tick, at_tick + 1)
    at_tick += 1
    put_context_grads(grad_context, do_ref, short_do_ref, me, long)
    do_spread = Spread(links, lambda b, p: do_ref.at[b, p], pairs, False, do_far, do_near, do_recv)
    aux_spread = Spread(links, lambda b, p: aux_ref.at[b, p], pairs, False, aux_far, aux_near, aux_recv)
    put_row_terms(r.context, r.lse, grad_context, aux_ref, short_aux_ref, me, long)
    for h in range(pairs):
        do_spread.send(h)
        aux_spread.send(h)
    red.tick(at_tick, at_tick, at_tick + 1)
    at_tick += 1
    sequence = types.SimpleNamespace(
        doc_row=r.doc_row, kv=r.kv, q=r.q, short_kv=r.short_kv, short_q=r.short_q,
        do=do_ref, aux=aux_ref, short_do=short_do_ref, short_aux=short_aux_ref, dq=dq_ref, dk=dk_ref, dv=dv_ref,
        mixed=mixed_ref,
    )

    def pair(h, _):
        attend_back_pair(n_dp, me, width, sequence, do_spread, aux_spread, h)
        red.tick(at_tick + h, at_tick, at_tick + pairs)
        return 0

    lax.fori_loop(0, pairs, pair, 0)
    at_tick += pairs
    grad_normed = jnp.zeros((up_ref.shape[0], width), jnp.float32)
    for i, third in enumerate(thirds):
        in_loads[i].wait()
        grad_normed = grad_normed + dot_rows(mixed_ref[:, i * width : (i + 1) * width], third[...])
    unit, inverse = norm_parts(r.first_x[...].astype(jnp.float32))
    r.grad_tokens[...] = (
        up_ref[...] + norm_back(unit, inverse, r.gains[0:1], grad_normed)
    ).astype(jnp.bfloat16)
    small_send[0, 0:1] = jnp.sum(grad_normed * unit, axis=0, keepdims=True)
    small_send[0, 4:5] = jnp.sum(grad_normed, axis=0, keepdims=True)

    def small_copy(i):
        return pltpu.make_async_remote_copy(
            src_ref=small_send.at[i],
            dst_ref=small_recv.at[i],
            send_sem=small_send_sem.at[i],
            recv_sem=small_recv_sem.at[i],
            device_id=red.peer(*levels[i]),
            device_id_type=MESH,
        )

    small_copy(0).start()

    if shared:
        for c in range(2):
            expert_loads(jnp.int32(c), lambda copy: copy.start())

    def rest(t, _):
        red.tick(t, at_tick, red.ticks)
        if shared:
            c = t - at_tick
            expert_loads(c, lambda copy: copy.wait())
            expert_red.tick(c, 0, red.ticks - at_tick)
            expert_loads(c + 2, lambda copy: copy.start())

        @pl.when(t == red.ticks - 2)
        def _():
            gate = jnp.broadcast_to(r.gate[...], (128, r.gate.shape[1])).T[:, 0:1]
            for first in range(0, width, 256):
                at = slice(first, first + 256)
                home = r.result_home[:, :, at].reshape(r.dispatch.shape[0], 256)
                result = dot_columns(r.dispatch[...], home)
                r.output[:, at] = (r.last_x[:, at] + gate * result).astype(jnp.bfloat16)

        for i in range(1, len(levels) + 1):

            @pl.when(t == at_tick + i)
            def _(i=i):
                small_copy(i - 1).wait()
                value = small_send[i - 1] + small_recv[i - 1]
                if i < len(levels):
                    small_send[i] = value
                    small_copy(i).start()
                else:
                    own = jnp.zeros((value.shape[0], rows), jnp.float32)
                    for q in range(n_dp):
                        own = own + jnp.where(me == q, value[:, q * rows : (q + 1) * rows], 0.0)
                    r.small_sum[...] = own

        return 0

    lax.fori_loop(at_tick, red.ticks, rest, 0)
    if shared:
        for c in range(red.ticks - at_tick, expert_red.ticks):
            expert_loads(jnp.int32(c), lambda copy: copy.wait())
            expert_red.tick(jnp.int32(c), c, c + 1)
            expert_loads(jnp.int32(c + 2), lambda copy: copy.start())
        expert_red.finish()
    red.finish()
    for h in range(pairs):
        do_spread.sent(h)
        aux_spread.sent(h)


def tail(n_dp, n_ex, collective_id, near, staged, far):
    arrays = {**near, **staged, **far}
    a = types.SimpleNamespace(**arrays)
    low, wide = jnp.bfloat16, jnp.float32
    tokens, width = a.up.shape
    hidden = a.dense_in.shape[1]
    mixed = a.attn_in.shape[2]
    rows = width // n_dp
    long, short, pairs = LONG_DEV, tokens - LONG_DEV, width // 128
    chunks = 2 * (hidden // width) + 2 * (1 + mixed // width)
    small = (8 + a.router_grad.shape[0], width)
    outs = dict(
        grad_tokens=jax.ShapeDtypeStruct((tokens, width), low),
        output=jax.ShapeDtypeStruct((tokens, width), low),
        small_sum=jax.ShapeDtypeStruct((small[0], rows), wide),
    )
    direct, shared = len(outs), n_dp == 4
    outs.update(chunks=jax.ShapeDtypeStruct((chunks, rows, width), low))
    if shared:
        slots, expert_hidden = a.expert_hidden.shape
        outs.update(expert_chunks=jax.ShapeDtypeStruct((2 * expert_hidden // width, rows, width), low))
    scratch = []
    for name in staged:
        scratch += [pltpu.VMEM(arrays[name].shape, arrays[name].dtype), pltpu.SemaphoreType.DMA]
    scratch += [pltpu.VMEM((2, width, width), low)] * 2
    scratch += [pltpu.VMEM((2, tokens, width), low), pltpu.SemaphoreType.DMA((2, 3))]
    scratch += [pltpu.SemaphoreType.DMA((4,))]
    scratch += [pltpu.VMEM((tokens, width), wide)]
    scratch += [pltpu.VMEM((tokens, n), low) for n in (width, hidden)]
    scratch += back_scratch(n_dp, pairs, long, short)
    hops = (n_dp * n_ex).bit_length() - 1
    scratch += [pltpu.VMEM((hops,) + small, wide)] * 2 + [pltpu.SemaphoreType.DMA((hops,))] * 2
    if shared:
        scratch += [pltpu.VMEM((2, 2, rows, slots), low), pltpu.VMEM((2, slots, width), low)]
        scratch += [pltpu.SemaphoreType.DMA((2, 3))]
    scratch += Reduction.scratch(n_dp, n_ex, rows, width, dense_lanes(width))
    if shared:
        scratch += Reduction.scratch(2, 1, rows, width, [((0, width), 0)])
    vmem, anywhere = pl.BlockSpec(memory_space=pltpu.VMEM), pl.BlockSpec(memory_space=pl.ANY)
    names = tuple(arrays) + tuple(outs)
    values = pl.pallas_call(
        functools.partial(tail_kernel, n_dp, n_ex, names, tuple(staged)),
        out_shape=list(outs.values()),
        in_specs=[vmem] * len(near) + [anywhere] * (len(staged) + len(far)),
        out_specs=[vmem] * direct + [anywhere] * (len(outs) - direct),
        scratch_shapes=scratch,
        compiler_params=pltpu.CompilerParams(
            collective_id=collective_id, has_side_effects=True, vmem_limit_bytes=62 * 1024 * 1024
        ),
        name="tail",
    )(*arrays.values())
    return types.SimpleNamespace(**dict(zip(outs, values)))


def shards(
    tokens,
    doc_lengths,
    assign,
    ln_gain,
    ln_bias,
    attn_in,
    attn_out,
    ffn_in,
    ffn_out,
    router,
    expert_in,
    expert_out,
    cotangent,
):
    n_dp, n_ex = lax.axis_size("dp"), lax.axis_size("expert")
    row_count = tokens.shape[1]
    lengths = doc_lengths[0, 0]
    order = jnp.arange(lengths.shape[0])
    doc_ends = jnp.sum(jnp.where(order[:, None] <= order[None, :], lengths[:, None], 0), axis=0)
    short_place = jnp.arange(row_count - LONG_DEV, dtype=jnp.int32)
    doc_row = jnp.sum((short_place[None, :] >= doc_ends[:, None]).astype(jnp.float32), axis=0, keepdims=True)
    weights_in, weights_out = lax.optimization_barrier((attn_in.transpose(1, 0, 2), attn_out.transpose(1, 0, 2)))
    gains, shifts = ln_gain.T, ln_bias.T
    assign_row = assign[0].T
    fore = front(
        n_dp,
        n_ex,
        2,
        dict(
            tokens=tokens[0],
            gains=gains,
            shifts=shifts,
            doc_row=doc_row,
            assign=assign_row,
            cot=cotangent[0],
        ),
        dict(attn_in=weights_in, attn_out=weights_out, dense_in=ffn_in, dense_out=ffn_out),
    )
    model_width = tokens.shape[2]
    rows = model_width // n_dp
    mid = middle(
        n_dp,
        n_ex,
        4,
        dict(
            stream=fore.stream2,
            gains=gains,
            shifts=shifts,
            router=router.T,
            assign=assign_row,
            cot=cotangent[0],
            far_cot=fore.far_cot,
            doc_row=doc_row,
            lse=fore.lse1,
        ),
        dict(
            attn_x=fore.stream1,
            context=fore.context1,
            kv=fore.kv1,
            q=fore.q1,
            short_kv=fore.short_kv1,
            short_q=fore.short_q1,
        ),
        dict(
            expert_in=expert_in[0],
            expert_out=expert_out[0],
            attn_in=weights_in,
            attn_out=weights_out,
        ),
    )
    def blocks_of(rows_t):
        return rows_t.reshape(n_dp, -1, rows, row_count)

    shared = n_dp == 4
    last = tail(
        n_dp,
        n_ex,
        5,
        dict(
            up=mid.up_next,
            gains=gains,
            doc_row=doc_row,
            lse=fore.lse0,
            second_sums=mid.attn_sums,
            last_sums=mid.sums,
            router_grad=mid.router_grad,
            dispatch=mid.dispatch,
            gate=mid.gate,
        ),
        dict(
            dense_x=fore.stream0,
            first_x=tokens[0],
            context=fore.context0,
            kv=fore.kv0,
            q=fore.q0,
            short_kv=fore.short_kv0,
            short_q=fore.short_q0,
            second_context_t=blocks_of(fore.context_t1),
            second_normed_t=blocks_of(fore.normed_t1),
            active_t=blocks_of(fore.active_t),
            dense_normed_t=blocks_of(fore.dense_normed_t),
            first_context_t=blocks_of(fore.context_t0),
            first_normed_t=blocks_of(fore.normed_t0),
            second_low=mid.up_low,
            result_home=mid.result_home,
            last_x=fore.stream2,
            second_mixed=mid.mixed,
        ),
        dict(
            dense_in=ffn_in,
            dense_out=ffn_out,
            slope=fore.slope,
            attn_in=weights_in,
            attn_out=weights_out,
            **(
                dict(
                    rows_t=mid.rows_t,
                    back=mid.back,
                    expert_active_t=mid.expert_active_t,
                    expert_hidden=mid.expert_hidden,
                )
                if shared
                else {}
            ),
        ),
    )
    expert_chunks = last.expert_chunks if shared else mid.chunks
    (
        attn_in_sum, attn_out_sum, ffn_in_sum, ffn_out_sum, expert_in_sum, expert_out_sum,
        gain_sum, shift_sum, router_sum, grad_tokens, output,
    ) = unpack(
        last.chunks, expert_chunks, last.small_sum, last.grad_tokens, last.output,
        attn_in.shape[2] // model_width, ffn_in.shape[1] // model_width,
    )
    return (
        output[None],
        mid.balance[0, 0],
        grad_tokens[None],
        gain_sum.T,
        shift_sum.T,
        attn_in_sum,
        attn_out_sum,
        ffn_in_sum,
        ffn_out_sum.reshape(-1, model_width),
        router_sum.T,
        expert_in_sum[None],
        expert_out_sum.reshape(1, -1, model_width),
    )


def solution(mesh):
    return jax.shard_map(
        shards,
        mesh=mesh,
        in_specs=(
            P("expert", "dp", None),
            P("expert", "dp", None),
            P("expert", "dp", None),
            P(),
            P(),
            P(),
            P(),
            P(),
            P(),
            P(),
            P("expert", None, None),
            P("expert", None, None),
            P("expert", "dp", None),
        ),
        out_specs=(
            P("expert", "dp", None),
            P(),
            P("expert", "dp", None),
            P("dp", None),
            P("dp", None),
            P("dp", None, None),
            P("dp", None, None),
            P("dp", None),
            P("dp", None),
            P("dp", None),
            P("expert", "dp", None),
            P("expert", "dp", None),
        ),
        check_vma=False,
    )
```

```python
import functools
import types

import jax
import jax.numpy as jnp
from jax import lax
from jax.experimental import pallas as pl
from jax.experimental.pallas import tpu as pltpu
from jax.sharding import PartitionSpec as P

MESH = pl.DeviceIdType.MESH
HEADS = 12
HEAD_DIM = 64
LONG_DEV = 256


epsilon = 1e-05
balance_weight = 0.01
masked_score = -1e30


def bit_of(index, level):
    return (index // (1 << level)) % 2


def flip(index, level):
    return index + (1 << level) * (1 - 2 * bit_of(index, level))


def partner_index(index, mask, levels):
    total = 0
    for level in range(levels):
        own = bit_of(index, level)
        total = total + (1 << level) * (1 - own if (mask >> level) & 1 else own)
    return total


def unpack_kernel(
    per_in, per_ffn,
    chunk_ref, expert_ref, small_ref, tokens_ref, output_ref,
    in_ref, out_ref, ffn_in_ref, ffn_out_ref, expert_in_ref, expert_out_ref,
    gain_ref, shift_ref, router_ref, tokens_out_ref, output_out_ref,
):
    per_expert = expert_ref.shape[0] // 2
    width = chunk_ref.shape[2]
    at = 0
    for layer in (1, 0):
        out_ref[:, layer, :] = chunk_ref[at].astype(jnp.float32)
        for j in range(per_in):
            in_ref[:, layer, width * j : width * j + width] = chunk_ref[at + 1 + j].astype(jnp.float32)
        at += 1 + per_in
        if layer:
            for j in range(per_ffn):
                ffn_out_ref[j] = chunk_ref[at + j].astype(jnp.float32)
                ffn_in_ref[:, width * j : width * j + width] = chunk_ref[at + per_ffn + j].astype(jnp.float32)
            at += 2 * per_ffn
    for j in range(per_expert):
        expert_in_ref[:, width * j : width * j + width] = expert_ref[j].astype(jnp.float32)
        expert_out_ref[j] = expert_ref[per_expert + j].astype(jnp.float32)
    gain_ref[...] = small_ref[0:4]
    shift_ref[...] = small_ref[4:8]
    router_ref[...] = small_ref[8:]
    tokens_out_ref[...] = tokens_ref[...]
    output_out_ref[...] = output_ref[...]


def unpack(chunks, expert_chunks, small, grad_tokens, output, per_in, per_ffn):
    count, rows, width = chunks.shape
    experts = expert_chunks.shape[0]
    tokens = output.shape[0]
    step = 48 if rows % 48 == 0 else rows
    wide, low = jnp.float32, jnp.bfloat16
    token_spec = pl.BlockSpec((tokens // (rows // step), width), lambda i: (i, 0))

    def fixed(shape):
        return pl.BlockSpec(shape, lambda i: (0, 0))

    return pl.pallas_call(
        functools.partial(unpack_kernel, per_in, per_ffn),
        grid=(rows // step,),
        out_shape=[
            jax.ShapeDtypeStruct((rows, 2, per_in * width), wide),
            jax.ShapeDtypeStruct((rows, 2, width), wide),
            jax.ShapeDtypeStruct((rows, per_ffn * width), wide),
            jax.ShapeDtypeStruct((per_ffn, rows, width), wide),
            jax.ShapeDtypeStruct((rows, experts // 2 * width), wide),
            jax.ShapeDtypeStruct((experts // 2, rows, width), wide),
            jax.ShapeDtypeStruct((4, rows), wide),
            jax.ShapeDtypeStruct((4, rows), wide),
            jax.ShapeDtypeStruct((small.shape[0] - 8, rows), wide),
            jax.ShapeDtypeStruct((tokens, width), low),
            jax.ShapeDtypeStruct((tokens, width), low),
        ],
        in_specs=[
            pl.BlockSpec((count, step, width), lambda i: (0, i, 0)),
            pl.BlockSpec((experts, step, width), lambda i: (0, i, 0)),
            fixed(small.shape),
            token_spec,
            token_spec,
        ],
        out_specs=[
            pl.BlockSpec((step, 2, per_in * width), lambda i: (i, 0, 0)),
            pl.BlockSpec((step, 2, width), lambda i: (i, 0, 0)),
            pl.BlockSpec((step, per_ffn * width), lambda i: (i, 0)),
            pl.BlockSpec((per_ffn, step, width), lambda i: (0, i, 0)),
            pl.BlockSpec((step, experts // 2 * width), lambda i: (i, 0)),
            pl.BlockSpec((experts // 2, step, width), lambda i: (0, i, 0)),
            fixed((4, rows)),
            fixed((4, rows)),
            fixed((small.shape[0] - 8, rows)),
            token_spec,
            token_spec,
        ],
        compiler_params=pltpu.CompilerParams(vmem_limit_bytes=62 * 1024 * 1024),
        name="unpack",
    )(chunks, expert_chunks, small, grad_tokens, output)


def dot(a, b):
    return jnp.dot(a, b, preferred_element_type=jnp.float32)


def dot_rows(a, b):
    return lax.dot_general(a, b, (((1,), (1,)), ((), ())), preferred_element_type=jnp.float32)


def dot_columns(a, b):
    return lax.dot_general(a, b, (((0,), (0,)), ((), ())), preferred_element_type=jnp.float32)


def gelu_parts(hidden):
    lower = 0.5 + 0.5 * lax.erf(hidden * 0.7071067811865476)
    slope = lower + hidden * jnp.exp(-0.5 * hidden * hidden) * 0.3989422804014327
    return hidden * lower, slope


def split(value):
    high = value.astype(jnp.bfloat16)
    rest = value - high.astype(jnp.float32)
    middle_part = rest.astype(jnp.bfloat16)
    low = (rest - middle_part.astype(jnp.float32)).astype(jnp.bfloat16)
    return jnp.concatenate([high, middle_part, low], axis=0)


def norm_parts(x):
    center = x - jnp.mean(x, axis=-1, keepdims=True)
    inverse = lax.rsqrt(jnp.mean(center * center, axis=-1, keepdims=True) + epsilon)
    return center * inverse, inverse


def norm_back(unit, inverse, gain, upstream):
    scaled = upstream * gain
    return inverse * (
        scaled - jnp.mean(scaled, axis=-1, keepdims=True) - unit * jnp.mean(scaled * unit, axis=-1, keepdims=True)
    )


def capacity_of(rows, experts):
    capacity = (5 * rows + 4 * experts - 1) // (4 * experts)
    return capacity, -(-capacity // 16) * 16


def chosen_rows(assign, experts):
    expert = lax.broadcasted_iota(jnp.int32, (experts, assign.shape[1]), 0)
    return jnp.where(assign == expert, 1.0, 0.0)


def dispatch_of(assign, experts):
    tokens = assign.shape[1]
    capacity, padded = capacity_of(tokens, experts)
    hot = chosen_rows(assign, experts)
    earlier = lax.broadcasted_iota(jnp.int32, (tokens, tokens), 0) < lax.broadcasted_iota(jnp.int32, (tokens, tokens), 1)
    before = dot(hot.astype(jnp.bfloat16), jnp.where(earlier, 1.0, 0.0).astype(jnp.bfloat16))
    place = jnp.sum(hot * before, axis=0, keepdims=True)
    slot = jnp.where(place < capacity, assign.astype(jnp.float32) * padded + place, -1.0)
    number = lax.broadcasted_iota(jnp.int32, (experts * padded, tokens), 0).astype(jnp.float32)
    return jnp.where(number == slot, 1.0, 0.0).astype(jnp.bfloat16)


class Across:
    def __init__(self, experts, out, into, send_sems, recv_sems):
        self.experts, self.out, self.into = experts, out, into
        self.send_sems, self.recv_sems = send_sems, recv_sems
        self.dp, self.me = lax.axis_index("dp"), lax.axis_index("expert")

    def copy(self, slab, place, to):
        return pltpu.make_async_remote_copy(
            src_ref=self.out.at[slab],
            dst_ref=self.into.at[place],
            send_sem=self.send_sems.at[slab],
            recv_sem=self.recv_sems.at[place],
            device_id=(self.dp, to),
            device_id_type=MESH,
        )

    def start(self, j):
        self.copy(j, self.me, j).start()

    def wait_from(self, j):
        self.copy(j, j, j).wait_recv()

    def wait_to(self, j):
        self.copy(j, self.me, j).wait_send()

    def others(self, use):
        def body(k, _):
            use(lax.rem(self.me + k, self.experts))
            return 0

        lax.fori_loop(1, self.experts, body, 0)

    def start_all(self):
        self.others(self.start)

    def wait_all(self):
        def both(j):
            self.wait_from(j)
            self.wait_to(j)

        self.others(both)


def greet(targets):
    barrier = pltpu.get_barrier_semaphore()
    for device in targets:
        pl.semaphore_signal(barrier, inc=1, device_id=device, device_id_type=MESH)
    pl.semaphore_wait(barrier, len(targets))


def across_peers(experts):
    d, e = lax.axis_index("dp"), lax.axis_index("expert")
    return [(d, lax.rem(e + k, experts)) for k in range(1, experts)]


def head_pair(rows):
    first = lax.broadcasted_iota(jnp.int32, rows.shape, 1) < HEAD_DIM
    zero = jnp.zeros_like(rows)
    return jnp.concatenate([jnp.where(first, rows, zero), jnp.where(first, zero, rows)], axis=0)


def pair_rows(both):
    n = both.shape[1] // 2
    return jnp.concatenate([both[:HEAD_DIM, :n], both[HEAD_DIM:, n:]], axis=0)


def causal(keys, queries):
    key = lax.broadcasted_iota(jnp.int32, (keys, 2 * queries), 0)
    query = lax.broadcasted_iota(jnp.int32, (keys, 2 * queries), 1)
    return key <= jnp.where(query >= queries, query - queries, query)


def short_seen(doc_row):
    n = doc_row.shape[1]
    doc_col = jnp.broadcast_to(doc_row, (n, n)).T
    same = jnp.concatenate([doc_col, doc_col], axis=1) == jnp.concatenate([doc_row, doc_row], axis=1)
    return same & causal(n, n)


class Links:
    def __init__(self, n_dp):
        self.me, self.expert = lax.axis_index("dp"), lax.axis_index("expert")
        self.chips = n_dp // 2
        self.chip, self.core = self.me // 2, self.me % 2
        self.twin = self.me + 1 - 2 * self.core

    def peers(self):
        ring = [lax.rem(self.chip + k, self.chips) for k in range(1, self.chips)]
        return [(self.twin, self.expert)] + [(2 * other + self.core, self.expert) for other in ring]

    def copy(self, ref, send_sem, recv_sem, index):
        return pltpu.make_async_remote_copy(
            src_ref=ref,
            dst_ref=ref,
            send_sem=send_sem,
            recv_sem=recv_sem,
            device_id=(index, self.expert),
            device_id_type=MESH,
        )

    def before(self, later, other):
        return other > self.chip if later else other < self.chip


class Spread:
    def __init__(self, links, at, parts, later, far_sems, near_sems, recv_sems):
        self.links, self.at, self.later = links, at, later
        self.far_sems, self.near_sems, self.recv_sems = far_sems, near_sems, recv_sems

    def _far(self, other, p):
        k = self.links
        return k.copy(self.at(k.me, p), self.far_sems.at[other, p], self.recv_sems.at[k.me, p], 2 * other + k.core)

    def _near(self, block, p):
        k = self.links
        return k.copy(self.at(block, p), self.near_sems.at[block, p], self.recv_sems.at[block, p], k.twin)

    def _twin_needs(self):
        return self.links.core == (0 if self.later else 1)

    def send(self, p):
        k = self.links
        for other in range(k.chips):

            @pl.when(k.before(self.later, other))
            def _():
                self._far(other, p).start()

        @pl.when(self._twin_needs())
        def _():
            self._near(k.me, p).start()

    def sent(self, p):
        k = self.links
        for other in range(k.chips):

            @pl.when(k.before(self.later, other))
            def _():
                self._far(other, p).wait_send()

            @pl.when(k.before(not self.later, other))
            def _():
                self._near(2 * other + k.core, p).wait_send()

        @pl.when(self._twin_needs())
        def _():
            self._near(k.me, p).wait_send()

    def relay(self, p):
        k = self.links
        for other in range(k.chips):

            @pl.when(k.before(not self.later, other))
            def _():
                block = 2 * other + k.core
                copy = self._near(block, p)
                copy.wait_recv()
                copy.start()

    def each(self, p, use):
        k = self.links

        @pl.when(k.core == (1 if self.later else 0))
        def _():
            self._near(k.twin, p).wait_recv()
            use(k.twin)

        for other in range(k.chips):

            @pl.when(k.before(not self.later, other))
            def _():
                use(2 * other + k.core)
                block = 2 * other + 1 - k.core
                self._near(block, p).wait_recv()
                use(block)


def spread_sems(n_dp, parts):
    return [
        pltpu.SemaphoreType.DMA((n_dp // 2, parts)),
        pltpu.SemaphoreType.DMA((n_dp, parts)),
        pltpu.SemaphoreType.DMA((n_dp, parts)),
    ]


def queries_of(rows, w_q):
    return (dot(rows, w_q).astype(jnp.bfloat16) * HEAD_DIM ** (-0.5)).astype(jnp.bfloat16)


def attend(n_dp, links, s, x, gain, shift, w_in, w_out, doc_row, ready, between):
    me = links.me
    pairs, long, width = s.kv.shape[1], s.kv.shape[3], x.shape[1]
    unit, _ = norm_parts(x)
    normed = (unit * gain + shift).astype(jnp.bfloat16)
    s.rows[me] = normed[:long]
    later = Spread(links, lambda b, p: s.rows.at[b], 1, True, *s.kv_sems)
    earlier = Spread(links, lambda b, p: s.rows.at[b], 1, False, *s.q_sems)
    later.send(0)
    earlier.send(0)
    ready(0)
    kv = dot(normed, w_in[:, width:]).astype(jnp.bfloat16)
    ready(1)
    q = queries_of(normed, w_in[:, :width])
    for h in range(pairs):
        at = slice(128 * h, 128 * h + 128)
        for part in range(2):
            piece = kv[:, part * width + 128 * h : part * width + 128 * h + 128]
            s.kv[me, h, part] = piece[:long]
            s.short_kv[h, part] = piece[long:]
        s.q[me, h] = q[:long, at]
        s.short_q[h] = q[long:, at]
    between()
    s.normed_t[...] = normed.T

    def put_context(h, rows_t, first, count):
        at = pl.ds(pl.multiple_of(128 * h, 128), 128)
        s.context_t[at, first : first + count] = rows_t.astype(jnp.bfloat16)
        s.context[first : first + count, at] = rows_t.T.astype(jnp.bfloat16)

    low = jnp.bfloat16
    short_mask, long_mask = short_seen(doc_row), causal(long, long)

    def own_part(i, _):
        hs = [2 * i, 2 * i + 1]
        scores = [dot_rows(s.short_kv[h, 0], head_pair(s.short_q[h])) for h in hs]
        scores = [jnp.where(short_mask, v, masked_score) for v in scores]
        long_scores = [dot_rows(s.kv[me, h, 0], head_pair(s.q[me, h])) for h in hs]
        tops = [jnp.max(v, axis=0, keepdims=True) for v in scores]
        weights = [jnp.exp(v - top) for v, top in zip(scores, tops)]
        totals = [jnp.sum(v, axis=0, keepdims=True) for v in weights]
        sums = [dot_columns(s.short_kv[h, 1], v.astype(low)) for h, v in zip(hs, weights)]
        long_scores = [jnp.where(long_mask, v, masked_score) for v in long_scores]
        long_tops = [jnp.max(v, axis=0, keepdims=True) for v in long_scores]
        long_weights = [jnp.exp(v - top) for v, top in zip(long_scores, long_tops)]
        long_sums = [dot_columns(s.kv[me, h, 1], v.astype(low)) for h, v in zip(hs, long_weights)]
        for n, h in enumerate(hs):
            rows_t = pair_rows(sums[n] / totals[n])
            short = rows_t.shape[1]
            put_context(h, rows_t, long, short)
            lse = tops[n] + jnp.log(totals[n])
            s.lse[h, 0:1, long:] = lse[:, :short]
            s.lse[h, 1:2, long:] = lse[:, short:]
            s.top[h] = long_tops[n]
            s.total[h] = jnp.sum(long_weights[n], axis=0, keepdims=True)
            s.acc[h] = long_sums[n]
        return 0

    lax.fori_loop(0, pairs // 2, own_part, 0)

    def keys_of(block):
        kv = dot(s.rows[block], w_in[:, width:]).astype(jnp.bfloat16)
        for h in range(pairs):
            for part in range(2):
                s.kv[block, h, part] = kv[:, part * width + 128 * h : part * width + 128 * h + 128]

    later.relay(0)
    later.each(0, keys_of)

    def other_part(i, _):
        hs = [2 * i, 2 * i + 1]

        def use(first, size):
            at = pl.ds(first, size)
            keys = [s.kv[at, h, 0].reshape(size * long, 128) for h in hs]
            values = [s.kv[at, h, 1].reshape(size * long, 128) for h in hs]
            scores = [dot_rows(v, head_pair(s.q[me, h])) for h, v in zip(hs, keys)]
            olds = [s.top[h] for h in hs]
            tops = [jnp.maximum(old, jnp.max(v, axis=0, keepdims=True)) for old, v in zip(olds, scores)]
            factors = [jnp.exp(old - top) for old, top in zip(olds, tops)]
            weights = [jnp.exp(v - top) for v, top in zip(scores, tops)]
            totals = [s.total[h] * f + jnp.sum(v, axis=0, keepdims=True) for h, f, v in zip(hs, factors, weights)]
            sums = [s.acc[h] * f + dot_columns(u, v.astype(low)) for h, f, u, v in zip(hs, factors, values, weights)]
            for n, h in enumerate(hs):
                s.top[h] = tops[n]
                s.total[h] = totals[n]
                s.acc[h] = sums[n]

        runs(n_dp - 1, me, use)
        for h in hs:
            total = s.total[h]
            put_context(h, pair_rows(s.acc[h] / total), 0, long)
            lse = s.top[h] + jnp.log(total)
            s.lse[h, 0:1, :long] = lse[:, :long]
            s.lse[h, 1:2, :long] = lse[:, long:]
        return 0

    lax.fori_loop(0, pairs // 2, other_part, 0)
    ready(2)
    following = x + dot(s.context[...], w_out[...])

    def settle():
        def ask(block):
            q = queries_of(s.rows[block], w_in[:, :width])
            for h in range(pairs):
                s.q[block, h] = q[:, 128 * h : 128 * h + 128]

        earlier.relay(0)
        earlier.each(0, ask)
        earlier.sent(0)
        later.sent(0)

    return following, settle


def front_kernel(n_dp, n_ex, names, saved, *refs):
    r = types.SimpleNamespace(**dict(zip(names, refs)))
    extra = iter(refs[len(names) :])
    buffers = []
    for layer in range(2):
        s = types.SimpleNamespace()
        for name in saved:
            setattr(s, name, next(extra))
        s.rows = next(extra)
        s.kv_sems = [next(extra) for _ in range(3)]
        s.q_sems = [next(extra) for _ in range(3)]
        s.stored = next(extra)
        buffers.append(s)
    sums = [next(extra) for _ in range(3)]
    for s in buffers:
        s.acc, s.top, s.total = sums
    w_in, w_out, w_sem, dense_in, dense_out, dense_sem = (next(extra) for _ in range(6))
    stream_ref, dense_normed, active_ref, slope_ref, dense_normed_t, far_cot = (next(extra) for _ in range(6))
    stored, cot_send, cot_send_sem, cot_recv_sem = (next(extra) for _ in range(4))
    links = Links(n_dp)
    tokens, width = r.tokens.shape
    blocks = r.dense_in.shape[1] // width
    low = jnp.bfloat16

    def block_loads(i):
        slot = lax.rem(i, 2)
        at = pl.ds(pl.multiple_of(i * width, width), width)
        return [
            pltpu.make_async_copy(r.dense_in.at[:, at], dense_in.at[slot], dense_sem.at[slot, 0]),
            pltpu.make_async_copy(r.dense_out.at[at, :], dense_out.at[slot], dense_sem.at[slot, 1]),
        ]

    def weight_loads(layer):
        return [
            pltpu.make_async_copy(
                r.attn_in.at[layer, :, pl.ds(width, 2 * width)], w_in.at[layer, :, pl.ds(width, 2 * width)], w_sem.at[layer, 0]
            ),
            pltpu.make_async_copy(
                r.attn_in.at[layer, :, pl.ds(0, width)], w_in.at[layer, :, pl.ds(0, width)], w_sem.at[layer, 1]
            ),
            pltpu.make_async_copy(r.attn_out.at[layer], w_out.at[layer], w_sem.at[layer, 2]),
        ]

    loads = [weight_loads(0), weight_loads(1)]
    for load in loads[0]:
        load.start()
    for i in range(min(2, blocks)):
        for load in block_loads(i):
            load.start()
    for load in loads[1]:
        load.start()
    greet(links.peers() + across_peers(n_ex))
    writes = []

    def write(source, target, sem):
        copy = pltpu.make_async_copy(source, target, sem)
        copy.start()
        writes.append(copy)

    def layer(number, x, between):
        s = buffers[number]
        column = 2 * number
        following, settle = attend(
            n_dp, links, s, x, r.gains[column : column + 1], r.shifts[column : column + 1], w_in.at[number], w_out.at[number],
            r.doc_row[...], lambda i: loads[number][i].wait(), between,
        )
        return following, settle

    def save(number, settle):
        s = buffers[number]
        settle()
        for i, name in enumerate(saved):
            write(getattr(s, name), getattr(r, name + str(number)), s.stored.at[i])

    x, settle = layer(0, r.tokens[...].astype(jnp.float32), lambda: None)
    r.stream0[...] = x
    stream_ref[...] = x
    unit, _ = norm_parts(x)
    normed = (unit * r.gains[1:2] + r.shifts[1:2]).astype(low)
    dense_normed[...] = normed
    save(0, settle)
    dense_normed_t[...] = normed.T

    def dense(i, _):
        slot = lax.rem(i, 2)
        for load in block_loads(i):
            load.wait()
        active, slope = gelu_parts(dot(dense_normed[...], dense_in[slot]))
        active = active.astype(low)
        at = pl.ds(pl.multiple_of(i * width, width), width)
        slope_ref[:, at] = slope.astype(low)
        active_ref[at, :] = active.T
        stream_ref[...] += dot(active, dense_out[slot])

        @pl.when(i + 2 < blocks)
        def _():
            for load in block_loads(i + 2):
                load.start()

        return 0

    lax.fori_loop(0, blocks, dense, 0)
    write(dense_normed_t, r.dense_normed_t, stored.at[0])
    write(active_ref, r.active_t, stored.at[1])
    write(slope_ref, r.slope, stored.at[2])
    x = stream_ref[...]
    r.stream1[...] = x

    cot_across = Across(n_ex, cot_send, far_cot, cot_send_sem, cot_recv_sem)

    def send_cotangent():
        cot_send[...] = dot(dispatch_of(r.assign[...], n_ex), r.cot[...]).astype(low).reshape(cot_send.shape)
        cot_across.start_all()
        far_cot[links.expert] = cot_send[links.expert]

    x, settle = layer(1, x, send_cotangent)
    r.stream2[...] = x
    save(1, settle)
    cot_across.wait_all()
    write(far_cot, r.far_cot, stored.at[3])
    for copy in writes:
        copy.wait()


def front(n_dp, n_ex, collective_id, near, far):
    arrays = {**near, **far}
    a = types.SimpleNamespace(**arrays)
    low, wide = jnp.bfloat16, jnp.float32
    tokens, width = a.tokens.shape
    hidden, mixed = a.dense_in.shape[1], a.attn_in.shape[2]
    long, short, pairs = LONG_DEV, tokens - LONG_DEV, width // 128
    slab = (n_ex, capacity_of(tokens, n_ex)[1], width)
    saved = dict(
        normed_t=jax.ShapeDtypeStruct((width, tokens), low),
        context=jax.ShapeDtypeStruct((tokens, width), low),
        context_t=jax.ShapeDtypeStruct((width, tokens), low),
        kv=jax.ShapeDtypeStruct((n_dp, pairs, 2, long, 128), low),
        q=jax.ShapeDtypeStruct((n_dp, pairs, long, 128), low),
        short_kv=jax.ShapeDtypeStruct((pairs, 2, short, 128), low),
        short_q=jax.ShapeDtypeStruct((pairs, short, 128), low),
        lse=jax.ShapeDtypeStruct((pairs, 2, tokens), wide),
    )
    stream = jax.ShapeDtypeStruct((tokens, width), wide)
    outs = dict(stream0=stream, stream1=stream, stream2=stream)
    direct = len(outs)
    for layer in range(2):
        for name, shape in saved.items():
            outs[name + str(layer)] = shape
    outs.update(
        dense_normed_t=jax.ShapeDtypeStruct((width, tokens), low),
        active_t=jax.ShapeDtypeStruct((hidden, tokens), low),
        slope=jax.ShapeDtypeStruct((tokens, hidden), low),
        far_cot=jax.ShapeDtypeStruct(slab, low),
    )
    scratch = []
    for layer in range(2):
        scratch += [pltpu.VMEM(shape.shape, shape.dtype) for shape in saved.values()]
        scratch += [pltpu.VMEM((n_dp, long, width), low)]
        scratch += spread_sems(n_dp, 1) + spread_sems(n_dp, 1)
        scratch += [pltpu.SemaphoreType.DMA((len(saved),))]
    scratch += [pltpu.VMEM((pairs, 128, 2 * long), wide)] + [pltpu.VMEM((pairs, 1, 2 * long), wide)] * 2
    scratch += [pltpu.VMEM((2, width, mixed), low), pltpu.VMEM((2, width, width), low), pltpu.SemaphoreType.DMA((2, 3))]
    scratch += [pltpu.VMEM((2, width, width), low)] * 2 + [pltpu.SemaphoreType.DMA((2, 2))]
    scratch += [
        pltpu.VMEM((tokens, width), wide),
        pltpu.VMEM((tokens, width), low),
        pltpu.VMEM((hidden, tokens), low),
        pltpu.VMEM((tokens, hidden), low),
        pltpu.VMEM((width, tokens), low),
        pltpu.VMEM(slab, low),
        pltpu.SemaphoreType.DMA((4,)),
        pltpu.VMEM(slab, low),
        pltpu.SemaphoreType.DMA((n_ex,)),
        pltpu.SemaphoreType.DMA((n_ex,)),
    ]
    vmem, anywhere = pl.BlockSpec(memory_space=pltpu.VMEM), pl.BlockSpec(memory_space=pl.ANY)
    names = tuple(arrays) + tuple(outs)
    values = pl.pallas_call(
        functools.partial(front_kernel, n_dp, n_ex, names, tuple(saved)),
        out_shape=list(outs.values()),
        in_specs=[vmem] * len(near) + [anywhere] * len(far),
        out_specs=[vmem] * direct + [anywhere] * (len(outs) - direct),
        scratch_shapes=scratch,
        compiler_params=pltpu.CompilerParams(
            collective_id=collective_id, has_side_effects=True, vmem_limit_bytes=63 * 1024 * 1024
        ),
        name="front",
    )(*arrays.values())
    return types.SimpleNamespace(**dict(zip(outs, values)))


def runs(most, count, use):
    for first in range(0, most, 3):
        for size in range(1, min(3, most - first) + 1):
            exactly = count - first == size if size < 3 else count - first >= size

            @pl.when(exactly)
            def _():
                use(first, size)


def put_context_grads(grad_context, do_ref, short_do_ref, me, long):
    for h in range(do_ref.shape[1]):
        piece = grad_context[:, 128 * h : 128 * h + 128]
        do_ref[me, h] = piece[:long]
        short_do_ref[h] = piece[long:]


def put_row_terms(context, lse, grad_context, aux_ref, short_aux_ref, me, long):
    width = grad_context.shape[1]
    rows = (width // HEAD_DIM + 15) // 16 * 16
    lane = lax.broadcasted_iota(jnp.int32, (rows, width), 1)
    head = lax.broadcasted_iota(jnp.int32, (rows, width), 0) * HEAD_DIM
    picks = jnp.where((lane >= head) & (lane < head + HEAD_DIM), 1.0, 0.0).astype(jnp.bfloat16)
    both = grad_context.astype(jnp.float32) * context[...].astype(jnp.float32)
    high = both.astype(jnp.bfloat16)
    delta = dot_rows(picks, high) + dot_rows(picks, (both - high.astype(jnp.float32)).astype(jnp.bfloat16))
    for h in range(aux_ref.shape[1]):
        aux_ref[me, h, 0:2] = lse[h, :, :long]
        aux_ref[me, h, 2:4] = delta[2 * h : 2 * h + 2, :long]
        short_aux_ref[h, 0:2] = lse[h, :, long:]
        short_aux_ref[h, 2:4] = delta[2 * h : 2 * h + 2, long:]


def attend_back_pairs(n_dp, me, width, r, do_spread, aux_spread, hs):
    scale = HEAD_DIM ** (-0.5)
    mixed_ref, low = r.mixed, jnp.bfloat16
    long = r.kv.shape[3]
    each = range(len(hs))

    def row_of(aux):
        return [jnp.concatenate([aux[i : i + 1], aux[i + 1 : i + 2]], axis=1) for i in (0, 2)]

    def score_grads(keys, values, queries, grads, rows, seen):
        each = range(len(keys))
        scores = [dot_rows(keys[n], queries[n]) for n in each]
        grad_probs = [dot_rows(values[n], grads[n]) for n in each]
        probs = [jnp.exp(scores[n] - rows[n][0]) for n in each]
        if seen is not None:
            probs = [jnp.where(seen, v, 0.0) for v in probs]
        grad_scores = [(probs[n] * (grad_probs[n] - rows[n][1])).astype(low) for n in each]
        return [v.astype(low) for v in probs], grad_scores

    def put(h, third, first, value):
        at = pl.ds(pl.multiple_of(third * width + 128 * h, 128), 128)
        mixed_ref[first : first + value.shape[0], at] = value.astype(low)

    seen = short_seen(r.doc_row[...])
    short_queries, short_grads = [head_pair(r.short_q[h]) for h in hs], [head_pair(r.short_do[h]) for h in hs]
    short_keys = [r.short_kv[h, 0] for h in hs]
    short_values = [r.short_kv[h, 1] for h in hs]
    short_rows = [row_of(r.short_aux[h]) for h in hs]
    probs, grad_scores = score_grads(short_keys, short_values, short_queries, short_grads, short_rows, seen)
    short_dq = [(pair_rows(dot_columns(short_keys[n], grad_scores[n])) * scale).T for n in each]
    short_dk = [dot(grad_scores[n], short_queries[n]) for n in each]
    short_dv = [dot(probs[n], short_grads[n]) for n in each]

    queries, grads = [head_pair(r.q[me, h]) for h in hs], [head_pair(r.do[me, h]) for h in hs]
    own_keys, own_values = [r.kv[me, h, 0] for h in hs], [r.kv[me, h, 1] for h in hs]
    own_rows = [row_of(r.aux[me, h]) for h in hs]
    probs, grad_scores = score_grads(own_keys, own_values, queries, grads, own_rows, causal(long, long))
    dq = [dot_columns(own_keys[n], grad_scores[n]) for n in each]
    dk = [dot(grad_scores[n], queries[n]) for n in each]
    dv = [dot(probs[n], grads[n]) for n in each]
    for n, h in enumerate(hs):
        for third, value in enumerate((short_dq[n], short_dk[n], short_dv[n])):
            put(h, third, long, value)
        r.dq[n], r.dk[n], r.dv[n] = dq[n], dk[n], dv[n]

    def earlier(first, size):
        at = pl.ds(first, size)
        for n, h in enumerate(hs):
            keys = r.kv[at, h, 0].reshape(size * long, 128)
            values = r.kv[at, h, 1].reshape(size * long, 128)
            _, (grad_scores,) = score_grads([keys], [values], [queries[n]], [grads[n]], [own_rows[n]], None)
            r.dq[n] += dot_columns(keys, grad_scores)

    runs(n_dp - 1, me, earlier)
    for n, h in enumerate(hs):
        put(h, 0, 0, (pair_rows(r.dq[n]) * scale).T)
    for h in hs:
        do_spread.relay(h)
        aux_spread.relay(h)

    def later(first, size):
        blocks = [me + 1 + first + i for i in range(size)]
        for n, h in enumerate(hs):
            queries = jnp.concatenate([head_pair(r.q[block, h]) for block in blocks], axis=0)
            grads = jnp.concatenate([head_pair(r.do[block, h]) for block in blocks], axis=0)
            parts = [row_of(r.aux[block, h]) for block in blocks]
            rows = [jnp.concatenate([part[i] for part in parts], axis=1) for i in range(2)]
            (probs,), (grad_scores,) = score_grads([own_keys[n]], [own_values[n]], [queries], [grads], [rows], None)
            r.dk[n] += dot(grad_scores, queries)
            r.dv[n] += dot(probs, grads)

    for h in hs:
        aux_spread.each(h, lambda block: None)
        do_spread.each(h, lambda block: None)
    runs(n_dp - 1, n_dp - 1 - me, later)
    for n, h in enumerate(hs):
        put(h, 1, 0, r.dk[n])
        put(h, 2, 0, r.dv[n])


def back_scratch(n_dp, pairs, long, short):
    return (
        [
            pltpu.VMEM((n_dp, pairs, long, 128), jnp.bfloat16),
            pltpu.VMEM((n_dp, pairs, 8, long), jnp.float32),
            pltpu.VMEM((pairs, short, 128), jnp.bfloat16),
            pltpu.VMEM((pairs, 8, short), jnp.float32),
            pltpu.VMEM((2, 128, 2 * long), jnp.float32),
            pltpu.VMEM((2, long, 128), jnp.float32),
            pltpu.VMEM((2, long, 128), jnp.float32),
        ]
        + spread_sems(n_dp, pairs)
        + spread_sems(n_dp, pairs)
    )


def lane_plan(n_dp, n_ex, rows, order):
    dp_levels = [("dp", b) for b in range(n_dp.bit_length() - 1)]
    ex_levels = n_ex.bit_length() - 1
    halved, piece = [], rows
    for level in ((0, 1), (1, 0))[order]:
        if level < ex_levels and piece % 32 == 0:
            halved.append(level)
            piece //= 2
    halves = [("half", b) for b in halved]
    if order:
        kinds = dp_levels[:1] + halves[:1] + dp_levels[1:] + halves[1:]
    else:
        kinds = dp_levels + halves
    kinds += [("both", b) for b in range(ex_levels) if b not in halved]
    kinds += [("back", b) for b in reversed(halved)]
    return kinds, halved


class Lane:
    def __init__(self, n_dp, n_ex, rows, columns, order, refs):
        self.rows, self.columns = rows, columns
        self.kinds, self.halved = lane_plan(n_dp, n_ex, rows, order)
        self.count = len(self.kinds)
        moving = [k[0] != "back" for k in self.kinds]
        self.send = [next(refs) if m else None for m in moving]
        self.recv = [next(refs) if m else None for m in moving]
        self.keep = [next(refs) if m else None for m in moving]
        self.fin = next(refs)
        self.send_sems = [next(refs) for _ in moving]
        self.recv_sems = [next(refs) for _ in moving]
        self.d, self.e = lax.axis_index("dp"), lax.axis_index("expert")

    @staticmethod
    def scratch(n_dp, n_ex, rows, columns, order):
        kinds, halved = lane_plan(n_dp, n_ex, rows, order)
        width, pieces, height, shapes = columns[1] - columns[0], n_dp, rows, []
        for kind, _ in kinds:
            if kind == "dp":
                pieces //= 2
            elif kind == "half":
                height //= 2
            if kind != "back":
                shapes.append((pieces, height, width))
        scratch = [pltpu.VMEM((2,) + s, jnp.bfloat16) for s in shapes]
        scratch += [pltpu.VMEM((4,) + s, jnp.bfloat16) for s in shapes]
        scratch += [pltpu.VMEM((2,) + s, jnp.float32) for s in shapes]
        scratch += [pltpu.VMEM((len(halved) + 3, rows, width) if halved else (1, 16, 128), jnp.bfloat16)]
        return scratch + [pltpu.SemaphoreType.DMA((4,)) for _ in kinds] * 2

    def peer(self, kind, level):
        return (flip(self.d, level), self.e) if kind == "dp" else (self.d, flip(self.e, level))

    def kept_rows(self, depth):
        start = 0
        for i, level in enumerate(self.halved[:depth]):
            start = start + bit_of(self.e, level) * (self.rows >> (i + 1))
        return start

    def copy_of(self, s, c):
        kind, level = self.kinds[s]
        slot, place = lax.rem(c, 2), lax.rem(c, 4)
        if kind == "back":
            depth = self.halved.index(level) + 1
            span = self.rows >> depth
            at = pl.ds(pl.multiple_of(self.kept_rows(depth), span), span)
            src = self.fin.at[lax.rem(c, len(self.halved) + 3), at]
            dst = src
        else:
            src, dst = self.send[s].at[slot], self.recv[s].at[place]
        return pltpu.make_async_remote_copy(
            src_ref=src,
            dst_ref=dst,
            send_sem=self.send_sems[s].at[place],
            recv_sem=self.recv_sems[s].at[place],
            device_id=self.peer(kind, level),
            device_id_type=MESH,
        )

    def arrive(self, s, c):
        self.copy_of(s, c).wait()
        slot, place = lax.rem(c, 2), lax.rem(c, 4)
        if self.kinds[s][0] == "back":
            return None
        return [
            self.keep[s][slot, i] + self.recv[s][place, i].astype(jnp.float32) for i in range(self.keep[s].shape[1])
        ]

    def leave(self, s, c, values):
        kind, level = self.kinds[s]
        slot = lax.rem(c, 2)
        kept = None
        if kind == "dp":
            sent, kept = values[1::2], values[0::2]
        elif kind == "half":
            half = values[0].shape[0] // 2
            own = bit_of(self.e, level)
            sent = [jnp.where(own == 0, v[half:], v[:half]) for v in values]
            kept = [jnp.where(own == 0, v[:half], v[half:]) for v in values]
        elif kind == "both":
            sent = values
            kept = [v.astype(jnp.bfloat16).astype(jnp.float32) for v in values]
        elif values is not None:
            span = values[0].shape[0]
            at = pl.ds(pl.multiple_of(self.kept_rows(len(self.halved)), span), span)
            self.fin[lax.rem(c, len(self.halved) + 3), at] = values[0].astype(jnp.bfloat16)
        if kept is not None:
            for i, v in enumerate(sent):
                self.send[s][slot, i] = v.astype(jnp.bfloat16)
        self.copy_of(s, c).start()
        if kept is not None:
            for i, v in enumerate(kept):
                self.keep[s][slot, i] = v

    def final(self, c):
        values = self.arrive(self.count - 1, c)
        if values is None:
            return self.fin[lax.rem(c, len(self.halved) + 3)]
        return values[0].astype(jnp.bfloat16)


class Reduction:
    def __init__(self, n_dp, n_ex, rows, groups, lanes, refs, out):
        self.n_dp, self.rows, self.groups = n_dp, rows, groups
        self.lanes = [Lane(n_dp, n_ex, rows, columns, order, refs) for columns, order in lanes]
        self.stage_ref, self.stage_sem, self.out = next(refs), next(refs), out
        self.count = self.lanes[0].count
        self.chunks = sum(g[0] for g in groups)
        self.firsts = [sum(g[0] for g in groups[:i]) for i in range(len(groups))]
        self.ticks = self.chunks + self.count
        self.d = lax.axis_index("dp")
        self.peer = self.lanes[0].peer

    @staticmethod
    def scratch(n_dp, n_ex, rows, width, lanes):
        scratch = []
        for columns, order in lanes:
            scratch += Lane.scratch(n_dp, n_ex, rows, columns, order)
        return scratch + [pltpu.VMEM((2, rows, width), jnp.bfloat16), pltpu.SemaphoreType.DMA((2,))]

    def out_copy(self, c):
        slot = lax.rem(c, 2)
        return pltpu.make_async_copy(self.stage_ref.at[slot], self.out.at[c], self.stage_sem.at[slot])

    def first(self, g, c):
        _, piece, factor = self.groups[g]
        j = c - self.firsts[g]
        dy = factor(j)
        slot = lax.rem(c, 2)
        levels = self.n_dp.bit_length() - 1
        half = self.n_dp // 2

        def products(odd):
            parts = [piece(j, partner_index(self.d, 2 * i + odd, levels)) for i in range(half)]
            return dot(jnp.concatenate(parts, axis=0), dy)

        value = products(1)
        for lane in self.lanes:
            for i in range(half):
                part = value[i * self.rows : (i + 1) * self.rows, slice(*lane.columns)]
                lane.send[0][slot, i] = part.astype(jnp.bfloat16)
            lane.copy_of(0, c).start()
        value = products(0)
        for lane in self.lanes:
            for i in range(half):
                lane.keep[0][slot, i] = value[i * self.rows : (i + 1) * self.rows, slice(*lane.columns)]

    def last(self, c):
        slot = lax.rem(c, 2)

        @pl.when(c >= 2)
        def _():
            self.out_copy(c - 2).wait()

        for lane in self.lanes:
            self.stage_ref[slot, :, slice(*lane.columns)] = lane.final(c)
        self.out_copy(c).start()

    def tick(self, t, low, high):
        for s in range(self.count + 1):
            if high - s <= 0 or low - s >= self.chunks:
                continue
            c = t - s
            if s > 0:

                @pl.when((c >= 0) & (c < self.chunks))
                def _(s=s, c=c):
                    if s < self.count:
                        for lane in self.lanes:
                            lane.leave(s, c, lane.arrive(s - 1, c))
                    else:
                        self.last(c)

                continue
            for g, (size, _, _) in enumerate(self.groups):
                begin, end = self.firsts[g], self.firsts[g] + size
                if high <= begin or low >= end:
                    continue

                @pl.when((c >= begin) & (c < end))
                def _(g=g):
                    self.first(g, c)

    def finish(self):
        for c in range(max(0, self.chunks - 2), self.chunks):
            self.out_copy(c).wait()


def dense_lanes(width):
    cut = width // 768 * 640
    return [((0, cut), 0), ((cut, width), 1)]


def middle_kernel(n_dp, n_ex, names, staged, *refs):
    r = types.SimpleNamespace(**dict(zip(names, refs)))
    extra = iter(refs[len(names) :])
    loads = types.SimpleNamespace()
    for name in staged:
        buffer, sem = next(extra), next(extra)
        setattr(loads, name, pltpu.make_async_copy(getattr(r, name), buffer, sem))
        setattr(r, name, buffer)
    w_in_ref, w_out_ref, weight_sem, factor_sem = (next(extra) for _ in range(4))
    rows_ref, send_ref, grad_ref, home_ref, result_ref = (next(extra) for _ in range(5))
    rows_t_ref, back_ref, active_t_ref, hidden_ref = (next(extra) for _ in range(4))
    dgate_ref, home_dgate_ref, stat_send, stat_recv, result_acc, grad_acc = (next(extra) for _ in range(6))
    (
        x_send_sem, x_recv_sem, grad_send_sem, grad_recv_sem, dgate_send_sem, dgate_recv_sem,
        result_send_sem, result_recv_sem, stat_send_sem, stat_recv_sem,
    ) = (next(extra) for _ in range(10))
    do_ref, aux_ref, short_do_ref, short_aux_ref, dq_ref, dk_ref, dv_ref = (next(extra) for _ in range(7))
    do_far, do_near, do_recv, aux_far, aux_near, aux_recv = (next(extra) for _ in range(6))
    links = Links(n_dp)
    d, e, me = links.me, links.expert, links.me
    shared = links.chips == 2
    if shared:
        peer_rows_ref, peer_cot_ref, peer_row_sems, peer_cot_sems = (next(extra) for _ in range(4))
    dp_levels, ex_levels = n_dp.bit_length() - 1, n_ex.bit_length() - 1
    tokens, width = r.stream.shape
    padded = send_ref.shape[1]
    blocks = r.expert_in.shape[1] // width
    pairs, long = r.kv.shape[1], r.kv.shape[3]
    group = min(max(4, 128 // padded), n_ex)
    groups = n_ex // group
    hops = [(flip(d, b), e) for b in range(dp_levels)] + [(d, flip(e, b)) for b in range(ex_levels)]

    def column(i):
        return pl.ds(i * width, width)

    expert_loads = [
        (
            pltpu.make_async_copy(r.expert_in.at[:, column(i)], w_in_ref.at[i], weight_sem.at[0, i]),
            pltpu.make_async_copy(r.expert_out.at[column(i), :], w_out_ref.at[i], weight_sem.at[1, i]),
        )
        for i in range(blocks)
    ]
    for both in expert_loads:
        for load in both:
            load.start()
    for name in staged:
        getattr(loads, name).start()
    greet(links.peers() + across_peers(n_ex))

    def peer_copy(source, target, sems):
        return pltpu.make_async_remote_copy(
            src_ref=source,
            dst_ref=target,
            send_sem=sems.at[0],
            recv_sem=sems.at[1],
            device_id=(flip(d, 1), e),
            device_id_type=MESH,
        )

    def row_copy(j):
        return peer_copy(rows_ref.at[j], peer_rows_ref.at[j], peer_row_sems.at[j])

    if shared:
        cot_copy = peer_copy(r.far_cot, peer_cot_ref, peer_cot_sems)
        cot_copy.start()

    unit, inverse = norm_parts(r.stream[...])
    routed = (unit * r.gains[3:4] + r.shifts[3:4]).astype(jnp.bfloat16)
    assign = r.assign[...]
    dispatch = dispatch_of(assign, n_ex)
    r.dispatch[...] = dispatch
    send_ref[...] = dot(dispatch, routed).astype(jnp.bfloat16).reshape(send_ref.shape)
    x_across = Across(n_ex, send_ref, rows_ref, x_send_sem, x_recv_sem)

    def place(k, i):
        return lax.rem(e // group + k, groups) * group + lax.rem(e + i, group)

    def source(k, i):
        return lax.rem(e // group + k, groups) * group + lax.rem(e + group - i, group)

    for i in range(group):
        if i:
            x_across.start(place(0, i))
        for k in range(1, groups):
            x_across.start(place(k, i))
    rows_ref[e] = send_ref[e]
    router = r.router[...]
    hot = chosen_rows(assign, n_ex)
    gate = jax.nn.sigmoid(jnp.sum(hot * dot_rows(router, routed), axis=0, keepdims=True))
    r.gate[...] = gate

    def stat_copy(i):
        return pltpu.make_async_remote_copy(
            src_ref=stat_send.at[i],
            dst_ref=stat_recv.at[i],
            send_sem=stat_send_sem.at[i],
            recv_sem=stat_recv_sem.at[i],
            device_id=hops[i],
            device_id_type=MESH,
        )

    lane = lax.broadcasted_iota(jnp.int32, r.stats.shape, 1)
    stat_send[0] = jnp.where(
        lane == 0, jnp.sum(hot, axis=1, keepdims=True), jnp.sum(hot * gate, axis=1, keepdims=True)
    )
    stat_copy(0).start()

    def stat_step(i):
        stat_copy(i).wait()
        value = stat_send[i] + stat_recv[i]
        if i + 1 < len(hops):
            stat_send[i + 1] = value
            stat_copy(i + 1).start()
        else:
            r.stats[...] = value

    grad_across = Across(n_ex, grad_ref, home_ref, grad_send_sem, grad_recv_sem)
    dgate_across = Across(n_ex, dgate_ref, home_dgate_ref, dgate_send_sem, dgate_recv_sem)
    steps = [[(0, i) for i in range(group)]]
    cut = group // 2 if (group // 2) * padded % 128 == 0 else group
    for k in range(1, groups):
        steps += [[(k, i) for i in range(first, first + cut)] for first in range(0, group, cut)]
    def expert_rows(rows, cot, at, whole):
        count = rows.shape[0]
        logits = dot_rows(rows, router)
        own = lax.broadcasted_iota(jnp.int32, logits.shape, 1) == e
        slot_gate = jax.nn.sigmoid(jnp.sum(jnp.where(own, logits, 0.0), axis=1, keepdims=True))
        back = (slot_gate * cot).astype(jnp.bfloat16)
        span = slice(at, at + count)
        back_ref[span] = back
        rows_t_ref[:, span] = rows.T
        if whole:
            result_acc[:count] = jnp.zeros((count, width), jnp.float32)
            grad_acc[:count] = jnp.zeros((count, width), jnp.float32)

        def block(i, _):
            cols = pl.ds(pl.multiple_of(i * width, width), width)
            active, slope = gelu_parts(dot(rows, w_in_ref[i]))
            active = active.astype(jnp.bfloat16)
            hidden = (slope * dot_rows(back, w_out_ref[i])).astype(jnp.bfloat16)
            active_t_ref[cols, span] = active.T
            hidden_ref[span, cols] = hidden
            if whole:
                result_acc[:count] += dot(active, w_out_ref[i])
                grad_acc[:count] += dot_rows(hidden, w_in_ref[i])
            return 0

        lax.fori_loop(0, blocks, block, 0)

    done, at = 0, 0
    for number, members in enumerate(steps):
        count = len(members) * padded
        sources = [source(k, i) for k, i in members]
        for (k, i), j in zip(members, sources):
            if (k, i) != (0, 0):
                x_across.wait_from(j)
            if shared:
                row_copy(j).start()
        rows = jnp.concatenate([rows_ref[j] for j in sources], axis=0)
        cot = jnp.concatenate([r.far_cot[j] for j in sources], axis=0).astype(jnp.float32)
        if number == 0:
            for both in expert_loads:
                for load in both:
                    load.wait()
        expert_rows(rows, cot, at, True)
        grad = grad_acc[:count].astype(jnp.bfloat16)
        result = result_acc[:count].astype(jnp.bfloat16)
        both = cot * result.astype(jnp.float32)
        high = both.astype(jnp.bfloat16)
        rest = both - high.astype(jnp.float32)
        ones = jnp.ones((16, width), jnp.bfloat16)
        dgate = dot_rows(ones, high) + dot_rows(ones, rest.astype(jnp.bfloat16))
        for m, (k, i) in enumerate(members):
            j, part = sources[m], slice(m * padded, (m + 1) * padded)
            grad_ref[j] = grad[part]
            result_ref[j] = result[part]
            dgate_ref[j, :, :padded] = dgate[:8, part]
            if (k, i) == (0, 0):
                home_ref[e] = grad_ref[e]
                home_dgate_ref[e] = dgate_ref[e]
            else:
                grad_across.start(j)
                dgate_across.start(j)
        at += count
        if done < len(hops):
            stat_step(done)
            done += 1

    if shared:
        cot_copy.wait()
        for k in range(groups):
            sources = [source(k, i) for i in range(group)]
            for j in sources:
                row_copy(j).wait()
            rows = jnp.concatenate([peer_rows_ref[j] for j in sources], axis=0)
            cot = jnp.concatenate([peer_cot_ref[j] for j in sources], axis=0).astype(jnp.float32)
            expert_rows(rows, cot, at, False)
            at += group * padded
            if done < len(hops):
                stat_step(done)
                done += 1

    thirds = [w_in_ref.at[i] for i in range(3)]
    in_loads = [
        pltpu.make_async_copy(r.attn_in.at[1, :, column(i)], third, weight_sem.at[0, i])
        for i, third in enumerate(thirds)
    ]
    out_load = pltpu.make_async_copy(r.attn_out.at[1], w_out_ref.at[0], weight_sem.at[1, 0])
    for load in in_loads + [out_load]:
        load.start()
    rows = width // n_dp

    def rows_of(ref, j, q):
        return ref[pl.ds(pl.multiple_of((q * (ref.shape[0] // width) + j) * rows, rows), rows), :]

    red, writes = None, []
    if shared:
        factors = ((rows_t_ref, r.rows_t), (back_ref, r.back), (active_t_ref, r.expert_active_t), (hidden_ref, r.expert_hidden))
        writes = [pltpu.make_async_copy(here, there, factor_sem.at[i]) for i, (here, there) in enumerate(factors)]
        for write in writes:
            write.start()
    else:
        factors = [
            (blocks, lambda j, q: rows_of(rows_t_ref, 0, q), lambda j: hidden_ref[:, pl.ds(pl.multiple_of(j * width, width), width)]),
            (blocks, lambda j, q: rows_of(active_t_ref, j, q), lambda j: back_ref[...]),
        ]
        red = Reduction(n_dp, 1, rows, factors, [((0, width), 0)], extra, r.chunks)
    early = 0
    if red:
        red.tick(0, 0, 1)
        early = 1
    while done < len(hops):
        stat_step(done)
        done += 1
    x_across.others(x_across.wait_to)
    if red:
        red.tick(1, 1, 2)
        early = 2
    dgate_across.wait_all()
    slot_grads = jnp.concatenate([home_dgate_ref[j, :, :padded] for j in range(n_ex)], axis=1)
    dgate = dot(split(slot_grads), r.dispatch[...])
    dgate = dgate[0:8] + dgate[8:16] + dgate[16:24]
    everyone = tokens * n_dp * n_ex
    share = jnp.sum(jnp.where(lane == 0, r.stats[...], 0.0), axis=1, keepdims=True) / everyone
    weight = balance_weight * n_ex * (share - 1.0 / n_ex) / everyone
    mean_gate = jnp.sum(jnp.where(lane == 1, r.stats[...], 0.0), axis=1, keepdims=True) / everyone
    balance = n_ex * jnp.sum((share - 1.0 / n_ex) * mean_gate, axis=0, keepdims=True)
    r.balance[...] = jnp.broadcast_to(balance, r.balance.shape)
    grad_gate = dgate[0:1] + jnp.sum(hot * weight, axis=0, keepdims=True)
    grad_logits = hot * (grad_gate * gate * (1.0 - gate))
    parts = split(grad_logits)
    product = dot(parts, routed)
    r.router_grad[...] = product[:n_ex] + product[n_ex : 2 * n_ex] + product[2 * n_ex :]
    grad_normed = dot_columns(parts, jnp.concatenate([router] * 3, axis=0))
    if red:
        red.tick(2, 2, 3)
        early = 3
    grad_across.wait_all()
    grad_normed = grad_normed + dot_columns(r.dispatch[...], home_ref[...].reshape(n_ex * padded, width))
    unit, inverse = norm_parts(r.stream[...])
    up = r.cot[...].astype(jnp.float32) + norm_back(unit, inverse, r.gains[3:4], grad_normed)
    r.sums[0:1] = jnp.sum(grad_normed * unit, axis=0, keepdims=True)
    r.sums[1:2] = jnp.sum(grad_normed, axis=0, keepdims=True)

    r.up_next[...] = up
    up_low = up.astype(jnp.bfloat16)
    r.up_low[...] = up_low
    out_load.wait()
    for name in staged:
        getattr(loads, name).wait()
    grad_context = dot_rows(up_low, w_out_ref[0]).astype(jnp.bfloat16)
    put_context_grads(grad_context, do_ref, short_do_ref, me, long)
    do_spread = Spread(links, lambda b, p: do_ref.at[b, p], pairs, False, do_far, do_near, do_recv)
    aux_spread = Spread(links, lambda b, p: aux_ref.at[b, p], pairs, False, aux_far, aux_near, aux_recv)
    put_row_terms(r.context, r.lse, grad_context, aux_ref, short_aux_ref, me, long)
    for h in range(pairs):
        do_spread.send(h)
        aux_spread.send(h)
    result_across = Across(n_ex, result_ref, r.result_home, result_send_sem, result_recv_sem)
    result_across.start_all()
    r.result_home[e] = result_ref[e]
    sequence = types.SimpleNamespace(
        doc_row=r.doc_row, kv=r.kv, q=r.q, short_kv=r.short_kv, short_q=r.short_q,
        do=do_ref, aux=aux_ref, short_do=short_do_ref, short_aux=short_aux_ref, dq=dq_ref, dk=dk_ref, dv=dv_ref,
        mixed=r.mixed,
    )

    def pair(i, _):
        attend_back_pairs(n_dp, me, width, sequence, do_spread, aux_spread, [2 * i, 2 * i + 1])
        if red:
            red.tick(early + 2 * i, early, early + pairs)
            red.tick(early + 2 * i + 1, early, early + pairs)
        return 0

    lax.fori_loop(0, pairs // 2, pair, 0)
    grad_normed = jnp.zeros((tokens, width), jnp.float32)
    for i, third in enumerate(thirds):
        in_loads[i].wait()
        grad_normed = grad_normed + dot_rows(r.mixed[:, i * width : (i + 1) * width], third[...])
    unit, inverse = norm_parts(r.attn_x[...])
    r.up_next[...] += norm_back(unit, inverse, r.gains[2:3], grad_normed)
    r.attn_sums[0:1] = jnp.sum(grad_normed * unit, axis=0, keepdims=True)
    r.attn_sums[1:2] = jnp.sum(grad_normed, axis=0, keepdims=True)

    if red:

        def rest(t, _):
            red.tick(t, early + pairs, red.ticks)
            return 0

        lax.fori_loop(early + pairs, red.ticks, rest, 0)
        red.finish()
    result_across.wait_all()
    for write in writes:
        write.wait()
    for h in range(pairs):
        do_spread.sent(h)
        aux_spread.sent(h)


def middle(n_dp, n_ex, collective_id, near, staged, far):
    arrays = {**near, **staged, **far}
    a = types.SimpleNamespace(**arrays)
    low, wide = jnp.bfloat16, jnp.float32
    tokens, width = a.stream.shape
    hidden = a.expert_in.shape[1]
    mixed = a.attn_in.shape[2]
    blocks, rows = hidden // width, width // n_dp
    long, short, pairs = LONG_DEV, tokens - LONG_DEV, width // 128
    _, padded = capacity_of(tokens, n_ex)
    slots = n_ex * padded
    group = min(max(4, 128 // padded), n_ex) * padded
    slab = (n_ex, padded, width)
    hops = (n_dp * n_ex).bit_length() - 1
    outs = dict(
        up_next=jax.ShapeDtypeStruct((tokens, width), wide),
        up_low=jax.ShapeDtypeStruct((tokens, width), low),
        mixed=jax.ShapeDtypeStruct((tokens, mixed), low),
        sums=jax.ShapeDtypeStruct((2, width), wide),
        attn_sums=jax.ShapeDtypeStruct((2, width), wide),
        router_grad=jax.ShapeDtypeStruct((n_ex, width), wide),
        stats=jax.ShapeDtypeStruct((n_ex, 128), wide),
        balance=jax.ShapeDtypeStruct((1, 128), wide),
        result_home=jax.ShapeDtypeStruct(slab, low),
        gate=jax.ShapeDtypeStruct((1, tokens), wide),
        dispatch=jax.ShapeDtypeStruct((slots, tokens), low),
    )
    direct, shared = len(outs), n_dp == 4
    known = 2 * slots if shared else slots
    if shared:
        outs.update(
            rows_t=jax.ShapeDtypeStruct((width, known), low),
            back=jax.ShapeDtypeStruct((known, width), low),
            expert_active_t=jax.ShapeDtypeStruct((hidden, known), low),
            expert_hidden=jax.ShapeDtypeStruct((known, hidden), low),
        )
    else:
        outs.update(chunks=jax.ShapeDtypeStruct((2 * blocks, rows, width), low))
    scratch = []
    for name in staged:
        scratch += [pltpu.VMEM(arrays[name].shape, arrays[name].dtype), pltpu.SemaphoreType.DMA]
    scratch += [pltpu.VMEM((blocks, width, width), low)] * 2 + [pltpu.SemaphoreType.DMA((2, blocks)), pltpu.SemaphoreType.DMA((4,))]
    scratch += [pltpu.VMEM(slab, low)] * 5
    scratch += [
        pltpu.VMEM((width, known), low),
        pltpu.VMEM((known, width), low),
        pltpu.VMEM((hidden, known), low),
        pltpu.VMEM((known, hidden), low),
        pltpu.VMEM((n_ex, 8, 128), wide),
        pltpu.VMEM((n_ex, 8, 128), wide),
        pltpu.VMEM((hops, n_ex, 128), wide),
        pltpu.VMEM((hops, n_ex, 128), wide),
        pltpu.VMEM((group, width), wide),
        pltpu.VMEM((group, width), wide),
    ]
    scratch += [pltpu.SemaphoreType.DMA((n_ex,))] * 8 + [pltpu.SemaphoreType.DMA((hops,))] * 2
    scratch += back_scratch(n_dp, pairs, long, short)
    if shared:
        scratch += [pltpu.VMEM(slab, low)] * 2 + [pltpu.SemaphoreType.DMA((n_ex, 2)), pltpu.SemaphoreType.DMA((2,))]
    else:
        scratch += Reduction.scratch(n_dp, 1, rows, width, [((0, width), 0)])
    vmem, anywhere = pl.BlockSpec(memory_space=pltpu.VMEM), pl.BlockSpec(memory_space=pl.ANY)
    names = tuple(arrays) + tuple(outs)
    values = pl.pallas_call(
        functools.partial(middle_kernel, n_dp, n_ex, names, tuple(staged)),
        out_shape=list(outs.values()),
        in_specs=[vmem] * len(near) + [anywhere] * (len(staged) + len(far)),
        out_specs=[vmem] * direct + [anywhere] * (len(outs) - direct),
        scratch_shapes=scratch,
        compiler_params=pltpu.CompilerParams(
            collective_id=collective_id, has_side_effects=True, vmem_limit_bytes=62 * 1024 * 1024
        ),
        name="middle",
    )(*arrays.values())
    return types.SimpleNamespace(**dict(zip(outs, values)))


def tail_kernel(n_dp, n_ex, names, staged, *refs):
    r = types.SimpleNamespace(**dict(zip(names, refs)))
    extra = iter(refs[len(names) :])
    loads = types.SimpleNamespace()
    for name in staged:
        buffer, sem = next(extra), next(extra)
        setattr(loads, name, pltpu.make_async_copy(getattr(r, name), buffer, sem))
        setattr(r, name, buffer)
    weights_in, weights_out, slopes, weight_sem = (next(extra) for _ in range(4))
    first_sem = next(extra)
    acc_ref, dense_low_ref, dense_hidden_ref = (next(extra) for _ in range(3))
    up_ref, first_low_ref, mixed_ref = acc_ref, r.second_low, r.second_mixed
    do_ref, aux_ref, short_do_ref, short_aux_ref, dq_ref, dk_ref, dv_ref = (next(extra) for _ in range(7))
    do_far, do_near, do_recv, aux_far, aux_near, aux_recv = (next(extra) for _ in range(6))
    small_send, small_recv, small_send_sem, small_recv_sem = (next(extra) for _ in range(4))
    shared = n_dp == 4
    if shared:
        expert_x, expert_y, expert_sem = (next(extra) for _ in range(3))
    links = Links(n_dp)
    me = links.me
    width = up_ref.shape[1]
    rows = width // n_dp
    pairs, long = r.kv.shape[1], r.kv.shape[3]
    blocks = r.dense_in.shape[1] // width
    per_in = mixed_ref.shape[1] // width

    def block_loads(i):
        slot = lax.rem(i, 2)
        at = pl.ds(pl.multiple_of(i * width, width), width)
        return [
            pltpu.make_async_copy(r.dense_out.at[at, :], weights_out.at[slot], weight_sem.at[slot, 0]),
            pltpu.make_async_copy(r.dense_in.at[:, at], weights_in.at[slot], weight_sem.at[slot, 1]),
            pltpu.make_async_copy(r.slope.at[:, at], slopes.at[slot], weight_sem.at[slot, 2]),
        ]

    ready = (loads.second_context_t, loads.second_low, loads.second_normed_t, loads.second_mixed)
    for load in ready:
        load.start()
    for i in range(min(2, blocks)):
        for load in block_loads(i):
            load.start()
    loads.active_t.start()
    for name in staged:
        if all(getattr(loads, name) is not load for load in ready + (loads.active_t,)):
            getattr(loads, name).start()
    free, busy = blocks % 2, (blocks - 1) % 2
    out_load = pltpu.make_async_copy(r.attn_out.at[0], weights_out.at[free], first_sem.at[0])
    thirds = [weights_in.at[free], weights_in.at[busy], weights_out.at[busy]]
    in_loads = [
        pltpu.make_async_copy(r.attn_in.at[0, :, pl.ds(i * width, width)], third, first_sem.at[1 + i])
        for i, third in enumerate(thirds)
    ]

    def columns(ref):
        return lambda j: ref[:, pl.ds(pl.multiple_of(j * width, width), width)]

    def one(ref):
        return lambda j, q: ref[q, 0]

    groups = [
        (1, one(r.second_context_t), columns(r.second_low)),
        (per_in, one(r.second_normed_t), columns(r.second_mixed)),
        (blocks, lambda j, q: r.active_t[q, j], lambda j: dense_low_ref[...]),
        (blocks, one(r.dense_normed_t), columns(dense_hidden_ref)),
        (1, one(r.first_context_t), columns(first_low_ref)),
        (per_in, one(r.first_normed_t), columns(mixed_ref)),
    ]
    red = Reduction(n_dp, n_ex, rows, groups, dense_lanes(width), extra, r.chunks)
    if shared:
        expert_blocks = r.expert_hidden.shape[1] // width
        base = 2 * links.chip

        def expert_loads(c, act):
            slot = lax.rem(c, 2)

            def load(rows_t, at, per, factor):
                for q in range(2):
                    row = pl.multiple_of(((base + q) * per + at) * rows, rows)
                    act(pltpu.make_async_copy(rows_t.at[pl.ds(row, rows), :], expert_x.at[slot, q], expert_sem.at[slot, q]))
                act(pltpu.make_async_copy(factor, expert_y.at[slot], expert_sem.at[slot, 2]))

            @pl.when(c < expert_blocks)
            def _():
                load(r.rows_t, 0, 1, r.expert_hidden.at[:, pl.ds(pl.multiple_of(c * width, width), width)])

            @pl.when((c >= expert_blocks) & (c < 2 * expert_blocks))
            def _():
                load(r.expert_active_t, c - expert_blocks, expert_blocks, r.back)

        def expert_part(j, q):
            return expert_x[lax.rem(j, 2), q]

        expert_groups = [(2 * expert_blocks, expert_part, lambda j: expert_y[lax.rem(j, 2)])]
        expert_red = Reduction(2, 1, rows, expert_groups, [((0, width), 0)], extra, r.expert_chunks)
    levels = [("dp", b) for b in range(n_dp.bit_length() - 1)] + [("ex", b) for b in range(n_ex.bit_length() - 1)]
    greet([red.peer(*level) for level in levels] + (links.peers()[1:] if links.chips > 2 else []))

    up = r.up[...]
    dense_low_ref[...] = up.astype(jnp.bfloat16)
    acc_ref[...] = jnp.zeros_like(acc_ref)
    for load in ready:
        load.wait()
    red.tick(0, 0, 1)
    loads.active_t.wait()

    def dense(i, _):
        slot = lax.rem(i, 2)
        for load in block_loads(i):
            load.wait()
        grad = dot_rows(dense_low_ref[...], weights_out[slot]) * slopes[slot].astype(jnp.float32)
        grad = grad.astype(jnp.bfloat16)
        dense_hidden_ref[:, pl.ds(pl.multiple_of(i * width, width), width)] = grad
        acc_ref[...] += dot_rows(grad, weights_in[slot])

        @pl.when(i + 2 < blocks)
        def _():
            for load in block_loads(i + 2):
                load.start()

        @pl.when(i == blocks - 2)
        def _():
            out_load.start()
            in_loads[0].start()

        red.tick(1 + i, 1, 1 + blocks)
        return 0

    lax.fori_loop(0, blocks, dense, 0)
    for load in in_loads[1:]:
        load.start()
    for name in staged:
        if all(getattr(loads, name) is not load for load in ready + (loads.active_t,)):
            getattr(loads, name).wait()
    unit, inverse = norm_parts(r.dense_x[...])
    grad_normed = acc_ref[...]
    up = up + norm_back(unit, inverse, r.gains[1:2], grad_normed)
    up_ref[...] = up
    for first, sums in ((2, r.second_sums), (3, r.last_sums)):
        small_send[0, first : first + 1] = sums[0:1]
        small_send[0, first + 4 : first + 5] = sums[1:2]
    small_send[0, 8:] = r.router_grad[...]
    small_send[0, 1:2] = jnp.sum(grad_normed * unit, axis=0, keepdims=True)
    small_send[0, 5:6] = jnp.sum(grad_normed, axis=0, keepdims=True)
    at_tick = 1 + blocks

    scale = HEAD_DIM ** (-0.5)
    up_low = up.astype(jnp.bfloat16)
    first_low_ref[...] = up_low
    out_load.wait()
    grad_context = dot_rows(up_low, weights_out[free]).astype(jnp.bfloat16)
    red.tick(at_tick, at_tick, at_tick + 1)
    at_tick += 1
    put_context_grads(grad_context, do_ref, short_do_ref, me, long)
    do_spread = Spread(links, lambda b, p: do_ref.at[b, p], pairs, False, do_far, do_near, do_recv)
    aux_spread = Spread(links, lambda b, p: aux_ref.at[b, p], pairs, False, aux_far, aux_near, aux_recv)
    put_row_terms(r.context, r.lse, grad_context, aux_ref, short_aux_ref, me, long)
    for h in range(pairs):
        do_spread.send(h)
        aux_spread.send(h)
    red.tick(at_tick, at_tick, at_tick + 1)
    at_tick += 1
    sequence = types.SimpleNamespace(
        doc_row=r.doc_row, kv=r.kv, q=r.q, short_kv=r.short_kv, short_q=r.short_q,
        do=do_ref, aux=aux_ref, short_do=short_do_ref, short_aux=short_aux_ref, dq=dq_ref, dk=dk_ref, dv=dv_ref,
        mixed=mixed_ref,
    )

    def pair(i, _):
        red.tick(at_tick + 2 * i, at_tick, at_tick + pairs)
        attend_back_pairs(n_dp, me, width, sequence, do_spread, aux_spread, [2 * i, 2 * i + 1])
        red.tick(at_tick + 2 * i + 1, at_tick, at_tick + pairs)
        return 0

    lax.fori_loop(0, pairs // 2, pair, 0)
    at_tick += pairs
    grad_normed = jnp.zeros((up_ref.shape[0], width), jnp.float32)
    for i, third in enumerate(thirds):
        in_loads[i].wait()
        grad_normed = grad_normed + dot_rows(mixed_ref[:, i * width : (i + 1) * width], third[...])
    unit, inverse = norm_parts(r.first_x[...].astype(jnp.float32))
    r.grad_tokens[...] = (
        up_ref[...] + norm_back(unit, inverse, r.gains[0:1], grad_normed)
    ).astype(jnp.bfloat16)
    small_send[0, 0:1] = jnp.sum(grad_normed * unit, axis=0, keepdims=True)
    small_send[0, 4:5] = jnp.sum(grad_normed, axis=0, keepdims=True)

    def small_copy(i):
        return pltpu.make_async_remote_copy(
            src_ref=small_send.at[i],
            dst_ref=small_recv.at[i],
            send_sem=small_send_sem.at[i],
            recv_sem=small_recv_sem.at[i],
            device_id=red.peer(*levels[i]),
            device_id_type=MESH,
        )

    small_copy(0).start()

    if shared:
        for c in range(2):
            expert_loads(jnp.int32(c), lambda copy: copy.start())

    def rest(t, _):
        red.tick(t, at_tick, red.ticks)
        if shared:
            c = t - at_tick
            expert_loads(c, lambda copy: copy.wait())
            expert_red.tick(c, 0, red.ticks - at_tick)
            expert_loads(c + 2, lambda copy: copy.start())

        @pl.when(t == red.ticks - 2)
        def _():
            gate = jnp.broadcast_to(r.gate[...], (128, r.gate.shape[1])).T[:, 0:1]
            for first in range(0, width, 256):
                at = slice(first, first + 256)
                home = r.result_home[:, :, at].reshape(r.dispatch.shape[0], 256)
                result = dot_columns(r.dispatch[...], home)
                r.output[:, at] = (r.last_x[:, at] + gate * result).astype(jnp.bfloat16)

        for i in range(1, len(levels) + 1):

            @pl.when(t == at_tick + i)
            def _(i=i):
                small_copy(i - 1).wait()
                value = small_send[i - 1] + small_recv[i - 1]
                if i < len(levels):
                    small_send[i] = value
                    small_copy(i).start()
                else:
                    own = jnp.zeros((value.shape[0], rows), jnp.float32)
                    for q in range(n_dp):
                        own = own + jnp.where(me == q, value[:, q * rows : (q + 1) * rows], 0.0)
                    r.small_sum[...] = own

        return 0

    lax.fori_loop(at_tick, red.ticks, rest, 0)
    if shared:
        for c in range(red.ticks - at_tick, expert_red.ticks):
            expert_loads(jnp.int32(c), lambda copy: copy.wait())
            expert_red.tick(jnp.int32(c), c, c + 1)
            expert_loads(jnp.int32(c + 2), lambda copy: copy.start())
        expert_red.finish()
    red.finish()
    for h in range(pairs):
        do_spread.sent(h)
        aux_spread.sent(h)


def tail(n_dp, n_ex, collective_id, near, staged, far):
    arrays = {**near, **staged, **far}
    a = types.SimpleNamespace(**arrays)
    low, wide = jnp.bfloat16, jnp.float32
    tokens, width = a.up.shape
    hidden = a.dense_in.shape[1]
    mixed = a.attn_in.shape[2]
    rows = width // n_dp
    long, short, pairs = LONG_DEV, tokens - LONG_DEV, width // 128
    chunks = 2 * (hidden // width) + 2 * (1 + mixed // width)
    small = (8 + a.router_grad.shape[0], width)
    outs = dict(
        grad_tokens=jax.ShapeDtypeStruct((tokens, width), low),
        output=jax.ShapeDtypeStruct((tokens, width), low),
        small_sum=jax.ShapeDtypeStruct((small[0], rows), wide),
    )
    direct, shared = len(outs), n_dp == 4
    outs.update(chunks=jax.ShapeDtypeStruct((chunks, rows, width), low))
    if shared:
        slots, expert_hidden = a.expert_hidden.shape
        outs.update(expert_chunks=jax.ShapeDtypeStruct((2 * expert_hidden // width, rows, width), low))
    scratch = []
    for name in staged:
        scratch += [pltpu.VMEM(arrays[name].shape, arrays[name].dtype), pltpu.SemaphoreType.DMA]
    scratch += [pltpu.VMEM((2, width, width), low)] * 2
    scratch += [pltpu.VMEM((2, tokens, width), low), pltpu.SemaphoreType.DMA((2, 3))]
    scratch += [pltpu.SemaphoreType.DMA((4,))]
    scratch += [pltpu.VMEM((tokens, width), wide)]
    scratch += [pltpu.VMEM((tokens, n), low) for n in (width, hidden)]
    scratch += back_scratch(n_dp, pairs, long, short)
    hops = (n_dp * n_ex).bit_length() - 1
    scratch += [pltpu.VMEM((hops,) + small, wide)] * 2 + [pltpu.SemaphoreType.DMA((hops,))] * 2
    if shared:
        scratch += [pltpu.VMEM((2, 2, rows, slots), low), pltpu.VMEM((2, slots, width), low)]
        scratch += [pltpu.SemaphoreType.DMA((2, 3))]
    scratch += Reduction.scratch(n_dp, n_ex, rows, width, dense_lanes(width))
    if shared:
        scratch += Reduction.scratch(2, 1, rows, width, [((0, width), 0)])
    vmem, anywhere = pl.BlockSpec(memory_space=pltpu.VMEM), pl.BlockSpec(memory_space=pl.ANY)
    names = tuple(arrays) + tuple(outs)
    values = pl.pallas_call(
        functools.partial(tail_kernel, n_dp, n_ex, names, tuple(staged)),
        out_shape=list(outs.values()),
        in_specs=[vmem] * len(near) + [anywhere] * (len(staged) + len(far)),
        out_specs=[vmem] * direct + [anywhere] * (len(outs) - direct),
        scratch_shapes=scratch,
        compiler_params=pltpu.CompilerParams(
            collective_id=collective_id, has_side_effects=True, vmem_limit_bytes=62 * 1024 * 1024
        ),
        name="tail",
    )(*arrays.values())
    return types.SimpleNamespace(**dict(zip(outs, values)))


def shards(
    tokens,
    doc_lengths,
    assign,
    ln_gain,
    ln_bias,
    attn_in,
    attn_out,
    ffn_in,
    ffn_out,
    router,
    expert_in,
    expert_out,
    cotangent,
):
    n_dp, n_ex = lax.axis_size("dp"), lax.axis_size("expert")
    row_count = tokens.shape[1]
    lengths = doc_lengths[0, 0]
    order = jnp.arange(lengths.shape[0])
    doc_ends = jnp.sum(jnp.where(order[:, None] <= order[None, :], lengths[:, None], 0), axis=0)
    short_place = jnp.arange(row_count - LONG_DEV, dtype=jnp.int32)
    doc_row = jnp.sum((short_place[None, :] >= doc_ends[:, None]).astype(jnp.float32), axis=0, keepdims=True)
    weights_in, weights_out = lax.optimization_barrier((attn_in.transpose(1, 0, 2), attn_out.transpose(1, 0, 2)))
    gains, shifts = ln_gain.T, ln_bias.T
    assign_row = assign[0].T
    fore = front(
        n_dp,
        n_ex,
        2,
        dict(
            tokens=tokens[0],
            gains=gains,
            shifts=shifts,
            doc_row=doc_row,
            assign=assign_row,
            cot=cotangent[0],
        ),
        dict(attn_in=weights_in, attn_out=weights_out, dense_in=ffn_in, dense_out=ffn_out),
    )
    model_width = tokens.shape[2]
    rows = model_width // n_dp
    mid = middle(
        n_dp,
        n_ex,
        4,
        dict(
            stream=fore.stream2,
            gains=gains,
            shifts=shifts,
            router=router.T,
            assign=assign_row,
            cot=cotangent[0],
            far_cot=fore.far_cot,
            doc_row=doc_row,
            lse=fore.lse1,
        ),
        dict(
            attn_x=fore.stream1,
            context=fore.context1,
            kv=fore.kv1,
            q=fore.q1,
            short_kv=fore.short_kv1,
            short_q=fore.short_q1,
        ),
        dict(
            expert_in=expert_in[0],
            expert_out=expert_out[0],
            attn_in=weights_in,
            attn_out=weights_out,
        ),
    )
    def blocks_of(rows_t):
        return rows_t.reshape(n_dp, -1, rows, row_count)

    shared = n_dp == 4
    last = tail(
        n_dp,
        n_ex,
        5,
        dict(
            up=mid.up_next,
            gains=gains,
            doc_row=doc_row,
            lse=fore.lse0,
            second_sums=mid.attn_sums,
            last_sums=mid.sums,
            router_grad=mid.router_grad,
            dispatch=mid.dispatch,
            gate=mid.gate,
        ),
        dict(
            dense_x=fore.stream0,
            first_x=tokens[0],
            context=fore.context0,
            kv=fore.kv0,
            q=fore.q0,
            short_kv=fore.short_kv0,
            short_q=fore.short_q0,
            second_context_t=blocks_of(fore.context_t1),
            second_normed_t=blocks_of(fore.normed_t1),
            active_t=blocks_of(fore.active_t),
            dense_normed_t=blocks_of(fore.dense_normed_t),
            first_context_t=blocks_of(fore.context_t0),
            first_normed_t=blocks_of(fore.normed_t0),
            second_low=mid.up_low,
            result_home=mid.result_home,
            last_x=fore.stream2,
            second_mixed=mid.mixed,
        ),
        dict(
            dense_in=ffn_in,
            dense_out=ffn_out,
            slope=fore.slope,
            attn_in=weights_in,
            attn_out=weights_out,
            **(
                dict(
                    rows_t=mid.rows_t,
                    back=mid.back,
                    expert_active_t=mid.expert_active_t,
                    expert_hidden=mid.expert_hidden,
                )
                if shared
                else {}
            ),
        ),
    )
    expert_chunks = last.expert_chunks if shared else mid.chunks
    (
        attn_in_sum, attn_out_sum, ffn_in_sum, ffn_out_sum, expert_in_sum, expert_out_sum,
        gain_sum, shift_sum, router_sum, grad_tokens, output,
    ) = unpack(
        last.chunks, expert_chunks, last.small_sum, last.grad_tokens, last.output,
        attn_in.shape[2] // model_width, ffn_in.shape[1] // model_width,
    )
    return (
        output[None],
        mid.balance[0, 0],
        grad_tokens[None],
        gain_sum.T,
        shift_sum.T,
        attn_in_sum,
        attn_out_sum,
        ffn_in_sum,
        ffn_out_sum.reshape(-1, model_width),
        router_sum.T,
        expert_in_sum[None],
        expert_out_sum.reshape(1, -1, model_width),
    )


def solution(mesh):
    return jax.shard_map(
        shards,
        mesh=mesh,
        in_specs=(
            P("expert", "dp", None),
            P("expert", "dp", None),
            P("expert", "dp", None),
            P(),
            P(),
            P(),
            P(),
            P(),
            P(),
            P(),
            P("expert", None, None),
            P("expert", None, None),
            P("expert", "dp", None),
        ),
        out_specs=(
            P("expert", "dp", None),
            P(),
            P("expert", "dp", None),
            P("dp", None),
            P("dp", None),
            P("dp", None, None),
            P("dp", None, None),
            P("dp", None),
            P("dp", None),
            P("dp", None),
            P("expert", "dp", None),
            P("expert", "dp", None),
        ),
        check_vma=False,
    )
```

```python
import functools
import types

import jax
import jax.numpy as jnp
from jax import lax
from jax.experimental import pallas as pl
from jax.experimental.pallas import tpu as pltpu
from jax.sharding import PartitionSpec as P

MESH = pl.DeviceIdType.MESH
HEADS = 12
HEAD_DIM = 64
LONG_DEV = 256


epsilon = 1e-05
balance_weight = 0.01
masked_score = -1e30


def bit_of(index, level):
    return (index // (1 << level)) % 2


def flip(index, level):
    return index + (1 << level) * (1 - 2 * bit_of(index, level))


def partner_index(index, mask, levels):
    total = 0
    for level in range(levels):
        own = bit_of(index, level)
        total = total + (1 << level) * (1 - own if (mask >> level) & 1 else own)
    return total


def unpack_kernel(
    per_in, per_ffn,
    chunk_ref, expert_ref, small_ref, tokens_ref, output_ref,
    in_ref, out_ref, ffn_in_ref, ffn_out_ref, expert_in_ref, expert_out_ref,
    gain_ref, shift_ref, router_ref, tokens_out_ref, output_out_ref,
):
    per_expert = expert_ref.shape[0] // 2
    width = chunk_ref.shape[2]
    at = 0
    for layer in (1, 0):
        out_ref[:, layer, :] = chunk_ref[at].astype(jnp.float32)
        for j in range(per_in):
            in_ref[:, layer, width * j : width * j + width] = chunk_ref[at + 1 + j].astype(jnp.float32)
        at += 1 + per_in
        if layer:
            for j in range(per_ffn):
                ffn_out_ref[j] = chunk_ref[at + j].astype(jnp.float32)
                ffn_in_ref[:, width * j : width * j + width] = chunk_ref[at + per_ffn + j].astype(jnp.float32)
            at += 2 * per_ffn
    for j in range(per_expert):
        expert_in_ref[:, width * j : width * j + width] = expert_ref[j].astype(jnp.float32)
        expert_out_ref[j] = expert_ref[per_expert + j].astype(jnp.float32)
    gain_ref[...] = small_ref[0:4]
    shift_ref[...] = small_ref[4:8]
    router_ref[...] = small_ref[8:]
    tokens_out_ref[...] = tokens_ref[...]
    output_out_ref[...] = output_ref[...]


def unpack(chunks, expert_chunks, small, grad_tokens, output, per_in, per_ffn):
    count, rows, width = chunks.shape
    experts = expert_chunks.shape[0]
    tokens = output.shape[0]
    step = 32 if rows % 32 == 0 else rows
    wide, low = jnp.float32, jnp.bfloat16
    token_spec = pl.BlockSpec((tokens // (rows // step), width), lambda i: (i, 0))

    def fixed(shape):
        return pl.BlockSpec(shape, lambda i: (0, 0))

    return pl.pallas_call(
        functools.partial(unpack_kernel, per_in, per_ffn),
        grid=(rows // step,),
        out_shape=[
            jax.ShapeDtypeStruct((rows, 2, per_in * width), wide),
            jax.ShapeDtypeStruct((rows, 2, width), wide),
            jax.ShapeDtypeStruct((rows, per_ffn * width), wide),
            jax.ShapeDtypeStruct((per_ffn, rows, width), wide),
            jax.ShapeDtypeStruct((rows, experts // 2 * width), wide),
            jax.ShapeDtypeStruct((experts // 2, rows, width), wide),
            jax.ShapeDtypeStruct((4, rows), wide),
            jax.ShapeDtypeStruct((4, rows), wide),
            jax.ShapeDtypeStruct((small.shape[0] - 8, rows), wide),
            jax.ShapeDtypeStruct((tokens, width), low),
            jax.ShapeDtypeStruct((tokens, width), low),
        ],
        in_specs=[
            pl.BlockSpec((count, step, width), lambda i: (0, i, 0)),
            pl.BlockSpec((experts, step, width), lambda i: (0, i, 0)),
            fixed(small.shape),
            token_spec,
            token_spec,
        ],
        out_specs=[
            pl.BlockSpec((step, 2, per_in * width), lambda i: (i, 0, 0)),
            pl.BlockSpec((step, 2, width), lambda i: (i, 0, 0)),
            pl.BlockSpec((step, per_ffn * width), lambda i: (i, 0)),
            pl.BlockSpec((per_ffn, step, width), lambda i: (0, i, 0)),
            pl.BlockSpec((step, experts // 2 * width), lambda i: (i, 0)),
            pl.BlockSpec((experts // 2, step, width), lambda i: (0, i, 0)),
            fixed((4, rows)),
            fixed((4, rows)),
            fixed((small.shape[0] - 8, rows)),
            token_spec,
            token_spec,
        ],
        compiler_params=pltpu.CompilerParams(vmem_limit_bytes=62 * 1024 * 1024),
        name="unpack",
    )(chunks, expert_chunks, small, grad_tokens, output)


def dot(a, b):
    return jnp.dot(a, b, preferred_element_type=jnp.float32)


def dot_rows(a, b):
    return lax.dot_general(a, b, (((1,), (1,)), ((), ())), preferred_element_type=jnp.float32)


def dot_columns(a, b):
    return lax.dot_general(a, b, (((0,), (0,)), ((), ())), preferred_element_type=jnp.float32)


def gelu_parts(hidden):
    lower = 0.5 + 0.5 * lax.erf(hidden * 0.7071067811865476)
    slope = lower + hidden * jnp.exp(-0.5 * hidden * hidden) * 0.3989422804014327
    return hidden * lower, slope


def split(value):
    high = value.astype(jnp.bfloat16)
    rest = value - high.astype(jnp.float32)
    middle_part = rest.astype(jnp.bfloat16)
    low = (rest - middle_part.astype(jnp.float32)).astype(jnp.bfloat16)
    return jnp.concatenate([high, middle_part, low], axis=0)


def norm_parts(x):
    center = x - jnp.mean(x, axis=-1, keepdims=True)
    inverse = lax.rsqrt(jnp.mean(center * center, axis=-1, keepdims=True) + epsilon)
    return center * inverse, inverse


def norm_back(unit, inverse, gain, upstream):
    scaled = upstream * gain
    return inverse * (
        scaled - jnp.mean(scaled, axis=-1, keepdims=True) - unit * jnp.mean(scaled * unit, axis=-1, keepdims=True)
    )


def capacity_of(rows, experts):
    capacity = (5 * rows + 4 * experts - 1) // (4 * experts)
    return capacity, -(-capacity // 16) * 16


def chosen_rows(assign, experts):
    expert = lax.broadcasted_iota(jnp.int32, (experts, assign.shape[1]), 0)
    return jnp.where(assign == expert, 1.0, 0.0)


def dispatch_of(assign, experts):
    tokens = assign.shape[1]
    capacity, padded = capacity_of(tokens, experts)
    hot = chosen_rows(assign, experts)
    earlier = lax.broadcasted_iota(jnp.int32, (tokens, tokens), 0) < lax.broadcasted_iota(jnp.int32, (tokens, tokens), 1)
    before = dot(hot.astype(jnp.bfloat16), jnp.where(earlier, 1.0, 0.0).astype(jnp.bfloat16))
    place = jnp.sum(hot * before, axis=0, keepdims=True)
    slot = jnp.where(place < capacity, assign.astype(jnp.float32) * padded + place, -1.0)
    number = lax.broadcasted_iota(jnp.int32, (experts * padded, tokens), 0).astype(jnp.float32)
    return jnp.where(number == slot, 1.0, 0.0).astype(jnp.bfloat16)


class Across:
    def __init__(self, experts, out, into, send_sems, recv_sems):
        self.experts, self.out, self.into = experts, out, into
        self.send_sems, self.recv_sems = send_sems, recv_sems
        self.dp, self.me = lax.axis_index("dp"), lax.axis_index("expert")

    def copy(self, slab, place, to):
        return pltpu.make_async_remote_copy(
            src_ref=self.out.at[slab],
            dst_ref=self.into.at[place],
            send_sem=self.send_sems.at[slab],
            recv_sem=self.recv_sems.at[place],
            device_id=(self.dp, to),
            device_id_type=MESH,
        )

    def start(self, j):
        self.copy(j, self.me, j).start()

    def wait_from(self, j):
        self.copy(j, j, j).wait_recv()

    def wait_to(self, j):
        self.copy(j, self.me, j).wait_send()

    def others(self, use):
        def body(k, _):
            use(lax.rem(self.me + k, self.experts))
            return 0

        lax.fori_loop(1, self.experts, body, 0)

    def start_all(self):
        self.others(self.start)

    def wait_all(self):
        def both(j):
            self.wait_from(j)
            self.wait_to(j)

        self.others(both)


def greet(targets):
    barrier = pltpu.get_barrier_semaphore()
    for device in targets:
        pl.semaphore_signal(barrier, inc=1, device_id=device, device_id_type=MESH)
    pl.semaphore_wait(barrier, len(targets))


def across_peers(experts):
    d, e = lax.axis_index("dp"), lax.axis_index("expert")
    return [(d, lax.rem(e + k, experts)) for k in range(1, experts)]


def head_pair(rows):
    first = lax.broadcasted_iota(jnp.int32, rows.shape, 1) < HEAD_DIM
    zero = jnp.zeros_like(rows)
    return jnp.concatenate([jnp.where(first, rows, zero), jnp.where(first, zero, rows)], axis=0)


def pair_rows(both):
    n = both.shape[1] // 2
    return jnp.concatenate([both[:HEAD_DIM, :n], both[HEAD_DIM:, n:]], axis=0)


def causal(keys, queries):
    key = lax.broadcasted_iota(jnp.int32, (keys, 2 * queries), 0)
    query = lax.broadcasted_iota(jnp.int32, (keys, 2 * queries), 1)
    return key <= jnp.where(query >= queries, query - queries, query)


def short_seen(doc_row):
    n = doc_row.shape[1]
    doc_col = jnp.broadcast_to(doc_row, (n, n)).T
    same = jnp.concatenate([doc_col, doc_col], axis=1) == jnp.concatenate([doc_row, doc_row], axis=1)
    return same & causal(n, n)


class Links:
    def __init__(self, n_dp):
        self.me, self.expert = lax.axis_index("dp"), lax.axis_index("expert")
        self.chips = n_dp // 2
        self.chip, self.core = self.me // 2, self.me % 2
        self.twin = self.me + 1 - 2 * self.core

    def peers(self):
        ring = [lax.rem(self.chip + k, self.chips) for k in range(1, self.chips)]
        return [(self.twin, self.expert)] + [(2 * other + self.core, self.expert) for other in ring]

    def copy(self, ref, send_sem, recv_sem, index):
        return pltpu.make_async_remote_copy(
            src_ref=ref,
            dst_ref=ref,
            send_sem=send_sem,
            recv_sem=recv_sem,
            device_id=(index, self.expert),
            device_id_type=MESH,
        )

    def before(self, later, other):
        return other > self.chip if later else other < self.chip


class Spread:
    def __init__(self, links, at, parts, later, far_sems, near_sems, recv_sems):
        self.links, self.at, self.later = links, at, later
        self.far_sems, self.near_sems, self.recv_sems = far_sems, near_sems, recv_sems

    def _far(self, other, p):
        k = self.links
        return k.copy(self.at(k.me, p), self.far_sems.at[other, p], self.recv_sems.at[k.me, p], 2 * other + k.core)

    def _near(self, block, p):
        k = self.links
        return k.copy(self.at(block, p), self.near_sems.at[block, p], self.recv_sems.at[block, p], k.twin)

    def _twin_needs(self):
        return self.links.core == (0 if self.later else 1)

    def send(self, p):
        k = self.links
        for other in range(k.chips):

            @pl.when(k.before(self.later, other))
            def _():
                self._far(other, p).start()

        @pl.when(self._twin_needs())
        def _():
            self._near(k.me, p).start()

    def sent(self, p):
        k = self.links
        for other in range(k.chips):

            @pl.when(k.before(self.later, other))
            def _():
                self._far(other, p).wait_send()

            @pl.when(k.before(not self.later, other))
            def _():
                self._near(2 * other + k.core, p).wait_send()

        @pl.when(self._twin_needs())
        def _():
            self._near(k.me, p).wait_send()

    def relay(self, p):
        k = self.links
        for other in range(k.chips):

            @pl.when(k.before(not self.later, other))
            def _():
                block = 2 * other + k.core
                copy = self._near(block, p)
                copy.wait_recv()
                copy.start()

    def each(self, p, use):
        k = self.links

        @pl.when(k.core == (1 if self.later else 0))
        def _():
            self._near(k.twin, p).wait_recv()
            use(k.twin)

        for other in range(k.chips):

            @pl.when(k.before(not self.later, other))
            def _():
                use(2 * other + k.core)
                block = 2 * other + 1 - k.core
                self._near(block, p).wait_recv()
                use(block)


def spread_sems(n_dp, parts):
    return [
        pltpu.SemaphoreType.DMA((n_dp // 2, parts)),
        pltpu.SemaphoreType.DMA((n_dp, parts)),
        pltpu.SemaphoreType.DMA((n_dp, parts)),
    ]


def queries_of(rows, w_q):
    return (dot(rows, w_q).astype(jnp.bfloat16) * HEAD_DIM ** (-0.5)).astype(jnp.bfloat16)


def attend(n_dp, links, s, x, gain, shift, w_in, w_out, doc_row, ready, between):
    me = links.me
    pairs, long, width = s.kv.shape[1], s.kv.shape[3], x.shape[1]
    unit, _ = norm_parts(x)
    normed = (unit * gain + shift).astype(jnp.bfloat16)
    s.rows[me] = normed[:long]
    later = Spread(links, lambda b, p: s.rows.at[b], 1, True, *s.kv_sems)
    earlier = Spread(links, lambda b, p: s.rows.at[b], 1, False, *s.q_sems)
    later.send(0)
    earlier.send(0)
    ready(0)
    kv = dot(normed, w_in[:, width:]).astype(jnp.bfloat16)
    ready(1)
    q = queries_of(normed, w_in[:, :width])
    for h in range(pairs):
        at = slice(128 * h, 128 * h + 128)
        for part in range(2):
            piece = kv[:, part * width + 128 * h : part * width + 128 * h + 128]
            s.kv[me, h, part] = piece[:long]
            s.short_kv[h, part] = piece[long:]
        s.q[me, h] = q[:long, at]
        s.short_q[h] = q[long:, at]
    between()
    s.normed_t[...] = normed.T

    def put_context(h, rows_t, first, count):
        at = pl.ds(pl.multiple_of(128 * h, 128), 128)
        s.context_t[at, first : first + count] = rows_t.astype(jnp.bfloat16)
        s.context[first : first + count, at] = rows_t.T.astype(jnp.bfloat16)

    low = jnp.bfloat16
    short_mask, long_mask = short_seen(doc_row), causal(long, long)

    def own_part(i, _):
        hs = [2 * i, 2 * i + 1]
        scores = [dot_rows(s.short_kv[h, 0], head_pair(s.short_q[h])) for h in hs]
        scores = [jnp.where(short_mask, v, masked_score) for v in scores]
        long_scores = [dot_rows(s.kv[me, h, 0], head_pair(s.q[me, h])) for h in hs]
        tops = [jnp.max(v, axis=0, keepdims=True) for v in scores]
        weights = [jnp.exp(v - top) for v, top in zip(scores, tops)]
        totals = [jnp.sum(v, axis=0, keepdims=True) for v in weights]
        sums = [dot_columns(s.short_kv[h, 1], v.astype(low)) for h, v in zip(hs, weights)]
        long_scores = [jnp.where(long_mask, v, masked_score) for v in long_scores]
        long_tops = [jnp.max(v, axis=0, keepdims=True) for v in long_scores]
        long_weights = [jnp.exp(v - top) for v, top in zip(long_scores, long_tops)]
        long_sums = [dot_columns(s.kv[me, h, 1], v.astype(low)) for h, v in zip(hs, long_weights)]
        for n, h in enumerate(hs):
            rows_t = pair_rows(sums[n] / totals[n])
            short = rows_t.shape[1]
            put_context(h, rows_t, long, short)
            lse = tops[n] + jnp.log(totals[n])
            s.lse[h, 0:1, long:] = lse[:, :short]
            s.lse[h, 1:2, long:] = lse[:, short:]
            s.top[h] = long_tops[n]
            s.total[h] = jnp.sum(long_weights[n], axis=0, keepdims=True)
            s.acc[h] = long_sums[n]
        return 0

    lax.fori_loop(0, pairs // 2, own_part, 0)

    def keys_of(block):
        kv = dot(s.rows[block], w_in[:, width:]).astype(jnp.bfloat16)
        for h in range(pairs):
            for part in range(2):
                s.kv[block, h, part] = kv[:, part * width + 128 * h : part * width + 128 * h + 128]

    later.relay(0)
    later.each(0, keys_of)

    def other_part(i, _):
        hs = [2 * i, 2 * i + 1]

        def use(first, size):
            at = pl.ds(first, size)
            keys = [s.kv[at, h, 0].reshape(size * long, 128) for h in hs]
            values = [s.kv[at, h, 1].reshape(size * long, 128) for h in hs]
            scores = [dot_rows(v, head_pair(s.q[me, h])) for h, v in zip(hs, keys)]
            olds = [s.top[h] for h in hs]
            tops = [jnp.maximum(old, jnp.max(v, axis=0, keepdims=True)) for old, v in zip(olds, scores)]
            factors = [jnp.exp(old - top) for old, top in zip(olds, tops)]
            weights = [jnp.exp(v - top) for v, top in zip(scores, tops)]
            totals = [s.total[h] * f + jnp.sum(v, axis=0, keepdims=True) for h, f, v in zip(hs, factors, weights)]
            sums = [s.acc[h] * f + dot_columns(u, v.astype(low)) for h, f, u, v in zip(hs, factors, values, weights)]
            for n, h in enumerate(hs):
                s.top[h] = tops[n]
                s.total[h] = totals[n]
                s.acc[h] = sums[n]

        runs(n_dp - 1, me, use)
        for h in hs:
            total = s.total[h]
            put_context(h, pair_rows(s.acc[h] / total), 0, long)
            lse = s.top[h] + jnp.log(total)
            s.lse[h, 0:1, :long] = lse[:, :long]
            s.lse[h, 1:2, :long] = lse[:, long:]
        return 0

    lax.fori_loop(0, pairs // 2, other_part, 0)
    ready(2)
    following = x + dot(s.context[...], w_out[...])

    def settle():
        def ask(block):
            q = queries_of(s.rows[block], w_in[:, :width])
            for h in range(pairs):
                s.q[block, h] = q[:, 128 * h : 128 * h + 128]

        earlier.relay(0)
        earlier.each(0, ask)
        earlier.sent(0)
        later.sent(0)

    return following, settle


def front_kernel(n_dp, n_ex, names, saved, *refs):
    r = types.SimpleNamespace(**dict(zip(names, refs)))
    extra = iter(refs[len(names) :])
    buffers = []
    for layer in range(2):
        s = types.SimpleNamespace()
        for name in saved:
            setattr(s, name, next(extra))
        s.rows = next(extra)
        s.kv_sems = [next(extra) for _ in range(3)]
        s.q_sems = [next(extra) for _ in range(3)]
        s.stored = next(extra)
        buffers.append(s)
    sums = [next(extra) for _ in range(3)]
    for s in buffers:
        s.acc, s.top, s.total = sums
    w_in, w_out, w_sem, dense_in, dense_out, dense_sem = (next(extra) for _ in range(6))
    stream_ref, dense_normed, active_ref, slope_ref, dense_normed_t, far_cot = (next(extra) for _ in range(6))
    stored, cot_send, cot_send_sem, cot_recv_sem = (next(extra) for _ in range(4))
    links = Links(n_dp)
    tokens, width = r.tokens.shape
    blocks = r.dense_in.shape[1] // width
    low = jnp.bfloat16

    def block_loads(i):
        slot = lax.rem(i, 2)
        at = pl.ds(pl.multiple_of(i * width, width), width)
        return [
            pltpu.make_async_copy(r.dense_in.at[:, at], dense_in.at[slot], dense_sem.at[slot, 0]),
            pltpu.make_async_copy(r.dense_out.at[at, :], dense_out.at[slot], dense_sem.at[slot, 1]),
        ]

    def weight_loads(layer):
        return [
            pltpu.make_async_copy(
                r.attn_in.at[layer, :, pl.ds(width, 2 * width)], w_in.at[layer, :, pl.ds(width, 2 * width)], w_sem.at[layer, 0]
            ),
            pltpu.make_async_copy(
                r.attn_in.at[layer, :, pl.ds(0, width)], w_in.at[layer, :, pl.ds(0, width)], w_sem.at[layer, 1]
            ),
            pltpu.make_async_copy(r.attn_out.at[layer], w_out.at[layer], w_sem.at[layer, 2]),
        ]

    loads = [weight_loads(0), weight_loads(1)]
    for load in loads[0]:
        load.start()
    for i in range(min(2, blocks)):
        for load in block_loads(i):
            load.start()
    for load in loads[1]:
        load.start()
    greet(links.peers() + across_peers(n_ex))
    writes = []

    def write(source, target, sem):
        copy = pltpu.make_async_copy(source, target, sem)
        copy.start()
        writes.append(copy)

    def layer(number, x, between):
        s = buffers[number]
        column = 2 * number
        following, settle = attend(
            n_dp, links, s, x, r.gains[column : column + 1], r.shifts[column : column + 1], w_in.at[number], w_out.at[number],
            r.doc_row[...], lambda i: loads[number][i].wait(), between,
        )
        return following, settle

    def save(number, settle):
        s = buffers[number]
        settle()
        for i, name in enumerate(saved):
            write(getattr(s, name), getattr(r, name + str(number)), s.stored.at[i])

    x, settle = layer(0, r.tokens[...].astype(jnp.float32), lambda: None)
    r.stream0[...] = x
    stream_ref[...] = x
    unit, _ = norm_parts(x)
    normed = (unit * r.gains[1:2] + r.shifts[1:2]).astype(low)
    dense_normed[...] = normed
    save(0, settle)
    dense_normed_t[...] = normed.T

    def dense(i, _):
        slot = lax.rem(i, 2)
        for load in block_loads(i):
            load.wait()
        active, slope = gelu_parts(dot(dense_normed[...], dense_in[slot]))
        active = active.astype(low)
        at = pl.ds(pl.multiple_of(i * width, width), width)
        slope_ref[:, at] = slope.astype(low)
        active_ref[at, :] = active.T
        stream_ref[...] += dot(active, dense_out[slot])

        @pl.when(i + 2 < blocks)
        def _():
            for load in block_loads(i + 2):
                load.start()

        return 0

    lax.fori_loop(0, blocks, dense, 0)
    write(dense_normed_t, r.dense_normed_t, stored.at[0])
    write(active_ref, r.active_t, stored.at[1])
    write(slope_ref, r.slope, stored.at[2])
    x = stream_ref[...]
    r.stream1[...] = x

    cot_across = Across(n_ex, cot_send, far_cot, cot_send_sem, cot_recv_sem)

    def send_cotangent():
        cot_send[...] = dot(dispatch_of(r.assign[...], n_ex), r.cot[...]).astype(low).reshape(cot_send.shape)
        cot_across.start_all()
        far_cot[links.expert] = cot_send[links.expert]

    x, settle = layer(1, x, send_cotangent)
    r.stream2[...] = x
    save(1, settle)
    cot_across.wait_all()
    write(far_cot, r.far_cot, stored.at[3])
    for copy in writes:
        copy.wait()


def front(n_dp, n_ex, collective_id, near, far):
    arrays = {**near, **far}
    a = types.SimpleNamespace(**arrays)
    low, wide = jnp.bfloat16, jnp.float32
    tokens, width = a.tokens.shape
    hidden, mixed = a.dense_in.shape[1], a.attn_in.shape[2]
    long, short, pairs = LONG_DEV, tokens - LONG_DEV, width // 128
    slab = (n_ex, capacity_of(tokens, n_ex)[1], width)
    saved = dict(
        normed_t=jax.ShapeDtypeStruct((width, tokens), low),
        context=jax.ShapeDtypeStruct((tokens, width), low),
        context_t=jax.ShapeDtypeStruct((width, tokens), low),
        kv=jax.ShapeDtypeStruct((n_dp, pairs, 2, long, 128), low),
        q=jax.ShapeDtypeStruct((n_dp, pairs, long, 128), low),
        short_kv=jax.ShapeDtypeStruct((pairs, 2, short, 128), low),
        short_q=jax.ShapeDtypeStruct((pairs, short, 128), low),
        lse=jax.ShapeDtypeStruct((pairs, 2, tokens), wide),
    )
    stream = jax.ShapeDtypeStruct((tokens, width), wide)
    outs = dict(stream0=stream, stream1=stream, stream2=stream)
    direct = len(outs)
    for layer in range(2):
        for name, shape in saved.items():
            outs[name + str(layer)] = shape
    outs.update(
        dense_normed_t=jax.ShapeDtypeStruct((width, tokens), low),
        active_t=jax.ShapeDtypeStruct((hidden, tokens), low),
        slope=jax.ShapeDtypeStruct((tokens, hidden), low),
        far_cot=jax.ShapeDtypeStruct(slab, low),
    )
    scratch = []
    for layer in range(2):
        scratch += [pltpu.VMEM(shape.shape, shape.dtype) for shape in saved.values()]
        scratch += [pltpu.VMEM((n_dp, long, width), low)]
        scratch += spread_sems(n_dp, 1) + spread_sems(n_dp, 1)
        scratch += [pltpu.SemaphoreType.DMA((len(saved),))]
    scratch += [pltpu.VMEM((pairs, 128, 2 * long), wide)] + [pltpu.VMEM((pairs, 1, 2 * long), wide)] * 2
    scratch += [pltpu.VMEM((2, width, mixed), low), pltpu.VMEM((2, width, width), low), pltpu.SemaphoreType.DMA((2, 3))]
    scratch += [pltpu.VMEM((2, width, width), low)] * 2 + [pltpu.SemaphoreType.DMA((2, 2))]
    scratch += [
        pltpu.VMEM((tokens, width), wide),
        pltpu.VMEM((tokens, width), low),
        pltpu.VMEM((hidden, tokens), low),
        pltpu.VMEM((tokens, hidden), low),
        pltpu.VMEM((width, tokens), low),
        pltpu.VMEM(slab, low),
        pltpu.SemaphoreType.DMA((4,)),
        pltpu.VMEM(slab, low),
        pltpu.SemaphoreType.DMA((n_ex,)),
        pltpu.SemaphoreType.DMA((n_ex,)),
    ]
    vmem, anywhere = pl.BlockSpec(memory_space=pltpu.VMEM), pl.BlockSpec(memory_space=pl.ANY)
    names = tuple(arrays) + tuple(outs)
    values = pl.pallas_call(
        functools.partial(front_kernel, n_dp, n_ex, names, tuple(saved)),
        out_shape=list(outs.values()),
        in_specs=[vmem] * len(near) + [anywhere] * len(far),
        out_specs=[vmem] * direct + [anywhere] * (len(outs) - direct),
        scratch_shapes=scratch,
        compiler_params=pltpu.CompilerParams(
            collective_id=collective_id, has_side_effects=True, vmem_limit_bytes=63 * 1024 * 1024
        ),
        name="front",
    )(*arrays.values())
    return types.SimpleNamespace(**dict(zip(outs, values)))


def runs(most, count, use):
    for first in range(0, most, 3):
        for size in range(1, min(3, most - first) + 1):
            exactly = count - first == size if size < 3 else count - first >= size

            @pl.when(exactly)
            def _():
                use(first, size)


def put_context_grads(grad_context, do_ref, short_do_ref, me, long):
    for h in range(do_ref.shape[1]):
        piece = grad_context[:, 128 * h : 128 * h + 128]
        do_ref[me, h] = piece[:long]
        short_do_ref[h] = piece[long:]


def put_row_terms(context, lse, grad_context, aux_ref, short_aux_ref, me, long):
    width = grad_context.shape[1]
    rows = (width // HEAD_DIM + 15) // 16 * 16
    lane = lax.broadcasted_iota(jnp.int32, (rows, width), 1)
    head = lax.broadcasted_iota(jnp.int32, (rows, width), 0) * HEAD_DIM
    picks = jnp.where((lane >= head) & (lane < head + HEAD_DIM), 1.0, 0.0).astype(jnp.bfloat16)
    both = grad_context.astype(jnp.float32) * context[...].astype(jnp.float32)
    high = both.astype(jnp.bfloat16)
    delta = dot_rows(picks, high) + dot_rows(picks, (both - high.astype(jnp.float32)).astype(jnp.bfloat16))
    for h in range(aux_ref.shape[1]):
        aux_ref[me, h, 0:2] = lse[h, :, :long]
        aux_ref[me, h, 2:4] = delta[2 * h : 2 * h + 2, :long]
        short_aux_ref[h, 0:2] = lse[h, :, long:]
        short_aux_ref[h, 2:4] = delta[2 * h : 2 * h + 2, long:]


def attend_back_pairs(n_dp, me, width, r, do_spread, aux_spread, hs):
    scale = HEAD_DIM ** (-0.5)
    mixed_ref, low = r.mixed, jnp.bfloat16
    long = r.kv.shape[3]
    each = range(len(hs))

    def row_of(aux):
        return [jnp.concatenate([aux[i : i + 1], aux[i + 1 : i + 2]], axis=1) for i in (0, 2)]

    def score_grads(keys, values, queries, grads, rows, seen):
        each = range(len(keys))
        scores = [dot_rows(keys[n], queries[n]) for n in each]
        grad_probs = [dot_rows(values[n], grads[n]) for n in each]
        probs = [jnp.exp(scores[n] - rows[n][0]) for n in each]
        if seen is not None:
            probs = [jnp.where(seen, v, 0.0) for v in probs]
        grad_scores = [(probs[n] * (grad_probs[n] - rows[n][1])).astype(low) for n in each]
        return [v.astype(low) for v in probs], grad_scores

    def put(h, third, first, value):
        at = pl.ds(pl.multiple_of(third * width + 128 * h, 128), 128)
        mixed_ref[first : first + value.shape[0], at] = value.astype(low)

    seen = short_seen(r.doc_row[...])
    short_queries, short_grads = [head_pair(r.short_q[h]) for h in hs], [head_pair(r.short_do[h]) for h in hs]
    short_keys = [r.short_kv[h, 0] for h in hs]
    short_values = [r.short_kv[h, 1] for h in hs]
    short_rows = [row_of(r.short_aux[h]) for h in hs]
    probs, grad_scores = score_grads(short_keys, short_values, short_queries, short_grads, short_rows, seen)
    short_dq = [(pair_rows(dot_columns(short_keys[n], grad_scores[n])) * scale).T for n in each]
    short_dk = [dot(grad_scores[n], short_queries[n]) for n in each]
    short_dv = [dot(probs[n], short_grads[n]) for n in each]

    queries, grads = [head_pair(r.q[me, h]) for h in hs], [head_pair(r.do[me, h]) for h in hs]
    own_keys, own_values = [r.kv[me, h, 0] for h in hs], [r.kv[me, h, 1] for h in hs]
    own_rows = [row_of(r.aux[me, h]) for h in hs]
    probs, grad_scores = score_grads(own_keys, own_values, queries, grads, own_rows, causal(long, long))
    dq = [dot_columns(own_keys[n], grad_scores[n]) for n in each]
    dk = [dot(grad_scores[n], queries[n]) for n in each]
    dv = [dot(probs[n], grads[n]) for n in each]
    for n, h in enumerate(hs):
        for third, value in enumerate((short_dq[n], short_dk[n], short_dv[n])):
            put(h, third, long, value)
        r.dq[n], r.dk[n], r.dv[n] = dq[n], dk[n], dv[n]

    def earlier(first, size):
        at = pl.ds(first, size)
        for n, h in enumerate(hs):
            keys = r.kv[at, h, 0].reshape(size * long, 128)
            values = r.kv[at, h, 1].reshape(size * long, 128)
            _, (grad_scores,) = score_grads([keys], [values], [queries[n]], [grads[n]], [own_rows[n]], None)
            r.dq[n] += dot_columns(keys, grad_scores)

    runs(n_dp - 1, me, earlier)
    for n, h in enumerate(hs):
        put(h, 0, 0, (pair_rows(r.dq[n]) * scale).T)
    for h in hs:
        do_spread.relay(h)
        aux_spread.relay(h)

    def later(first, size):
        blocks = [me + 1 + first + i for i in range(size)]
        for n, h in enumerate(hs):
            queries = jnp.concatenate([head_pair(r.q[block, h]) for block in blocks], axis=0)
            grads = jnp.concatenate([head_pair(r.do[block, h]) for block in blocks], axis=0)
            parts = [row_of(r.aux[block, h]) for block in blocks]
            rows = [jnp.concatenate([part[i] for part in parts], axis=1) for i in range(2)]
            (probs,), (grad_scores,) = score_grads([own_keys[n]], [own_values[n]], [queries], [grads], [rows], None)
            r.dk[n] += dot(grad_scores, queries)
            r.dv[n] += dot(probs, grads)

    for h in hs:
        aux_spread.each(h, lambda block: None)
        do_spread.each(h, lambda block: None)
    runs(n_dp - 1, n_dp - 1 - me, later)
    for n, h in enumerate(hs):
        put(h, 1, 0, r.dk[n])
        put(h, 2, 0, r.dv[n])


def back_scratch(n_dp, pairs, long, short):
    return (
        [
            pltpu.VMEM((n_dp, pairs, long, 128), jnp.bfloat16),
            pltpu.VMEM((n_dp, pairs, 8, long), jnp.float32),
            pltpu.VMEM((pairs, short, 128), jnp.bfloat16),
            pltpu.VMEM((pairs, 8, short), jnp.float32),
            pltpu.VMEM((2, 128, 2 * long), jnp.float32),
            pltpu.VMEM((2, long, 128), jnp.float32),
            pltpu.VMEM((2, long, 128), jnp.float32),
        ]
        + spread_sems(n_dp, pairs)
        + spread_sems(n_dp, pairs)
    )


def lane_plan(n_dp, n_ex, rows, order):
    dp_levels = [("dp", b) for b in range(n_dp.bit_length() - 1)]
    ex_levels = n_ex.bit_length() - 1
    halved, piece = [], rows
    for level in ((0, 1), (1, 0))[order]:
        if level < ex_levels and piece % 32 == 0:
            halved.append(level)
            piece //= 2
    halves = [("half", b) for b in halved]
    if order:
        kinds = dp_levels[:1] + halves[:1] + dp_levels[1:] + halves[1:]
    else:
        kinds = dp_levels + halves
    kinds += [("both", b) for b in range(ex_levels) if b not in halved]
    kinds += [("back", b) for b in reversed(halved)]
    return kinds, halved


class Lane:
    def __init__(self, n_dp, n_ex, rows, columns, order, refs):
        self.rows, self.columns = rows, columns
        self.kinds, self.halved = lane_plan(n_dp, n_ex, rows, order)
        self.count = len(self.kinds)
        moving = [k[0] != "back" for k in self.kinds]
        self.send = [next(refs) if m else None for m in moving]
        self.recv = [next(refs) if m else None for m in moving]
        self.keep = [next(refs) if m else None for m in moving]
        self.fin = next(refs)
        self.send_sems = [next(refs) for _ in moving]
        self.recv_sems = [next(refs) for _ in moving]
        self.d, self.e = lax.axis_index("dp"), lax.axis_index("expert")

    @staticmethod
    def scratch(n_dp, n_ex, rows, columns, order):
        kinds, halved = lane_plan(n_dp, n_ex, rows, order)
        width, pieces, height, shapes = columns[1] - columns[0], n_dp, rows, []
        for kind, _ in kinds:
            if kind == "dp":
                pieces //= 2
            elif kind == "half":
                height //= 2
            if kind != "back":
                shapes.append((pieces, height, width))
        scratch = [pltpu.VMEM((2,) + s, jnp.bfloat16) for s in shapes]
        scratch += [pltpu.VMEM((4,) + s, jnp.bfloat16) for s in shapes]
        scratch += [pltpu.VMEM((2,) + s, jnp.float32) for s in shapes]
        scratch += [pltpu.VMEM((len(halved) + 3, rows, width) if halved else (1, 16, 128), jnp.bfloat16)]
        return scratch + [pltpu.SemaphoreType.DMA((4,)) for _ in kinds] * 2

    def peer(self, kind, level):
        return (flip(self.d, level), self.e) if kind == "dp" else (self.d, flip(self.e, level))

    def kept_rows(self, depth):
        start = 0
        for i, level in enumerate(self.halved[:depth]):
            start = start + bit_of(self.e, level) * (self.rows >> (i + 1))
        return start

    def copy_of(self, s, c):
        kind, level = self.kinds[s]
        slot, place = lax.rem(c, 2), lax.rem(c, 4)
        if kind == "back":
            depth = self.halved.index(level) + 1
            span = self.rows >> depth
            at = pl.ds(pl.multiple_of(self.kept_rows(depth), span), span)
            src = self.fin.at[lax.rem(c, len(self.halved) + 3), at]
            dst = src
        else:
            src, dst = self.send[s].at[slot], self.recv[s].at[place]
        return pltpu.make_async_remote_copy(
            src_ref=src,
            dst_ref=dst,
            send_sem=self.send_sems[s].at[place],
            recv_sem=self.recv_sems[s].at[place],
            device_id=self.peer(kind, level),
            device_id_type=MESH,
        )

    def arrive(self, s, c):
        self.copy_of(s, c).wait()
        slot, place = lax.rem(c, 2), lax.rem(c, 4)
        if self.kinds[s][0] == "back":
            return None
        return [
            self.keep[s][slot, i] + self.recv[s][place, i].astype(jnp.float32) for i in range(self.keep[s].shape[1])
        ]

    def leave(self, s, c, values):
        kind, level = self.kinds[s]
        slot = lax.rem(c, 2)
        kept = None
        if kind == "dp":
            sent, kept = values[1::2], values[0::2]
        elif kind == "half":
            half = values[0].shape[0] // 2
            own = bit_of(self.e, level)
            sent = [jnp.where(own == 0, v[half:], v[:half]) for v in values]
            kept = [jnp.where(own == 0, v[:half], v[half:]) for v in values]
        elif kind == "both":
            sent = values
            kept = [v.astype(jnp.bfloat16).astype(jnp.float32) for v in values]
        elif values is not None:
            span = values[0].shape[0]
            at = pl.ds(pl.multiple_of(self.kept_rows(len(self.halved)), span), span)
            self.fin[lax.rem(c, len(self.halved) + 3), at] = values[0].astype(jnp.bfloat16)
        if kept is not None:
            for i, v in enumerate(sent):
                self.send[s][slot, i] = v.astype(jnp.bfloat16)
        self.copy_of(s, c).start()
        if kept is not None:
            for i, v in enumerate(kept):
                self.keep[s][slot, i] = v

    def final(self, c):
        values = self.arrive(self.count - 1, c)
        if values is None:
            return self.fin[lax.rem(c, len(self.halved) + 3)]
        return values[0].astype(jnp.bfloat16)


class Reduction:
    def __init__(self, n_dp, n_ex, rows, groups, lanes, refs, out):
        self.n_dp, self.rows, self.groups = n_dp, rows, groups
        self.lanes = [Lane(n_dp, n_ex, rows, columns, order, refs) for columns, order in lanes]
        self.stage_ref, self.stage_sem, self.out = next(refs), next(refs), out
        self.count = self.lanes[0].count
        self.chunks = sum(g[0] for g in groups)
        self.firsts = [sum(g[0] for g in groups[:i]) for i in range(len(groups))]
        self.ticks = self.chunks + self.count
        self.d = lax.axis_index("dp")
        self.peer = self.lanes[0].peer

    @staticmethod
    def scratch(n_dp, n_ex, rows, width, lanes):
        scratch = []
        for columns, order in lanes:
            scratch += Lane.scratch(n_dp, n_ex, rows, columns, order)
        return scratch + [pltpu.VMEM((2, rows, width), jnp.bfloat16), pltpu.SemaphoreType.DMA((2,))]

    def out_copy(self, c):
        slot = lax.rem(c, 2)
        return pltpu.make_async_copy(self.stage_ref.at[slot], self.out.at[c], self.stage_sem.at[slot])

    def first(self, g, c):
        _, piece, factor = self.groups[g]
        j = c - self.firsts[g]
        dy = factor(j)
        slot = lax.rem(c, 2)
        levels = self.n_dp.bit_length() - 1
        half = self.n_dp // 2

        def products(odd):
            parts = [piece(j, partner_index(self.d, 2 * i + odd, levels)) for i in range(half)]
            return dot(jnp.concatenate(parts, axis=0), dy)

        value = products(1)
        for lane in self.lanes:
            for i in range(half):
                part = value[i * self.rows : (i + 1) * self.rows, slice(*lane.columns)]
                lane.send[0][slot, i] = part.astype(jnp.bfloat16)
            lane.copy_of(0, c).start()
        value = products(0)
        for lane in self.lanes:
            for i in range(half):
                lane.keep[0][slot, i] = value[i * self.rows : (i + 1) * self.rows, slice(*lane.columns)]

    def last(self, c):
        slot = lax.rem(c, 2)

        @pl.when(c >= 2)
        def _():
            self.out_copy(c - 2).wait()

        for lane in self.lanes:
            self.stage_ref[slot, :, slice(*lane.columns)] = lane.final(c)
        self.out_copy(c).start()

    def tick(self, t, low, high):
        for s in range(self.count + 1):
            if high - s <= 0 or low - s >= self.chunks:
                continue
            c = t - s
            if s > 0:

                @pl.when((c >= 0) & (c < self.chunks))
                def _(s=s, c=c):
                    if s < self.count:
                        for lane in self.lanes:
                            lane.leave(s, c, lane.arrive(s - 1, c))
                    else:
                        self.last(c)

                continue
            for g, (size, _, _) in enumerate(self.groups):
                begin, end = self.firsts[g], self.firsts[g] + size
                if high <= begin or low >= end:
                    continue

                @pl.when((c >= begin) & (c < end))
                def _(g=g):
                    self.first(g, c)

    def finish(self):
        for c in range(max(0, self.chunks - 2), self.chunks):
            self.out_copy(c).wait()


def dense_lanes(width):
    cut = width // 768 * 640
    return [((0, cut), 0), ((cut, width), 1)]


def middle_kernel(n_dp, n_ex, names, staged, *refs):
    r = types.SimpleNamespace(**dict(zip(names, refs)))
    extra = iter(refs[len(names) :])
    loads = types.SimpleNamespace()
    for name in staged:
        buffer, sem = next(extra), next(extra)
        setattr(loads, name, pltpu.make_async_copy(getattr(r, name), buffer, sem))
        setattr(r, name, buffer)
    w_in_ref, w_out_ref, weight_sem, factor_sem = (next(extra) for _ in range(4))
    rows_ref, send_ref, grad_ref, home_ref, result_ref = (next(extra) for _ in range(5))
    rows_t_ref, back_ref, active_t_ref, hidden_ref = (next(extra) for _ in range(4))
    dgate_ref, home_dgate_ref, stat_send, stat_recv, result_acc, grad_acc = (next(extra) for _ in range(6))
    (
        x_send_sem, x_recv_sem, grad_send_sem, grad_recv_sem, dgate_send_sem, dgate_recv_sem,
        result_send_sem, result_recv_sem, stat_send_sem, stat_recv_sem,
    ) = (next(extra) for _ in range(10))
    do_ref, aux_ref, short_do_ref, short_aux_ref, dq_ref, dk_ref, dv_ref = (next(extra) for _ in range(7))
    do_far, do_near, do_recv, aux_far, aux_near, aux_recv = (next(extra) for _ in range(6))
    links = Links(n_dp)
    d, e, me = links.me, links.expert, links.me
    shared = links.chips == 2
    if shared:
        peer_rows_ref, peer_cot_ref, peer_row_sems, peer_cot_sems = (next(extra) for _ in range(4))
    dp_levels, ex_levels = n_dp.bit_length() - 1, n_ex.bit_length() - 1
    tokens, width = r.stream.shape
    padded = send_ref.shape[1]
    blocks = r.expert_in.shape[1] // width
    pairs, long = r.kv.shape[1], r.kv.shape[3]
    group = min(max(4, 128 // padded), n_ex)
    groups = n_ex // group
    hops = [(flip(d, b), e) for b in range(dp_levels)] + [(d, flip(e, b)) for b in range(ex_levels)]

    def column(i):
        return pl.ds(i * width, width)

    expert_loads = [
        (
            pltpu.make_async_copy(r.expert_in.at[:, column(i)], w_in_ref.at[i], weight_sem.at[0, i]),
            pltpu.make_async_copy(r.expert_out.at[column(i), :], w_out_ref.at[i], weight_sem.at[1, i]),
        )
        for i in range(blocks)
    ]
    for both in expert_loads:
        for load in both:
            load.start()
    for name in staged:
        getattr(loads, name).start()
    greet(links.peers() + across_peers(n_ex))

    def peer_copy(source, target, sems):
        return pltpu.make_async_remote_copy(
            src_ref=source,
            dst_ref=target,
            send_sem=sems.at[0],
            recv_sem=sems.at[1],
            device_id=(flip(d, 1), e),
            device_id_type=MESH,
        )

    def row_copy(j):
        return peer_copy(rows_ref.at[j], peer_rows_ref.at[j], peer_row_sems.at[j])

    if shared:
        cot_copy = peer_copy(r.far_cot, peer_cot_ref, peer_cot_sems)
        cot_copy.start()

    unit, inverse = norm_parts(r.stream[...])
    routed = (unit * r.gains[3:4] + r.shifts[3:4]).astype(jnp.bfloat16)
    assign = r.assign[...]
    dispatch = dispatch_of(assign, n_ex)
    r.dispatch[...] = dispatch
    send_ref[...] = dot(dispatch, routed).astype(jnp.bfloat16).reshape(send_ref.shape)
    x_across = Across(n_ex, send_ref, rows_ref, x_send_sem, x_recv_sem)

    def place(k, i):
        return lax.rem(e // group + k, groups) * group + lax.rem(e + i, group)

    def source(k, i):
        return lax.rem(e // group + k, groups) * group + lax.rem(e + group - i, group)

    for i in range(group):
        if i:
            x_across.start(place(0, i))
        for k in range(1, groups):
            x_across.start(place(k, i))
    rows_ref[e] = send_ref[e]
    router = r.router[...]
    hot = chosen_rows(assign, n_ex)
    gate = jax.nn.sigmoid(jnp.sum(hot * dot_rows(router, routed), axis=0, keepdims=True))
    r.gate[...] = gate

    def stat_copy(i):
        return pltpu.make_async_remote_copy(
            src_ref=stat_send.at[i],
            dst_ref=stat_recv.at[i],
            send_sem=stat_send_sem.at[i],
            recv_sem=stat_recv_sem.at[i],
            device_id=hops[i],
            device_id_type=MESH,
        )

    lane = lax.broadcasted_iota(jnp.int32, r.stats.shape, 1)
    stat_send[0] = jnp.where(
        lane == 0, jnp.sum(hot, axis=1, keepdims=True), jnp.sum(hot * gate, axis=1, keepdims=True)
    )
    stat_copy(0).start()

    def stat_step(i):
        stat_copy(i).wait()
        value = stat_send[i] + stat_recv[i]
        if i + 1 < len(hops):
            stat_send[i + 1] = value
            stat_copy(i + 1).start()
        else:
            r.stats[...] = value

    grad_across = Across(n_ex, grad_ref, home_ref, grad_send_sem, grad_recv_sem)
    dgate_across = Across(n_ex, dgate_ref, home_dgate_ref, dgate_send_sem, dgate_recv_sem)
    steps = [[(k, i) for i in range(group)] for k in range(groups)]

    def expert_rows(rows, cot, at, whole):
        count = rows.shape[0]
        logits = dot_rows(rows, router)
        own = lax.broadcasted_iota(jnp.int32, logits.shape, 1) == e
        slot_gate = jax.nn.sigmoid(jnp.sum(jnp.where(own, logits, 0.0), axis=1, keepdims=True))
        back = (slot_gate * cot).astype(jnp.bfloat16)
        span = slice(at, at + count)
        back_ref[span] = back
        rows_t_ref[:, span] = rows.T
        if whole:
            result_acc[:count] = jnp.zeros((count, width), jnp.float32)
            grad_acc[:count] = jnp.zeros((count, width), jnp.float32)

        def block(i, _):
            cols = pl.ds(pl.multiple_of(i * width, width), width)
            active, slope = gelu_parts(dot(rows, w_in_ref[i]))
            active = active.astype(jnp.bfloat16)
            hidden = (slope * dot_rows(back, w_out_ref[i])).astype(jnp.bfloat16)
            active_t_ref[cols, span] = active.T
            hidden_ref[span, cols] = hidden
            if whole:
                result_acc[:count] += dot(active, w_out_ref[i])
                grad_acc[:count] += dot_rows(hidden, w_in_ref[i])
            return 0

        lax.fori_loop(0, blocks, block, 0)

    done, at = 0, 0
    for number, members in enumerate(steps):
        count = len(members) * padded
        sources = [source(k, i) for k, i in members]
        for (k, i), j in zip(members, sources):
            if (k, i) != (0, 0):
                x_across.wait_from(j)
            if shared:
                row_copy(j).start()
        rows = jnp.concatenate([rows_ref[j] for j in sources], axis=0)
        cot = jnp.concatenate([r.far_cot[j] for j in sources], axis=0).astype(jnp.float32)
        if number == 0:
            for both in expert_loads:
                for load in both:
                    load.wait()
        expert_rows(rows, cot, at, True)
        grad = grad_acc[:count].astype(jnp.bfloat16)
        result = result_acc[:count].astype(jnp.bfloat16)
        both = cot * result.astype(jnp.float32)
        high = both.astype(jnp.bfloat16)
        rest = both - high.astype(jnp.float32)
        ones = jnp.ones((16, width), jnp.bfloat16)
        dgate = dot_rows(ones, high) + dot_rows(ones, rest.astype(jnp.bfloat16))
        for m, (k, i) in enumerate(members):
            j, part = sources[m], slice(m * padded, (m + 1) * padded)
            grad_ref[j] = grad[part]
            result_ref[j] = result[part]
            dgate_ref[j, :, :padded] = dgate[:8, part]
            if (k, i) == (0, 0):
                home_ref[e] = grad_ref[e]
                home_dgate_ref[e] = dgate_ref[e]
            else:
                grad_across.start(j)
                dgate_across.start(j)
        at += count
        if done < len(hops):
            stat_step(done)
            done += 1

    if shared:
        cot_copy.wait()
        for k in range(groups):
            sources = [source(k, i) for i in range(group)]
            for j in sources:
                row_copy(j).wait()
            rows = jnp.concatenate([peer_rows_ref[j] for j in sources], axis=0)
            cot = jnp.concatenate([peer_cot_ref[j] for j in sources], axis=0).astype(jnp.float32)
            expert_rows(rows, cot, at, False)
            at += group * padded
            if done < len(hops):
                stat_step(done)
                done += 1

    thirds = [w_in_ref.at[i] for i in range(3)]
    in_loads = [
        pltpu.make_async_copy(r.attn_in.at[1, :, column(i)], third, weight_sem.at[0, i])
        for i, third in enumerate(thirds)
    ]
    out_load = pltpu.make_async_copy(r.attn_out.at[1], w_out_ref.at[0], weight_sem.at[1, 0])
    for load in in_loads + [out_load]:
        load.start()
    rows = width // n_dp

    def rows_of(ref, j, q):
        return ref[pl.ds(pl.multiple_of((q * (ref.shape[0] // width) + j) * rows, rows), rows), :]

    red, writes = None, []
    if shared:
        factors = ((rows_t_ref, r.rows_t), (back_ref, r.back), (active_t_ref, r.expert_active_t), (hidden_ref, r.expert_hidden))
        writes = [pltpu.make_async_copy(here, there, factor_sem.at[i]) for i, (here, there) in enumerate(factors)]
        for write in writes:
            write.start()
    else:
        factors = [
            (blocks, lambda j, q: rows_of(rows_t_ref, 0, q), lambda j: hidden_ref[:, pl.ds(pl.multiple_of(j * width, width), width)]),
            (blocks, lambda j, q: rows_of(active_t_ref, j, q), lambda j: back_ref[...]),
        ]
        red = Reduction(n_dp, 1, rows, factors, [((0, width), 0)], extra, r.chunks)
    early = 0
    if red:
        red.tick(0, 0, 1)
        early = 1
    while done < len(hops):
        stat_step(done)
        done += 1
    x_across.others(x_across.wait_to)
    if red:
        red.tick(1, 1, 2)
        early = 2
    dgate_across.wait_all()
    slot_grads = jnp.concatenate([home_dgate_ref[j, :, :padded] for j in range(n_ex)], axis=1)
    dgate = dot(split(slot_grads), r.dispatch[...])
    dgate = dgate[0:8] + dgate[8:16] + dgate[16:24]
    everyone = tokens * n_dp * n_ex
    share = jnp.sum(jnp.where(lane == 0, r.stats[...], 0.0), axis=1, keepdims=True) / everyone
    weight = balance_weight * n_ex * (share - 1.0 / n_ex) / everyone
    mean_gate = jnp.sum(jnp.where(lane == 1, r.stats[...], 0.0), axis=1, keepdims=True) / everyone
    balance = n_ex * jnp.sum((share - 1.0 / n_ex) * mean_gate, axis=0, keepdims=True)
    r.balance[...] = jnp.broadcast_to(balance, r.balance.shape)
    grad_gate = dgate[0:1] + jnp.sum(hot * weight, axis=0, keepdims=True)
    grad_logits = hot * (grad_gate * gate * (1.0 - gate))
    parts = split(grad_logits)
    product = dot(parts, routed)
    r.router_grad[...] = product[:n_ex] + product[n_ex : 2 * n_ex] + product[2 * n_ex :]
    grad_normed = dot_columns(parts, jnp.concatenate([router] * 3, axis=0))
    if red:
        red.tick(2, 2, 3)
        early = 3
    grad_across.wait_all()
    grad_normed = grad_normed + dot_columns(r.dispatch[...], home_ref[...].reshape(n_ex * padded, width))
    unit, inverse = norm_parts(r.stream[...])
    up = r.cot[...].astype(jnp.float32) + norm_back(unit, inverse, r.gains[3:4], grad_normed)
    r.sums[0:1] = jnp.sum(grad_normed * unit, axis=0, keepdims=True)
    r.sums[1:2] = jnp.sum(grad_normed, axis=0, keepdims=True)

    r.up_next[...] = up
    up_low = up.astype(jnp.bfloat16)
    r.up_low[...] = up_low
    out_load.wait()
    for name in staged:
        getattr(loads, name).wait()
    grad_context = dot_rows(up_low, w_out_ref[0]).astype(jnp.bfloat16)
    put_context_grads(grad_context, do_ref, short_do_ref, me, long)
    do_spread = Spread(links, lambda b, p: do_ref.at[b, p], pairs, False, do_far, do_near, do_recv)
    aux_spread = Spread(links, lambda b, p: aux_ref.at[b, p], pairs, False, aux_far, aux_near, aux_recv)
    put_row_terms(r.context, r.lse, grad_context, aux_ref, short_aux_ref, me, long)
    for h in range(pairs):
        do_spread.send(h)
        aux_spread.send(h)
    result_across = Across(n_ex, result_ref, r.result_home, result_send_sem, result_recv_sem)
    result_across.start_all()
    r.result_home[e] = result_ref[e]
    sequence = types.SimpleNamespace(
        doc_row=r.doc_row, kv=r.kv, q=r.q, short_kv=r.short_kv, short_q=r.short_q,
        do=do_ref, aux=aux_ref, short_do=short_do_ref, short_aux=short_aux_ref, dq=dq_ref, dk=dk_ref, dv=dv_ref,
        mixed=r.mixed,
    )

    def pair(i, _):
        attend_back_pairs(n_dp, me, width, sequence, do_spread, aux_spread, [2 * i, 2 * i + 1])
        if red:
            red.tick(early + 2 * i, early, early + pairs)
            red.tick(early + 2 * i + 1, early, early + pairs)
        return 0

    lax.fori_loop(0, pairs // 2, pair, 0)
    grad_normed = jnp.zeros((tokens, width), jnp.float32)
    for i, third in enumerate(thirds):
        in_loads[i].wait()
        grad_normed = grad_normed + dot_rows(r.mixed[:, i * width : (i + 1) * width], third[...])
    unit, inverse = norm_parts(r.attn_x[...])
    r.up_next[...] += norm_back(unit, inverse, r.gains[2:3], grad_normed)
    r.attn_sums[0:1] = jnp.sum(grad_normed * unit, axis=0, keepdims=True)
    r.attn_sums[1:2] = jnp.sum(grad_normed, axis=0, keepdims=True)

    if red:

        def rest(t, _):
            red.tick(t, early + pairs, red.ticks)
            return 0

        lax.fori_loop(early + pairs, red.ticks, rest, 0)
        red.finish()
    result_across.wait_all()
    for write in writes:
        write.wait()
    for h in range(pairs):
        do_spread.sent(h)
        aux_spread.sent(h)


def middle(n_dp, n_ex, collective_id, near, staged, far):
    arrays = {**near, **staged, **far}
    a = types.SimpleNamespace(**arrays)
    low, wide = jnp.bfloat16, jnp.float32
    tokens, width = a.stream.shape
    hidden = a.expert_in.shape[1]
    mixed = a.attn_in.shape[2]
    blocks, rows = hidden // width, width // n_dp
    long, short, pairs = LONG_DEV, tokens - LONG_DEV, width // 128
    _, padded = capacity_of(tokens, n_ex)
    slots = n_ex * padded
    group = min(max(4, 128 // padded), n_ex) * padded
    slab = (n_ex, padded, width)
    hops = (n_dp * n_ex).bit_length() - 1
    outs = dict(
        up_next=jax.ShapeDtypeStruct((tokens, width), wide),
        up_low=jax.ShapeDtypeStruct((tokens, width), low),
        mixed=jax.ShapeDtypeStruct((tokens, mixed), low),
        sums=jax.ShapeDtypeStruct((2, width), wide),
        attn_sums=jax.ShapeDtypeStruct((2, width), wide),
        router_grad=jax.ShapeDtypeStruct((n_ex, width), wide),
        stats=jax.ShapeDtypeStruct((n_ex, 128), wide),
        balance=jax.ShapeDtypeStruct((1, 128), wide),
        result_home=jax.ShapeDtypeStruct(slab, low),
        gate=jax.ShapeDtypeStruct((1, tokens), wide),
        dispatch=jax.ShapeDtypeStruct((slots, tokens), low),
    )
    direct, shared = len(outs), n_dp == 4
    known = 2 * slots if shared else slots
    if shared:
        outs.update(
            rows_t=jax.ShapeDtypeStruct((width, known), low),
            back=jax.ShapeDtypeStruct((known, width), low),
            expert_active_t=jax.ShapeDtypeStruct((hidden, known), low),
            expert_hidden=jax.ShapeDtypeStruct((known, hidden), low),
        )
    else:
        outs.update(chunks=jax.ShapeDtypeStruct((2 * blocks, rows, width), low))
    scratch = []
    for name in staged:
        scratch += [pltpu.VMEM(arrays[name].shape, arrays[name].dtype), pltpu.SemaphoreType.DMA]
    scratch += [pltpu.VMEM((blocks, width, width), low)] * 2 + [pltpu.SemaphoreType.DMA((2, blocks)), pltpu.SemaphoreType.DMA((4,))]
    scratch += [pltpu.VMEM(slab, low)] * 5
    scratch += [
        pltpu.VMEM((width, known), low),
        pltpu.VMEM((known, width), low),
        pltpu.VMEM((hidden, known), low),
        pltpu.VMEM((known, hidden), low),
        pltpu.VMEM((n_ex, 8, 128), wide),
        pltpu.VMEM((n_ex, 8, 128), wide),
        pltpu.VMEM((hops, n_ex, 128), wide),
        pltpu.VMEM((hops, n_ex, 128), wide),
        pltpu.VMEM((group, width), wide),
        pltpu.VMEM((group, width), wide),
    ]
    scratch += [pltpu.SemaphoreType.DMA((n_ex,))] * 8 + [pltpu.SemaphoreType.DMA((hops,))] * 2
    scratch += back_scratch(n_dp, pairs, long, short)
    if shared:
        scratch += [pltpu.VMEM(slab, low)] * 2 + [pltpu.SemaphoreType.DMA((n_ex, 2)), pltpu.SemaphoreType.DMA((2,))]
    else:
        scratch += Reduction.scratch(n_dp, 1, rows, width, [((0, width), 0)])
    vmem, anywhere = pl.BlockSpec(memory_space=pltpu.VMEM), pl.BlockSpec(memory_space=pl.ANY)
    names = tuple(arrays) + tuple(outs)
    values = pl.pallas_call(
        functools.partial(middle_kernel, n_dp, n_ex, names, tuple(staged)),
        out_shape=list(outs.values()),
        in_specs=[vmem] * len(near) + [anywhere] * (len(staged) + len(far)),
        out_specs=[vmem] * direct + [anywhere] * (len(outs) - direct),
        scratch_shapes=scratch,
        compiler_params=pltpu.CompilerParams(
            collective_id=collective_id, has_side_effects=True, vmem_limit_bytes=62 * 1024 * 1024
        ),
        name="middle",
    )(*arrays.values())
    return types.SimpleNamespace(**dict(zip(outs, values)))


def tail_kernel(n_dp, n_ex, names, staged, *refs):
    r = types.SimpleNamespace(**dict(zip(names, refs)))
    extra = iter(refs[len(names) :])
    loads = types.SimpleNamespace()
    for name in staged:
        buffer, sem = next(extra), next(extra)
        setattr(loads, name, pltpu.make_async_copy(getattr(r, name), buffer, sem))
        setattr(r, name, buffer)
    weights_in, weights_out, slopes, weight_sem = (next(extra) for _ in range(4))
    first_sem = next(extra)
    acc_ref, dense_low_ref, dense_hidden_ref = (next(extra) for _ in range(3))
    up_ref, first_low_ref, mixed_ref = acc_ref, r.second_low, r.second_mixed
    do_ref, aux_ref, short_do_ref, short_aux_ref, dq_ref, dk_ref, dv_ref = (next(extra) for _ in range(7))
    do_far, do_near, do_recv, aux_far, aux_near, aux_recv = (next(extra) for _ in range(6))
    small_send, small_recv, small_send_sem, small_recv_sem = (next(extra) for _ in range(4))
    shared = n_dp == 4
    if shared:
        expert_x, expert_y, expert_sem = (next(extra) for _ in range(3))
    links = Links(n_dp)
    me = links.me
    width = up_ref.shape[1]
    rows = width // n_dp
    pairs, long = r.kv.shape[1], r.kv.shape[3]
    blocks = r.dense_in.shape[1] // width
    per_in = mixed_ref.shape[1] // width

    def block_loads(i):
        slot = lax.rem(i, 2)
        at = pl.ds(pl.multiple_of(i * width, width), width)
        return [
            pltpu.make_async_copy(r.dense_out.at[at, :], weights_out.at[slot], weight_sem.at[slot, 0]),
            pltpu.make_async_copy(r.dense_in.at[:, at], weights_in.at[slot], weight_sem.at[slot, 1]),
            pltpu.make_async_copy(r.slope.at[:, at], slopes.at[slot], weight_sem.at[slot, 2]),
        ]

    ready = (loads.second_context_t, loads.second_low, loads.second_normed_t, loads.second_mixed)
    for load in ready:
        load.start()
    for i in range(min(2, blocks)):
        for load in block_loads(i):
            load.start()
    loads.active_t.start()
    for name in staged:
        if all(getattr(loads, name) is not load for load in ready + (loads.active_t,)):
            getattr(loads, name).start()
    free, busy = blocks % 2, (blocks - 1) % 2
    out_load = pltpu.make_async_copy(r.attn_out.at[0], weights_out.at[free], first_sem.at[0])
    thirds = [weights_in.at[free], weights_in.at[busy], weights_out.at[busy]]
    in_loads = [
        pltpu.make_async_copy(r.attn_in.at[0, :, pl.ds(i * width, width)], third, first_sem.at[1 + i])
        for i, third in enumerate(thirds)
    ]

    def columns(ref):
        return lambda j: ref[:, pl.ds(pl.multiple_of(j * width, width), width)]

    def one(ref):
        return lambda j, q: ref[q, 0]

    groups = [
        (1, one(r.second_context_t), columns(r.second_low)),
        (per_in, one(r.second_normed_t), columns(r.second_mixed)),
        (blocks, lambda j, q: r.active_t[q, j], lambda j: dense_low_ref[...]),
        (blocks, one(r.dense_normed_t), columns(dense_hidden_ref)),
        (1, one(r.first_context_t), columns(first_low_ref)),
        (per_in, one(r.first_normed_t), columns(mixed_ref)),
    ]
    red = Reduction(n_dp, n_ex, rows, groups, dense_lanes(width), extra, r.chunks)
    if shared:
        expert_blocks = r.expert_hidden.shape[1] // width
        base = 2 * links.chip

        def expert_loads(c, act):
            slot = lax.rem(c, 2)

            def load(rows_t, at, per, factor):
                for q in range(2):
                    row = pl.multiple_of(((base + q) * per + at) * rows, rows)
                    act(pltpu.make_async_copy(rows_t.at[pl.ds(row, rows), :], expert_x.at[slot, q], expert_sem.at[slot, q]))
                act(pltpu.make_async_copy(factor, expert_y.at[slot], expert_sem.at[slot, 2]))

            @pl.when(c < expert_blocks)
            def _():
                load(r.rows_t, 0, 1, r.expert_hidden.at[:, pl.ds(pl.multiple_of(c * width, width), width)])

            @pl.when((c >= expert_blocks) & (c < 2 * expert_blocks))
            def _():
                load(r.expert_active_t, c - expert_blocks, expert_blocks, r.back)

        def expert_part(j, q):
            return expert_x[lax.rem(j, 2), q]

        expert_groups = [(2 * expert_blocks, expert_part, lambda j: expert_y[lax.rem(j, 2)])]
        expert_red = Reduction(2, 1, rows, expert_groups, [((0, width), 0)], extra, r.expert_chunks)
    levels = [("dp", b) for b in range(n_dp.bit_length() - 1)] + [("ex", b) for b in range(n_ex.bit_length() - 1)]
    greet([red.peer(*level) for level in levels] + (links.peers()[1:] if links.chips > 2 else []))

    up = r.up[...]
    dense_low_ref[...] = up.astype(jnp.bfloat16)
    acc_ref[...] = jnp.zeros_like(acc_ref)
    for load in ready:
        load.wait()
    red.tick(0, 0, 1)
    loads.active_t.wait()

    def dense(i, _):
        slot = lax.rem(i, 2)
        for load in block_loads(i):
            load.wait()
        grad = dot_rows(dense_low_ref[...], weights_out[slot]) * slopes[slot].astype(jnp.float32)
        grad = grad.astype(jnp.bfloat16)
        dense_hidden_ref[:, pl.ds(pl.multiple_of(i * width, width), width)] = grad
        acc_ref[...] += dot_rows(grad, weights_in[slot])

        @pl.when(i + 2 < blocks)
        def _():
            for load in block_loads(i + 2):
                load.start()

        @pl.when(i == blocks - 2)
        def _():
            out_load.start()
            in_loads[0].start()

        red.tick(1 + i, 1, 1 + blocks)
        return 0

    lax.fori_loop(0, blocks, dense, 0)
    for load in in_loads[1:]:
        load.start()
    for name in staged:
        if all(getattr(loads, name) is not load for load in ready + (loads.active_t,)):
            getattr(loads, name).wait()
    unit, inverse = norm_parts(r.dense_x[...])
    grad_normed = acc_ref[...]
    up = up + norm_back(unit, inverse, r.gains[1:2], grad_normed)
    up_ref[...] = up
    for first, sums in ((2, r.second_sums), (3, r.last_sums)):
        small_send[0, first : first + 1] = sums[0:1]
        small_send[0, first + 4 : first + 5] = sums[1:2]
    small_send[0, 8:] = r.router_grad[...]
    small_send[0, 1:2] = jnp.sum(grad_normed * unit, axis=0, keepdims=True)
    small_send[0, 5:6] = jnp.sum(grad_normed, axis=0, keepdims=True)
    at_tick = 1 + blocks

    scale = HEAD_DIM ** (-0.5)
    up_low = up.astype(jnp.bfloat16)
    first_low_ref[...] = up_low
    out_load.wait()
    grad_context = dot_rows(up_low, weights_out[free]).astype(jnp.bfloat16)
    red.tick(at_tick, at_tick, at_tick + 1)
    at_tick += 1
    put_context_grads(grad_context, do_ref, short_do_ref, me, long)
    do_spread = Spread(links, lambda b, p: do_ref.at[b, p], pairs, False, do_far, do_near, do_recv)
    aux_spread = Spread(links, lambda b, p: aux_ref.at[b, p], pairs, False, aux_far, aux_near, aux_recv)
    put_row_terms(r.context, r.lse, grad_context, aux_ref, short_aux_ref, me, long)
    for h in range(pairs):
        do_spread.send(h)
        aux_spread.send(h)
    red.tick(at_tick, at_tick, at_tick + 1)
    at_tick += 1
    sequence = types.SimpleNamespace(
        doc_row=r.doc_row, kv=r.kv, q=r.q, short_kv=r.short_kv, short_q=r.short_q,
        do=do_ref, aux=aux_ref, short_do=short_do_ref, short_aux=short_aux_ref, dq=dq_ref, dk=dk_ref, dv=dv_ref,
        mixed=mixed_ref,
    )

    def pair(i, _):
        red.tick(at_tick + 2 * i, at_tick, at_tick + pairs)
        attend_back_pairs(n_dp, me, width, sequence, do_spread, aux_spread, [2 * i, 2 * i + 1])
        red.tick(at_tick + 2 * i + 1, at_tick, at_tick + pairs)
        return 0

    lax.fori_loop(0, pairs // 2, pair, 0)
    at_tick += pairs
    grad_normed = jnp.zeros((up_ref.shape[0], width), jnp.float32)
    for i, third in enumerate(thirds):
        in_loads[i].wait()
        grad_normed = grad_normed + dot_rows(mixed_ref[:, i * width : (i + 1) * width], third[...])
    unit, inverse = norm_parts(r.first_x[...].astype(jnp.float32))
    r.grad_tokens[...] = (
        up_ref[...] + norm_back(unit, inverse, r.gains[0:1], grad_normed)
    ).astype(jnp.bfloat16)
    small_send[0, 0:1] = jnp.sum(grad_normed * unit, axis=0, keepdims=True)
    small_send[0, 4:5] = jnp.sum(grad_normed, axis=0, keepdims=True)

    def small_copy(i):
        return pltpu.make_async_remote_copy(
            src_ref=small_send.at[i],
            dst_ref=small_recv.at[i],
            send_sem=small_send_sem.at[i],
            recv_sem=small_recv_sem.at[i],
            device_id=red.peer(*levels[i]),
            device_id_type=MESH,
        )

    small_copy(0).start()

    if shared:
        for c in range(2):
            expert_loads(jnp.int32(c), lambda copy: copy.start())

    def rest(t, _):
        red.tick(t, at_tick, red.ticks)
        if shared:
            c = t - at_tick
            expert_loads(c, lambda copy: copy.wait())
            expert_red.tick(c, 0, red.ticks - at_tick)
            expert_loads(c + 2, lambda copy: copy.start())

        @pl.when(t == red.ticks - 2)
        def _():
            gate = jnp.broadcast_to(r.gate[...], (128, r.gate.shape[1])).T[:, 0:1]
            for first in range(0, width, 256):
                at = slice(first, first + 256)
                home = r.result_home[:, :, at].reshape(r.dispatch.shape[0], 256)
                result = dot_columns(r.dispatch[...], home)
                r.output[:, at] = (r.last_x[:, at] + gate * result).astype(jnp.bfloat16)

        for i in range(1, len(levels) + 1):

            @pl.when(t == at_tick + i)
            def _(i=i):
                small_copy(i - 1).wait()
                value = small_send[i - 1] + small_recv[i - 1]
                if i < len(levels):
                    small_send[i] = value
                    small_copy(i).start()
                else:
                    own = jnp.zeros((value.shape[0], rows), jnp.float32)
                    for q in range(n_dp):
                        own = own + jnp.where(me == q, value[:, q * rows : (q + 1) * rows], 0.0)
                    r.small_sum[...] = own

        return 0

    lax.fori_loop(at_tick, red.ticks, rest, 0)
    if shared:
        for c in range(red.ticks - at_tick, expert_red.ticks):
            expert_loads(jnp.int32(c), lambda copy: copy.wait())
            expert_red.tick(jnp.int32(c), c, c + 1)
            expert_loads(jnp.int32(c + 2), lambda copy: copy.start())
        expert_red.finish()
    red.finish()
    for h in range(pairs):
        do_spread.sent(h)
        aux_spread.sent(h)


def tail(n_dp, n_ex, collective_id, near, staged, far):
    arrays = {**near, **staged, **far}
    a = types.SimpleNamespace(**arrays)
    low, wide = jnp.bfloat16, jnp.float32
    tokens, width = a.up.shape
    hidden = a.dense_in.shape[1]
    mixed = a.attn_in.shape[2]
    rows = width // n_dp
    long, short, pairs = LONG_DEV, tokens - LONG_DEV, width // 128
    chunks = 2 * (hidden // width) + 2 * (1 + mixed // width)
    small = (8 + a.router_grad.shape[0], width)
    outs = dict(
        grad_tokens=jax.ShapeDtypeStruct((tokens, width), low),
        output=jax.ShapeDtypeStruct((tokens, width), low),
        small_sum=jax.ShapeDtypeStruct((small[0], rows), wide),
    )
    direct, shared = len(outs), n_dp == 4
    outs.update(chunks=jax.ShapeDtypeStruct((chunks, rows, width), low))
    if shared:
        slots, expert_hidden = a.expert_hidden.shape
        outs.update(expert_chunks=jax.ShapeDtypeStruct((2 * expert_hidden // width, rows, width), low))
    scratch = []
    for name in staged:
        scratch += [pltpu.VMEM(arrays[name].shape, arrays[name].dtype), pltpu.SemaphoreType.DMA]
    scratch += [pltpu.VMEM((2, width, width), low)] * 2
    scratch += [pltpu.VMEM((2, tokens, width), low), pltpu.SemaphoreType.DMA((2, 3))]
    scratch += [pltpu.SemaphoreType.DMA((4,))]
    scratch += [pltpu.VMEM((tokens, width), wide)]
    scratch += [pltpu.VMEM((tokens, n), low) for n in (width, hidden)]
    scratch += back_scratch(n_dp, pairs, long, short)
    hops = (n_dp * n_ex).bit_length() - 1
    scratch += [pltpu.VMEM((hops,) + small, wide)] * 2 + [pltpu.SemaphoreType.DMA((hops,))] * 2
    if shared:
        scratch += [pltpu.VMEM((2, 2, rows, slots), low), pltpu.VMEM((2, slots, width), low)]
        scratch += [pltpu.SemaphoreType.DMA((2, 3))]
    scratch += Reduction.scratch(n_dp, n_ex, rows, width, dense_lanes(width))
    if shared:
        scratch += Reduction.scratch(2, 1, rows, width, [((0, width), 0)])
    vmem, anywhere = pl.BlockSpec(memory_space=pltpu.VMEM), pl.BlockSpec(memory_space=pl.ANY)
    names = tuple(arrays) + tuple(outs)
    values = pl.pallas_call(
        functools.partial(tail_kernel, n_dp, n_ex, names, tuple(staged)),
        out_shape=list(outs.values()),
        in_specs=[vmem] * len(near) + [anywhere] * (len(staged) + len(far)),
        out_specs=[vmem] * direct + [anywhere] * (len(outs) - direct),
        scratch_shapes=scratch,
        compiler_params=pltpu.CompilerParams(
            collective_id=collective_id, has_side_effects=True, vmem_limit_bytes=62 * 1024 * 1024
        ),
        name="tail",
    )(*arrays.values())
    return types.SimpleNamespace(**dict(zip(outs, values)))


def shards(
    tokens,
    doc_lengths,
    assign,
    ln_gain,
    ln_bias,
    attn_in,
    attn_out,
    ffn_in,
    ffn_out,
    router,
    expert_in,
    expert_out,
    cotangent,
):
    n_dp, n_ex = lax.axis_size("dp"), lax.axis_size("expert")
    row_count = tokens.shape[1]
    lengths = doc_lengths[0, 0]
    order = jnp.arange(lengths.shape[0])
    doc_ends = jnp.sum(jnp.where(order[:, None] <= order[None, :], lengths[:, None], 0), axis=0)
    short_place = jnp.arange(row_count - LONG_DEV, dtype=jnp.int32)
    doc_row = jnp.sum((short_place[None, :] >= doc_ends[:, None]).astype(jnp.float32), axis=0, keepdims=True)
    weights_in, weights_out = lax.optimization_barrier((attn_in.transpose(1, 0, 2), attn_out.transpose(1, 0, 2)))
    gains, shifts = ln_gain.T, ln_bias.T
    assign_row = assign[0].T
    fore = front(
        n_dp,
        n_ex,
        2,
        dict(
            tokens=tokens[0],
            gains=gains,
            shifts=shifts,
            doc_row=doc_row,
            assign=assign_row,
            cot=cotangent[0],
        ),
        dict(attn_in=weights_in, attn_out=weights_out, dense_in=ffn_in, dense_out=ffn_out),
    )
    model_width = tokens.shape[2]
    rows = model_width // n_dp
    mid = middle(
        n_dp,
        n_ex,
        4,
        dict(
            stream=fore.stream2,
            gains=gains,
            shifts=shifts,
            router=router.T,
            assign=assign_row,
            cot=cotangent[0],
            far_cot=fore.far_cot,
            doc_row=doc_row,
            lse=fore.lse1,
        ),
        dict(
            attn_x=fore.stream1,
            context=fore.context1,
            kv=fore.kv1,
            q=fore.q1,
            short_kv=fore.short_kv1,
            short_q=fore.short_q1,
        ),
        dict(
            expert_in=expert_in[0],
            expert_out=expert_out[0],
            attn_in=weights_in,
            attn_out=weights_out,
        ),
    )
    def blocks_of(rows_t):
        return rows_t.reshape(n_dp, -1, rows, row_count)

    shared = n_dp == 4
    last = tail(
        n_dp,
        n_ex,
        5,
        dict(
            up=mid.up_next,
            gains=gains,
            doc_row=doc_row,
            lse=fore.lse0,
            second_sums=mid.attn_sums,
            last_sums=mid.sums,
            router_grad=mid.router_grad,
            dispatch=mid.dispatch,
            gate=mid.gate,
        ),
        dict(
            dense_x=fore.stream0,
            first_x=tokens[0],
            context=fore.context0,
            kv=fore.kv0,
            q=fore.q0,
            short_kv=fore.short_kv0,
            short_q=fore.short_q0,
            second_context_t=blocks_of(fore.context_t1),
            second_normed_t=blocks_of(fore.normed_t1),
            active_t=blocks_of(fore.active_t),
            dense_normed_t=blocks_of(fore.dense_normed_t),
            first_context_t=blocks_of(fore.context_t0),
            first_normed_t=blocks_of(fore.normed_t0),
            second_low=mid.up_low,
            result_home=mid.result_home,
            last_x=fore.stream2,
            second_mixed=mid.mixed,
        ),
        dict(
            dense_in=ffn_in,
            dense_out=ffn_out,
            slope=fore.slope,
            attn_in=weights_in,
            attn_out=weights_out,
            **(
                dict(
                    rows_t=mid.rows_t,
                    back=mid.back,
                    expert_active_t=mid.expert_active_t,
                    expert_hidden=mid.expert_hidden,
                )
                if shared
                else {}
            ),
        ),
    )
    expert_chunks = last.expert_chunks if shared else mid.chunks
    (
        attn_in_sum, attn_out_sum, ffn_in_sum, ffn_out_sum, expert_in_sum, expert_out_sum,
        gain_sum, shift_sum, router_sum, grad_tokens, output,
    ) = unpack(
        last.chunks, expert_chunks, last.small_sum, last.grad_tokens, last.output,
        attn_in.shape[2] // model_width, ffn_in.shape[1] // model_width,
    )
    return (
        output[None],
        mid.balance[0, 0],
        grad_tokens[None],
        gain_sum.T,
        shift_sum.T,
        attn_in_sum,
        attn_out_sum,
        ffn_in_sum,
        ffn_out_sum.reshape(-1, model_width),
        router_sum.T,
        expert_in_sum[None],
        expert_out_sum.reshape(1, -1, model_width),
    )


def solution(mesh):
    return jax.shard_map(
        shards,
        mesh=mesh,
        in_specs=(
            P("expert", "dp", None),
            P("expert", "dp", None),
            P("expert", "dp", None),
            P(),
            P(),
            P(),
            P(),
            P(),
            P(),
            P(),
            P("expert", None, None),
            P("expert", None, None),
            P("expert", "dp", None),
        ),
        out_specs=(
            P("expert", "dp", None),
            P(),
            P("expert", "dp", None),
            P("dp", None),
            P("dp", None),
            P("dp", None, None),
            P("dp", None, None),
            P("dp", None),
            P("dp", None),
            P("dp", None),
            P("expert", "dp", None),
            P("expert", "dp", None),
        ),
        check_vma=False,
    )
```

```python
import functools
import types

import jax
import jax.numpy as jnp
from jax import lax
from jax.experimental import pallas as pl
from jax.experimental.pallas import tpu as pltpu
from jax.sharding import PartitionSpec as P

MESH = pl.DeviceIdType.MESH
HEADS = 12
HEAD_DIM = 64
LONG_DEV = 256


epsilon = 1e-05
balance_weight = 0.01
masked_score = -1e30


def bit_of(index, level):
    return (index // (1 << level)) % 2


def flip(index, level):
    return index + (1 << level) * (1 - 2 * bit_of(index, level))


def partner_index(index, mask, levels):
    total = 0
    for level in range(levels):
        own = bit_of(index, level)
        total = total + (1 << level) * (1 - own if (mask >> level) & 1 else own)
    return total


def unpack_kernel(
    per_in, per_ffn,
    chunk_ref, expert_ref, small_ref, tokens_ref, output_ref,
    in_ref, out_ref, ffn_in_ref, ffn_out_ref, expert_in_ref, expert_out_ref,
    gain_ref, shift_ref, router_ref, tokens_out_ref, output_out_ref,
):
    per_expert = expert_ref.shape[0] // 2
    width = chunk_ref.shape[2]
    at = 0
    for layer in (1, 0):
        out_ref[:, layer, :] = chunk_ref[at].astype(jnp.float32)
        for j in range(per_in):
            in_ref[:, layer, width * j : width * j + width] = chunk_ref[at + 1 + j].astype(jnp.float32)
        at += 1 + per_in
        if layer:
            for j in range(per_ffn):
                ffn_out_ref[j] = chunk_ref[at + j].astype(jnp.float32)
                ffn_in_ref[:, width * j : width * j + width] = chunk_ref[at + per_ffn + j].astype(jnp.float32)
            at += 2 * per_ffn
    for j in range(per_expert):
        expert_in_ref[:, width * j : width * j + width] = expert_ref[j].astype(jnp.float32)
        expert_out_ref[j] = expert_ref[per_expert + j].astype(jnp.float32)
    gain_ref[...] = small_ref[0:4]
    shift_ref[...] = small_ref[4:8]
    router_ref[...] = small_ref[8:]
    tokens_out_ref[...] = tokens_ref[...]
    output_out_ref[...] = output_ref[...]


def unpack(chunks, expert_chunks, small, grad_tokens, output, per_in, per_ffn):
    count, rows, width = chunks.shape
    experts = expert_chunks.shape[0]
    tokens = output.shape[0]
    step = 32 if rows % 32 == 0 else rows
    wide, low = jnp.float32, jnp.bfloat16
    token_spec = pl.BlockSpec((tokens // (rows // step), width), lambda i: (i, 0))

    def fixed(shape):
        return pl.BlockSpec(shape, lambda i: (0, 0))

    return pl.pallas_call(
        functools.partial(unpack_kernel, per_in, per_ffn),
        grid=(rows // step,),
        out_shape=[
            jax.ShapeDtypeStruct((rows, 2, per_in * width), wide),
            jax.ShapeDtypeStruct((rows, 2, width), wide),
            jax.ShapeDtypeStruct((rows, per_ffn * width), wide),
            jax.ShapeDtypeStruct((per_ffn, rows, width), wide),
            jax.ShapeDtypeStruct((rows, experts // 2 * width), wide),
            jax.ShapeDtypeStruct((experts // 2, rows, width), wide),
            jax.ShapeDtypeStruct((4, rows), wide),
            jax.ShapeDtypeStruct((4, rows), wide),
            jax.ShapeDtypeStruct((small.shape[0] - 8, rows), wide),
            jax.ShapeDtypeStruct((tokens, width), low),
            jax.ShapeDtypeStruct((tokens, width), low),
        ],
        in_specs=[
            pl.BlockSpec((count, step, width), lambda i: (0, i, 0)),
            pl.BlockSpec((experts, step, width), lambda i: (0, i, 0)),
            fixed(small.shape),
            token_spec,
            token_spec,
        ],
        out_specs=[
            pl.BlockSpec((step, 2, per_in * width), lambda i: (i, 0, 0)),
            pl.BlockSpec((step, 2, width), lambda i: (i, 0, 0)),
            pl.BlockSpec((step, per_ffn * width), lambda i: (i, 0)),
            pl.BlockSpec((per_ffn, step, width), lambda i: (0, i, 0)),
            pl.BlockSpec((step, experts // 2 * width), lambda i: (i, 0)),
            pl.BlockSpec((experts // 2, step, width), lambda i: (0, i, 0)),
            fixed((4, rows)),
            fixed((4, rows)),
            fixed((small.shape[0] - 8, rows)),
            token_spec,
            token_spec,
        ],
        compiler_params=pltpu.CompilerParams(vmem_limit_bytes=62 * 1024 * 1024),
        name="unpack",
    )(chunks, expert_chunks, small, grad_tokens, output)


def dot(a, b):
    return jnp.dot(a, b, preferred_element_type=jnp.float32)


def dot_rows(a, b):
    return lax.dot_general(a, b, (((1,), (1,)), ((), ())), preferred_element_type=jnp.float32)


def dot_columns(a, b):
    return lax.dot_general(a, b, (((0,), (0,)), ((), ())), preferred_element_type=jnp.float32)


def gelu_parts(hidden):
    lower = 0.5 + 0.5 * lax.erf(hidden * 0.7071067811865476)
    slope = lower + hidden * jnp.exp(-0.5 * hidden * hidden) * 0.3989422804014327
    return hidden * lower, slope


def split(value):
    high = value.astype(jnp.bfloat16)
    rest = value - high.astype(jnp.float32)
    middle_part = rest.astype(jnp.bfloat16)
    low = (rest - middle_part.astype(jnp.float32)).astype(jnp.bfloat16)
    return jnp.concatenate([high, middle_part, low], axis=0)


def norm_parts(x):
    center = x - jnp.mean(x, axis=-1, keepdims=True)
    inverse = lax.rsqrt(jnp.mean(center * center, axis=-1, keepdims=True) + epsilon)
    return center * inverse, inverse


def norm_back(unit, inverse, gain, upstream):
    scaled = upstream * gain
    return inverse * (
        scaled - jnp.mean(scaled, axis=-1, keepdims=True) - unit * jnp.mean(scaled * unit, axis=-1, keepdims=True)
    )


def capacity_of(rows, experts):
    capacity = (5 * rows + 4 * experts - 1) // (4 * experts)
    return capacity, -(-capacity // 16) * 16


def chosen_rows(assign, experts):
    expert = lax.broadcasted_iota(jnp.int32, (experts, assign.shape[1]), 0)
    return jnp.where(assign == expert, 1.0, 0.0)


def dispatch_of(assign, experts):
    tokens = assign.shape[1]
    capacity, padded = capacity_of(tokens, experts)
    hot = chosen_rows(assign, experts)
    earlier = lax.broadcasted_iota(jnp.int32, (tokens, tokens), 0) < lax.broadcasted_iota(jnp.int32, (tokens, tokens), 1)
    before = dot(hot.astype(jnp.bfloat16), jnp.where(earlier, 1.0, 0.0).astype(jnp.bfloat16))
    place = jnp.sum(hot * before, axis=0, keepdims=True)
    slot = jnp.where(place < capacity, assign.astype(jnp.float32) * padded + place, -1.0)
    number = lax.broadcasted_iota(jnp.int32, (experts * padded, tokens), 0).astype(jnp.float32)
    return jnp.where(number == slot, 1.0, 0.0).astype(jnp.bfloat16)


class Across:
    def __init__(self, experts, out, into, send_sems, recv_sems):
        self.experts, self.out, self.into = experts, out, into
        self.send_sems, self.recv_sems = send_sems, recv_sems
        self.dp, self.me = lax.axis_index("dp"), lax.axis_index("expert")

    def copy(self, slab, place, to):
        return pltpu.make_async_remote_copy(
            src_ref=self.out.at[slab],
            dst_ref=self.into.at[place],
            send_sem=self.send_sems.at[slab],
            recv_sem=self.recv_sems.at[place],
            device_id=(self.dp, to),
            device_id_type=MESH,
        )

    def start(self, j):
        self.copy(j, self.me, j).start()

    def wait_from(self, j):
        self.copy(j, j, j).wait_recv()

    def wait_to(self, j):
        self.copy(j, self.me, j).wait_send()

    def others(self, use):
        def body(k, _):
            use(lax.rem(self.me + k, self.experts))
            return 0

        lax.fori_loop(1, self.experts, body, 0)

    def start_all(self):
        self.others(self.start)

    def wait_all(self):
        def both(j):
            self.wait_from(j)
            self.wait_to(j)

        self.others(both)


def greet(targets):
    barrier = pltpu.get_barrier_semaphore()
    for device in targets:
        pl.semaphore_signal(barrier, inc=1, device_id=device, device_id_type=MESH)
    pl.semaphore_wait(barrier, len(targets))


def across_peers(experts):
    d, e = lax.axis_index("dp"), lax.axis_index("expert")
    return [(d, lax.rem(e + k, experts)) for k in range(1, experts)]


def head_pair(rows):
    first = lax.broadcasted_iota(jnp.int32, rows.shape, 1) < HEAD_DIM
    zero = jnp.zeros_like(rows)
    return jnp.concatenate([jnp.where(first, rows, zero), jnp.where(first, zero, rows)], axis=0)


def pair_rows(both):
    n = both.shape[1] // 2
    return jnp.concatenate([both[:HEAD_DIM, :n], both[HEAD_DIM:, n:]], axis=0)


def causal(keys, queries):
    key = lax.broadcasted_iota(jnp.int32, (keys, 2 * queries), 0)
    query = lax.broadcasted_iota(jnp.int32, (keys, 2 * queries), 1)
    return key <= jnp.where(query >= queries, query - queries, query)


def short_seen(doc_row):
    n = doc_row.shape[1]
    doc_col = jnp.broadcast_to(doc_row, (n, n)).T
    same = jnp.concatenate([doc_col, doc_col], axis=1) == jnp.concatenate([doc_row, doc_row], axis=1)
    return same & causal(n, n)


class Links:
    def __init__(self, n_dp):
        self.me, self.expert = lax.axis_index("dp"), lax.axis_index("expert")
        self.chips = n_dp // 2
        self.chip, self.core = self.me // 2, self.me % 2
        self.twin = self.me + 1 - 2 * self.core

    def peers(self):
        ring = [lax.rem(self.chip + k, self.chips) for k in range(1, self.chips)]
        return [(self.twin, self.expert)] + [(2 * other + self.core, self.expert) for other in ring]

    def copy(self, ref, send_sem, recv_sem, index):
        return pltpu.make_async_remote_copy(
            src_ref=ref,
            dst_ref=ref,
            send_sem=send_sem,
            recv_sem=recv_sem,
            device_id=(index, self.expert),
            device_id_type=MESH,
        )

    def before(self, later, other):
        return other > self.chip if later else other < self.chip


class Spread:
    def __init__(self, links, at, parts, later, far_sems, near_sems, recv_sems):
        self.links, self.at, self.later = links, at, later
        self.far_sems, self.near_sems, self.recv_sems = far_sems, near_sems, recv_sems

    def _far(self, other, p):
        k = self.links
        return k.copy(self.at(k.me, p), self.far_sems.at[other, p], self.recv_sems.at[k.me, p], 2 * other + k.core)

    def _near(self, block, p):
        k = self.links
        return k.copy(self.at(block, p), self.near_sems.at[block, p], self.recv_sems.at[block, p], k.twin)

    def _twin_needs(self):
        return self.links.core == (0 if self.later else 1)

    def send(self, p):
        k = self.links
        for other in range(k.chips):

            @pl.when(k.before(self.later, other))
            def _():
                self._far(other, p).start()

        @pl.when(self._twin_needs())
        def _():
            self._near(k.me, p).start()

    def sent(self, p):
        k = self.links
        for other in range(k.chips):

            @pl.when(k.before(self.later, other))
            def _():
                self._far(other, p).wait_send()

            @pl.when(k.before(not self.later, other))
            def _():
                self._near(2 * other + k.core, p).wait_send()

        @pl.when(self._twin_needs())
        def _():
            self._near(k.me, p).wait_send()

    def relay(self, p):
        k = self.links
        for other in range(k.chips):

            @pl.when(k.before(not self.later, other))
            def _():
                block = 2 * other + k.core
                copy = self._near(block, p)
                copy.wait_recv()
                copy.start()

    def each(self, p, use):
        k = self.links

        @pl.when(k.core == (1 if self.later else 0))
        def _():
            self._near(k.twin, p).wait_recv()
            use(k.twin)

        for other in range(k.chips):

            @pl.when(k.before(not self.later, other))
            def _():
                use(2 * other + k.core)
                block = 2 * other + 1 - k.core
                self._near(block, p).wait_recv()
                use(block)


def spread_sems(n_dp, parts):
    return [
        pltpu.SemaphoreType.DMA((n_dp // 2, parts)),
        pltpu.SemaphoreType.DMA((n_dp, parts)),
        pltpu.SemaphoreType.DMA((n_dp, parts)),
    ]


def queries_of(rows, w_q):
    return (dot(rows, w_q).astype(jnp.bfloat16) * HEAD_DIM ** (-0.5)).astype(jnp.bfloat16)


def attend(n_dp, links, s, x, gain, shift, w_in, w_out, doc_row, ready, between):
    me = links.me
    pairs, long, width = s.kv.shape[1], s.kv.shape[3], x.shape[1]
    unit, _ = norm_parts(x)
    normed = (unit * gain + shift).astype(jnp.bfloat16)
    s.rows[me] = normed[:long]
    later = Spread(links, lambda b, p: s.rows.at[b], 1, True, *s.kv_sems)
    earlier = Spread(links, lambda b, p: s.rows.at[b], 1, False, *s.q_sems)
    later.send(0)
    earlier.send(0)
    ready(0)
    kv = dot(normed, w_in[:, width:]).astype(jnp.bfloat16)
    ready(1)
    q = queries_of(normed, w_in[:, :width])
    for h in range(pairs):
        at = slice(128 * h, 128 * h + 128)
        for part in range(2):
            piece = kv[:, part * width + 128 * h : part * width + 128 * h + 128]
            s.kv[me, h, part] = piece[:long]
            s.short_kv[h, part] = piece[long:]
        s.q[me, h] = q[:long, at]
        s.short_q[h] = q[long:, at]
    between()
    s.normed_t[...] = normed.T

    def put_context(h, rows_t, first, count):
        at = pl.ds(pl.multiple_of(128 * h, 128), 128)
        s.context_t[at, first : first + count] = rows_t.astype(jnp.bfloat16)
        s.context[first : first + count, at] = rows_t.T.astype(jnp.bfloat16)

    low = jnp.bfloat16
    short_mask, long_mask = short_seen(doc_row), causal(long, long)

    def own_part(i, _):
        hs = [2 * i, 2 * i + 1]
        scores = [dot_rows(s.short_kv[h, 0], head_pair(s.short_q[h])) for h in hs]
        scores = [jnp.where(short_mask, v, masked_score) for v in scores]
        long_scores = [dot_rows(s.kv[me, h, 0], head_pair(s.q[me, h])) for h in hs]
        tops = [jnp.max(v, axis=0, keepdims=True) for v in scores]
        weights = [jnp.exp(v - top) for v, top in zip(scores, tops)]
        totals = [jnp.sum(v, axis=0, keepdims=True) for v in weights]
        sums = [dot_columns(s.short_kv[h, 1], v.astype(low)) for h, v in zip(hs, weights)]
        long_scores = [jnp.where(long_mask, v, masked_score) for v in long_scores]
        long_tops = [jnp.max(v, axis=0, keepdims=True) for v in long_scores]
        long_weights = [jnp.exp(v - top) for v, top in zip(long_scores, long_tops)]
        long_sums = [dot_columns(s.kv[me, h, 1], v.astype(low)) for h, v in zip(hs, long_weights)]
        for n, h in enumerate(hs):
            rows_t = pair_rows(sums[n] / totals[n])
            short = rows_t.shape[1]
            put_context(h, rows_t, long, short)
            lse = tops[n] + jnp.log(totals[n])
            s.lse[h, 0:1, long:] = lse[:, :short]
            s.lse[h, 1:2, long:] = lse[:, short:]
            s.top[h] = long_tops[n]
            s.total[h] = jnp.sum(long_weights[n], axis=0, keepdims=True)
            s.acc[h] = long_sums[n]
        return 0

    lax.fori_loop(0, pairs // 2, own_part, 0)

    def keys_of(block):
        kv = dot(s.rows[block], w_in[:, width:]).astype(jnp.bfloat16)
        for h in range(pairs):
            for part in range(2):
                s.kv[block, h, part] = kv[:, part * width + 128 * h : part * width + 128 * h + 128]

    later.relay(0)
    later.each(0, keys_of)

    def other_part(i, _):
        hs = [2 * i, 2 * i + 1]

        def use(first, size):
            at = pl.ds(first, size)
            keys = [s.kv[at, h, 0].reshape(size * long, 128) for h in hs]
            values = [s.kv[at, h, 1].reshape(size * long, 128) for h in hs]
            scores = [dot_rows(v, head_pair(s.q[me, h])) for h, v in zip(hs, keys)]
            olds = [s.top[h] for h in hs]
            tops = [jnp.maximum(old, jnp.max(v, axis=0, keepdims=True)) for old, v in zip(olds, scores)]
            factors = [jnp.exp(old - top) for old, top in zip(olds, tops)]
            weights = [jnp.exp(v - top) for v, top in zip(scores, tops)]
            totals = [s.total[h] * f + jnp.sum(v, axis=0, keepdims=True) for h, f, v in zip(hs, factors, weights)]
            sums = [s.acc[h] * f + dot_columns(u, v.astype(low)) for h, f, u, v in zip(hs, factors, values, weights)]
            for n, h in enumerate(hs):
                s.top[h] = tops[n]
                s.total[h] = totals[n]
                s.acc[h] = sums[n]

        runs(n_dp - 1, me, use)
        for h in hs:
            total = s.total[h]
            put_context(h, pair_rows(s.acc[h] / total), 0, long)
            lse = s.top[h] + jnp.log(total)
            s.lse[h, 0:1, :long] = lse[:, :long]
            s.lse[h, 1:2, :long] = lse[:, long:]
        return 0

    lax.fori_loop(0, pairs // 2, other_part, 0)
    ready(2)
    following = x + dot(s.context[...], w_out[...])

    def settle():
        def ask(block):
            q = queries_of(s.rows[block], w_in[:, :width])
            for h in range(pairs):
                s.q[block, h] = q[:, 128 * h : 128 * h + 128]

        earlier.relay(0)
        earlier.each(0, ask)
        earlier.sent(0)
        later.sent(0)

    return following, settle


def front_kernel(n_dp, n_ex, names, saved, *refs):
    r = types.SimpleNamespace(**dict(zip(names, refs)))
    extra = iter(refs[len(names) :])
    buffers = []
    for layer in range(2):
        s = types.SimpleNamespace()
        for name in saved:
            setattr(s, name, next(extra))
        s.rows = next(extra)
        s.kv_sems = [next(extra) for _ in range(3)]
        s.q_sems = [next(extra) for _ in range(3)]
        s.stored = next(extra)
        buffers.append(s)
    sums = [next(extra) for _ in range(3)]
    for s in buffers:
        s.acc, s.top, s.total = sums
    w_in, w_out, w_sem, dense_in, dense_out, dense_sem = (next(extra) for _ in range(6))
    stream_ref, dense_normed, active_ref, slope_ref, dense_normed_t, far_cot = (next(extra) for _ in range(6))
    stored, cot_send, cot_send_sem, cot_recv_sem = (next(extra) for _ in range(4))
    links = Links(n_dp)
    tokens, width = r.tokens.shape
    blocks = r.dense_in.shape[1] // width
    low = jnp.bfloat16

    def block_loads(i):
        slot = lax.rem(i, 2)
        at = pl.ds(pl.multiple_of(i * width, width), width)
        return [
            pltpu.make_async_copy(r.dense_in.at[:, at], dense_in.at[slot], dense_sem.at[slot, 0]),
            pltpu.make_async_copy(r.dense_out.at[at, :], dense_out.at[slot], dense_sem.at[slot, 1]),
        ]

    def weight_loads(layer):
        return [
            pltpu.make_async_copy(
                r.attn_in.at[layer, :, pl.ds(width, 2 * width)], w_in.at[layer, :, pl.ds(width, 2 * width)], w_sem.at[layer, 0]
            ),
            pltpu.make_async_copy(
                r.attn_in.at[layer, :, pl.ds(0, width)], w_in.at[layer, :, pl.ds(0, width)], w_sem.at[layer, 1]
            ),
            pltpu.make_async_copy(r.attn_out.at[layer], w_out.at[layer], w_sem.at[layer, 2]),
        ]

    loads = [weight_loads(0), weight_loads(1)]
    for load in loads[0]:
        load.start()
    for i in range(min(2, blocks)):
        for load in block_loads(i):
            load.start()
    for load in loads[1]:
        load.start()
    greet(links.peers() + across_peers(n_ex))
    writes = []

    def write(source, target, sem):
        copy = pltpu.make_async_copy(source, target, sem)
        copy.start()
        writes.append(copy)

    def layer(number, x, between):
        s = buffers[number]
        column = 2 * number
        following, settle = attend(
            n_dp, links, s, x, r.gains[column : column + 1], r.shifts[column : column + 1], w_in.at[number], w_out.at[number],
            r.doc_row[...], lambda i: loads[number][i].wait(), between,
        )
        return following, settle

    def save(number, settle):
        s = buffers[number]
        settle()
        for i, name in enumerate(saved):
            write(getattr(s, name), getattr(r, name + str(number)), s.stored.at[i])

    x, settle = layer(0, r.tokens[...].astype(jnp.float32), lambda: None)
    r.stream0[...] = x
    stream_ref[...] = x
    unit, _ = norm_parts(x)
    normed = (unit * r.gains[1:2] + r.shifts[1:2]).astype(low)
    dense_normed[...] = normed
    save(0, settle)
    dense_normed_t[...] = normed.T

    def dense(i, _):
        slot = lax.rem(i, 2)
        for load in block_loads(i):
            load.wait()
        active, slope = gelu_parts(dot(dense_normed[...], dense_in[slot]))
        active = active.astype(low)
        at = pl.ds(pl.multiple_of(i * width, width), width)
        slope_ref[:, at] = slope.astype(low)
        active_ref[at, :] = active.T
        stream_ref[...] += dot(active, dense_out[slot])

        @pl.when(i + 2 < blocks)
        def _():
            for load in block_loads(i + 2):
                load.start()

        return 0

    lax.fori_loop(0, blocks, dense, 0)
    write(dense_normed_t, r.dense_normed_t, stored.at[0])
    write(active_ref, r.active_t, stored.at[1])
    write(slope_ref, r.slope, stored.at[2])
    x = stream_ref[...]
    r.stream1[...] = x

    cot_across = Across(n_ex, cot_send, far_cot, cot_send_sem, cot_recv_sem)

    def send_cotangent():
        cot_send[...] = dot(dispatch_of(r.assign[...], n_ex), r.cot[...]).astype(low).reshape(cot_send.shape)
        cot_across.start_all()
        far_cot[links.expert] = cot_send[links.expert]

    x, settle = layer(1, x, send_cotangent)
    r.stream2[...] = x
    save(1, settle)
    cot_across.wait_all()
    write(far_cot, r.far_cot, stored.at[3])
    for copy in writes:
        copy.wait()


def front(n_dp, n_ex, collective_id, near, far):
    arrays = {**near, **far}
    a = types.SimpleNamespace(**arrays)
    low, wide = jnp.bfloat16, jnp.float32
    tokens, width = a.tokens.shape
    hidden, mixed = a.dense_in.shape[1], a.attn_in.shape[2]
    long, short, pairs = LONG_DEV, tokens - LONG_DEV, width // 128
    slab = (n_ex, capacity_of(tokens, n_ex)[1], width)
    saved = dict(
        normed_t=jax.ShapeDtypeStruct((width, tokens), low),
        context=jax.ShapeDtypeStruct((tokens, width), low),
        context_t=jax.ShapeDtypeStruct((width, tokens), low),
        kv=jax.ShapeDtypeStruct((n_dp, pairs, 2, long, 128), low),
        q=jax.ShapeDtypeStruct((n_dp, pairs, long, 128), low),
        short_kv=jax.ShapeDtypeStruct((pairs, 2, short, 128), low),
        short_q=jax.ShapeDtypeStruct((pairs, short, 128), low),
        lse=jax.ShapeDtypeStruct((pairs, 2, tokens), wide),
    )
    stream = jax.ShapeDtypeStruct((tokens, width), wide)
    outs = dict(stream0=stream, stream1=stream, stream2=stream)
    direct = len(outs)
    for layer in range(2):
        for name, shape in saved.items():
            outs[name + str(layer)] = shape
    outs.update(
        dense_normed_t=jax.ShapeDtypeStruct((width, tokens), low),
        active_t=jax.ShapeDtypeStruct((hidden, tokens), low),
        slope=jax.ShapeDtypeStruct((tokens, hidden), low),
        far_cot=jax.ShapeDtypeStruct(slab, low),
    )
    scratch = []
    for layer in range(2):
        scratch += [pltpu.VMEM(shape.shape, shape.dtype) for shape in saved.values()]
        scratch += [pltpu.VMEM((n_dp, long, width), low)]
        scratch += spread_sems(n_dp, 1) + spread_sems(n_dp, 1)
        scratch += [pltpu.SemaphoreType.DMA((len(saved),))]
    scratch += [pltpu.VMEM((pairs, 128, 2 * long), wide)] + [pltpu.VMEM((pairs, 1, 2 * long), wide)] * 2
    scratch += [pltpu.VMEM((2, width, mixed), low), pltpu.VMEM((2, width, width), low), pltpu.SemaphoreType.DMA((2, 3))]
    scratch += [pltpu.VMEM((2, width, width), low)] * 2 + [pltpu.SemaphoreType.DMA((2, 2))]
    scratch += [
        pltpu.VMEM((tokens, width), wide),
        pltpu.VMEM((tokens, width), low),
        pltpu.VMEM((hidden, tokens), low),
        pltpu.VMEM((tokens, hidden), low),
        pltpu.VMEM((width, tokens), low),
        pltpu.VMEM(slab, low),
        pltpu.SemaphoreType.DMA((4,)),
        pltpu.VMEM(slab, low),
        pltpu.SemaphoreType.DMA((n_ex,)),
        pltpu.SemaphoreType.DMA((n_ex,)),
    ]
    vmem, anywhere = pl.BlockSpec(memory_space=pltpu.VMEM), pl.BlockSpec(memory_space=pl.ANY)
    names = tuple(arrays) + tuple(outs)
    values = pl.pallas_call(
        functools.partial(front_kernel, n_dp, n_ex, names, tuple(saved)),
        out_shape=list(outs.values()),
        in_specs=[vmem] * len(near) + [anywhere] * len(far),
        out_specs=[vmem] * direct + [anywhere] * (len(outs) - direct),
        scratch_shapes=scratch,
        compiler_params=pltpu.CompilerParams(
            collective_id=collective_id, has_side_effects=True, vmem_limit_bytes=63 * 1024 * 1024
        ),
        name="front",
    )(*arrays.values())
    return types.SimpleNamespace(**dict(zip(outs, values)))


def runs(most, count, use):
    for first in range(0, most, 3):
        for size in range(1, min(3, most - first) + 1):
            exactly = count - first == size if size < 3 else count - first >= size

            @pl.when(exactly)
            def _():
                use(first, size)


def put_context_grads(grad_context, do_ref, short_do_ref, me, long):
    for h in range(do_ref.shape[1]):
        piece = grad_context[:, 128 * h : 128 * h + 128]
        do_ref[me, h] = piece[:long]
        short_do_ref[h] = piece[long:]


def put_row_terms(context, lse, grad_context, aux_ref, short_aux_ref, me, long):
    width = grad_context.shape[1]
    rows = (width // HEAD_DIM + 15) // 16 * 16
    lane = lax.broadcasted_iota(jnp.int32, (rows, width), 1)
    head = lax.broadcasted_iota(jnp.int32, (rows, width), 0) * HEAD_DIM
    picks = jnp.where((lane >= head) & (lane < head + HEAD_DIM), 1.0, 0.0).astype(jnp.bfloat16)
    both = grad_context.astype(jnp.float32) * context[...].astype(jnp.float32)
    high = both.astype(jnp.bfloat16)
    delta = dot_rows(picks, high) + dot_rows(picks, (both - high.astype(jnp.float32)).astype(jnp.bfloat16))
    for h in range(aux_ref.shape[1]):
        aux_ref[me, h, 0:2] = lse[h, :, :long]
        aux_ref[me, h, 2:4] = delta[2 * h : 2 * h + 2, :long]
        short_aux_ref[h, 0:2] = lse[h, :, long:]
        short_aux_ref[h, 2:4] = delta[2 * h : 2 * h + 2, long:]


def attend_back_pairs(n_dp, me, width, r, do_spread, aux_spread, hs):
    scale = HEAD_DIM ** (-0.5)
    mixed_ref, low = r.mixed, jnp.bfloat16
    long = r.kv.shape[3]
    each = range(len(hs))

    def row_of(aux):
        return [jnp.concatenate([aux[i : i + 1], aux[i + 1 : i + 2]], axis=1) for i in (0, 2)]

    def score_grads(keys, values, queries, grads, rows, seen):
        each = range(len(keys))
        scores = [dot_rows(keys[n], queries[n]) for n in each]
        grad_probs = [dot_rows(values[n], grads[n]) for n in each]
        probs = [jnp.exp(scores[n] - rows[n][0]) for n in each]
        if seen is not None:
            probs = [jnp.where(seen, v, 0.0) for v in probs]
        grad_scores = [(probs[n] * (grad_probs[n] - rows[n][1])).astype(low) for n in each]
        return [v.astype(low) for v in probs], grad_scores

    def put(h, third, first, value):
        at = pl.ds(pl.multiple_of(third * width + 128 * h, 128), 128)
        mixed_ref[first : first + value.shape[0], at] = value.astype(low)

    seen = short_seen(r.doc_row[...])
    short_queries, short_grads = [head_pair(r.short_q[h]) for h in hs], [head_pair(r.short_do[h]) for h in hs]
    short_keys = [r.short_kv[h, 0] for h in hs]
    short_values = [r.short_kv[h, 1] for h in hs]
    short_rows = [row_of(r.short_aux[h]) for h in hs]
    probs, grad_scores = score_grads(short_keys, short_values, short_queries, short_grads, short_rows, seen)
    short_dq = [(pair_rows(dot_columns(short_keys[n], grad_scores[n])) * scale).T for n in each]
    short_dk = [dot(grad_scores[n], short_queries[n]) for n in each]
    short_dv = [dot(probs[n], short_grads[n]) for n in each]

    queries, grads = [head_pair(r.q[me, h]) for h in hs], [head_pair(r.do[me, h]) for h in hs]
    own_keys, own_values = [r.kv[me, h, 0] for h in hs], [r.kv[me, h, 1] for h in hs]
    own_rows = [row_of(r.aux[me, h]) for h in hs]
    probs, grad_scores = score_grads(own_keys, own_values, queries, grads, own_rows, causal(long, long))
    dq = [dot_columns(own_keys[n], grad_scores[n]) for n in each]
    dk = [dot(grad_scores[n], queries[n]) for n in each]
    dv = [dot(probs[n], grads[n]) for n in each]
    for n, h in enumerate(hs):
        for third, value in enumerate((short_dq[n], short_dk[n], short_dv[n])):
            put(h, third, long, value)
        r.dq[n], r.dk[n], r.dv[n] = dq[n], dk[n], dv[n]

    def earlier(first, size):
        at = pl.ds(first, size)
        for n, h in enumerate(hs):
            keys = r.kv[at, h, 0].reshape(size * long, 128)
            values = r.kv[at, h, 1].reshape(size * long, 128)
            _, (grad_scores,) = score_grads([keys], [values], [queries[n]], [grads[n]], [own_rows[n]], None)
            r.dq[n] += dot_columns(keys, grad_scores)

    runs(n_dp - 1, me, earlier)
    for n, h in enumerate(hs):
        put(h, 0, 0, (pair_rows(r.dq[n]) * scale).T)
    for h in hs:
        do_spread.relay(h)
        aux_spread.relay(h)

    def later(first, size):
        blocks = [me + 1 + first + i for i in range(size)]
        for n, h in enumerate(hs):
            queries = jnp.concatenate([head_pair(r.q[block, h]) for block in blocks], axis=0)
            grads = jnp.concatenate([head_pair(r.do[block, h]) for block in blocks], axis=0)
            parts = [row_of(r.aux[block, h]) for block in blocks]
            rows = [jnp.concatenate([part[i] for part in parts], axis=1) for i in range(2)]
            (probs,), (grad_scores,) = score_grads([own_keys[n]], [own_values[n]], [queries], [grads], [rows], None)
            r.dk[n] += dot(grad_scores, queries)
            r.dv[n] += dot(probs, grads)

    for h in hs:
        aux_spread.each(h, lambda block: None)
        do_spread.each(h, lambda block: None)
    runs(n_dp - 1, n_dp - 1 - me, later)
    for n, h in enumerate(hs):
        put(h, 1, 0, r.dk[n])
        put(h, 2, 0, r.dv[n])


def back_scratch(n_dp, pairs, long, short):
    return (
        [
            pltpu.VMEM((n_dp, pairs, long, 128), jnp.bfloat16),
            pltpu.VMEM((n_dp, pairs, 8, long), jnp.float32),
            pltpu.VMEM((pairs, short, 128), jnp.bfloat16),
            pltpu.VMEM((pairs, 8, short), jnp.float32),
            pltpu.VMEM((2, 128, 2 * long), jnp.float32),
            pltpu.VMEM((2, long, 128), jnp.float32),
            pltpu.VMEM((2, long, 128), jnp.float32),
        ]
        + spread_sems(n_dp, pairs)
        + spread_sems(n_dp, pairs)
    )


def lane_plan(n_dp, n_ex, rows, order):
    dp_levels = [("dp", b) for b in range(n_dp.bit_length() - 1)]
    ex_levels = n_ex.bit_length() - 1
    halved, piece = [], rows
    for level in ((0, 1), (1, 0))[order]:
        if level < ex_levels and piece % 32 == 0:
            halved.append(level)
            piece //= 2
    halves = [("half", b) for b in halved]
    if order:
        kinds = dp_levels[:1] + halves[:1] + dp_levels[1:] + halves[1:]
    else:
        kinds = dp_levels + halves
    kinds += [("both", b) for b in range(ex_levels) if b not in halved]
    kinds += [("back", b) for b in reversed(halved)]
    return kinds, halved


class Lane:
    def __init__(self, n_dp, n_ex, rows, columns, order, refs):
        self.rows, self.columns = rows, columns
        self.kinds, self.halved = lane_plan(n_dp, n_ex, rows, order)
        self.count = len(self.kinds)
        moving = [k[0] != "back" for k in self.kinds]
        self.send = [next(refs) if m else None for m in moving]
        self.recv = [next(refs) if m else None for m in moving]
        self.keep = [next(refs) if m else None for m in moving]
        self.fin = next(refs)
        self.send_sems = [next(refs) for _ in moving]
        self.recv_sems = [next(refs) for _ in moving]
        self.d, self.e = lax.axis_index("dp"), lax.axis_index("expert")

    @staticmethod
    def scratch(n_dp, n_ex, rows, columns, order):
        kinds, halved = lane_plan(n_dp, n_ex, rows, order)
        width, pieces, height, shapes = columns[1] - columns[0], n_dp, rows, []
        for kind, _ in kinds:
            if kind == "dp":
                pieces //= 2
            elif kind == "half":
                height //= 2
            if kind != "back":
                shapes.append((pieces, height, width))
        scratch = [pltpu.VMEM((2,) + s, jnp.bfloat16) for s in shapes]
        scratch += [pltpu.VMEM((4,) + s, jnp.bfloat16) for s in shapes]
        scratch += [pltpu.VMEM((2,) + s, jnp.float32) for s in shapes]
        scratch += [pltpu.VMEM((len(halved) + 3, rows, width) if halved else (1, 16, 128), jnp.bfloat16)]
        return scratch + [pltpu.SemaphoreType.DMA((4,)) for _ in kinds] * 2

    def peer(self, kind, level):
        return (flip(self.d, level), self.e) if kind == "dp" else (self.d, flip(self.e, level))

    def kept_rows(self, depth):
        start = 0
        for i, level in enumerate(self.halved[:depth]):
            start = start + bit_of(self.e, level) * (self.rows >> (i + 1))
        return start

    def copy_of(self, s, c):
        kind, level = self.kinds[s]
        slot, place = lax.rem(c, 2), lax.rem(c, 4)
        if kind == "back":
            depth = self.halved.index(level) + 1
            span = self.rows >> depth
            at = pl.ds(pl.multiple_of(self.kept_rows(depth), span), span)
            src = self.fin.at[lax.rem(c, len(self.halved) + 3), at]
            dst = src
        else:
            src, dst = self.send[s].at[slot], self.recv[s].at[place]
        return pltpu.make_async_remote_copy(
            src_ref=src,
            dst_ref=dst,
            send_sem=self.send_sems[s].at[place],
            recv_sem=self.recv_sems[s].at[place],
            device_id=self.peer(kind, level),
            device_id_type=MESH,
        )

    def arrive(self, s, c):
        self.copy_of(s, c).wait()
        slot, place = lax.rem(c, 2), lax.rem(c, 4)
        if self.kinds[s][0] == "back":
            return None
        return [
            self.keep[s][slot, i] + self.recv[s][place, i].astype(jnp.float32) for i in range(self.keep[s].shape[1])
        ]

    def leave(self, s, c, values):
        kind, level = self.kinds[s]
        slot = lax.rem(c, 2)
        kept = None
        if kind == "dp":
            sent, kept = values[1::2], values[0::2]
        elif kind == "half":
            half = values[0].shape[0] // 2
            own = bit_of(self.e, level)
            sent = [jnp.where(own == 0, v[half:], v[:half]) for v in values]
            kept = [jnp.where(own == 0, v[:half], v[half:]) for v in values]
        elif kind == "both":
            sent = values
            kept = [v.astype(jnp.bfloat16).astype(jnp.float32) for v in values]
        elif values is not None:
            span = values[0].shape[0]
            at = pl.ds(pl.multiple_of(self.kept_rows(len(self.halved)), span), span)
            self.fin[lax.rem(c, len(self.halved) + 3), at] = values[0].astype(jnp.bfloat16)
        if kept is not None:
            for i, v in enumerate(sent):
                self.send[s][slot, i] = v.astype(jnp.bfloat16)
        self.copy_of(s, c).start()
        if kept is not None:
            for i, v in enumerate(kept):
                self.keep[s][slot, i] = v

    def final(self, c):
        values = self.arrive(self.count - 1, c)
        if values is None:
            return self.fin[lax.rem(c, len(self.halved) + 3)]
        return values[0].astype(jnp.bfloat16)


class Reduction:
    def __init__(self, n_dp, n_ex, rows, groups, lanes, refs, out):
        self.n_dp, self.rows, self.groups = n_dp, rows, groups
        self.lanes = [Lane(n_dp, n_ex, rows, columns, order, refs) for columns, order in lanes]
        self.stage_ref, self.stage_sem, self.out = next(refs), next(refs), out
        self.count = self.lanes[0].count
        self.chunks = sum(g[0] for g in groups)
        self.firsts = [sum(g[0] for g in groups[:i]) for i in range(len(groups))]
        self.ticks = self.chunks + self.count
        self.d = lax.axis_index("dp")
        self.peer = self.lanes[0].peer

    @staticmethod
    def scratch(n_dp, n_ex, rows, width, lanes):
        scratch = []
        for columns, order in lanes:
            scratch += Lane.scratch(n_dp, n_ex, rows, columns, order)
        return scratch + [pltpu.VMEM((2, rows, width), jnp.bfloat16), pltpu.SemaphoreType.DMA((2,))]

    def out_copy(self, c):
        slot = lax.rem(c, 2)
        return pltpu.make_async_copy(self.stage_ref.at[slot], self.out.at[c], self.stage_sem.at[slot])

    def first(self, g, c):
        _, piece, factor = self.groups[g]
        j = c - self.firsts[g]
        dy = factor(j)
        slot = lax.rem(c, 2)
        levels = self.n_dp.bit_length() - 1
        half = self.n_dp // 2

        def products(odd):
            parts = [piece(j, partner_index(self.d, 2 * i + odd, levels)) for i in range(half)]
            return dot(jnp.concatenate(parts, axis=0), dy)

        value = products(1)
        for lane in self.lanes:
            for i in range(half):
                part = value[i * self.rows : (i + 1) * self.rows, slice(*lane.columns)]
                lane.send[0][slot, i] = part.astype(jnp.bfloat16)
            lane.copy_of(0, c).start()
        value = products(0)
        for lane in self.lanes:
            for i in range(half):
                lane.keep[0][slot, i] = value[i * self.rows : (i + 1) * self.rows, slice(*lane.columns)]

    def last(self, c):
        slot = lax.rem(c, 2)

        @pl.when(c >= 2)
        def _():
            self.out_copy(c - 2).wait()

        for lane in self.lanes:
            self.stage_ref[slot, :, slice(*lane.columns)] = lane.final(c)
        self.out_copy(c).start()

    def tick(self, t, low, high):
        for s in range(self.count + 1):
            if high - s <= 0 or low - s >= self.chunks:
                continue
            c = t - s
            if s > 0:

                @pl.when((c >= 0) & (c < self.chunks))
                def _(s=s, c=c):
                    if s < self.count:
                        for lane in self.lanes:
                            lane.leave(s, c, lane.arrive(s - 1, c))
                    else:
                        self.last(c)

                continue
            for g, (size, _, _) in enumerate(self.groups):
                begin, end = self.firsts[g], self.firsts[g] + size
                if high <= begin or low >= end:
                    continue

                @pl.when((c >= begin) & (c < end))
                def _(g=g):
                    self.first(g, c)

    def finish(self):
        for c in range(max(0, self.chunks - 2), self.chunks):
            self.out_copy(c).wait()


def dense_lanes(width):
    cut = width // 768 * 640
    return [((0, cut), 0), ((cut, width), 1)]


def middle_kernel(n_dp, n_ex, names, staged, *refs):
    r = types.SimpleNamespace(**dict(zip(names, refs)))
    extra = iter(refs[len(names) :])
    loads = types.SimpleNamespace()
    for name in staged:
        buffer, sem = next(extra), next(extra)
        setattr(loads, name, pltpu.make_async_copy(getattr(r, name), buffer, sem))
        setattr(r, name, buffer)
    w_in_ref, w_out_ref, weight_sem, factor_sem = (next(extra) for _ in range(4))
    rows_ref, send_ref, grad_ref, home_ref, result_ref = (next(extra) for _ in range(5))
    rows_t_ref, back_ref, active_t_ref, hidden_ref = (next(extra) for _ in range(4))
    dgate_ref, home_dgate_ref, stat_send, stat_recv, result_acc, grad_acc = (next(extra) for _ in range(6))
    (
        x_send_sem, x_recv_sem, grad_send_sem, grad_recv_sem, dgate_send_sem, dgate_recv_sem,
        result_send_sem, result_recv_sem, stat_send_sem, stat_recv_sem,
    ) = (next(extra) for _ in range(10))
    do_ref, aux_ref, short_do_ref, short_aux_ref, dq_ref, dk_ref, dv_ref = (next(extra) for _ in range(7))
    do_far, do_near, do_recv, aux_far, aux_near, aux_recv = (next(extra) for _ in range(6))
    links = Links(n_dp)
    d, e, me = links.me, links.expert, links.me
    shared = links.chips == 2
    if shared:
        peer_rows_ref, peer_cot_ref, peer_row_sems, peer_cot_sems = (next(extra) for _ in range(4))
    dp_levels, ex_levels = n_dp.bit_length() - 1, n_ex.bit_length() - 1
    tokens, width = r.stream.shape
    padded = send_ref.shape[1]
    blocks = r.expert_in.shape[1] // width
    pairs, long = r.kv.shape[1], r.kv.shape[3]
    group = min(max(4, 128 // padded), n_ex)
    groups = n_ex // group
    hops = [(flip(d, b), e) for b in range(dp_levels)] + [(d, flip(e, b)) for b in range(ex_levels)]

    def column(i):
        return pl.ds(i * width, width)

    expert_loads = [
        (
            pltpu.make_async_copy(r.expert_in.at[:, column(i)], w_in_ref.at[i], weight_sem.at[0, i]),
            pltpu.make_async_copy(r.expert_out.at[column(i), :], w_out_ref.at[i], weight_sem.at[1, i]),
        )
        for i in range(blocks)
    ]
    for both in expert_loads:
        for load in both:
            load.start()
    for name in staged:
        getattr(loads, name).start()
    greet(links.peers() + across_peers(n_ex))

    def peer_copy(source, target, sems):
        return pltpu.make_async_remote_copy(
            src_ref=source,
            dst_ref=target,
            send_sem=sems.at[0],
            recv_sem=sems.at[1],
            device_id=(flip(d, 1), e),
            device_id_type=MESH,
        )

    def row_copy(j):
        return peer_copy(rows_ref.at[j], peer_rows_ref.at[j], peer_row_sems.at[j])

    if shared:
        cot_copy = peer_copy(r.far_cot, peer_cot_ref, peer_cot_sems)
        cot_copy.start()

    unit, inverse = norm_parts(r.stream[...])
    routed = (unit * r.gains[3:4] + r.shifts[3:4]).astype(jnp.bfloat16)
    assign = r.assign[...]
    dispatch = dispatch_of(assign, n_ex)
    r.dispatch[...] = dispatch
    send_ref[...] = dot(dispatch, routed).astype(jnp.bfloat16).reshape(send_ref.shape)
    x_across = Across(n_ex, send_ref, rows_ref, x_send_sem, x_recv_sem)

    def place(k, i):
        return lax.rem(e // group + k, groups) * group + lax.rem(e + i, group)

    def source(k, i):
        return lax.rem(e // group + k, groups) * group + lax.rem(e + group - i, group)

    for i in range(group):
        if i:
            x_across.start(place(0, i))
        for k in range(1, groups):
            x_across.start(place(k, i))
    rows_ref[e] = send_ref[e]
    router = r.router[...]
    hot = chosen_rows(assign, n_ex)
    gate = jax.nn.sigmoid(jnp.sum(hot * dot_rows(router, routed), axis=0, keepdims=True))
    r.gate[...] = gate

    def stat_copy(i):
        return pltpu.make_async_remote_copy(
            src_ref=stat_send.at[i],
            dst_ref=stat_recv.at[i],
            send_sem=stat_send_sem.at[i],
            recv_sem=stat_recv_sem.at[i],
            device_id=hops[i],
            device_id_type=MESH,
        )

    lane = lax.broadcasted_iota(jnp.int32, r.stats.shape, 1)
    stat_send[0] = jnp.where(
        lane == 0, jnp.sum(hot, axis=1, keepdims=True), jnp.sum(hot * gate, axis=1, keepdims=True)
    )
    stat_copy(0).start()

    def stat_step(i):
        stat_copy(i).wait()
        value = stat_send[i] + stat_recv[i]
        if i + 1 < len(hops):
            stat_send[i + 1] = value
            stat_copy(i + 1).start()
        else:
            r.stats[...] = value

    grad_across = Across(n_ex, grad_ref, home_ref, grad_send_sem, grad_recv_sem)
    dgate_across = Across(n_ex, dgate_ref, home_dgate_ref, dgate_send_sem, dgate_recv_sem)
    steps = [[(k, i) for i in range(group)] for k in range(groups)]

    def expert_rows(rows, cot, at, whole):
        count = rows.shape[0]
        logits = dot_rows(rows, router)
        own = lax.broadcasted_iota(jnp.int32, logits.shape, 1) == e
        slot_gate = jax.nn.sigmoid(jnp.sum(jnp.where(own, logits, 0.0), axis=1, keepdims=True))
        back = (slot_gate * cot).astype(jnp.bfloat16)
        span = slice(at, at + count)
        back_ref[span] = back
        rows_t_ref[:, span] = rows.T
        if whole:
            result_acc[:count] = jnp.zeros((count, width), jnp.float32)
            grad_acc[:count] = jnp.zeros((count, width), jnp.float32)

        def block(i, _):
            cols = pl.ds(pl.multiple_of(i * width, width), width)
            active, slope = gelu_parts(dot(rows, w_in_ref[i]))
            active = active.astype(jnp.bfloat16)
            hidden = (slope * dot_rows(back, w_out_ref[i])).astype(jnp.bfloat16)
            active_t_ref[cols, span] = active.T
            hidden_ref[span, cols] = hidden
            if whole:
                result_acc[:count] += dot(active, w_out_ref[i])
                grad_acc[:count] += dot_rows(hidden, w_in_ref[i])
            return 0

        lax.fori_loop(0, blocks, block, 0)

    done, at = 0, 0
    for number, members in enumerate(steps):
        count = len(members) * padded
        sources = [source(k, i) for k, i in members]
        for (k, i), j in zip(members, sources):
            if (k, i) != (0, 0):
                x_across.wait_from(j)
            if shared:
                row_copy(j).start()
        rows = jnp.concatenate([rows_ref[j] for j in sources], axis=0)
        cot = jnp.concatenate([r.far_cot[j] for j in sources], axis=0).astype(jnp.float32)
        if number == 0:
            for both in expert_loads:
                for load in both:
                    load.wait()
        expert_rows(rows, cot, at, True)
        grad = grad_acc[:count].astype(jnp.bfloat16)
        result = result_acc[:count].astype(jnp.bfloat16)
        both = cot * result.astype(jnp.float32)
        high = both.astype(jnp.bfloat16)
        rest = both - high.astype(jnp.float32)
        ones = jnp.ones((16, width), jnp.bfloat16)
        dgate = dot_rows(ones, high) + dot_rows(ones, rest.astype(jnp.bfloat16))
        for m, (k, i) in enumerate(members):
            j, part = sources[m], slice(m * padded, (m + 1) * padded)
            grad_ref[j] = grad[part]
            result_ref[j] = result[part]
            dgate_ref[j, :, :padded] = dgate[:8, part]
            if (k, i) == (0, 0):
                home_ref[e] = grad_ref[e]
                home_dgate_ref[e] = dgate_ref[e]
            else:
                grad_across.start(j)
                dgate_across.start(j)
        at += count
        if done < len(hops):
            stat_step(done)
            done += 1

    if shared:
        cot_copy.wait()
        for k in range(groups):
            sources = [source(k, i) for i in range(group)]
            for j in sources:
                row_copy(j).wait()
            rows = jnp.concatenate([peer_rows_ref[j] for j in sources], axis=0)
            cot = jnp.concatenate([peer_cot_ref[j] for j in sources], axis=0).astype(jnp.float32)
            expert_rows(rows, cot, at, False)
            at += group * padded
            if done < len(hops):
                stat_step(done)
                done += 1

    thirds = [w_in_ref.at[i] for i in range(3)]
    in_loads = [
        pltpu.make_async_copy(r.attn_in.at[1, :, column(i)], third, weight_sem.at[0, i])
        for i, third in enumerate(thirds)
    ]
    out_load = pltpu.make_async_copy(r.attn_out.at[1], w_out_ref.at[0], weight_sem.at[1, 0])
    for load in in_loads + [out_load]:
        load.start()
    rows = width // n_dp

    def rows_of(ref, j, q):
        return ref[pl.ds(pl.multiple_of((q * (ref.shape[0] // width) + j) * rows, rows), rows), :]

    red, writes = None, []
    if shared:
        factors = ((rows_t_ref, r.rows_t), (back_ref, r.back), (active_t_ref, r.expert_active_t), (hidden_ref, r.expert_hidden))
        writes = [pltpu.make_async_copy(here, there, factor_sem.at[i]) for i, (here, there) in enumerate(factors)]
        for write in writes:
            write.start()
    else:
        factors = [
            (blocks, lambda j, q: rows_of(rows_t_ref, 0, q), lambda j: hidden_ref[:, pl.ds(pl.multiple_of(j * width, width), width)]),
            (blocks, lambda j, q: rows_of(active_t_ref, j, q), lambda j: back_ref[...]),
        ]
        red = Reduction(n_dp, 1, rows, factors, [((0, width), 0)], extra, r.chunks)
    early = 0
    if red:
        red.tick(0, 0, 1)
        early = 1
    while done < len(hops):
        stat_step(done)
        done += 1
    x_across.others(x_across.wait_to)
    if red:
        red.tick(1, 1, 2)
        early = 2
    dgate_across.wait_all()
    slot_grads = jnp.concatenate([home_dgate_ref[j, :, :padded] for j in range(n_ex)], axis=1)
    dgate = dot(split(slot_grads), r.dispatch[...])
    dgate = dgate[0:8] + dgate[8:16] + dgate[16:24]
    everyone = tokens * n_dp * n_ex
    share = jnp.sum(jnp.where(lane == 0, r.stats[...], 0.0), axis=1, keepdims=True) / everyone
    weight = balance_weight * n_ex * (share - 1.0 / n_ex) / everyone
    mean_gate = jnp.sum(jnp.where(lane == 1, r.stats[...], 0.0), axis=1, keepdims=True) / everyone
    balance = n_ex * jnp.sum((share - 1.0 / n_ex) * mean_gate, axis=0, keepdims=True)
    r.balance[...] = jnp.broadcast_to(balance, r.balance.shape)
    grad_gate = dgate[0:1] + jnp.sum(hot * weight, axis=0, keepdims=True)
    grad_logits = hot * (grad_gate * gate * (1.0 - gate))
    parts = split(grad_logits)
    product = dot(parts, routed)
    r.router_grad[...] = product[:n_ex] + product[n_ex : 2 * n_ex] + product[2 * n_ex :]
    grad_normed = dot_columns(parts, jnp.concatenate([router] * 3, axis=0))
    if red:
        red.tick(2, 2, 3)
        early = 3
    grad_across.wait_all()
    grad_normed = grad_normed + dot_columns(r.dispatch[...], home_ref[...].reshape(n_ex * padded, width))
    unit, inverse = norm_parts(r.stream[...])
    up = r.cot[...].astype(jnp.float32) + norm_back(unit, inverse, r.gains[3:4], grad_normed)
    r.sums[0:1] = jnp.sum(grad_normed * unit, axis=0, keepdims=True)
    r.sums[1:2] = jnp.sum(grad_normed, axis=0, keepdims=True)

    r.up_next[...] = up
    up_low = up.astype(jnp.bfloat16)
    r.up_low[...] = up_low
    out_load.wait()
    for name in staged:
        getattr(loads, name).wait()
    grad_context = dot_rows(up_low, w_out_ref[0]).astype(jnp.bfloat16)
    put_context_grads(grad_context, do_ref, short_do_ref, me, long)
    do_spread = Spread(links, lambda b, p: do_ref.at[b, p], pairs, False, do_far, do_near, do_recv)
    aux_spread = Spread(links, lambda b, p: aux_ref.at[b, p], pairs, False, aux_far, aux_near, aux_recv)
    put_row_terms(r.context, r.lse, grad_context, aux_ref, short_aux_ref, me, long)
    for h in range(pairs):
        do_spread.send(h)
        aux_spread.send(h)
    result_across = Across(n_ex, result_ref, r.result_home, result_send_sem, result_recv_sem)
    result_across.start_all()
    r.result_home[e] = result_ref[e]
    sequence = types.SimpleNamespace(
        doc_row=r.doc_row, kv=r.kv, q=r.q, short_kv=r.short_kv, short_q=r.short_q,
        do=do_ref, aux=aux_ref, short_do=short_do_ref, short_aux=short_aux_ref, dq=dq_ref, dk=dk_ref, dv=dv_ref,
        mixed=r.mixed,
    )

    def pair(i, _):
        attend_back_pairs(n_dp, me, width, sequence, do_spread, aux_spread, [2 * i, 2 * i + 1])
        if red:
            red.tick(early + 2 * i, early, early + pairs)
            red.tick(early + 2 * i + 1, early, early + pairs)
        return 0

    lax.fori_loop(0, pairs // 2, pair, 0)
    grad_normed = jnp.zeros((tokens, width), jnp.float32)
    for i, third in enumerate(thirds):
        in_loads[i].wait()
        grad_normed = grad_normed + dot_rows(r.mixed[:, i * width : (i + 1) * width], third[...])
    unit, inverse = norm_parts(r.attn_x[...])
    r.up_next[...] += norm_back(unit, inverse, r.gains[2:3], grad_normed)
    r.attn_sums[0:1] = jnp.sum(grad_normed * unit, axis=0, keepdims=True)
    r.attn_sums[1:2] = jnp.sum(grad_normed, axis=0, keepdims=True)

    if red:

        def rest(t, _):
            red.tick(t, early + pairs, red.ticks)
            return 0

        lax.fori_loop(early + pairs, red.ticks, rest, 0)
        red.finish()
    result_across.wait_all()
    for write in writes:
        write.wait()
    for h in range(pairs):
        do_spread.sent(h)
        aux_spread.sent(h)


def middle(n_dp, n_ex, collective_id, near, staged, far):
    arrays = {**near, **staged, **far}
    a = types.SimpleNamespace(**arrays)
    low, wide = jnp.bfloat16, jnp.float32
    tokens, width = a.stream.shape
    hidden = a.expert_in.shape[1]
    mixed = a.attn_in.shape[2]
    blocks, rows = hidden // width, width // n_dp
    long, short, pairs = LONG_DEV, tokens - LONG_DEV, width // 128
    _, padded = capacity_of(tokens, n_ex)
    slots = n_ex * padded
    group = min(max(4, 128 // padded), n_ex) * padded
    slab = (n_ex, padded, width)
    hops = (n_dp * n_ex).bit_length() - 1
    outs = dict(
        up_next=jax.ShapeDtypeStruct((tokens, width), wide),
        up_low=jax.ShapeDtypeStruct((tokens, width), low),
        mixed=jax.ShapeDtypeStruct((tokens, mixed), low),
        sums=jax.ShapeDtypeStruct((2, width), wide),
        attn_sums=jax.ShapeDtypeStruct((2, width), wide),
        router_grad=jax.ShapeDtypeStruct((n_ex, width), wide),
        stats=jax.ShapeDtypeStruct((n_ex, 128), wide),
        balance=jax.ShapeDtypeStruct((1, 128), wide),
        result_home=jax.ShapeDtypeStruct(slab, low),
        gate=jax.ShapeDtypeStruct((1, tokens), wide),
        dispatch=jax.ShapeDtypeStruct((slots, tokens), low),
    )
    direct, shared = len(outs), n_dp == 4
    known = 2 * slots if shared else slots
    if shared:
        outs.update(
            rows_t=jax.ShapeDtypeStruct((width, known), low),
            back=jax.ShapeDtypeStruct((known, width), low),
            expert_active_t=jax.ShapeDtypeStruct((hidden, known), low),
            expert_hidden=jax.ShapeDtypeStruct((known, hidden), low),
        )
    else:
        outs.update(chunks=jax.ShapeDtypeStruct((2 * blocks, rows, width), low))
    scratch = []
    for name in staged:
        scratch += [pltpu.VMEM(arrays[name].shape, arrays[name].dtype), pltpu.SemaphoreType.DMA]
    scratch += [pltpu.VMEM((blocks, width, width), low)] * 2 + [pltpu.SemaphoreType.DMA((2, blocks)), pltpu.SemaphoreType.DMA((4,))]
    scratch += [pltpu.VMEM(slab, low)] * 5
    scratch += [
        pltpu.VMEM((width, known), low),
        pltpu.VMEM((known, width), low),
        pltpu.VMEM((hidden, known), low),
        pltpu.VMEM((known, hidden), low),
        pltpu.VMEM((n_ex, 8, 128), wide),
        pltpu.VMEM((n_ex, 8, 128), wide),
        pltpu.VMEM((hops, n_ex, 128), wide),
        pltpu.VMEM((hops, n_ex, 128), wide),
        pltpu.VMEM((group, width), wide),
        pltpu.VMEM((group, width), wide),
    ]
    scratch += [pltpu.SemaphoreType.DMA((n_ex,))] * 8 + [pltpu.SemaphoreType.DMA((hops,))] * 2
    scratch += back_scratch(n_dp, pairs, long, short)
    if shared:
        scratch += [pltpu.VMEM(slab, low)] * 2 + [pltpu.SemaphoreType.DMA((n_ex, 2)), pltpu.SemaphoreType.DMA((2,))]
    else:
        scratch += Reduction.scratch(n_dp, 1, rows, width, [((0, width), 0)])
    vmem, anywhere = pl.BlockSpec(memory_space=pltpu.VMEM), pl.BlockSpec(memory_space=pl.ANY)
    names = tuple(arrays) + tuple(outs)
    values = pl.pallas_call(
        functools.partial(middle_kernel, n_dp, n_ex, names, tuple(staged)),
        out_shape=list(outs.values()),
        in_specs=[vmem] * len(near) + [anywhere] * (len(staged) + len(far)),
        out_specs=[vmem] * direct + [anywhere] * (len(outs) - direct),
        scratch_shapes=scratch,
        compiler_params=pltpu.CompilerParams(
            collective_id=collective_id, has_side_effects=True, vmem_limit_bytes=62 * 1024 * 1024
        ),
        name="middle",
    )(*arrays.values())
    return types.SimpleNamespace(**dict(zip(outs, values)))


def tail_kernel(n_dp, n_ex, names, staged, *refs):
    r = types.SimpleNamespace(**dict(zip(names, refs)))
    extra = iter(refs[len(names) :])
    loads = types.SimpleNamespace()
    for name in staged:
        buffer, sem = next(extra), next(extra)
        setattr(loads, name, pltpu.make_async_copy(getattr(r, name), buffer, sem))
        setattr(r, name, buffer)
    weights_in, weights_out, slopes, weight_sem = (next(extra) for _ in range(4))
    first_sem = next(extra)
    acc_ref, dense_low_ref, dense_hidden_ref = (next(extra) for _ in range(3))
    up_ref, first_low_ref, mixed_ref = acc_ref, r.second_low, r.second_mixed
    do_ref, aux_ref, short_do_ref, short_aux_ref, dq_ref, dk_ref, dv_ref = (next(extra) for _ in range(7))
    do_far, do_near, do_recv, aux_far, aux_near, aux_recv = (next(extra) for _ in range(6))
    small_send, small_recv, small_send_sem, small_recv_sem = (next(extra) for _ in range(4))
    shared = n_dp == 4
    if shared:
        expert_x, expert_y, expert_sem = (next(extra) for _ in range(3))
    links = Links(n_dp)
    me = links.me
    width = up_ref.shape[1]
    rows = width // n_dp
    pairs, long = r.kv.shape[1], r.kv.shape[3]
    blocks = r.dense_in.shape[1] // width
    per_in = mixed_ref.shape[1] // width

    def block_loads(i):
        slot = lax.rem(i, 2)
        at = pl.ds(pl.multiple_of(i * width, width), width)
        return [
            pltpu.make_async_copy(r.dense_out.at[at, :], weights_out.at[slot], weight_sem.at[slot, 0]),
            pltpu.make_async_copy(r.dense_in.at[:, at], weights_in.at[slot], weight_sem.at[slot, 1]),
            pltpu.make_async_copy(r.slope.at[:, at], slopes.at[slot], weight_sem.at[slot, 2]),
        ]

    ready = (loads.second_context_t, loads.second_low, loads.second_normed_t, loads.second_mixed)
    for load in ready:
        load.start()
    for i in range(min(2, blocks)):
        for load in block_loads(i):
            load.start()
    loads.active_t.start()
    for name in staged:
        if all(getattr(loads, name) is not load for load in ready + (loads.active_t,)):
            getattr(loads, name).start()
    free, busy = blocks % 2, (blocks - 1) % 2
    out_load = pltpu.make_async_copy(r.attn_out.at[0], weights_out.at[free], first_sem.at[0])
    thirds = [weights_in.at[free], weights_in.at[busy], weights_out.at[busy]]
    in_loads = [
        pltpu.make_async_copy(r.attn_in.at[0, :, pl.ds(i * width, width)], third, first_sem.at[1 + i])
        for i, third in enumerate(thirds)
    ]

    def columns(ref):
        return lambda j: ref[:, pl.ds(pl.multiple_of(j * width, width), width)]

    def one(ref):
        return lambda j, q: ref[q, 0]

    groups = [
        (1, one(r.second_context_t), columns(r.second_low)),
        (per_in, one(r.second_normed_t), columns(r.second_mixed)),
        (blocks, lambda j, q: r.active_t[q, j], lambda j: dense_low_ref[...]),
        (blocks, one(r.dense_normed_t), columns(dense_hidden_ref)),
        (1, one(r.first_context_t), columns(first_low_ref)),
        (per_in, one(r.first_normed_t), columns(mixed_ref)),
    ]
    red = Reduction(n_dp, n_ex, rows, groups, dense_lanes(width), extra, r.chunks)
    if shared:
        expert_blocks = r.expert_hidden.shape[1] // width
        base = 2 * links.chip

        def expert_loads(c, act):
            slot = lax.rem(c, 2)

            def load(rows_t, at, per, factor):
                for q in range(2):
                    row = pl.multiple_of(((base + q) * per + at) * rows, rows)
                    act(pltpu.make_async_copy(rows_t.at[pl.ds(row, rows), :], expert_x.at[slot, q], expert_sem.at[slot, q]))
                act(pltpu.make_async_copy(factor, expert_y.at[slot], expert_sem.at[slot, 2]))

            @pl.when(c < expert_blocks)
            def _():
                load(r.rows_t, 0, 1, r.expert_hidden.at[:, pl.ds(pl.multiple_of(c * width, width), width)])

            @pl.when((c >= expert_blocks) & (c < 2 * expert_blocks))
            def _():
                load(r.expert_active_t, c - expert_blocks, expert_blocks, r.back)

        def expert_part(j, q):
            return expert_x[lax.rem(j, 2), q]

        expert_groups = [(2 * expert_blocks, expert_part, lambda j: expert_y[lax.rem(j, 2)])]
        expert_red = Reduction(2, 1, rows, expert_groups, [((0, width), 0)], extra, r.expert_chunks)
    levels = [("dp", b) for b in range(n_dp.bit_length() - 1)] + [("ex", b) for b in range(n_ex.bit_length() - 1)]
    greet([red.peer(*level) for level in levels] + (links.peers()[1:] if links.chips > 2 else []))

    up = r.up[...]
    dense_low_ref[...] = up.astype(jnp.bfloat16)
    acc_ref[...] = jnp.zeros_like(acc_ref)
    for load in ready:
        load.wait()
    red.tick(0, 0, 1)
    loads.active_t.wait()

    def dense(i, _):
        slot = lax.rem(i, 2)
        for load in block_loads(i):
            load.wait()
        grad = dot_rows(dense_low_ref[...], weights_out[slot]) * slopes[slot].astype(jnp.float32)
        grad = grad.astype(jnp.bfloat16)
        dense_hidden_ref[:, pl.ds(pl.multiple_of(i * width, width), width)] = grad
        acc_ref[...] += dot_rows(grad, weights_in[slot])

        @pl.when(i + 2 < blocks)
        def _():
            for load in block_loads(i + 2):
                load.start()

        @pl.when(i == blocks - 2)
        def _():
            out_load.start()
            in_loads[0].start()

        red.tick(1 + i, 1, 1 + blocks)
        return 0

    lax.fori_loop(0, blocks, dense, 0)
    for load in in_loads[1:]:
        load.start()
    for name in staged:
        if all(getattr(loads, name) is not load for load in ready + (loads.active_t,)):
            getattr(loads, name).wait()
    unit, inverse = norm_parts(r.dense_x[...])
    grad_normed = acc_ref[...]
    up = up + norm_back(unit, inverse, r.gains[1:2], grad_normed)
    up_ref[...] = up
    for first, sums in ((2, r.second_sums), (3, r.last_sums)):
        small_send[0, first : first + 1] = sums[0:1]
        small_send[0, first + 4 : first + 5] = sums[1:2]
    small_send[0, 8:] = r.router_grad[...]
    small_send[0, 1:2] = jnp.sum(grad_normed * unit, axis=0, keepdims=True)
    small_send[0, 5:6] = jnp.sum(grad_normed, axis=0, keepdims=True)
    at_tick = 1 + blocks

    scale = HEAD_DIM ** (-0.5)
    up_low = up.astype(jnp.bfloat16)
    first_low_ref[...] = up_low
    out_load.wait()
    grad_context = dot_rows(up_low, weights_out[free]).astype(jnp.bfloat16)
    red.tick(at_tick, at_tick, at_tick + 1)
    at_tick += 1
    put_context_grads(grad_context, do_ref, short_do_ref, me, long)
    do_spread = Spread(links, lambda b, p: do_ref.at[b, p], pairs, False, do_far, do_near, do_recv)
    aux_spread = Spread(links, lambda b, p: aux_ref.at[b, p], pairs, False, aux_far, aux_near, aux_recv)
    put_row_terms(r.context, r.lse, grad_context, aux_ref, short_aux_ref, me, long)
    for h in range(pairs):
        do_spread.send(h)
        aux_spread.send(h)
    red.tick(at_tick, at_tick, at_tick + 1)
    at_tick += 1
    sequence = types.SimpleNamespace(
        doc_row=r.doc_row, kv=r.kv, q=r.q, short_kv=r.short_kv, short_q=r.short_q,
        do=do_ref, aux=aux_ref, short_do=short_do_ref, short_aux=short_aux_ref, dq=dq_ref, dk=dk_ref, dv=dv_ref,
        mixed=mixed_ref,
    )

    def pair(i, _):
        red.tick(at_tick + 2 * i, at_tick, at_tick + pairs)
        attend_back_pairs(n_dp, me, width, sequence, do_spread, aux_spread, [2 * i, 2 * i + 1])
        red.tick(at_tick + 2 * i + 1, at_tick, at_tick + pairs)
        return 0

    lax.fori_loop(0, pairs // 2, pair, 0)
    at_tick += pairs
    red.tick(at_tick, at_tick, at_tick + 1)
    at_tick += 1
    grad_normed = jnp.zeros((up_ref.shape[0], width), jnp.float32)
    for i, third in enumerate(thirds):
        in_loads[i].wait()
        grad_normed = grad_normed + dot_rows(mixed_ref[:, i * width : (i + 1) * width], third[...])
    unit, inverse = norm_parts(r.first_x[...].astype(jnp.float32))
    r.grad_tokens[...] = (
        up_ref[...] + norm_back(unit, inverse, r.gains[0:1], grad_normed)
    ).astype(jnp.bfloat16)
    small_send[0, 0:1] = jnp.sum(grad_normed * unit, axis=0, keepdims=True)
    small_send[0, 4:5] = jnp.sum(grad_normed, axis=0, keepdims=True)

    def small_copy(i):
        return pltpu.make_async_remote_copy(
            src_ref=small_send.at[i],
            dst_ref=small_recv.at[i],
            send_sem=small_send_sem.at[i],
            recv_sem=small_recv_sem.at[i],
            device_id=red.peer(*levels[i]),
            device_id_type=MESH,
        )

    small_copy(0).start()

    if shared:
        for c in range(2):
            expert_loads(jnp.int32(c), lambda copy: copy.start())

    def rest(t, _):
        red.tick(t, at_tick, red.ticks)
        if shared:
            c = t - at_tick
            expert_loads(c, lambda copy: copy.wait())
            expert_red.tick(c, 0, red.ticks - at_tick)
            expert_loads(c + 2, lambda copy: copy.start())

        @pl.when(t == red.ticks - 2)
        def _():
            gate = jnp.broadcast_to(r.gate[...], (128, r.gate.shape[1])).T[:, 0:1]
            for first in range(0, width, 256):
                at = slice(first, first + 256)
                home = r.result_home[:, :, at].reshape(r.dispatch.shape[0], 256)
                result = dot_columns(r.dispatch[...], home)
                r.output[:, at] = (r.last_x[:, at] + gate * result).astype(jnp.bfloat16)

        for i in range(1, len(levels) + 1):

            @pl.when(t == at_tick + i)
            def _(i=i):
                small_copy(i - 1).wait()
                value = small_send[i - 1] + small_recv[i - 1]
                if i < len(levels):
                    small_send[i] = value
                    small_copy(i).start()
                else:
                    own = jnp.zeros((value.shape[0], rows), jnp.float32)
                    for q in range(n_dp):
                        own = own + jnp.where(me == q, value[:, q * rows : (q + 1) * rows], 0.0)
                    r.small_sum[...] = own

        return 0

    lax.fori_loop(at_tick, red.ticks, rest, 0)
    if shared:
        for c in range(red.ticks - at_tick, expert_red.ticks):
            expert_loads(jnp.int32(c), lambda copy: copy.wait())
            expert_red.tick(jnp.int32(c), c, c + 1)
            expert_loads(jnp.int32(c + 2), lambda copy: copy.start())
        expert_red.finish()
    red.finish()
    for h in range(pairs):
        do_spread.sent(h)
        aux_spread.sent(h)


def tail(n_dp, n_ex, collective_id, near, staged, far):
    arrays = {**near, **staged, **far}
    a = types.SimpleNamespace(**arrays)
    low, wide = jnp.bfloat16, jnp.float32
    tokens, width = a.up.shape
    hidden = a.dense_in.shape[1]
    mixed = a.attn_in.shape[2]
    rows = width // n_dp
    long, short, pairs = LONG_DEV, tokens - LONG_DEV, width // 128
    chunks = 2 * (hidden // width) + 2 * (1 + mixed // width)
    small = (8 + a.router_grad.shape[0], width)
    outs = dict(
        grad_tokens=jax.ShapeDtypeStruct((tokens, width), low),
        output=jax.ShapeDtypeStruct((tokens, width), low),
        small_sum=jax.ShapeDtypeStruct((small[0], rows), wide),
    )
    direct, shared = len(outs), n_dp == 4
    outs.update(chunks=jax.ShapeDtypeStruct((chunks, rows, width), low))
    if shared:
        slots, expert_hidden = a.expert_hidden.shape
        outs.update(expert_chunks=jax.ShapeDtypeStruct((2 * expert_hidden // width, rows, width), low))
    scratch = []
    for name in staged:
        scratch += [pltpu.VMEM(arrays[name].shape, arrays[name].dtype), pltpu.SemaphoreType.DMA]
    scratch += [pltpu.VMEM((2, width, width), low)] * 2
    scratch += [pltpu.VMEM((2, tokens, width), low), pltpu.SemaphoreType.DMA((2, 3))]
    scratch += [pltpu.SemaphoreType.DMA((4,))]
    scratch += [pltpu.VMEM((tokens, width), wide)]
    scratch += [pltpu.VMEM((tokens, n), low) for n in (width, hidden)]
    scratch += back_scratch(n_dp, pairs, long, short)
    hops = (n_dp * n_ex).bit_length() - 1
    scratch += [pltpu.VMEM((hops,) + small, wide)] * 2 + [pltpu.SemaphoreType.DMA((hops,))] * 2
    if shared:
        scratch += [pltpu.VMEM((2, 2, rows, slots), low), pltpu.VMEM((2, slots, width), low)]
        scratch += [pltpu.SemaphoreType.DMA((2, 3))]
    scratch += Reduction.scratch(n_dp, n_ex, rows, width, dense_lanes(width))
    if shared:
        scratch += Reduction.scratch(2, 1, rows, width, [((0, width), 0)])
    vmem, anywhere = pl.BlockSpec(memory_space=pltpu.VMEM), pl.BlockSpec(memory_space=pl.ANY)
    names = tuple(arrays) + tuple(outs)
    values = pl.pallas_call(
        functools.partial(tail_kernel, n_dp, n_ex, names, tuple(staged)),
        out_shape=list(outs.values()),
        in_specs=[vmem] * len(near) + [anywhere] * (len(staged) + len(far)),
        out_specs=[vmem] * direct + [anywhere] * (len(outs) - direct),
        scratch_shapes=scratch,
        compiler_params=pltpu.CompilerParams(
            collective_id=collective_id, has_side_effects=True, vmem_limit_bytes=62 * 1024 * 1024
        ),
        name="tail",
    )(*arrays.values())
    return types.SimpleNamespace(**dict(zip(outs, values)))


def shards(
    tokens,
    doc_lengths,
    assign,
    ln_gain,
    ln_bias,
    attn_in,
    attn_out,
    ffn_in,
    ffn_out,
    router,
    expert_in,
    expert_out,
    cotangent,
):
    n_dp, n_ex = lax.axis_size("dp"), lax.axis_size("expert")
    row_count = tokens.shape[1]
    lengths = doc_lengths[0, 0]
    order = jnp.arange(lengths.shape[0])
    doc_ends = jnp.sum(jnp.where(order[:, None] <= order[None, :], lengths[:, None], 0), axis=0)
    short_place = jnp.arange(row_count - LONG_DEV, dtype=jnp.int32)
    doc_row = jnp.sum((short_place[None, :] >= doc_ends[:, None]).astype(jnp.float32), axis=0, keepdims=True)
    weights_in, weights_out = lax.optimization_barrier((attn_in.transpose(1, 0, 2), attn_out.transpose(1, 0, 2)))
    gains, shifts = ln_gain.T, ln_bias.T
    assign_row = assign[0].T
    fore = front(
        n_dp,
        n_ex,
        2,
        dict(
            tokens=tokens[0],
            gains=gains,
            shifts=shifts,
            doc_row=doc_row,
            assign=assign_row,
            cot=cotangent[0],
        ),
        dict(attn_in=weights_in, attn_out=weights_out, dense_in=ffn_in, dense_out=ffn_out),
    )
    model_width = tokens.shape[2]
    rows = model_width // n_dp
    mid = middle(
        n_dp,
        n_ex,
        4,
        dict(
            stream=fore.stream2,
            gains=gains,
            shifts=shifts,
            router=router.T,
            assign=assign_row,
            cot=cotangent[0],
            far_cot=fore.far_cot,
            doc_row=doc_row,
            lse=fore.lse1,
        ),
        dict(
            attn_x=fore.stream1,
            context=fore.context1,
            kv=fore.kv1,
            q=fore.q1,
            short_kv=fore.short_kv1,
            short_q=fore.short_q1,
        ),
        dict(
            expert_in=expert_in[0],
            expert_out=expert_out[0],
            attn_in=weights_in,
            attn_out=weights_out,
        ),
    )
    def blocks_of(rows_t):
        return rows_t.reshape(n_dp, -1, rows, row_count)

    shared = n_dp == 4
    last = tail(
        n_dp,
        n_ex,
        5,
        dict(
            up=mid.up_next,
            gains=gains,
            doc_row=doc_row,
            lse=fore.lse0,
            second_sums=mid.attn_sums,
            last_sums=mid.sums,
            router_grad=mid.router_grad,
            dispatch=mid.dispatch,
            gate=mid.gate,
        ),
        dict(
            dense_x=fore.stream0,
            first_x=tokens[0],
            context=fore.context0,
            kv=fore.kv0,
            q=fore.q0,
            short_kv=fore.short_kv0,
            short_q=fore.short_q0,
            second_context_t=blocks_of(fore.context_t1),
            second_normed_t=blocks_of(fore.normed_t1),
            active_t=blocks_of(fore.active_t),
            dense_normed_t=blocks_of(fore.dense_normed_t),
            first_context_t=blocks_of(fore.context_t0),
            first_normed_t=blocks_of(fore.normed_t0),
            second_low=mid.up_low,
            result_home=mid.result_home,
            last_x=fore.stream2,
            second_mixed=mid.mixed,
        ),
        dict(
            dense_in=ffn_in,
            dense_out=ffn_out,
            slope=fore.slope,
            attn_in=weights_in,
            attn_out=weights_out,
            **(
                dict(
                    rows_t=mid.rows_t,
                    back=mid.back,
                    expert_active_t=mid.expert_active_t,
                    expert_hidden=mid.expert_hidden,
                )
                if shared
                else {}
            ),
        ),
    )
    expert_chunks = last.expert_chunks if shared else mid.chunks
    (
        attn_in_sum, attn_out_sum, ffn_in_sum, ffn_out_sum, expert_in_sum, expert_out_sum,
        gain_sum, shift_sum, router_sum, grad_tokens, output,
    ) = unpack(
        last.chunks, expert_chunks, last.small_sum, last.grad_tokens, last.output,
        attn_in.shape[2] // model_width, ffn_in.shape[1] // model_width,
    )
    return (
        output[None],
        mid.balance[0, 0],
        grad_tokens[None],
        gain_sum.T,
        shift_sum.T,
        attn_in_sum,
        attn_out_sum,
        ffn_in_sum,
        ffn_out_sum.reshape(-1, model_width),
        router_sum.T,
        expert_in_sum[None],
        expert_out_sum.reshape(1, -1, model_width),
    )


def solution(mesh):
    return jax.shard_map(
        shards,
        mesh=mesh,
        in_specs=(
            P("expert", "dp", None),
            P("expert", "dp", None),
            P("expert", "dp", None),
            P(),
            P(),
            P(),
            P(),
            P(),
            P(),
            P(),
            P("expert", None, None),
            P("expert", None, None),
            P("expert", "dp", None),
        ),
        out_specs=(
            P("expert", "dp", None),
            P(),
            P("expert", "dp", None),
            P("dp", None),
            P("dp", None),
            P("dp", None, None),
            P("dp", None, None),
            P("dp", None),
            P("dp", None),
            P("dp", None),
            P("expert", "dp", None),
            P("expert", "dp", None),
        ),
        check_vma=False,
    )
```
